32 devices in a mesh: ctx: 16 (over z, x, core), fsdp: 2 (over y).
Axes of the slice: x: 2, y: 2, z: 4, core: 2. Of those that a mesh axis runs over, the one named last changes fastest.
Arguments:
- hidden: bfloat16 [2, 4096, 1024], P('fsdp', 'ctx'), may hold values from -6 to 6
- out_grad: bfloat16 [2, 4096, 1024], P('fsdp', 'ctx'), may hold values from -6 to 6
- decay_log: float32 [2, 24, 4096], P('fsdp', None, 'ctx'), may hold values from -1.2 to 0, as said below
- doc_lengths: int32 [2, 2], P('fsdp'), may hold values from 1 to 3072, 4096 in all within a row
- weights: float32 [1024, 12288], P(('ctx', 'fsdp')), may hold values from -2 to 2
- first_moment: float32 [1024, 12288], P(('ctx', 'fsdp')), may hold values from -8 to 8
- second_moment: float32 [1024, 12288], P(('ctx', 'fsdp')), may hold values from 0.5 to 50
- small_params: float32 [12568], replicated, may hold values from -2 to 2, as said below
- small_first: float32 [12568], replicated, may hold values from -8 to 8
- small_second: float32 [12568], replicated, may hold values from 1 to 1000
Outputs:
- out_hidden: bfloat16 [2, 4096, 1024], P('fsdp', 'ctx')
- grad_hidden: float32 [2, 4096, 1024], P('fsdp', 'ctx')
- grad_weights: float32 [1024, 12288], P(('ctx', 'fsdp'))
- new_weights: float32 [1024, 12288], P(('ctx', 'fsdp'))
- new_first: float32 [1024, 12288], P(('ctx', 'fsdp'))
- new_second: float32 [1024, 12288], P(('ctx', 'fsdp'))
- small_grads: float32 [12568], replicated
- small_step: float32 [12568], replicated
- small_first_new: float32 [12568], replicated
- small_second_new: float32 [12568], replicated
The draws below stay inside these ranges and needn't reach their ends.
Inputs may be any that keep to these rules, and one draw needn't show every extreme that they name: `doc_lengths`: each row holds the lengths of the 2 documents of that sequence in order; they sum to 4096 and none is longer than 3072. `decay_log`: negative everywhere. `small_params`: the three gains and the skip gains are positive.
All inputs are finite; a program needn't handle non-finite values.
Results may differ from the reference program's by a relative error of at most 0.025.
Values may be sent and summed in bfloat16 or wider, within the bound.
A program may use at most 384 MiB of HBM per device.

```python
import math
import jax
import jax.numpy as jnp
import numpy as np
from jax import lax

D = 1024
QUERY_HEADS = 8
KEY_VALUE_HEADS = 2
HEAD_WIDTH = 64
MH = 24
MP = 64
NS = 128
FF = 2048
CONV = 4
DOCS = 2
STEP = 3
TOK_DEV = 256
SEQUENCE_LENGTH = 4096
SEQUENCE_COUNT = 2
QUERY_WIDTH = 512
KEY_WIDTH = 128
INNER = 1536
XBC = 1792
MIXIN = 4096
MIXOUT = 2048
COLS = 12288
SMALL = 12568


def draw_hidden(key, part):
    drawn = jnp.clip(jax.random.normal(jax.random.fold_in(key, 2), (SEQUENCE_COUNT, SEQUENCE_LENGTH, D), jnp.float32), -6.0, 6.0)
    return drawn.astype(jnp.bfloat16)


def draw_weights(key, part):
    drawn = jnp.clip(jax.random.normal(jax.random.fold_in(key, 1), (D, COLS), jnp.float32), -6.0, 6.0)
    columns = jnp.arange(COLS)
    col_scale = jnp.where(columns < MIXIN, D ** (-0.5), jnp.where(columns < MIXIN + QUERY_WIDTH, 2.5 * QUERY_WIDTH ** (-0.5), jnp.where(columns < MIXIN + MIXOUT, INNER ** (-0.5), jnp.where(columns < MIXIN + MIXOUT + 2 * FF, D ** (-0.5), FF ** (-0.5)))))
    return drawn * col_scale[None, :]


def draw_decay_log(key, part):
    fast_share = 0.5
    fast_heads = jax.random.bernoulli(jax.random.fold_in(key, 21), fast_share, (SEQUENCE_COUNT, MH, 1))
    fast_rate = jnp.exp(jax.random.uniform(jax.random.fold_in(key, 22), (SEQUENCE_COUNT, MH, 1), jnp.float32, math.log(1.0 / 50.0), math.log(1.0 / 30.0)))
    slow_rate = jnp.exp(jax.random.uniform(jax.random.fold_in(key, 23), (SEQUENCE_COUNT, MH, 1), jnp.float32, math.log(0.2), 0.0)) / SEQUENCE_LENGTH
    rotary_base_rate = jnp.where(fast_heads, fast_rate, slow_rate)
    block_count = SEQUENCE_LENGTH // TOK_DEV
    block_multiplier = jnp.exp(jax.random.uniform(jax.random.fold_in(key, 24), (SEQUENCE_COUNT, MH, block_count, 1), jnp.float32, math.log(0.5), 0.0))
    block_multiplier = jnp.broadcast_to(block_multiplier, (SEQUENCE_COUNT, MH, block_count, TOK_DEV)).reshape(SEQUENCE_COUNT, MH, SEQUENCE_LENGTH)
    token_multiplier = jax.random.uniform(jax.random.fold_in(key, 25), (SEQUENCE_COUNT, MH, SEQUENCE_LENGTH), jnp.float32, 0.5, 1.5)
    spike_position = jax.random.randint(jax.random.fold_in(key, 26), (SEQUENCE_COUNT, 1, 2), 0, SEQUENCE_LENGTH)
    spike_keep_mask = jax.random.uniform(jax.random.fold_in(key, 27), (SEQUENCE_COUNT, 1, 2), jnp.float32, 0.6, 0.8)
    token_positions = jnp.arange(SEQUENCE_LENGTH)[None, :, None]
    spike_log_scale = jnp.sum(jnp.where(token_positions == spike_position, jnp.log(spike_keep_mask), 0.0), axis=-1)
    return -rotary_base_rate * block_multiplier * token_multiplier + spike_log_scale[:, None, :]


def draw_small_params(key, part):
    uniforms = jax.random.uniform(jax.random.fold_in(key, 31), (SMALL,), jnp.float32, 0.0, 1.0)
    normals = jnp.clip(0.5 * jax.random.normal(jax.random.fold_in(key, 32), (SMALL,), jnp.float32), -2.0, 2.0)
    entries = jnp.arange(SMALL)
    gains_end = 2 * D + INNER
    conv_end = gains_end + CONV * XBC
    bias_end = conv_end + XBC
    return jnp.where(entries < gains_end, 0.5 + uniforms, jnp.where(entries < conv_end, normals, jnp.where(entries < bias_end, uniforms - 0.5, 0.5 + uniforms)))


def levels(key, shape, cuts, smallest, high):
    factor_of = 1.0
    for axis_at, parts in cuts:
        steps = jax.random.uniform(jax.random.fold_in(jax.random.fold_in(key, 6), axis_at), (parts,), jnp.float32, smallest / len(cuts), high / len(cuts))
        factor_of = factor_of * jnp.repeat(jnp.exp(steps), shape[axis_at] // parts).reshape((-1,) + (1,) * (len(shape) - 1 - axis_at))
    return factor_of


def split_up(amount, total, most, skew):
    loads = [(1 << 20) // math.isqrt(rank ** skew) + 1 for rank in range(2, amount + 1)]
    rest, given = total - most - (amount - 1), [1] * (amount - 1)
    while rest > 0:
        movable = [i for i in range(amount - 1) if given[i] < most]
        mass, remaining = sum([loads[i] for i in movable]), rest
        for i in movable:
            addition = min(most - given[i], max(1, remaining * loads[i] // mass), rest)
            given[i] = given[i] + addition
            rest = rest - addition
    return np.array([most] + given)


def ragged(stream_key, number_of, total, most, lean):
    if number_of == 2:
        one = jax.random.randint(stream_key, (), max(1, total - most), min(most, total - 1) + 1)
        return jnp.stack([one, total - one])
    sizes = jnp.asarray(split_up(number_of, total, most, lean), jnp.int32)
    twos = (number_of - 1) // 2
    donor, taker = sizes[1:1 + 2 * twos:2], sizes[2:2 + 2 * twos:2]
    room = jnp.minimum(donor - 1, most - taker)
    shifted = jax.random.randint(jax.random.fold_in(stream_key, 1), (twos,), 0, 1 << 20) % (room + 1)
    sizes = sizes.at[1:1 + 2 * twos:2].set(donor - shifted).at[2:2 + 2 * twos:2].set(taker + shifted)
    return sizes[jax.random.permutation(jax.random.fold_in(stream_key, 2), number_of)]


def centred(rng, shape, scale, bound, split=(), held_as=jnp.bfloat16):
    values = scale * jax.random.normal(rng, shape, jnp.float32)
    if split:
        values = values * levels(rng, shape, split, -0.22, 0.18)
    return jnp.clip(values, -bound, bound).astype(held_as)


def setup_inputs(seed: int = 0) -> dict:
    arg_keys = jax.random.split(jax.random.key(seed), 11)
    hidden = draw_hidden(jax.random.fold_in(arg_keys[10], 71), 0)
    out_grad = centred(arg_keys[1], (SEQUENCE_COUNT, SEQUENCE_LENGTH, D), 1.0, 6.0, ((0, 2), (1, 16)))
    decay_log = draw_decay_log(jax.random.fold_in(arg_keys[10], 71), 0)
    doc_lengths = jax.vmap(lambda own: ragged(own, DOCS, SEQUENCE_LENGTH, 3 * SEQUENCE_LENGTH // 4, 0))(jax.random.split(arg_keys[3], SEQUENCE_COUNT)).reshape((SEQUENCE_COUNT, DOCS)).astype(jnp.int32)
    weights = draw_weights(jax.random.fold_in(arg_keys[10], 71), 0)
    first_moment = centred(arg_keys[5], (D, COLS), 2.0, 8.0, ((0, 32),), jnp.float32)
    second_moment = jnp.clip(jnp.exp(math.log(50.0) - 4.6051702 * jax.random.uniform(arg_keys[6], (D, COLS), jnp.float32) ** levels(arg_keys[6], (D, COLS), ((0, 32),), -0.2, 0.2)), 0.5, 50.0)
    small_params = draw_small_params(jax.random.fold_in(arg_keys[10], 71), 0)
    small_first = centred(arg_keys[8], (SMALL,), 2.0, 8.0, (), jnp.float32)
    small_second = jnp.clip(jnp.exp(jax.random.uniform(arg_keys[9], (SMALL,), jnp.float32, math.log(1.0), math.log(1000.0))), 1.0, 1000.0)
    return dict(hidden=hidden, out_grad=out_grad, decay_log=decay_log, doc_lengths=doc_lengths, weights=weights, first_moment=first_moment, second_moment=second_moment, small_params=small_params, small_first=small_first, small_second=small_second)


norm_eps = 1e-05
rope_base = 100000000000.0
large_negative = -1e+30
learn_rate = 0.02
beta_one = 0.9
beta_two = 0.95
adam_eps = 1e-08
decay_rate = 0.1
highest = lax.Precision.HIGHEST

def round_trip(values):
    return lax.optimization_barrier(values.astype(jnp.bfloat16)).astype(jnp.float32)

def doc_layout(lengths, token_positions):
    starts = (jnp.cumsum(lengths) - lengths).astype(jnp.int32)
    inside = token_positions[:, None] >= starts[None, :]
    document_index = (lax.optimization_barrier(jnp.sum(inside.astype(jnp.int32), axis=1)) - 1).astype(jnp.int32)
    begins = lax.optimization_barrier(jnp.max(jnp.where(inside, starts[None, :], 0), axis=1))
    return (document_index, (token_positions - begins).astype(jnp.int32))

def rope_tables(rel_pos):
    half_dim = HEAD_WIDTH // 2
    inv_freq = rope_base ** (-2.0 * jnp.arange(half_dim, dtype=jnp.float32) / HEAD_WIDTH)
    angles = rel_pos.astype(jnp.float32)[:, None] * inv_freq[None, :]
    return (jnp.cos(angles), jnp.sin(angles))

def apply_rotary(values, cosine_table, sine_table):
    half_dim = values.shape[-1] // 2
    lower_half = values[..., :half_dim]
    upper_half = values[..., half_dim:]
    cos_rows = cosine_table[:, None, :]
    sin_rows = sine_table[:, None, :]
    return jnp.concatenate([lower_half * cos_rows - upper_half * sin_rows, upper_half * cos_rows + lower_half * sin_rows], axis=-1)

def inverse_rotary(grads, cosine_table, sine_table):
    half_dim = grads.shape[-1] // 2
    lower_half = grads[..., :half_dim]
    upper_half = grads[..., half_dim:]
    cos_rows = cosine_table[:, None, :]
    sin_rows = sine_table[:, None, :]
    return jnp.concatenate([lower_half * cos_rows + upper_half * sin_rows, upper_half * cos_rows - lower_half * sin_rows], axis=-1)

def split_small(vector):
    widths = (D, D, INNER, CONV * XBC, XBC, MH)
    pieces = []
    offset = 0
    for span_width in widths:
        pieces.append(vector[offset:offset + span_width])
        offset += span_width
    return (pieces[0], pieces[1], pieces[2], pieces[3].reshape(CONV, XBC), pieces[4], pieces[5])

def conv_block(xbc_ext, doc_ext, document_index, conv_weights, conv_biases):
    rows_out = document_index.shape[0]
    summed = jnp.broadcast_to(conv_biases[None, :], (rows_out, conv_biases.shape[0]))
    for tap_index in range(conv_weights.shape[0]):
        same_doc = (doc_ext[tap_index:tap_index + rows_out] == document_index).astype(xbc_ext.dtype)[:, None]
        summed = summed + conv_weights[tap_index][None, :] * xbc_ext[tap_index:tap_index + rows_out] * same_doc
    return jax.nn.silu(summed)

def scan_consts(log_decay, is_start, document_index, doc_before):
    cum_decay = jnp.cumsum(log_decay, axis=1)
    steps_in = jnp.where(is_start[None, :], jnp.float32(1.0), jnp.sqrt(-jnp.expm1(2.0 * log_decay)))
    row_order = jnp.arange(document_index.shape[0], dtype=jnp.int32)
    same_mask = (document_index[:, None] == document_index[None, :]) & (row_order[None, :] <= row_order[:, None])
    spread = jnp.minimum(cum_decay[:, :, None] - cum_decay[:, None, :], 0.0)
    decay_mat = jnp.where(same_mask[None], jnp.exp(spread), 0.0)
    decay_in = jnp.where((document_index == doc_before)[None, :], jnp.exp(cum_decay), 0.0)
    return (decay_mat, steps_in, decay_in)

def split_conv(conv_out):
    heads_x = conv_out[:, :INNER].reshape(conv_out.shape[0], MH, MP)
    return (heads_x, conv_out[:, INNER:INNER + NS], conv_out[:, INNER + NS:])

def state_local(conv_out, consts):
    decay_mat, steps_in, decay_in = consts
    heads_x, b_rows, c_rows = split_conv(conv_out)
    weight_end = decay_mat[:, -1, :] * steps_in
    return jnp.einsum('hs,shp,sn->hpn', weight_end, heads_x, b_rows, precision=highest)

def out_local(conv_out, state_vals, skip_vals, consts):
    decay_mat, steps_in, decay_in = consts
    heads_x, b_rows, c_rows = split_conv(conv_out)
    intersection = jnp.dot(c_rows, b_rows.T, precision=highest)
    mixing = decay_mat * intersection[None] * steps_in[:, None, :]
    within = jnp.einsum('hts,shp->thp', mixing, heads_x, precision=highest)
    carried = decay_in.T[:, :, None] * jnp.einsum('hpn,tn->thp', state_vals, c_rows, precision=highest)
    result = within + carried + skip_vals[None, :, None] * heads_x
    return result.reshape(result.shape[0], INNER)

def local_mamba(conv_out, skip_vals, log_decay, is_start, document_index, doc_before):
    total_length = conv_out.shape[0]
    block_length = math.gcd(total_length, 256)
    block_count = total_length // block_length
    prev_ids = jnp.concatenate([jnp.reshape(doc_before, (1,)).astype(jnp.int32), document_index[:-1]])
    befores = prev_ids.reshape(block_count, block_length)[:, 0]
    scan_result = (conv_out.reshape(block_count, block_length, XBC), jnp.transpose(log_decay.reshape(MH, block_count, block_length), (1, 0, 2)), is_start.reshape(block_count, block_length), document_index.reshape(block_count, block_length), befores)

    def advance(carried_state, blocks):
        xblock, lblock, sblock, dblock, before_doc = blocks
        consts = scan_consts(lblock, sblock, dblock, before_doc)
        result = out_local(xblock, carried_state, skip_vals, consts)
        carried_state = consts[2][:, -1][:, None, None] * carried_state + state_local(xblock, consts)
        return (carried_state, result)
    zero_state = jnp.zeros((MH, MP, NS), conv_out.dtype)
    final_state, mixed = lax.scan(advance, zero_state, scan_result)
    return (mixed.reshape(total_length, INNER), final_state)

def gate_norm(mixed, gate_vals, gain_vals):
    gated = mixed * jax.nn.silu(gate_vals)
    factor = lax.rsqrt(lax.optimization_barrier(jnp.mean(gated * gated, axis=1, keepdims=True)) + norm_eps)
    return gated * factor * gain_vals

def mamba_sequence(xbc_vals, gate_vals, conv_weights, conv_biases, skip_vals, gain_vals, log_decay, document_index, is_start):
    pad_rows = conv_weights.shape[0] - 1
    padded = jnp.concatenate([jnp.zeros((pad_rows, xbc_vals.shape[1]), xbc_vals.dtype), xbc_vals], axis=0)
    doc_ext = jnp.concatenate([jnp.full((pad_rows,), -1, jnp.int32), document_index])
    conv_out = conv_block(padded, doc_ext, document_index, conv_weights, conv_biases)
    mixed, final_state = local_mamba(conv_out, skip_vals, log_decay, is_start, document_index, jnp.int32(-1))
    return gate_norm(mixed, gate_vals, gain_vals)

def norm_backward(grad_normed, values, factor, gain_vals):
    weighted = grad_normed * gain_vals
    grad_values = factor * (weighted - values * factor * factor * lax.optimization_barrier(jnp.mean(weighted * values, axis=1, keepdims=True)))
    grad_gain = lax.optimization_barrier(jnp.sum(grad_normed * values * factor, axis=0))
    return (grad_values, grad_gain)

def adamw_step(param_vals, grad_vals, first_vals, second_vals, weight_decay):
    first_new = beta_one * first_vals + (1.0 - beta_one) * grad_vals
    second_new = beta_two * second_vals + (1.0 - beta_two) * grad_vals * grad_vals
    update = first_new / (1.0 - beta_one ** STEP) / (jnp.sqrt(second_new / (1.0 - beta_two ** STEP)) + adam_eps)
    return (param_vals - learn_rate * (update + weight_decay * param_vals), first_new, second_new)

def adam_direction(grad_vals, first_vals, second_vals):
    first_new = beta_one * first_vals + (1.0 - beta_one) * grad_vals
    second_new = beta_two * second_vals + (1.0 - beta_two) * grad_vals * grad_vals
    update = first_new / (1.0 - beta_one ** STEP) / (jnp.sqrt(second_new / (1.0 - beta_two ** STEP)) + adam_eps)
    return (update, first_new, second_new)

def attention_forward(query_rows, key_row_values, value_row_values, document_index, token_positions):
    total_length = query_rows.shape[0]
    query_groups = QUERY_HEADS // KEY_VALUE_HEADS
    block_length = math.gcd(total_length, 512)
    block_count = total_length // block_length
    key_f = key_row_values.astype(jnp.float32)
    value_f = value_row_values.astype(jnp.float32)

    def one_block(blocks):
        q_blk, q_pos, q_doc = blocks
        scores = jnp.einsum('tgqd,sgd->tgqs', q_blk.astype(jnp.float32), key_f, precision=highest) * HEAD_WIDTH ** (-0.5)
        allowed = ((token_positions[None, :] <= q_pos[:, None]) & (document_index[None, :] == q_doc[:, None]))[:, None, None, :]
        row_top = lax.optimization_barrier(jnp.max(jnp.where(allowed, scores, large_negative), axis=-1, keepdims=True))
        log_sum_exp = row_top + jnp.log(lax.optimization_barrier(jnp.sum(jnp.where(allowed, jnp.exp(scores - row_top), 0.0), axis=-1, keepdims=True)))
        probs_b = round_trip(jnp.where(allowed, jnp.exp(scores - log_sum_exp), 0.0))
        attention_result = jnp.einsum('tgqs,sgd->tgqd', probs_b, value_f, precision=highest).astype(jnp.bfloat16)
        return (attention_result, log_sum_exp[..., 0])
    query_blocks = query_rows.reshape(block_count, block_length, KEY_VALUE_HEADS, query_groups, HEAD_WIDTH)
    attention_result, log_sum_exp = lax.map(one_block, (query_blocks, token_positions.reshape(block_count, block_length), document_index.reshape(block_count, block_length)))
    return (attention_result.reshape(total_length, KEY_VALUE_HEADS, query_groups, HEAD_WIDTH), log_sum_exp.reshape(total_length, KEY_VALUE_HEADS, query_groups))

def attention_backward(query_rows, key_row_values, value_row_values, attention_result, attention_gradient, log_sum_exp, document_index, token_positions):
    total_length = query_rows.shape[0]
    query_groups = QUERY_HEADS // KEY_VALUE_HEADS
    block_length = math.gcd(total_length, 512)
    block_count = total_length // block_length
    key_f = key_row_values.astype(jnp.float32)
    value_f = value_row_values.astype(jnp.float32)
    grouped_gradient = attention_gradient.reshape(total_length, KEY_VALUE_HEADS, query_groups, HEAD_WIDTH)
    row_correction = lax.optimization_barrier(jnp.sum(grouped_gradient.astype(jnp.float32) * attention_result.astype(jnp.float32), axis=-1))

    def one_block(carried, blocks):
        grad_key, grad_value = carried
        q_blk, g_blk, l_blk, d_blk, q_pos, q_doc = blocks
        q_f = q_blk.astype(jnp.float32)
        g_f = g_blk.astype(jnp.float32)
        scores = jnp.einsum('tgqd,sgd->tgqs', q_f, key_f, precision=highest) * HEAD_WIDTH ** (-0.5)
        allowed = ((token_positions[None, :] <= q_pos[:, None]) & (document_index[None, :] == q_doc[:, None]))[:, None, None, :]
        probs_f = jnp.where(allowed, jnp.exp(scores - l_blk[..., None]), 0.0)
        probs_b = round_trip(probs_f)
        grad_prob = jnp.einsum('tgqd,sgd->tgqs', g_f, value_f, precision=highest)
        dscores = round_trip(probs_f * (grad_prob - d_blk[..., None]))
        grad_query = jnp.einsum('tgqs,sgd->tgqd', dscores, key_f, precision=highest) * HEAD_WIDTH ** (-0.5)
        grad_key = grad_key + jnp.einsum('tgqs,tgqd->sgd', dscores, q_f, precision=highest) * HEAD_WIDTH ** (-0.5)
        grad_value = grad_value + jnp.einsum('tgqs,tgqd->sgd', probs_b, g_f, precision=highest)
        return ((grad_key, grad_value), grad_query)
    initial_key_value = jnp.zeros((total_length, KEY_VALUE_HEADS, HEAD_WIDTH), jnp.float32)
    scan_result = (query_rows.reshape(block_count, block_length, KEY_VALUE_HEADS, query_groups, HEAD_WIDTH), grouped_gradient.reshape(block_count, block_length, KEY_VALUE_HEADS, query_groups, HEAD_WIDTH), log_sum_exp.reshape(block_count, block_length, KEY_VALUE_HEADS, query_groups), row_correction.reshape(block_count, block_length, KEY_VALUE_HEADS, query_groups), token_positions.reshape(block_count, block_length), document_index.reshape(block_count, block_length))
    kv_grads, grad_query = lax.scan(one_block, (initial_key_value, initial_key_value), scan_result)
    return (grad_query.reshape(total_length, QUERY_HEADS, HEAD_WIDTH), kv_grads[0], kv_grads[1])

def reference(hidden, out_grad, decay_log, doc_lengths, weights, first_moment, second_moment, small_params, small_first, small_second):
    weights_b = weights.astype(jnp.bfloat16)
    gain_one, gain_two, gate_gain, conv_w, conv_bias, skip_gain = split_small(small_params)
    token_positions = jnp.arange(SEQUENCE_LENGTH, dtype=jnp.int32)
    mix_in_w = weights_b[:, :MIXIN]
    mix_out_w = weights_b[:, MIXIN:MIXIN + MIXOUT]
    gateup_w = weights_b[:, MIXIN + MIXOUT:MIXIN + MIXOUT + 2 * FF]
    down_w = weights_b[:, MIXIN + MIXOUT + 2 * FF:]
    outputs = []
    input_grads = []
    grad_total = jnp.zeros(weights.shape, jnp.float32)
    small_total = jnp.zeros(small_params.shape, jnp.float32)
    for seq_index in range(SEQUENCE_COUNT):
        document_index, rel_pos = doc_layout(doc_lengths[seq_index], token_positions)
        prev_ids = jnp.concatenate([jnp.full((1,), -1, jnp.int32), document_index[:-1]])
        is_start = document_index != prev_ids
        cosine_table, sine_table = rope_tables(rel_pos)
        tok_f = hidden[seq_index].astype(jnp.float32)
        scale_one = lax.rsqrt(lax.optimization_barrier(jnp.mean(tok_f * tok_f, axis=1, keepdims=True)) + norm_eps)
        normed_one = (tok_f * scale_one * gain_one).astype(jnp.bfloat16)
        projected_output = jnp.dot(normed_one, mix_in_w, preferred_element_type=jnp.float32)
        query_rows = apply_rotary(projected_output[:, :QUERY_WIDTH].reshape(SEQUENCE_LENGTH, QUERY_HEADS, HEAD_WIDTH), cosine_table, sine_table).astype(jnp.bfloat16)
        key_row_values = apply_rotary(projected_output[:, QUERY_WIDTH:QUERY_WIDTH + KEY_WIDTH].reshape(SEQUENCE_LENGTH, KEY_VALUE_HEADS, HEAD_WIDTH), cosine_table, sine_table).astype(jnp.bfloat16)
        value_row_values = projected_output[:, QUERY_WIDTH + KEY_WIDTH:QUERY_WIDTH + 2 * KEY_WIDTH].astype(jnp.bfloat16).reshape(SEQUENCE_LENGTH, KEY_VALUE_HEADS, HEAD_WIDTH)
        gate_in = projected_output[:, QUERY_WIDTH + 2 * KEY_WIDTH:QUERY_WIDTH + 2 * KEY_WIDTH + INNER]
        xbc_b = projected_output[:, QUERY_WIDTH + 2 * KEY_WIDTH + INNER:MIXIN].astype(jnp.bfloat16)
        attention_result, log_sum_exp = attention_forward(query_rows, key_row_values, value_row_values, document_index, token_positions)
        log_decay = decay_log[seq_index]

        def mamba_local(xbc_vals, gate_vals, conv_weights, conv_biases, skip_vals, gain_vals):
            return mamba_sequence(xbc_vals, gate_vals, conv_weights, conv_biases, skip_vals, gain_vals, log_decay, document_index, is_start)
        mamba_f, mamba_vjp = jax.vjp(mamba_local, xbc_b.astype(jnp.float32), gate_in, conv_w, conv_bias, skip_gain, gate_gain)
        mamba_b = mamba_f.astype(jnp.bfloat16)
        branch = jnp.concatenate([attention_result.reshape(SEQUENCE_LENGTH, QUERY_WIDTH), mamba_b], axis=1)
        resid_one = tok_f + jnp.dot(branch, mix_out_w.T, preferred_element_type=jnp.float32)
        scale_two = lax.rsqrt(lax.optimization_barrier(jnp.mean(resid_one * resid_one, axis=1, keepdims=True)) + norm_eps)
        normed_two = (resid_one * scale_two * gain_two).astype(jnp.bfloat16)
        gate_up = jnp.dot(normed_two, gateup_w, preferred_element_type=jnp.float32)
        gate_part = gate_up[:, :FF]
        up_part = gate_up[:, FF:]
        sigma_gate = jax.nn.sigmoid(gate_part)
        silu_gate = gate_part * sigma_gate
        hidden_mid = (silu_gate * up_part).astype(jnp.bfloat16)
        block_out = resid_one + jnp.dot(hidden_mid, down_w.T, preferred_element_type=jnp.float32)
        outputs.append(block_out.astype(jnp.bfloat16))
        grad_out = out_grad[seq_index]
        grad_mid = jnp.dot(grad_out, down_w, preferred_element_type=jnp.float32)
        silu_slope = sigma_gate * (1.0 + gate_part * (1.0 - sigma_gate))
        grad_gate_up = jnp.concatenate([grad_mid * up_part * silu_slope, grad_mid * silu_gate], axis=1).astype(jnp.bfloat16)
        grad_normed_two = jnp.dot(grad_gate_up, gateup_w.T, preferred_element_type=jnp.float32)
        grad_norm_two, grad_gain_two = norm_backward(grad_normed_two, resid_one, scale_two, gain_two)
        grad_resid_one = grad_out.astype(jnp.float32) + grad_norm_two
        grad_resid_b = grad_resid_one.astype(jnp.bfloat16)
        grad_branch = jnp.dot(grad_resid_b, mix_out_w, preferred_element_type=jnp.float32)
        attention_gradient = grad_branch[:, :QUERY_WIDTH].astype(jnp.bfloat16)
        grad_mamba = grad_branch[:, QUERY_WIDTH:]
        grad_xbc, grad_gate_in, grad_conv_w, grad_conv_bias, grad_skip, grad_gate_gain = mamba_vjp(grad_mamba)
        grad_query, grad_key, grad_value = attention_backward(query_rows, key_row_values, value_row_values, attention_result, attention_gradient, log_sum_exp, document_index, token_positions)
        grad_q = inverse_rotary(grad_query, cosine_table, sine_table).reshape(SEQUENCE_LENGTH, QUERY_WIDTH)
        key_gradient = inverse_rotary(grad_key, cosine_table, sine_table).reshape(SEQUENCE_LENGTH, KEY_WIDTH)
        grad_proj = jnp.concatenate([grad_q, key_gradient, grad_value.reshape(SEQUENCE_LENGTH, KEY_WIDTH), grad_gate_in, grad_xbc], axis=1).astype(jnp.bfloat16)
        grad_normed_one = jnp.dot(grad_proj, mix_in_w.T, preferred_element_type=jnp.float32)
        grad_norm_one, grad_gain_one = norm_backward(grad_normed_one, tok_f, scale_one, gain_one)
        input_grads.append(grad_resid_one + grad_norm_one)
        grad_cols = jnp.concatenate([jnp.dot(normed_one.T, grad_proj, preferred_element_type=jnp.float32), jnp.dot(grad_resid_b.T, branch, preferred_element_type=jnp.float32), jnp.dot(normed_two.T, grad_gate_up, preferred_element_type=jnp.float32), jnp.dot(grad_out.T, hidden_mid, preferred_element_type=jnp.float32)], axis=1)
        grad_total = grad_total + grad_cols
        small_total = small_total + jnp.concatenate([grad_gain_one, grad_gain_two, grad_gate_gain, grad_conv_w.reshape(-1), grad_conv_bias, grad_skip])
    new_weights, new_first, new_second = adamw_step(weights, grad_total, first_moment, second_moment, decay_rate)
    small_step, small_first_new, small_second_new = adam_direction(small_total, small_first, small_second)
    return (jnp.stack(outputs), jnp.stack(input_grads), grad_total, new_weights, new_first, new_second, small_total, small_step, small_first_new, small_second_new)
```

```python
import functools
import math

import jax
import jax.numpy as jnp
from jax import lax
from jax.experimental import pallas as pl
from jax.experimental.pallas import tpu as pltpu
from jax.sharding import PartitionSpec as P

D = 1024
QUERY_HEADS = 8
KEY_VALUE_HEADS = 2
HEAD_WIDTH = 64
MH = 24
MP = 64
NS = 128
FF = 2048
CONV = 4
STEP = 3
QUERY_WIDTH = 512
KEY_WIDTH = 128
INNER = 1536
XBC = 1792
MIXIN = 4096
MIXOUT = 2048
SMALL_ROWS = 104

norm_eps = 1e-05
rope_base = 100000000000.0
large_negative = -1e30
learn_rate = 0.02
beta_one = 0.9
beta_two = 0.95
adam_eps = 1e-08
decay_rate = 0.1

MESH = pl.DeviceIdType.MESH
BF = jnp.bfloat16
F32 = jnp.float32
VM = pl.BlockSpec(memory_space=pltpu.VMEM)
SM = pl.BlockSpec(memory_space=pltpu.SMEM)
HB = pl.BlockSpec(memory_space=pl.ANY)
DMA = pltpu.SemaphoreType.DMA


def params(collective=None):
    if collective is None:
        return pltpu.CompilerParams(vmem_limit_bytes=56 * 2**20)
    return pltpu.CompilerParams(
        collective_id=collective, has_side_effects=True, vmem_limit_bytes=56 * 2**20
    )


def nt(a, b):
    return lax.dot_general(a, b, (((1,), (1,)), ((), ())), preferred_element_type=F32)


def tn(a, b):
    return lax.dot_general(a, b, (((0,), (0,)), ((), ())), preferred_element_type=F32)


def nn(a, b):
    return lax.dot_general(a, b, (((1,), (0,)), ((), ())), preferred_element_type=F32)


class Place:
    def __init__(self, planes):
        ctx = lax.axis_index("ctx")
        self.ctx = ctx
        self.Z, self.z, self.x, self.c = planes, ctx // 4, (ctx // 2) % 2, ctx % 2
        self.y = lax.axis_index("fsdp")
        self.up, self.down = self.z + 1 < planes, self.z > 0

    def shard(self, z, x, y, c):
        return ((z * 2 + x) * 2 + c) * 2 + y

    def spot(self, z, x, c):
        return (z * 2 + x) * 2 + c

    def dev(self, z, x, y, c):
        return ((z * 2 + x) * 2 + c, y)

    def near(self, d):
        z, x, y, c = self.z, self.x, self.y, self.c
        return {
            "x": self.dev(z, 1 - x, y, c),
            "y": self.dev(z, x, 1 - y, c),
            "c": self.dev(z, x, y, 1 - c),
            "u": self.dev(z + 1, x, y, c),
            "d": self.dev(z - 1, x, y, c),
        }[d]

    def zord(self, k):
        if k == self.Z - 1:
            return self.z
        low = self.Z - 1 - k
        z = self.z
        return jnp.where(
            2 * z < self.Z, jnp.where(low > z, low, low - 1), jnp.where(k < z, k, k + 1)
        )


def greet(pc, dims="xyc", chain=True):
    bar = pltpu.get_barrier_semaphore()

    def sig(d):
        pl.semaphore_signal(bar, inc=1, device_id=pc.near(d), device_id_type=MESH)

    for d in dims:
        sig(d)
    if chain:
        pl.when(pc.up)(lambda: sig("u"))
        pl.when(pc.down)(lambda: sig("d"))
    peers = len(dims)
    if chain:
        peers = peers + pc.up.astype(jnp.int32) + pc.down.astype(jnp.int32)
    pl.semaphore_wait(bar, peers)


def greet_row(pc):
    bar = pltpu.get_barrier_semaphore()
    n = 4 * pc.Z

    @pl.loop(1, n)
    def _(d):
        pl.semaphore_signal(
            bar, inc=1, device_id=(lax.rem(pc.ctx + d, n), pc.y), device_id_type=MESH
        )

    pl.semaphore_wait(bar, n - 1)


def rcopy(pc, src, dst, ssem, rsem, d):
    return pltpu.make_async_remote_copy(
        src_ref=src,
        dst_ref=dst,
        send_sem=ssem,
        recv_sem=rsem,
        device_id=pc.near(d) if isinstance(d, str) else d,
        device_id_type=MESH,
    )


def add_into(dst, parts, width=512):
    columns = dst.shape[-1]
    step = width if columns % width == 0 else (256 if columns % 256 == 0 else 128)

    @pl.loop(0, columns // step)
    def _(i):
        sl = pl.ds(pl.multiple_of(i * step, step), step)
        total = parts[0][:, sl].astype(F32)
        for r in parts[1:]:
            total = total + r[:, sl].astype(F32)
        dst[:, sl] = total.astype(dst.dtype)


def gather_scratch(planes):
    n = 8 * planes
    return [
        DMA((2, planes, 2)),
        DMA((2, planes)),
        DMA((2, planes, 2)),
        DMA((2, planes, 4)),
        DMA((2, n)),
        DMA,
    ]


def gather_steps(pc, w_ref, out_ref, scratch):
    zs, xs, ys, cs, rs, loc = scratch
    Z, z, x, y, c = pc.Z, pc.z, pc.x, pc.y, pc.c
    half = w_ref.shape[-1] // 2
    me = pc.shard(z, x, y, c)

    def cp(p, s, sem, d, own=False):
        sl = pl.ds(p * half, half)
        src = w_ref.at[:, sl] if own else out_ref.at[s, :, sl]
        return rcopy(pc, src, out_ref.at[s, :, sl], sem, rs.at[p, s], d)

    def along(p, zz, up, own=False):
        return cp(p, pc.shard(zz, x, y, c), zs.at[p, zz, int(up)], "u" if up else "d", own)

    def first(p, zz, own=False):
        return cp(p, pc.shard(zz, x, y, c), xs.at[p, zz], "x" if p == 0 else "y", own)

    def second(p, zz, q, own=False):
        if p == 0:
            return cp(p, pc.shard(zz, x if q == 0 else 1 - x, y, c), ys.at[p, zz, q], "y", own)
        return cp(p, pc.shard(zz, x, y if q == 0 else 1 - y, c), ys.at[p, zz, q], "x", own)

    def core(p, zz, q, r, own=False):
        s = pc.shard(zz, x if q == 0 else 1 - x, y if r == 0 else 1 - y, c)
        return cp(p, s, cs.at[p, zz, q * 2 + r], "c", own)

    def arrived(p, s):
        sl = pl.ds(p * half, half)
        rcopy(pc, w_ref.at[:, sl], out_ref.at[s, :, sl], loc, rs.at[p, s], "c").wait_recv()

    keep = pltpu.make_async_copy(w_ref, out_ref.at[me], loc)
    keep.start()
    for p in (0, 1):
        pl.when(pc.up)(lambda: along(p, z, True, True).start())
        pl.when(pc.down)(lambda: along(p, z, False, True).start())
        first(p, z, True).start()
    for p in (0, 1):
        second(p, z, 0, True).start()
        core(p, z, 0, 0, True).start()
    yield
    for d in range(1, Z):
        for p in (0, 1):

            def onward(zz, up, more):
                arrived(p, pc.shard(zz, x, y, c))
                pl.when(more)(lambda: along(p, zz, up).start())
                first(p, zz).start()
                second(p, zz, 0).start()
                core(p, zz, 0, 0).start()

            pl.when(z - d >= 0)(lambda: onward(z - d, True, pc.up))
            pl.when(z + d < Z)(lambda: onward(z + d, False, pc.down))
        yield
    near = [lax.rem(z + k, Z) for k in range(Z)]
    for zz in near:
        for p in (0, 1):
            xx, yy = (1 - x, y) if p == 0 else (x, 1 - y)
            arrived(p, pc.shard(zz, xx, yy, c))
            second(p, zz, 1).start()
            core(p, zz, *((1, 0) if p == 0 else (0, 1))).start()
        yield
    for q in (0, 1):
        for zz in near:
            for p in (0, 1):
                if p == 0:
                    xx, yy, a, b = (x if q == 0 else 1 - x), 1 - y, q, 1
                else:
                    xx, yy, a, b = 1 - x, (y if q == 0 else 1 - y), 1, q
                arrived(p, pc.shard(zz, xx, yy, c))
                core(p, zz, a, b).start()
            yield
    for q in range(4):
        for zz in near:
            for p in (0, 1):
                xx = x if q < 2 else 1 - x
                yy = y if q % 2 == 0 else 1 - y
                arrived(p, pc.shard(zz, xx, yy, 1 - c))
        yield
    keep.wait()
    for p in (0, 1):
        for zz in range(Z):
            pl.when(pc.up & (zz <= z))(lambda: along(p, zz, True).wait_send())
            pl.when(pc.down & (zz >= z))(lambda: along(p, zz, False).wait_send())
            first(p, zz).wait_send()
            for q in (0, 1):
                second(p, zz, q).wait_send()
            for q in range(4):
                core(p, zz, q // 2, q % 2).wait_send()


def gather_kernel(planes, w_ref, out_ref, *scratch):
    pc = Place(planes)
    greet(pc)
    for _ in gather_steps(pc, w_ref, out_ref, scratch):
        pass


def gather_rows(w, planes, collective):
    rows, columns = w.shape
    return pl.pallas_call(
        functools.partial(gather_kernel, planes),
        out_shape=jax.ShapeDtypeStruct((8 * planes, rows, columns), w.dtype),
        in_specs=[HB],
        out_specs=HB,
        scratch_shapes=gather_scratch(planes),
        compiler_params=params(collective),
    )(w)


def scatter_scratch(planes, rows, columns):
    h = columns // 2
    return [
        pltpu.VMEM((planes, 4, rows, columns), BF),
        pltpu.VMEM((2, planes, 2, rows, h), BF),
        pltpu.VMEM((2, planes, rows, h), BF),
        pltpu.VMEM((2, 2, planes, rows, h), BF),
        DMA((planes, 4)),
        DMA((planes, 4)),
        DMA((2, planes, 2)),
        DMA((2, planes, 2)),
        DMA((2, planes)),
        DMA((2, planes)),
        DMA((2, 2, planes)),
        DMA((2, 2, planes)),
    ]


def scatter_steps(pc, make_plane, g_ref, out_ref, scratch):
    rc, r2, r3, rz, cs, cr, s2, q2, s3, q3, sz, qz = scratch
    Z, z, x, y, c = pc.Z, pc.z, pc.x, pc.y, pc.c
    h = g_ref.shape[-1] // 2

    def cols(p):
        return pl.ds(p * h, h)

    def other(q):
        return (x if q < 2 else 1 - x), (y if q % 2 == 0 else 1 - y)

    def ccopy(zz, q):
        xx, yy = other(q)
        return rcopy(
            pc, g_ref.at[pc.shard(zz, xx, yy, 1 - c)], rc.at[zz, q], cs.at[zz, q], cr.at[zz, q], "c"
        )

    def copy2(p, zz, j):
        q = (1 + 2 * j) if p == 0 else (2 + j)
        return rcopy(
            pc,
            rc.at[zz, q, :, cols(p)],
            r2.at[p, zz, j],
            s2.at[p, zz, j],
            q2.at[p, zz, j],
            "y" if p == 0 else "x",
        )

    def copy3(p, zz):
        q = 2 if p == 0 else 1
        return rcopy(
            pc, rc.at[zz, q, :, cols(p)], r3.at[p, zz], s3.at[p, zz], q3.at[p, zz], "x" if p == 0 else "y"
        )

    def copyz(p, zz, up):
        u = int(up)
        return rcopy(
            pc,
            rc.at[zz, 0, :, cols(p)],
            rz.at[p, u, zz],
            sz.at[p, u, zz],
            qz.at[p, u, zz],
            "u" if up else "d",
        )

    order = (3, 1, 2, 0)
    for k in range(Z):
        zz = pc.zord(k)
        make_plane(zz)
        for q in order:
            ccopy(zz, q).start()
        yield
    for q in order:
        for k in range(Z):
            zz = pc.zord(k)
            xx, yy = other(q)
            ccopy(zz, q).wait_recv()
            add_into(rc.at[zz, q], [g_ref.at[pc.shard(zz, xx, yy, c)], rc.at[zz, q]])
            if q == 3:
                copy2(0, zz, 1).start()
                copy2(1, zz, 1).start()
            if q == 1:
                copy2(0, zz, 0).start()
            if q == 2:
                copy2(1, zz, 0).start()
            yield
    for k in range(Z):
        zz = pc.zord(k)
        for p in (0, 1):
            copy2(p, zz, 1).wait_recv()
            a = rc.at[zz, 2 if p == 0 else 1, :, cols(p)]
            add_into(a, [a, r2.at[p, zz, 1]])
            copy3(p, zz).start()
        yield

    def own(p, zz):
        copy2(p, zz, 0).wait_recv()
        copy3(p, zz).wait_recv()
        a = rc.at[zz, 0, :, cols(p)]
        return a, [a, r2.at[p, zz, 0], r3.at[p, zz]]

    def chain(p, zz, up, more):
        a, parts = own(p, zz)
        add_into(a, parts)

        @pl.when(more)
        def _():
            copyz(p, zz, up).wait_recv()
            add_into(a, [a, rz.at[p, int(up), zz]])

        copyz(p, zz, up).start()

    for t in range(Z - 1):
        for p in (0, 1):
            below, above = t - (Z - 1 - z), Z - 1 - (t - z)
            pl.when((below >= 0) & (below < z))(lambda: chain(p, below, False, pc.up))
            pl.when((above > z) & (above < Z))(lambda: chain(p, above, True, pc.down))
        yield
    for p in (0, 1):
        a, parts = own(p, z)
        o = out_ref.at[:, cols(p)]
        add_into(o, parts)

        def last(u):
            copyz(p, z, bool(u)).wait_recv()
            add_into(o, [o, rz.at[p, u, z]])

        pl.when(pc.up)(lambda: last(0))
        pl.when(pc.down)(lambda: last(1))
        yield
    for zz in range(Z):
        for q in range(4):
            ccopy(zz, q).wait_send()
        for p in (0, 1):
            for j in (0, 1):
                copy2(p, zz, j).wait_send()
            copy3(p, zz).wait_send()
            pl.when(zz < z)(lambda: copyz(p, zz, False).wait_send())
            pl.when(zz > z)(lambda: copyz(p, zz, True).wait_send())


def plane_maker(planes, pairs, g_ref):
    rows = g_ref.shape[1]
    depth = 8 * rows

    def make_plane(zz):
        base = 0
        for left, right in pairs:
            lhs = left[pl.ds(pl.multiple_of(zz * depth, depth), depth), :]
            width = right.shape[1]

            @pl.loop(0, width // 512)
            def _(i):
                at = pl.multiple_of(i * 512, 512)
                tile = nn(lhs, right[:, pl.ds(at, 512)]).reshape(8, rows, 512).astype(BF)
                g_ref[pl.ds(zz * 8, 8), :, pl.ds(pl.multiple_of(base + at, 512), 512)] = tile

            base += width

    return make_plane


def scatter_kernel(planes, l1, r1, l2, r2, out_ref, g_ref, *scratch):
    pc = Place(planes)
    greet(pc)
    for _ in scatter_steps(
        pc, plane_maker(planes, ((l1, r1), (l2, r2)), g_ref), g_ref, out_ref, scratch
    ):
        pass


def scatter_rows(planes, l1, r1, l2, r2, collective):
    rows = l1.shape[0] // (8 * planes)
    columns = r1.shape[1] + r2.shape[1]
    return pl.pallas_call(
        functools.partial(scatter_kernel, planes),
        out_shape=jax.ShapeDtypeStruct((rows, columns), F32),
        in_specs=[VM] * 4,
        out_specs=VM,
        scratch_shapes=[pltpu.VMEM((8 * planes, rows, columns), BF)]
        + scatter_scratch(planes, rows, columns),
        compiler_params=params(collective),
    )(l1, r1, l2, r2)


def spread_scratch(planes):
    n = 4 * planes
    return [DMA((planes,)), DMA((planes,)), DMA((planes, 2)), DMA((n,)), DMA((n,)), DMA((n,)), DMA((3,))]


def spread_kernel(planes, kv_ref, edge_ref, dec_ref, all_ref, got_ref, decs_ref, *scratch):
    us, xs, cs, rs, ds, dr, one = scratch
    pc = Place(planes)
    Z, z, x, c = pc.Z, pc.z, pc.x, pc.c
    n = 4 * Z
    me = pc.ctx
    greet_row(pc)

    def cp(zz, xx, sem, d, own=False):
        s = pc.spot(zz, xx, c)
        return rcopy(pc, kv_ref if own else all_ref.at[s], all_ref.at[s], sem, rs.at[s], d)

    def arrived(s):
        rcopy(pc, kv_ref, all_ref.at[s], one.at[0], rs.at[s], "c").wait_recv()

    def decay_copy(d, to):
        return rcopy(pc, dec_ref, decs_ref.at[me], ds.at[d], dr.at[d], (lax.rem(to, n), pc.y))

    edge = rcopy(pc, edge_ref, got_ref, one.at[1], one.at[2], (lax.rem(me + 1, n), pc.y))
    keep = pltpu.make_async_copy(kv_ref, all_ref.at[me], one.at[0])
    keep.start()
    pl.when(pc.up)(lambda: cp(z, x, us.at[z], "u", True).start())
    cp(z, x, xs.at[z], "x", True).start()
    cp(z, x, cs.at[z, 0], "c", True).start()
    pl.when(me < n - 1)(lambda: edge.start())
    decs_ref[me] = dec_ref[...]

    @pl.loop(1, n)
    def _(d):
        decay_copy(d, me + d).start()

    for d in range(1, Z):

        @pl.when(z - d >= 0)
        def _():
            zz = z - d
            arrived(pc.spot(zz, x, c))
            pl.when(pc.up)(lambda: cp(zz, x, us.at[zz], "u").start())
            cp(zz, x, xs.at[zz], "x").start()
            cp(zz, x, cs.at[zz, 0], "c").start()

    for d in range(Z):

        @pl.when(z - d >= 0)
        def _():
            arrived(pc.spot(z - d, 1 - x, c))
            cp(z - d, 1 - x, cs.at[z - d, 1], "c").start()

    for d in range(Z):

        @pl.when(z - d >= 0)
        def _():
            for xx in (x, 1 - x):
                arrived(pc.spot(z - d, xx, 1 - c))

    keep.wait()
    for zz in range(Z):

        @pl.when(zz <= z)
        def _():
            pl.when(pc.up)(lambda: cp(zz, x, us.at[zz], "u").wait_send())
            cp(zz, x, xs.at[zz], "x").wait_send()
            cp(zz, x, cs.at[zz, 0], "c").wait_send()
            cp(zz, 1 - x, cs.at[zz, 1], "c").wait_send()

    @pl.when(me < n - 1)
    def _():
        edge.wait_send()

    @pl.when(me > 0)
    def _():
        edge.wait_recv()

    @pl.when(me == 0)
    def _():
        got_ref[...] = jnp.zeros_like(got_ref)

    @pl.loop(1, n)
    def _(d):
        decay_copy(d, me + d).wait()


def spread(planes, kv, edge, dec, collective):
    n = 4 * planes
    return pl.pallas_call(
        functools.partial(spread_kernel, planes),
        out_shape=(
            jax.ShapeDtypeStruct((n,) + kv.shape, kv.dtype),
            jax.ShapeDtypeStruct(edge.shape, edge.dtype),
            jax.ShapeDtypeStruct((n,) + dec.shape, dec.dtype),
        ),
        in_specs=[VM] * 3,
        out_specs=(VM,) * 3,
        scratch_shapes=spread_scratch(planes),
        compiler_params=params(collective),
    )(kv, edge, dec)


def fold_kernel(planes, g_ref, edge_ref, out_ref, got_ref, rc, rx, rz, acc, *scratch):
    cs, cr, xs, xr, zs, zr, one = scratch
    pc = Place(planes)
    Z, z, x, c = pc.Z, pc.z, pc.x, pc.c
    n = 4 * Z
    me = pc.ctx
    greet_row(pc)
    edge = rcopy(pc, edge_ref, got_ref, one.at[0], one.at[1], (lax.rem(me + n - 1, n), pc.y))
    pl.when(me > 0)(lambda: edge.start())

    def ccopy(zz, q):
        xx = x if q == 0 else 1 - x
        return rcopy(
            pc, g_ref.at[pc.spot(zz, xx, 1 - c)], rc.at[zz, q], cs.at[zz, q], cr.at[zz, q], "c"
        )

    def xcopy(zz):
        return rcopy(pc, acc.at[zz, 1], rx.at[zz], xs.at[zz], xr.at[zz], "x")

    def zcopy(zz):
        return rcopy(pc, acc.at[zz, 0], rz.at[zz], zs.at[zz], zr.at[zz], "d")

    def each(f):
        for zz in range(Z):
            pl.when(zz <= z)(functools.partial(f, zz))

    def a(zz):
        ccopy(zz, 1).start()
        ccopy(zz, 0).start()

    def b(zz):
        ccopy(zz, 1).wait_recv()
        add_into(acc.at[zz, 1], [g_ref.at[pc.spot(zz, 1 - x, c)], rc.at[zz, 1]], 128)
        xcopy(zz).start()

    def m(zz):
        ccopy(zz, 0).wait_recv()
        add_into(acc.at[zz, 0], [g_ref.at[pc.spot(zz, x, c)], rc.at[zz, 0]], 128)

    def e(zz):
        xcopy(zz).wait_recv()

        @pl.when(pc.up)
        def _():
            zcopy(zz).wait_recv()

            @pl.when(zz < z)
            def _():
                add_into(acc.at[zz, 0], [acc.at[zz, 0], rx.at[zz], rz.at[zz]], 128)
                zcopy(zz).start()

            @pl.when(zz == z)
            def _():
                add_into(out_ref, [acc.at[zz, 0], rx.at[zz], rz.at[zz]], 128)

        @pl.when(jnp.logical_not(pc.up))
        def _():
            @pl.when(zz < z)
            def _():
                add_into(acc.at[zz, 0], [acc.at[zz, 0], rx.at[zz]], 128)
                zcopy(zz).start()

            @pl.when(zz == z)
            def _():
                add_into(out_ref, [acc.at[zz, 0], rx.at[zz]], 128)

    def w(zz):
        ccopy(zz, 1).wait_send()
        ccopy(zz, 0).wait_send()
        xcopy(zz).wait_send()
        pl.when(zz < z)(lambda: zcopy(zz).wait_send())

    for f in (a, b, m, e, w):
        each(f)
    pl.when(me > 0)(lambda: edge.wait_send())
    pl.when(me < n - 1)(lambda: edge.wait_recv())

    @pl.when(me == n - 1)
    def _():
        got_ref[...] = jnp.zeros_like(got_ref)


def fold(planes, grads, edge, collective):
    n, rows, columns = grads.shape
    return pl.pallas_call(
        functools.partial(fold_kernel, planes),
        out_shape=(
            jax.ShapeDtypeStruct((rows, columns), F32),
            jax.ShapeDtypeStruct(edge.shape, edge.dtype),
        ),
        in_specs=[VM] * 2,
        out_specs=(VM,) * 2,
        scratch_shapes=[
            pltpu.VMEM((planes, 2, rows, columns), BF),
            pltpu.VMEM((planes, rows, columns), BF),
            pltpu.VMEM((planes, rows, columns), BF),
            pltpu.VMEM((planes, 2, rows, columns), BF),
            DMA((planes, 2)),
            DMA((planes, 2)),
            DMA((planes,)),
            DMA((planes,)),
            DMA((planes,)),
            DMA((planes,)),
            DMA((2,)),
        ],
        compiler_params=params(collective),
    )(grads, edge)


def relay_kernel(planes, reverse, s_ref, dec_ref, out_ref, got, part, ss, sr, bs, br):
    pc = Place(planes)
    n = 4 * planes
    me = pc.ctx
    greet_row(pc)

    def to(d):
        return lax.rem(me + d, n)

    def there(d):
        return rcopy(pc, s_ref.at[to(d)], got.at[me], ss.at[d], sr.at[d], (to(d), pc.y))

    def back(d):
        return rcopy(pc, part.at[to(d)], out_ref.at[me], bs.at[d], br.at[d], (to(d), pc.y))

    pl.loop(1, n)(lambda d: there(d).start())
    got[me] = s_ref[me]
    pl.loop(1, n)(lambda d: there(d).wait_recv())
    total = jnp.zeros(got.shape[1:], F32)
    for k in range(n):
        j = n - 1 - k if reverse else k
        part[j] = total.astype(BF)
        total = total * dec_ref[pl.ds(j, 1), :] + got[j].astype(F32)
    pl.loop(1, n)(lambda d: back(d).start())
    out_ref[me] = part[me]

    @pl.loop(1, n)
    def _(d):
        there(d).wait_send()
        back(d).wait()


def relay(planes, reverse, state, decays, collective):
    n = 4 * planes
    piece = state.reshape(n, NS // n, INNER)
    out = pl.pallas_call(
        functools.partial(relay_kernel, planes, reverse),
        out_shape=jax.ShapeDtypeStruct(piece.shape, BF),
        in_specs=[VM] * 2,
        out_specs=VM,
        scratch_shapes=[pltpu.VMEM(piece.shape, BF), pltpu.VMEM(piece.shape, BF)]
        + [DMA((n,))] * 4,
        compiler_params=params(collective),
    )(piece, decays)
    return out.reshape(NS, INNER)


def total_kernel(planes, a_ref, out_ref, rx, rz, ss, sr, zs, zr):
    pc = Place(planes)
    Z, z = pc.Z, pc.z
    bar = pltpu.get_barrier_semaphore()

    def plane(d):
        return pc.dev(lax.rem(z + d, Z), pc.x, pc.y, pc.c)

    for d in "cxy":
        pl.semaphore_signal(bar, inc=1, device_id=pc.near(d), device_id_type=MESH)
    for d in range(1, Z):
        pl.semaphore_signal(bar, inc=1, device_id=plane(d), device_id_type=MESH)
    pl.semaphore_wait(bar, 2 + Z)
    out_ref[...] = a_ref[...]
    for i, d in enumerate("cxy"):
        src = rx.at[2 * i]
        src[...] = out_ref[...]
        cp = rcopy(pc, src, rx.at[2 * i + 1], ss.at[i], sr.at[i], d)
        cp.start()
        cp.wait()
        out_ref[...] = out_ref[...] + rx[2 * i + 1]
    rz[z] = out_ref[...]
    copies = [rcopy(pc, rz.at[z], rz.at[z], zs.at[d], zr.at[d], plane(d)) for d in range(1, Z)]
    for cp in copies:
        cp.start()
    for cp in copies:
        cp.wait()
    total = rz[0]
    for k in range(1, Z):
        total = total + rz[k]
    out_ref[...] = total


def total_small(planes, a, collective):
    return pl.pallas_call(
        functools.partial(total_kernel, planes),
        out_shape=jax.ShapeDtypeStruct(a.shape, F32),
        in_specs=[VM],
        out_specs=VM,
        scratch_shapes=[
            pltpu.VMEM((6,) + a.shape, F32),
            pltpu.VMEM((planes,) + a.shape, F32),
            DMA((3,)),
            DMA((3,)),
            DMA((planes,)),
            DMA((planes,)),
        ],
        compiler_params=params(collective),
    )(a)


def visible(start, block, pos_ref):
    kpos = start + lax.broadcasted_iota(jnp.int32, (block, pos_ref.shape[1]), 0)
    return (kpos <= pos_ref[0:1, :]) & (kpos >= pos_ref[1:2, :])


def attend_kernel(block, span_ref, q_ref, kv_ref, pos_ref, o_ref, lse_ref, m_ref, l_ref, acc_ref):
    rows = pos_ref.shape[1]
    m_ref[...] = jnp.full_like(m_ref, large_negative)
    l_ref[...] = jnp.zeros_like(l_ref)
    acc_ref[...] = jnp.zeros_like(acc_ref)

    @pl.loop(span_ref[0], span_ref[1])
    def _(j):
        start = pl.multiple_of(j * block, block)
        ok = visible(start, block, pos_ref)
        for h in range(QUERY_HEADS):
            g = h // (QUERY_HEADS // KEY_VALUE_HEADS)
            keys = kv_ref[pl.ds(start, block), pl.ds(g * HEAD_WIDTH, HEAD_WIDTH)]
            vals = kv_ref[pl.ds(start, block), pl.ds(KEY_WIDTH + g * HEAD_WIDTH, HEAD_WIDTH)]
            s = jnp.where(ok, nt(keys, q_ref[pl.ds(h * rows, rows), :]), large_negative)
            m0 = m_ref[h : h + 1, :]
            m1 = jnp.maximum(m0, jnp.max(s, axis=0, keepdims=True))
            p = jnp.where(ok, jnp.exp(s - m1), 0.0)
            a = jnp.exp(m0 - m1)
            l_ref[h : h + 1, :] = l_ref[h : h + 1, :] * a + jnp.sum(p, axis=0, keepdims=True)
            m_ref[h : h + 1, :] = m1
            r = pl.ds(h * HEAD_WIDTH, HEAD_WIDTH)
            acc_ref[r, :] = acc_ref[r, :] * a + tn(vals, p.astype(BF))

    lse_ref[...] = m_ref[...] + jnp.log(l_ref[...])
    inv = 1.0 / l_ref[...]
    for h in range(QUERY_HEADS):
        r = pl.ds(h * HEAD_WIDTH, HEAD_WIDTH)
        acc_ref[r, :] = acc_ref[r, :] * inv[h : h + 1, :]
    o_ref[...] = acc_ref[...].T.astype(o_ref.dtype)


def attend(span, q, kv, pos, block):
    rows = pos.shape[1]
    return pl.pallas_call(
        functools.partial(attend_kernel, block),
        out_shape=(
            jax.ShapeDtypeStruct((rows, QUERY_WIDTH), BF),
            jax.ShapeDtypeStruct((QUERY_HEADS, rows), F32),
        ),
        in_specs=[SM, VM, VM, VM],
        out_specs=(VM, VM),
        scratch_shapes=[
            pltpu.VMEM((QUERY_HEADS, rows), F32),
            pltpu.VMEM((QUERY_HEADS, rows), F32),
            pltpu.VMEM((QUERY_WIDTH, rows), F32),
        ],
        compiler_params=params(),
    )(span, q, kv, pos)


def attend_back_kernel(
    block, span_ref, q_ref, do_ref, kv_ref, pos_ref, lse_ref, dl_ref, dq_ref, dkv_ref, acc_ref
):
    rows = pos_ref.shape[1]
    acc_ref[...] = jnp.zeros_like(acc_ref)

    def blank(j):
        dkv_ref[pl.ds(pl.multiple_of(j * block, block), block), :] = jnp.zeros((block, 256), BF)

    pl.loop(0, span_ref[0])(blank)
    pl.loop(span_ref[1], kv_ref.shape[0] // block)(blank)

    @pl.loop(span_ref[0], span_ref[1])
    def _(j):
        start = pl.multiple_of(j * block, block)
        ok = visible(start, block, pos_ref)
        at = pl.ds(start, block)
        dks, dvs = [], []
        for g in range(KEY_VALUE_HEADS):
            keys = kv_ref[at, pl.ds(g * HEAD_WIDTH, HEAD_WIDTH)]
            vals = kv_ref[at, pl.ds(KEY_WIDTH + g * HEAD_WIDTH, HEAD_WIDTH)]
            dk = dv = None
            for h in range(4 * g, 4 * g + 4):
                q = q_ref[pl.ds(h * rows, rows), :]
                do = do_ref[pl.ds(h * rows, rows), :]
                p = jnp.where(ok, jnp.exp(nt(keys, q) - lse_ref[h : h + 1, :]), 0.0)
                ds = (p * (nt(vals, do) - dl_ref[h : h + 1, :])).astype(BF)
                r = pl.ds(h * HEAD_WIDTH, HEAD_WIDTH)
                acc_ref[r, :] += tn(keys, ds)
                a, b = nn(ds, q), nn(p.astype(BF), do)
                dk = a if dk is None else dk + a
                dv = b if dv is None else dv + b
            dks.append(dk)
            dvs.append(dv)
        dkv_ref[at, :] = jnp.concatenate(dks + dvs, axis=1).astype(BF)

    dq_ref[...] = acc_ref[...].T * (HEAD_WIDTH**-0.5)


def attend_back(span, q, do, kv, pos, lse, delta, block):
    rows = pos.shape[1]
    return pl.pallas_call(
        functools.partial(attend_back_kernel, block),
        out_shape=(
            jax.ShapeDtypeStruct((rows, QUERY_WIDTH), F32),
            jax.ShapeDtypeStruct((kv.shape[0], 2 * KEY_WIDTH), BF),
        ),
        in_specs=[SM] + [VM] * 6,
        out_specs=(VM, VM),
        scratch_shapes=[pltpu.VMEM((QUERY_WIDTH, rows), F32)],
        compiler_params=params(),
    )(span, q, do, kv, pos, lse, delta)


def two(left, right, lanes):
    return jnp.where(lanes < MP, left, right)


def pair_columns(ref, p, lanes):
    return two(ref[:, 2 * p : 2 * p + 1], ref[:, 2 * p + 1 : 2 * p + 2], lanes)


def mixer_kernel(
    xe, mk, cw, cb, cum_t, cum, dt_t, we_t, skip, doc_c, doc_r, pre, xo, mix, so, xw, bias
):
    rows = pre.shape[0]
    for i in range(XBC // 256):
        sl = pl.ds(i * 256, 256)
        acc = jnp.broadcast_to(cb[:, sl], (rows, 256))
        for j in range(CONV):
            acc = acc + cw[j : j + 1, sl] * (xe[pl.ds(5 + j, rows), sl] * mk[:, j : j + 1])
        pre[:, sl] = acc
        act = acc * jax.nn.sigmoid(acc)
        xo[:, sl] = act.astype(BF)
        if i < INNER // 256:
            mix[:, sl] = skip[:, sl] * act
    b_rows, c_rows = xo[:, pl.ds(INNER, NS)], xo[:, pl.ds(INNER + NS, NS)]
    cross = nt(c_rows, b_rows)
    t_at = lax.broadcasted_iota(jnp.int32, (rows, rows), 0)
    s_at = lax.broadcasted_iota(jnp.int32, (rows, rows), 1)
    bias[...] = jnp.where((doc_c[...] == doc_r[...]) & (s_at <= t_at), 0.0, large_negative)
    lanes = lax.broadcasted_iota(jnp.int32, (rows, 2 * MP), 1)
    for p in range(MH // 2):
        sl = pl.ds(p * 2 * MP, 2 * MP)
        xd = xo[:, sl].astype(F32) * pair_columns(dt_t, p, lanes)
        xw[:, sl] = (xd * pair_columns(we_t, p, lanes)).astype(BF)
        xb = xd.astype(BF)
        outs = []
        for h in (2 * p, 2 * p + 1):
            low = jnp.exp(jnp.minimum(cum_t[:, h : h + 1] - cum[h : h + 1, :], bias[...]))
            outs.append(nn((low * cross).astype(BF), xb))
        mix[:, sl] = mix[:, sl] + two(outs[0], outs[1], lanes)
    so[...] = tn(b_rows, xw[...]).astype(BF)


def mixer(xe, mk, cw, cb, cum_t, cum, dt_t, we_t, skip, doc_c, doc_r):
    rows = mk.shape[0]
    return pl.pallas_call(
        mixer_kernel,
        out_shape=(
            jax.ShapeDtypeStruct((rows, XBC), F32),
            jax.ShapeDtypeStruct((rows, XBC), BF),
            jax.ShapeDtypeStruct((rows, INNER), F32),
            jax.ShapeDtypeStruct((NS, INNER), BF),
        ),
        in_specs=[VM] * 11,
        out_specs=(VM,) * 4,
        scratch_shapes=[pltpu.VMEM((rows, INNER), BF), pltpu.VMEM((rows, rows), F32)],
        compiler_params=params(),
    )(xe, mk, cw, cb, cum_t, cum, dt_t, we_t, skip, doc_c, doc_r)


def spread_heads():
    head = lax.broadcasted_iota(jnp.int32, (MH, INNER), 0)
    lane = lax.broadcasted_iota(jnp.int32, (MH, INNER), 1)
    return (lane // MP == head).astype(F32)


def wide(columns, spread_mat):
    return lax.dot_general(
        columns,
        spread_mat,
        (((1,), (0,)), ((), ())),
        precision=lax.Precision.HIGHEST,
        preferred_element_type=F32,
    )


def gate_kernel(mix, xo, state, din_t, gate, gain, att, mixed, branch):
    rows = mix.shape[0]
    spread_mat = spread_heads()

    @pl.loop(0, rows // 64)
    def _(i):
        r = pl.ds(pl.multiple_of(i * 64, 64), 64)
        carried = nn(xo[r, pl.ds(INNER + NS, NS)], state[...])
        m = mix[r, :] + carried * wide(din_t[r, :], spread_mat)
        mixed[r, :] = m
        gv = gate[r, :]
        gated = m * (gv * jax.nn.sigmoid(gv))
        factor = lax.rsqrt(jnp.mean(gated * gated, axis=1, keepdims=True) + norm_eps)
        branch[r, pl.ds(0, QUERY_WIDTH)] = att[r, :]
        branch[r, pl.ds(QUERY_WIDTH, INNER)] = (gated * factor * gain[...]).astype(BF)


def gate_out(mix, xo, state, din_t, gate, gain, att):
    rows = mix.shape[0]
    return pl.pallas_call(
        gate_kernel,
        out_shape=(
            jax.ShapeDtypeStruct((rows, INNER), F32),
            jax.ShapeDtypeStruct((rows, MIXOUT), BF),
        ),
        in_specs=[VM] * 7,
        out_specs=(VM,) * 2,
        compiler_params=params(),
    )(mix, xo, state, din_t, gate, gain, att)


def gate_back_kernel(grad, mixed, gate, gain, din_t, xo, state, dm, dgate, dgain, dstate, dc, dinc):
    rows = mixed.shape[0]
    spread_mat = spread_heads()
    dgain[...] = jnp.zeros_like(dgain)

    @pl.loop(0, rows // 64)
    def _(i):
        r = pl.ds(pl.multiple_of(i * 64, 64), 64)
        m, gv, gr = mixed[r, :], gate[r, :], grad[r, :]
        sig = jax.nn.sigmoid(gv)
        sil = gv * sig
        gated = m * sil
        factor = lax.rsqrt(jnp.mean(gated * gated, axis=1, keepdims=True) + norm_eps)
        w = gr * gain[...]
        dg = factor * (w - gated * factor * factor * jnp.mean(w * gated, axis=1, keepdims=True))
        dgain[...] += jnp.sum(gr * gated * factor, axis=0, keepdims=True)
        dgate[r, :] = (dg * m * (sig * (1.0 + gv * (1.0 - sig)))).astype(BF)
        d = dg * sil
        dm[r, :] = d.astype(BF)
        dinc[r, :] = (d * wide(din_t[r, :], spread_mat)).astype(BF)

    dstate[...] = tn(xo[:, pl.ds(INNER + NS, NS)], dinc[...]).astype(BF)
    dc[...] = nt(dinc[...], state[...])


def gate_back(grad, mixed, gate, gain, din_t, xo, state):
    rows = mixed.shape[0]
    return pl.pallas_call(
        gate_back_kernel,
        out_shape=(
            jax.ShapeDtypeStruct((rows, INNER), BF),
            jax.ShapeDtypeStruct((rows, INNER), BF),
            jax.ShapeDtypeStruct((1, INNER), F32),
            jax.ShapeDtypeStruct((NS, INNER), BF),
            jax.ShapeDtypeStruct((rows, NS), F32),
        ),
        in_specs=[VM] * 7,
        out_specs=(VM,) * 5,
        scratch_shapes=[pltpu.VMEM((rows, INNER), BF)],
        compiler_params=params(),
    )(grad, mixed, gate, gain, din_t, xo, state)


def mixer_back_kernel(
    xe, mk, cw, cum_t, cum, dt_t, we_t, skip, doc_c, doc_r, pre, xo, dm, dc_in, ds,
    dpre, dcw, dskip, xw, bias,
):
    rows = pre.shape[0]
    b_rows, c_rows = xo[:, pl.ds(INNER, NS)], xo[:, pl.ds(INNER + NS, NS)]
    cross = nt(b_rows, c_rows)
    s_at = lax.broadcasted_iota(jnp.int32, (rows, rows), 0)
    t_at = lax.broadcasted_iota(jnp.int32, (rows, rows), 1)
    bias[...] = jnp.where((doc_c[...] == doc_r[...]) & (s_at <= t_at), 0.0, large_negative)
    lanes = lax.broadcasted_iota(jnp.int32, (rows, 2 * MP), 1)

    def slope(sl):
        v = pre[:, sl]
        sig = jax.nn.sigmoid(v)
        return sig * (1.0 + v * (1.0 - sig))

    dcross = jnp.zeros((rows, rows), F32)
    for p in range(MH // 2):
        sl = pl.ds(p * 2 * MP, 2 * MP)
        xv = xo[:, sl].astype(F32)
        dt2, we2 = pair_columns(dt_t, p, lanes), pair_columns(we_t, p, lanes)
        xd = xv * dt2
        xw[:, sl] = (xd * we2).astype(BF)
        g = dm[:, sl]
        outs = []
        for k in (0, 1):
            h = 2 * p + k
            low = jnp.exp(jnp.minimum(cum[h : h + 1, :] - cum_t[:, h : h + 1], bias[...]))
            outs.append(nn((low * cross).astype(BF), g))
            part = jnp.where((lanes < MP) == (k == 0), xd, 0.0).astype(BF)
            dcross = dcross + nt(part, g) * low
        dxd = two(outs[0], outs[1], lanes) + we2 * nn(b_rows, ds[:, sl])
        gf = g.astype(F32)
        dskip[:, sl] = jnp.sum(gf * xv, axis=0, keepdims=True)
        dpre[:, sl] = (dxd * dt2 + skip[:, sl] * gf) * slope(sl)
    db16 = dcross.astype(BF)
    slb, slc = pl.ds(INNER, NS), pl.ds(INNER + NS, NS)
    dpre[:, slb] = (nn(db16, c_rows) + nt(xw[...], ds[...])) * slope(slb)
    dpre[:, slc] = (tn(db16, b_rows) + dc_in[...]) * slope(slc)
    for i in range(XBC // 256):
        sl = pl.ds(i * 256, 256)
        d = dpre[:, sl]
        for j in range(CONV):
            dcw[j : j + 1, sl] = jnp.sum(
                d * (xe[pl.ds(5 + j, rows), sl] * mk[:, j : j + 1]), axis=0, keepdims=True
            )
        dcw[CONV : CONV + 1, sl] = jnp.sum(d, axis=0, keepdims=True)


def mixer_back(xe, mk, cw, cum_t, cum, dt_t, we_t, skip, doc_c, doc_r, pre, xo, dm, dc_in, ds):
    rows = mk.shape[0]
    return pl.pallas_call(
        mixer_back_kernel,
        out_shape=(
            jax.ShapeDtypeStruct((rows, XBC), F32),
            jax.ShapeDtypeStruct((CONV + 1, XBC), F32),
            jax.ShapeDtypeStruct((1, INNER), F32),
        ),
        in_specs=[VM] * 15,
        out_specs=(VM,) * 3,
        scratch_shapes=[pltpu.VMEM((rows, INNER), BF), pltpu.VMEM((rows, rows), F32)],
        compiler_params=params(),
    )(xe, mk, cw, cum_t, cum, dt_t, we_t, skip, doc_c, doc_r, pre, xo, dm, dc_in, ds)


def doc_layout(lengths, token_positions):
    starts = jnp.cumsum(lengths) - lengths
    inside = token_positions[:, None] >= starts[None, :]
    document_index = jnp.sum(inside.astype(jnp.int32), axis=1) - 1
    begins = jnp.max(jnp.where(inside, starts[None, :], 0), axis=1)
    return (document_index, token_positions - begins)


def rope_tables(rel_pos):
    half_dim = HEAD_WIDTH // 2
    inv_freq = rope_base ** (-2.0 * jnp.arange(half_dim, dtype=jnp.float32) / HEAD_WIDTH)
    angles = rel_pos.astype(jnp.float32)[:, None] * inv_freq[None, :]
    return (jnp.cos(angles), jnp.sin(angles))


def apply_rotary(values, cosine_table, sine_table):
    half_dim = values.shape[-1] // 2
    lower_half = values[..., :half_dim]
    upper_half = values[..., half_dim:]
    cos_rows = cosine_table[:, None, :]
    sin_rows = sine_table[:, None, :]
    return jnp.concatenate(
        [
            lower_half * cos_rows - upper_half * sin_rows,
            upper_half * cos_rows + lower_half * sin_rows,
        ],
        axis=-1,
    )


def inverse_rotary(grads, cosine_table, sine_table):
    half_dim = grads.shape[-1] // 2
    lower_half = grads[..., :half_dim]
    upper_half = grads[..., half_dim:]
    cos_rows = cosine_table[:, None, :]
    sin_rows = sine_table[:, None, :]
    return jnp.concatenate(
        [
            lower_half * cos_rows + upper_half * sin_rows,
            upper_half * cos_rows - lower_half * sin_rows,
        ],
        axis=-1,
    )


def split_small(vector):
    widths = (D, D, INNER, CONV * XBC, XBC, MH)
    pieces = []
    offset = 0
    for span_width in widths:
        pieces.append(vector[offset : offset + span_width])
        offset += span_width
    return (pieces[0], pieces[1], pieces[2], pieces[3].reshape(CONV, XBC), pieces[4], pieces[5])


def norm_backward(grad_normed, values, factor, gain_vals):
    weighted = grad_normed * gain_vals
    grad_values = factor * (
        weighted - values * factor * factor * jnp.mean(weighted * values, axis=1, keepdims=True)
    )
    grad_gain = jnp.sum(grad_normed * values * factor, axis=0)
    return (grad_values, grad_gain)


def adamw_step(param_vals, grad_vals, first_vals, second_vals, weight_decay):
    first_new = beta_one * first_vals + (1.0 - beta_one) * grad_vals
    second_new = beta_two * second_vals + (1.0 - beta_two) * grad_vals * grad_vals
    update = (
        first_new
        / (1.0 - beta_one**STEP)
        / (jnp.sqrt(second_new / (1.0 - beta_two**STEP)) + adam_eps)
    )
    return (param_vals - learn_rate * (update + weight_decay * param_vals), first_new, second_new)


def adam_direction(grad_vals, first_vals, second_vals):
    first_new = beta_one * first_vals + (1.0 - beta_one) * grad_vals
    second_new = beta_two * second_vals + (1.0 - beta_two) * grad_vals * grad_vals
    update = (
        first_new
        / (1.0 - beta_one**STEP)
        / (jnp.sqrt(second_new / (1.0 - beta_two**STEP)) + adam_eps)
    )
    return (update, first_new, second_new)


def by_head(rows):
    tokens = rows.shape[0]
    return (
        rows.reshape(tokens, QUERY_HEADS, HEAD_WIDTH)
        .transpose(1, 0, 2)
        .reshape(QUERY_HEADS * tokens, HEAD_WIDTH)
    )


def shards(
    planes,
    hidden,
    out_grad,
    decay_log,
    doc_lengths,
    weights,
    first_moment,
    second_moment,
    small_params,
    small_first,
    small_second,
):
    local_rows = hidden.shape[1]
    count = 4 * planes
    ctx_index = lax.axis_index("ctx")
    first_pos = ctx_index * local_rows
    scale_qk = HEAD_WIDTH ** (-0.5)
    contract_last = (((1,), (1,)), ((), ()))
    gain_one, gain_two, gate_gain, conv_w, conv_bias, skip_gain = split_small(small_params)
    lengths = doc_lengths[0]
    token_positions = first_pos + jnp.arange(local_rows, dtype=jnp.int32)
    near_positions = first_pos + jnp.arange(-(CONV - 1), local_rows + CONV - 1, dtype=jnp.int32)
    near_doc = doc_layout(lengths, near_positions)[0]
    document_index, rel_pos = doc_layout(lengths, token_positions)
    doc_before = near_doc[CONV - 2]
    is_start = document_index != near_doc[CONV - 2 : CONV - 2 + local_rows]
    cosine_table, sine_table = rope_tables(rel_pos)
    begins = token_positions - rel_pos
    pos = jnp.stack([token_positions, begins])
    block = 512
    span = jnp.stack([jnp.min(begins) // block, (first_pos + local_rows - 1) // block + 1])

    tok_f = hidden[0].astype(jnp.float32)
    scale_one = lax.rsqrt(jnp.mean(tok_f * tok_f, axis=1, keepdims=True) + norm_eps)
    normed_one = (tok_f * scale_one * gain_one).astype(jnp.bfloat16)
    own_b = weights.astype(jnp.bfloat16)
    mixer_w = gather_rows(own_b[:, : MIXIN + MIXOUT], planes, 0).reshape(D, MIXIN + MIXOUT)
    mlp_w = lax.all_gather(own_b[:, MIXIN + MIXOUT :], ("ctx", "fsdp"), axis=0, tiled=True)
    projected = jnp.dot(normed_one, mixer_w[:, :MIXIN], preferred_element_type=jnp.float32)
    query_rows = apply_rotary(
        projected[:, :QUERY_WIDTH].reshape(local_rows, QUERY_HEADS, HEAD_WIDTH),
        cosine_table,
        sine_table,
    ).astype(jnp.bfloat16)
    key_rows = apply_rotary(
        projected[:, QUERY_WIDTH : QUERY_WIDTH + KEY_WIDTH].reshape(
            local_rows, KEY_VALUE_HEADS, HEAD_WIDTH
        ),
        cosine_table,
        sine_table,
    ).reshape(local_rows, KEY_WIDTH)
    kv_rows = jnp.concatenate(
        [key_rows, projected[:, QUERY_WIDTH + KEY_WIDTH : QUERY_WIDTH + 2 * KEY_WIDTH]], axis=1
    ).astype(jnp.bfloat16)
    gate_in = projected[:, QUERY_WIDTH + 2 * KEY_WIDTH : QUERY_WIDTH + 2 * KEY_WIDTH + INNER]
    xbc_b = projected[:, QUERY_WIDTH + 2 * KEY_WIDTH + INNER :].astype(jnp.bfloat16)
    query_heads = by_head(query_rows.reshape(local_rows, QUERY_WIDTH) * jnp.bfloat16(scale_qk))

    log_decay = decay_log[0]
    cum = jnp.cumsum(log_decay, axis=1)
    steps_in = jnp.where(is_start[None, :], 1.0, jnp.sqrt(-jnp.expm1(2.0 * log_decay)))
    decay_in = jnp.where((document_index == doc_before)[None, :], jnp.exp(cum), 0.0)
    same_end = (document_index == document_index[-1])[None, :]
    to_end = jnp.where(same_end, jnp.exp(jnp.minimum(cum[:, -1:] - cum, 0.0)), 0.0)
    cum_t, dt_t, we_t, din_t = cum.T, steps_in.T, to_end.T, decay_in.T
    own_decay = jnp.zeros((8, 128), jnp.float32).at[0, :MH].set(decay_in[:, -1])

    kv_all, edge_in, decays = spread(planes, kv_rows, xbc_b[local_rows - 16 :], own_decay, 1)
    decays = jnp.repeat(decays[:, 0, :MH], MP, axis=1)
    kv_flat = kv_all.reshape(count * local_rows, 2 * KEY_WIDTH)

    same_doc = jnp.stack(
        [near_doc[j : j + local_rows] == document_index for j in range(CONV)], axis=1
    ).astype(jnp.float32)
    xe = jnp.concatenate(
        [
            jnp.zeros((9 - CONV, XBC), jnp.float32),
            edge_in[17 - CONV :].astype(jnp.float32),
            xbc_b.astype(jnp.float32),
        ],
        axis=0,
    )
    skip_wide = jnp.repeat(skip_gain, MP)[None, :]
    doc_c, doc_r = document_index[:, None], document_index[None, :]
    pre, xo, mix_local, state_out = mixer(
        xe, same_doc, conv_w, conv_bias[None, :], cum_t, cum, dt_t, we_t, skip_wide, doc_c, doc_r
    )
    state_in = relay(planes, False, state_out, decays, 2)
    attended, log_sums = attend(span, query_heads, kv_flat, pos, block)
    mixed, branch = gate_out(
        mix_local, xo, state_in, din_t, gate_in, gate_gain[None, :], attended
    )

    resid_one = tok_f + lax.dot_general(
        branch, mixer_w[:, MIXIN:], contract_last, preferred_element_type=jnp.float32
    )
    scale_two = lax.rsqrt(jnp.mean(resid_one * resid_one, axis=1, keepdims=True) + norm_eps)
    normed_two = (resid_one * scale_two * gain_two).astype(jnp.bfloat16)
    gate_up = jnp.dot(normed_two, mlp_w[:, : 2 * FF], preferred_element_type=jnp.float32)
    gate_part = gate_up[:, :FF]
    up_part = gate_up[:, FF:]
    sigma_gate = jax.nn.sigmoid(gate_part)
    silu_gate = gate_part * sigma_gate
    hidden_mid = (silu_gate * up_part).astype(jnp.bfloat16)
    block_out = resid_one + lax.dot_general(
        hidden_mid, mlp_w[:, 2 * FF :], contract_last, preferred_element_type=jnp.float32
    )
    out_hidden = block_out.astype(jnp.bfloat16)[None]
    grad_out = out_grad[0]
    grad_mid = jnp.dot(grad_out, mlp_w[:, 2 * FF :], preferred_element_type=jnp.float32)
    silu_slope = sigma_gate * (1.0 + gate_part * (1.0 - sigma_gate))
    grad_gate_up = jnp.concatenate(
        [grad_mid * up_part * silu_slope, grad_mid * silu_gate], axis=1
    ).astype(jnp.bfloat16)
    grad_normed_two = lax.dot_general(
        grad_gate_up, mlp_w[:, : 2 * FF], contract_last, preferred_element_type=jnp.float32
    )
    grad_norm_two, grad_gain_two = norm_backward(grad_normed_two, resid_one, scale_two, gain_two)
    grad_resid_one = grad_out.astype(jnp.float32) + grad_norm_two
    grad_resid_b = grad_resid_one.astype(jnp.bfloat16)
    mlp_grads = scatter_rows(planes, normed_two.T, grad_gate_up, grad_out.T, hidden_mid, 3)

    grad_branch = jnp.dot(grad_resid_b, mixer_w[:, MIXIN:], preferred_element_type=jnp.float32)
    grad_attended = grad_branch[:, :QUERY_WIDTH].astype(jnp.bfloat16)
    grad_mixed, grad_gate_in, grad_gate_gain, grad_state, grad_c = gate_back(
        grad_branch[:, QUERY_WIDTH:], mixed, gate_in, gate_gain[None, :], din_t, xo, state_in
    )
    grad_state_out = relay(planes, True, grad_state, decays, 4)
    delta = jnp.sum(
        (grad_attended.astype(jnp.float32) * attended.astype(jnp.float32)).reshape(
            local_rows, QUERY_HEADS, HEAD_WIDTH
        ),
        axis=-1,
    ).T
    grad_query, kv_grads = attend_back(
        span, query_heads, by_head(grad_attended), kv_flat, pos, log_sums, delta, block
    )
    grad_pre, conv_grads, skip_grads = mixer_back(
        xe, same_doc, conv_w, cum_t, cum, dt_t, we_t, skip_wide, doc_c, doc_r,
        pre, xo, grad_mixed, grad_c, grad_state_out,
    )
    key_gradients, pre_next = fold(
        planes, kv_grads.reshape(count, local_rows, 2 * KEY_WIDTH), grad_pre[:8], 5
    )
    pre_ext = jnp.concatenate([grad_pre, pre_next[: CONV - 1]], axis=0)
    doc_next = near_doc[CONV - 1 :]
    grad_xbc = sum(
        conv_w[j][None, :]
        * pre_ext[CONV - 1 - j : CONV - 1 - j + local_rows]
        * (doc_next[CONV - 1 - j : CONV - 1 - j + local_rows] == document_index)[:, None]
        for j in range(CONV)
    )
    grad_q = inverse_rotary(
        grad_query.reshape(local_rows, QUERY_HEADS, HEAD_WIDTH), cosine_table, sine_table
    ).reshape(local_rows, QUERY_WIDTH)
    key_gradient = inverse_rotary(
        key_gradients[:, :KEY_WIDTH].reshape(local_rows, KEY_VALUE_HEADS, HEAD_WIDTH),
        cosine_table,
        sine_table,
    ).reshape(local_rows, KEY_WIDTH)
    grad_proj = jnp.concatenate(
        [
            grad_q.astype(jnp.bfloat16),
            key_gradient.astype(jnp.bfloat16),
            key_gradients[:, KEY_WIDTH:].astype(jnp.bfloat16),
            grad_gate_in,
            grad_xbc.astype(jnp.bfloat16),
        ],
        axis=1,
    )
    mixer_grads = scatter_rows(planes, normed_one.T, grad_proj, grad_resid_b.T, branch, 6)
    grad_normed_one = lax.dot_general(
        grad_proj, mixer_w[:, :MIXIN], contract_last, preferred_element_type=jnp.float32
    )
    grad_norm_one, grad_gain_one = norm_backward(grad_normed_one, tok_f, scale_one, gain_one)
    grad_hidden = (grad_resid_one + grad_norm_one)[None]
    small_local = jnp.concatenate(
        [
            grad_gain_one,
            grad_gain_two,
            grad_gate_gain[0],
            conv_grads.reshape(-1),
            jnp.sum(skip_grads.reshape(MH, MP), axis=1),
        ]
    )
    size = small_local.shape[0]
    padded = jnp.pad(small_local, (0, SMALL_ROWS * 128 - size)).reshape(SMALL_ROWS, 128)
    small_grads = total_small(planes, padded, 7).reshape(-1)[:size]
    grad_weights = jnp.concatenate([mixer_grads, mlp_grads], axis=1)
    new_weights, new_first, new_second = adamw_step(
        weights, grad_weights, first_moment, second_moment, decay_rate
    )
    small_step, small_first_new, small_second_new = adam_direction(
        small_grads, small_first, small_second
    )
    return (
        out_hidden,
        grad_hidden,
        grad_weights,
        new_weights,
        new_first,
        new_second,
        small_grads,
        small_step,
        small_first_new,
        small_second_new,
    )


def solution(mesh):
    placed = (
        P("fsdp", "ctx", None),
        P("fsdp", "ctx", None),
        P("fsdp", None, "ctx"),
        P("fsdp", None),
        P(("ctx", "fsdp"), None),
        P(("ctx", "fsdp"), None),
        P(("ctx", "fsdp"), None),
        P(),
        P(),
        P(),
    )
    return jax.shard_map(
        functools.partial(shards, mesh.shape["ctx"] // 4),
        mesh=mesh,
        in_specs=placed,
        out_specs=(
            P("fsdp", "ctx", None),
            P("fsdp", "ctx", None),
            P(("ctx", "fsdp"), None),
            P(("ctx", "fsdp"), None),
            P(("ctx", "fsdp"), None),
            P(("ctx", "fsdp"), None),
            P(),
            P(),
            P(),
            P(),
        ),
        check_vma=False,
    )
```

```python
import functools
import math

import jax
import jax.numpy as jnp
from jax import lax
from jax.experimental import pallas as pl
from jax.experimental.pallas import tpu as pltpu
from jax.sharding import PartitionSpec as P

D = 1024
QUERY_HEADS = 8
KEY_VALUE_HEADS = 2
HEAD_WIDTH = 64
MH = 24
MP = 64
NS = 128
FF = 2048
CONV = 4
STEP = 3
QUERY_WIDTH = 512
KEY_WIDTH = 128
INNER = 1536
XBC = 1792
MIXIN = 4096
MIXOUT = 2048
SMALL_ROWS = 104
TOKENS = 256
PIECE = 512

norm_eps = 1e-05
rope_base = 100000000000.0
large_negative = -1e30
learn_rate = 0.02
beta_one = 0.9
beta_two = 0.95
adam_eps = 1e-08
decay_rate = 0.1

MESH = pl.DeviceIdType.MESH
BF = jnp.bfloat16
F32 = jnp.float32
VM = pl.BlockSpec(memory_space=pltpu.VMEM)
SM = pl.BlockSpec(memory_space=pltpu.SMEM)
HB = pl.BlockSpec(memory_space=pl.ANY)
DMA = pltpu.SemaphoreType.DMA


def params(collective=None):
    if collective is None:
        return pltpu.CompilerParams(vmem_limit_bytes=62 * 2**20)
    return pltpu.CompilerParams(
        collective_id=collective, has_side_effects=True, vmem_limit_bytes=62 * 2**20
    )


def nt(a, b):
    return lax.dot_general(a, b, (((1,), (1,)), ((), ())), preferred_element_type=F32)


def tn(a, b):
    return lax.dot_general(a, b, (((0,), (0,)), ((), ())), preferred_element_type=F32)


def nn(a, b):
    return lax.dot_general(a, b, (((1,), (0,)), ((), ())), preferred_element_type=F32)


class Place:
    def __init__(self, planes):
        ctx = lax.axis_index("ctx")
        self.ctx = ctx
        self.Z, self.z, self.x, self.c = planes, ctx // 4, (ctx // 2) % 2, ctx % 2
        self.y = lax.axis_index("fsdp")
        self.up, self.down = self.z + 1 < planes, self.z > 0

    def shard(self, z, x, y, c):
        return ((z * 2 + x) * 2 + c) * 2 + y

    def spot(self, z, x, c):
        return (z * 2 + x) * 2 + c

    def dev(self, z, x, y, c):
        return ((z * 2 + x) * 2 + c, y)

    def near(self, d):
        z, x, y, c = self.z, self.x, self.y, self.c
        return {
            "x": self.dev(z, 1 - x, y, c),
            "y": self.dev(z, x, 1 - y, c),
            "c": self.dev(z, x, y, 1 - c),
            "u": self.dev(z + 1, x, y, c),
            "d": self.dev(z - 1, x, y, c),
        }[d]

    def zord(self, k):
        if k == self.Z - 1:
            return self.z
        low = self.Z - 1 - k
        z = self.z
        return jnp.where(
            2 * z < self.Z, jnp.where(low > z, low, low - 1), jnp.where(k < z, k, k + 1)
        )


def greet(pc, dims="xyc", chain=True):
    bar = pltpu.get_barrier_semaphore()

    def sig(d):
        pl.semaphore_signal(bar, inc=1, device_id=pc.near(d), device_id_type=MESH)

    for d in dims:
        sig(d)
    if chain:
        pl.when(pc.up)(lambda: sig("u"))
        pl.when(pc.down)(lambda: sig("d"))
    peers = len(dims)
    if chain:
        peers = peers + pc.up.astype(jnp.int32) + pc.down.astype(jnp.int32)
    pl.semaphore_wait(bar, peers)


def greet_row(pc, across=False):
    bar = pltpu.get_barrier_semaphore()
    n = 4 * pc.Z

    @pl.loop(1, n)
    def _(d):
        pl.semaphore_signal(
            bar, inc=1, device_id=(lax.rem(pc.ctx + d, n), pc.y), device_id_type=MESH
        )

    if across:
        pl.semaphore_signal(bar, inc=1, device_id=pc.near("y"), device_id_type=MESH)
    pl.semaphore_wait(bar, n - 1 + int(across))


def rcopy(pc, src, dst, ssem, rsem, d):
    return pltpu.make_async_remote_copy(
        src_ref=src,
        dst_ref=dst,
        send_sem=ssem,
        recv_sem=rsem,
        device_id=pc.near(d) if isinstance(d, str) else d,
        device_id_type=MESH,
    )


def add_into(dst, parts, width=512):
    columns = dst.shape[-1]
    step = width if columns % width == 0 else (256 if columns % 256 == 0 else 128)

    @pl.loop(0, columns // step)
    def _(i):
        sl = pl.ds(pl.multiple_of(i * step, step), step)
        total = parts[0][:, sl].astype(F32)
        for r in parts[1:]:
            total = total + r[:, sl].astype(F32)
        dst[:, sl] = total.astype(dst.dtype)


def gather_scratch(planes):
    n = 8 * planes
    return [
        DMA((2, planes, 2)),
        DMA((2, planes)),
        DMA((2, planes, 2)),
        DMA((2, planes, 4)),
        DMA((2, n)),
        DMA,
    ]


def gather_steps(pc, w_ref, out_ref, scratch):
    zs, xs, ys, cs, rs, loc = scratch
    Z, z, x, y, c = pc.Z, pc.z, pc.x, pc.y, pc.c
    half = w_ref.shape[-1] // 2
    me = pc.shard(z, x, y, c)

    def cp(p, s, sem, d, own=False):
        sl = pl.ds(p * half, half)
        src = w_ref.at[:, sl] if own else out_ref.at[s, :, sl]
        return rcopy(pc, src, out_ref.at[s, :, sl], sem, rs.at[p, s], d)

    def along(p, zz, up, own=False):
        return cp(p, pc.shard(zz, x, y, c), zs.at[p, zz, int(up)], "u" if up else "d", own)

    def first(p, zz, own=False):
        return cp(p, pc.shard(zz, x, y, c), xs.at[p, zz], "x" if p == 0 else "y", own)

    def second(p, zz, q, own=False):
        if p == 0:
            return cp(p, pc.shard(zz, x if q == 0 else 1 - x, y, c), ys.at[p, zz, q], "y", own)
        return cp(p, pc.shard(zz, x, y if q == 0 else 1 - y, c), ys.at[p, zz, q], "x", own)

    def core(p, zz, q, r, own=False):
        s = pc.shard(zz, x if q == 0 else 1 - x, y if r == 0 else 1 - y, c)
        return cp(p, s, cs.at[p, zz, q * 2 + r], "c", own)

    def arrived(p, s):
        sl = pl.ds(p * half, half)
        rcopy(pc, w_ref.at[:, sl], out_ref.at[s, :, sl], loc, rs.at[p, s], "c").wait_recv()

    keep = pltpu.make_async_copy(w_ref, out_ref.at[me], loc)
    keep.start()
    for p in (0, 1):
        pl.when(pc.up)(lambda: along(p, z, True, True).start())
        pl.when(pc.down)(lambda: along(p, z, False, True).start())
        first(p, z, True).start()
    for p in (0, 1):
        second(p, z, 0, True).start()
        core(p, z, 0, 0, True).start()
    yield
    for d in range(1, Z):
        for p in (0, 1):

            def onward(zz, up, more):
                arrived(p, pc.shard(zz, x, y, c))
                pl.when(more)(lambda: along(p, zz, up).start())
                first(p, zz).start()
                second(p, zz, 0).start()
                core(p, zz, 0, 0).start()

            pl.when(z - d >= 0)(lambda: onward(z - d, True, pc.up))
            pl.when(z + d < Z)(lambda: onward(z + d, False, pc.down))
        yield
    near = [lax.rem(z + k, Z) for k in range(Z)]
    for zz in near:
        for p in (0, 1):
            xx, yy = (1 - x, y) if p == 0 else (x, 1 - y)
            arrived(p, pc.shard(zz, xx, yy, c))
            second(p, zz, 1).start()
            core(p, zz, *((1, 0) if p == 0 else (0, 1))).start()
        yield
    for q in (0, 1):
        for zz in near:
            for p in (0, 1):
                if p == 0:
                    xx, yy, a, b = (x if q == 0 else 1 - x), 1 - y, q, 1
                else:
                    xx, yy, a, b = 1 - x, (y if q == 0 else 1 - y), 1, q
                arrived(p, pc.shard(zz, xx, yy, c))
                core(p, zz, a, b).start()
            yield
    for q in range(4):
        for zz in near:
            for p in (0, 1):
                xx = x if q < 2 else 1 - x
                yy = y if q % 2 == 0 else 1 - y
                arrived(p, pc.shard(zz, xx, yy, 1 - c))
        yield
    keep.wait()
    for p in (0, 1):
        for zz in range(Z):
            pl.when(pc.up & (zz <= z))(lambda: along(p, zz, True).wait_send())
            pl.when(pc.down & (zz >= z))(lambda: along(p, zz, False).wait_send())
            first(p, zz).wait_send()
            for q in (0, 1):
                second(p, zz, q).wait_send()
            for q in range(4):
                core(p, zz, q // 2, q % 2).wait_send()


def gather_kernel(planes, w_ref, out_ref, *scratch):
    pc = Place(planes)
    greet(pc)
    for _ in gather_steps(pc, w_ref, out_ref, scratch):
        pass


def gather_rows(w, planes, collective):
    rows, columns = w.shape
    return pl.pallas_call(
        functools.partial(gather_kernel, planes),
        out_shape=jax.ShapeDtypeStruct((8 * planes, rows, columns), w.dtype),
        in_specs=[HB],
        out_specs=HB,
        scratch_shapes=gather_scratch(planes),
        compiler_params=params(collective),
    )(w)


def spread_scratch(planes):
    n = 4 * planes
    return [DMA((planes,)), DMA((planes,)), DMA((planes, 2)), DMA((n,)), DMA((n,)), DMA((n,)), DMA((3,))]


def spread_kernel(planes, kv_ref, edge_ref, dec_ref, all_ref, got_ref, decs_ref, *scratch):
    us, xs, cs, rs, ds, dr, one = scratch
    pc = Place(planes)
    Z, z, x, c = pc.Z, pc.z, pc.x, pc.c
    n = 4 * Z
    me = pc.ctx
    greet_row(pc)

    def cp(zz, xx, sem, d, own=False):
        s = pc.spot(zz, xx, c)
        return rcopy(pc, kv_ref if own else all_ref.at[s], all_ref.at[s], sem, rs.at[s], d)

    def arrived(s):
        rcopy(pc, kv_ref, all_ref.at[s], one.at[0], rs.at[s], "c").wait_recv()

    def decay_copy(d, to):
        return rcopy(pc, dec_ref, decs_ref.at[me], ds.at[d], dr.at[d], (lax.rem(to, n), pc.y))

    edge = rcopy(pc, edge_ref, got_ref, one.at[1], one.at[2], (lax.rem(me + 1, n), pc.y))
    keep = pltpu.make_async_copy(kv_ref, all_ref.at[me], one.at[0])
    keep.start()
    pl.when(pc.up)(lambda: cp(z, x, us.at[z], "u", True).start())
    cp(z, x, xs.at[z], "x", True).start()
    cp(z, x, cs.at[z, 0], "c", True).start()
    pl.when(me < n - 1)(lambda: edge.start())
    decs_ref[me] = dec_ref[...]

    @pl.loop(1, n)
    def _(d):
        decay_copy(d, me + d).start()

    for d in range(1, Z):

        @pl.when(z - d >= 0)
        def _():
            zz = z - d
            arrived(pc.spot(zz, x, c))
            pl.when(pc.up)(lambda: cp(zz, x, us.at[zz], "u").start())
            cp(zz, x, xs.at[zz], "x").start()
            cp(zz, x, cs.at[zz, 0], "c").start()

    for d in range(Z):

        @pl.when(z - d >= 0)
        def _():
            arrived(pc.spot(z - d, 1 - x, c))
            cp(z - d, 1 - x, cs.at[z - d, 1], "c").start()

    for d in range(Z):

        @pl.when(z - d >= 0)
        def _():
            for xx in (x, 1 - x):
                arrived(pc.spot(z - d, xx, 1 - c))

    keep.wait()
    for zz in range(Z):

        @pl.when(zz <= z)
        def _():
            pl.when(pc.up)(lambda: cp(zz, x, us.at[zz], "u").wait_send())
            cp(zz, x, xs.at[zz], "x").wait_send()
            cp(zz, x, cs.at[zz, 0], "c").wait_send()
            cp(zz, 1 - x, cs.at[zz, 1], "c").wait_send()

    @pl.when(me < n - 1)
    def _():
        edge.wait_send()

    @pl.when(me > 0)
    def _():
        edge.wait_recv()

    @pl.when(me == 0)
    def _():
        got_ref[...] = jnp.zeros_like(got_ref)

    @pl.loop(1, n)
    def _(d):
        decay_copy(d, me + d).wait()


def spread(planes, kv, edge, dec, collective):
    n = 4 * planes
    return pl.pallas_call(
        functools.partial(spread_kernel, planes),
        out_shape=(
            jax.ShapeDtypeStruct((n,) + kv.shape, kv.dtype),
            jax.ShapeDtypeStruct(edge.shape, edge.dtype),
            jax.ShapeDtypeStruct((n,) + dec.shape, dec.dtype),
        ),
        in_specs=[VM] * 3,
        out_specs=(VM,) * 3,
        scratch_shapes=spread_scratch(planes),
        compiler_params=params(collective),
    )(kv, edge, dec)


def scatter_scratch(planes, rows, widths):
    columns = sum(widths)
    w, h = columns // 4, columns // 8 * 3
    half = 4 * planes * rows
    return [
        pltpu.VMEM((planes, 2, 2, rows, columns), BF),
        pltpu.VMEM((2, planes, 2, rows, h), BF),
        pltpu.VMEM((2, planes, rows, h), BF),
        pltpu.VMEM((2, planes + 1, rows, h), BF),
        pltpu.VMEM((planes + 1, 2, 2, rows, w), BF),
        pltpu.VMEM((3, rows, w), BF),
        pltpu.VMEM((len(widths), half, TOKENS), BF),
        pltpu.VMEM((TOKENS, columns), BF),
        DMA((len(widths),)),
        DMA((len(widths),)),
        DMA((columns // PIECE,)),
        DMA((columns // PIECE,)),
        DMA((2, planes, 2)),
        DMA((2, planes, 2)),
        DMA((2, planes)),
        DMA((2, planes)),
        DMA((3, planes)),
        DMA((3, planes + 1)),
        DMA((3,)),
        DMA((3,)),
    ]


def scatter_steps(pc, pairs, out_ref, scratch):
    g, r2, r3, rz, rw, rt, la, rb, as_, ar, bs, br, s2, q2, s3, q3, sz, qz, st, qt = scratch
    Z, z, x, y, c = pc.Z, pc.z, pc.x, pc.y, pc.c
    rows = g.shape[3]
    w = g.shape[-1] // 4
    h = g.shape[-1] // 8 * 3
    depth = 4 * rows

    def cols(p):
        return pl.ds(0, w) if p == 2 else pl.ds(w + p * h, h)

    pieces = []
    base = 0
    for i, (left, right) in enumerate(pairs):
        for at in range(0, right.shape[1], PIECE):
            pieces.append((i, at, base + at))
        base += right.shape[1]

    def acopy(i):
        return rcopy(pc, pairs[i][0].at[1 - c], la.at[i], as_.at[i], ar.at[i], "c")

    def bcopy(k):
        i, at, to = pieces[k]
        return rcopy(
            pc, pairs[i][1].at[:, pl.ds(at, PIECE)], rb.at[:, pl.ds(to, PIECE)], bs.at[k], br.at[k], "c"
        )

    def make(zz, k, first):
        i, at, to = pieces[k]
        if first:
            if at == 0:
                acopy(i).wait_recv()
            bcopy(k).wait_recv()
        here = pl.ds(pl.multiple_of(zz * depth, depth), depth)
        mine, theirs = pairs[i][0][c, here, :], la[i, here, :]
        for t in range(0, PIECE, 512):
            tile = nn(mine, pairs[i][1][:, pl.ds(at + t, 512)]) + nn(theirs, rb[:, pl.ds(to + t, 512)])
            g[zz, :, :, :, pl.ds(to + t, 512)] = tile.reshape(2, 2, rows, 512).astype(BF)

    def copy2(p, zz, j):
        xx, yy = (x if j == 0 else 1 - x, 1 - y) if p == 0 else (1 - x, y if j == 0 else 1 - y)
        return rcopy(
            pc, g.at[zz, xx, yy, :, cols(p)], r2.at[p, zz, j], s2.at[p, zz, j], q2.at[p, zz, j],
            "y" if p == 0 else "x",
        )

    def copy3(p, zz):
        xx, yy = (1 - x, y) if p == 0 else (x, 1 - y)
        return rcopy(
            pc, g.at[zz, xx, yy, :, cols(p)], r3.at[p, zz], s3.at[p, zz], q3.at[p, zz],
            "x" if p == 0 else "y",
        )

    def views(p, zz, slot):
        if p == 2:
            return g.at[zz, :, :, :, cols(p)], rw.at[slot]
        return g.at[zz, x, y, :, cols(p)], rz.at[p, slot]

    def sendz(p, zz, up):
        slot = jnp.where(zz == z + 1, Z, zz) if up else zz
        src, dst = views(p, zz, slot)
        return rcopy(pc, src, dst, sz.at[p, zz], qz.at[p, slot], "u" if up else "d")

    def gotz(p, slot):
        src, dst = views(p, 0, slot)
        rcopy(pc, src, dst, sz.at[p, 0], qz.at[p, slot], "c").wait_recv()

    def add_plane(zz, slots):
        for xx in (0, 1):
            for yy in (0, 1):
                a = g.at[zz, xx, yy, :, cols(2)]
                add_into(a, [a] + [rw.at[k, xx, yy] for k in slots])

    def at_time(t, f):
        below, above = t - (Z - 1 - z), Z - 1 - (t - z)
        pl.when((below >= 0) & (below < z))(lambda: f(below, False, pc.up))
        pl.when((above > z) & (above < Z))(lambda: f(above, True, pc.down))

    def chain_first(zz, up, more):
        @pl.when(more)
        def _():
            gotz(2, zz)
            add_plane(zz, [zz])

        sendz(2, zz, up).start()

    def tail(k):
        if k < 2:
            return rcopy(pc, g.at[z, k, 1 - y, :, cols(2)], rt.at[k], st.at[k], qt.at[k], "y")
        return rcopy(pc, g.at[z, 1 - x, y, :, cols(2)], rt.at[2], st.at[2], qt.at[2], "x")

    for i in range(len(pairs)):
        acopy(i).start()
        for k in range(len(pieces)):
            if pieces[k][0] == i:
                bcopy(k).start()
    yield
    ends = {w + h: 0, w + 2 * h: 1}
    for k in range(Z + 1):
        if k < Z:
            zz = pc.zord(k)
            for n in range(len(pieces)):
                make(zz, n, k == 0)
                end = pieces[n][2] + PIECE
                if end == w and k == 0 and Z > 1:
                    at_time(0, chain_first)
                if end in ends:
                    copy2(ends[end], zz, 1).start()
            yield
        if k > 0:
            zz = pc.zord(k - 1)
            for p in (0, 1):
                copy2(p, zz, 1).wait_recv()
                a = g.at[(zz,) + ((1 - x, y) if p == 0 else (x, 1 - y)) + (slice(None), cols(p))]
                add_into(a, [a, r2.at[p, zz, 1]])
                copy3(p, zz).start()
            for p in (0, 1):
                copy2(p, zz, 0).start()
            if 0 < k - 1 < Z - 1:
                at_time(k - 1, chain_first)
            yield

    def own(p, zz):
        copy2(p, zz, 0).wait_recv()
        copy3(p, zz).wait_recv()
        a = g.at[zz, x, y, :, cols(p)]
        return a, [a, r2.at[p, zz, 0], r3.at[p, zz]]

    def chain(p, zz, up, more):
        a, parts = own(p, zz)

        @pl.when(more)
        def _():
            gotz(p, zz)
            add_into(a, parts + [rz.at[p, zz]])

        @pl.when(jnp.logical_not(more))
        def _():
            add_into(a, parts)

        sendz(p, zz, up).start()

    def gather_plane(slot):
        gotz(2, slot)
        add_plane(z, [slot])

    pl.when(pc.up)(lambda: gather_plane(z))
    pl.when(pc.down)(lambda: gather_plane(Z))
    for k in (0, 1):
        tail(k).start()
    yield
    for t in range(Z - 1):
        for p in (0, 1):
            at_time(t, functools.partial(chain, p))
        if t == 0:
            for k in (0, 1):
                tail(k).wait_recv()
                a = g.at[z, k, y, :, cols(2)]
                add_into(a, [a, rt.at[k]])
            tail(2).start()
        yield
    tail(2).wait_recv()
    add_into(out_ref.at[:, cols(2)], [g.at[z, x, y, :, cols(2)], rt.at[2]])
    for p in (0, 1):
        a, parts = own(p, z)
        o = out_ref.at[:, cols(p)]
        add_into(o, parts)

        def last(slot):
            gotz(p, slot)
            add_into(o, [o, rz.at[p, slot]])

        pl.when(pc.up)(lambda: last(z))
        pl.when(pc.down)(lambda: last(Z))
        yield
    for i in range(len(pairs)):
        acopy(i).wait_send()
    for k in range(len(pieces)):
        bcopy(k).wait_send()
    for k in range(3):
        tail(k).wait_send()
    for zz in range(Z):
        for p in (0, 1):
            for j in (0, 1):
                copy2(p, zz, j).wait_send()
            copy3(p, zz).wait_send()
        for p in (0, 1, 2):
            pl.when(zz < z)(lambda: sendz(p, zz, False).wait_send())
            pl.when(zz > z)(lambda: sendz(p, zz, True).wait_send())


def scatter_kernel(planes, count, *refs):
    pc = Place(planes)
    greet(pc)
    pairs = tuple(zip(refs[:count], refs[count : 2 * count]))
    for _ in scatter_steps(pc, pairs, refs[2 * count], refs[2 * count + 1 :]):
        pass


def scatter_rows(planes, lefts, rights, collective):
    rows = lefts[0].shape[1] // (4 * planes)
    widths = [r.shape[1] for r in rights]
    return pl.pallas_call(
        functools.partial(scatter_kernel, planes, len(lefts)),
        out_shape=jax.ShapeDtypeStruct((rows, sum(widths)), F32),
        in_specs=[VM] * (2 * len(lefts)),
        out_specs=VM,
        scratch_shapes=scatter_scratch(planes, rows, widths),
        compiler_params=params(collective),
    )(*lefts, *rights)


def by_core(rows, planes):
    tokens = rows.shape[0]
    each = D // (8 * planes)
    cut = rows.T.reshape(2 * planes, 2, 2 * each, tokens)
    return cut.transpose(1, 0, 2, 3).reshape(2, D // 2, tokens)


def fold_scratch(planes, rows, columns):
    return [
        pltpu.VMEM((planes, 2, rows, columns), BF),
        pltpu.VMEM((planes, rows, columns), BF),
        pltpu.VMEM((planes, rows, columns), BF),
        pltpu.VMEM((planes, 2, rows, columns), BF),
        DMA((planes, 2)),
        DMA((planes, 2)),
        DMA((planes,)),
        DMA((planes,)),
        DMA((planes,)),
        DMA((planes,)),
    ]


def fold_steps(pc, block, out_ref, scratch):
    rc, rx, rz, acc, cs, cr, xs, xr, zs, zr = scratch
    Z, z, x, c = pc.Z, pc.z, pc.x, pc.c

    def ccopy(zz, q):
        xx = x if q == 0 else 1 - x
        return rcopy(pc, block(pc.spot(zz, xx, 1 - c)), rc.at[zz, q], cs.at[zz, q], cr.at[zz, q], "c")

    def xcopy(zz):
        return rcopy(pc, acc.at[zz, 1], rx.at[zz], xs.at[zz], xr.at[zz], "x")

    def zcopy(zz):
        return rcopy(pc, acc.at[zz, 0], rz.at[zz], zs.at[zz], zr.at[zz], "d")

    def each(f):
        for zz in range(Z):
            pl.when(zz <= z)(functools.partial(f, zz))

    def a(zz):
        ccopy(zz, 1).start()
        ccopy(zz, 0).start()

    def b(zz):
        ccopy(zz, 1).wait_recv()
        add_into(acc.at[zz, 1], [block(pc.spot(zz, 1 - x, c)), rc.at[zz, 1]], 128)
        xcopy(zz).start()

    def m(zz):
        ccopy(zz, 0).wait_recv()
        add_into(acc.at[zz, 0], [block(pc.spot(zz, x, c)), rc.at[zz, 0]], 128)

    def e(zz):
        xcopy(zz).wait_recv()

        def finish(parts):
            @pl.when(zz < z)
            def _():
                add_into(acc.at[zz, 0], parts, 128)
                zcopy(zz).start()

            pl.when(zz == z)(lambda: add_into(out_ref, parts, 128))

        @pl.when(pc.up)
        def _():
            zcopy(zz).wait_recv()
            finish([acc.at[zz, 0], rx.at[zz], rz.at[zz]])

        pl.when(jnp.logical_not(pc.up))(lambda: finish([acc.at[zz, 0], rx.at[zz]]))

    def w(zz):
        ccopy(zz, 1).wait_send()
        ccopy(zz, 0).wait_send()
        xcopy(zz).wait_send()
        pl.when(zz < z)(lambda: zcopy(zz).wait_send())

    for f in (a, b, m, e):
        each(f)
        yield
    each(w)


def relay_scratch(planes):
    n = 4 * planes
    piece = pltpu.VMEM((n, NS // n, INNER), BF)
    return [piece, piece, DMA((n,)), DMA((n,)), DMA((n,)), DMA((n,))]


def relay_steps(pc, reverse, s_ref, dec_ref, out_ref, scratch):
    got, part, ss, sr, bs, br = scratch
    n = 4 * pc.Z
    me = pc.ctx

    def to(d):
        return lax.rem(me + d, n)

    def there(d):
        return rcopy(pc, s_ref.at[to(d)], got.at[me], ss.at[d], sr.at[d], (to(d), pc.y))

    def back(d):
        return rcopy(pc, part.at[to(d)], out_ref.at[me], bs.at[d], br.at[d], (to(d), pc.y))

    pl.loop(1, n)(lambda d: there(d).start())
    got[me] = s_ref[me]
    yield
    pl.loop(1, n)(lambda d: there(d).wait_recv())
    total = jnp.zeros(got.shape[1:], F32)
    for k in range(n):
        j = n - 1 - k if reverse else k
        part[j] = total.astype(BF)
        total = total * dec_ref[pl.ds(j, 1), :] + got[j].astype(F32)
    pl.loop(1, n)(lambda d: back(d).start())
    out_ref[me] = part[me]
    yield
    pl.loop(1, n)(lambda d: back(d).wait_recv())
    yield

    @pl.loop(1, n)
    def _(d):
        there(d).wait_send()
        back(d).wait_send()


def relay_kernel(planes, reverse, s_ref, dec_ref, out_ref, *scratch):
    pc = Place(planes)
    greet_row(pc)
    for _ in relay_steps(pc, reverse, s_ref, dec_ref, out_ref, scratch):
        pass


def relay(planes, reverse, state, decays, collective):
    n = 4 * planes
    piece = state.reshape(n, NS // n, INNER)
    out = pl.pallas_call(
        functools.partial(relay_kernel, planes, reverse),
        out_shape=jax.ShapeDtypeStruct(piece.shape, BF),
        in_specs=[VM] * 2,
        out_specs=VM,
        scratch_shapes=relay_scratch(planes),
        compiler_params=params(collective),
    )(piece, decays)
    return out.reshape(NS, INNER)


def total_scratch(planes):
    shape = (SMALL_ROWS, 128)
    return [
        pltpu.VMEM((6,) + shape, F32),
        pltpu.VMEM((planes,) + shape, F32),
        DMA((3,)),
        DMA((3,)),
        DMA((planes,)),
        DMA((planes,)),
    ]


def plane_peers(pc):
    return [pc.dev(lax.rem(pc.z + d, pc.Z), pc.x, pc.y, pc.c) for d in range(1, pc.Z)]


def total_steps(pc, out_ref, scratch):
    rx, rz, ss, sr, zs, zr = scratch
    Z, z = pc.Z, pc.z
    for i, d in enumerate("cxy"):
        rx[2 * i] = out_ref[...]
        cp = rcopy(pc, rx.at[2 * i], rx.at[2 * i + 1], ss.at[i], sr.at[i], d)
        cp.start()
        yield
        cp.wait()
        out_ref[...] = out_ref[...] + rx[2 * i + 1]
    rz[z] = out_ref[...]
    copies = [rcopy(pc, rz.at[z], rz.at[z], zs.at[d], zr.at[d], to) for d, to in enumerate(plane_peers(pc))]
    for cp in copies:
        cp.start()
    yield
    for cp in copies:
        cp.wait()
    total = rz[0]
    for k in range(1, Z):
        total = total + rz[k]
    out_ref[...] = total


def visible(start, block, pos_ref):
    kpos = start + lax.broadcasted_iota(jnp.int32, (block, pos_ref.shape[1]), 0)
    return (kpos <= pos_ref[0:1, :]) & (kpos >= pos_ref[1:2, :])


def split_heads(src, dst, scale=None):
    rows = src.shape[0]
    for h in range(QUERY_HEADS):
        v = src[:, pl.ds(h * HEAD_WIDTH, HEAD_WIDTH)]
        dst[pl.ds(h * rows, rows), :] = v if scale is None else v * scale


def swap_halves(v):
    width = v.shape[1]
    lane = lax.broadcasted_iota(jnp.int32, v.shape, 1)
    low = lax.rem(lane, HEAD_WIDTH) < HEAD_WIDTH // 2
    ahead = pltpu.roll(v, width - HEAD_WIDTH // 2, 1)
    behind = pltpu.roll(v, HEAD_WIDTH // 2, 1)
    return jnp.where(low, ahead, behind)


def rotate(v, cos_ref, sin_ref):
    return v * cos_ref[...] + swap_halves(v) * sin_ref[...]


def attend_kernel(block, span_ref, q_ref, kv_ref, pos_ref, o_ref, lse_ref, m_ref, l_ref, acc_ref):
    rows = pos_ref.shape[1]
    m_ref[...] = jnp.full_like(m_ref, large_negative)
    l_ref[...] = jnp.zeros_like(l_ref)
    acc_ref[...] = jnp.zeros_like(acc_ref)

    @pl.loop(span_ref[0], span_ref[1])
    def _(j):
        attend_block(j, block, q_ref, kv_ref, pos_ref, m_ref, l_ref, acc_ref)

    attend_end(o_ref, lse_ref, m_ref, l_ref, acc_ref)


def attend_block(j, block, q_ref, kv_ref, pos_ref, m_ref, l_ref, acc_ref):
    rows = pos_ref.shape[1]
    start = pl.multiple_of(j * block, block)
    ok = visible(start, block, pos_ref)
    for h in range(QUERY_HEADS):
        g = h // (QUERY_HEADS // KEY_VALUE_HEADS)
        keys = kv_ref[pl.ds(start, block), pl.ds(g * HEAD_WIDTH, HEAD_WIDTH)]
        vals = kv_ref[pl.ds(start, block), pl.ds(KEY_WIDTH + g * HEAD_WIDTH, HEAD_WIDTH)]
        s = jnp.where(ok, nt(keys, q_ref[pl.ds(h * rows, rows), :]), large_negative)
        m0 = m_ref[h : h + 1, :]
        m1 = jnp.maximum(m0, jnp.max(s, axis=0, keepdims=True))
        p = jnp.where(ok, jnp.exp(s - m1), 0.0)
        a = jnp.exp(m0 - m1)
        l_ref[h : h + 1, :] = l_ref[h : h + 1, :] * a + jnp.sum(p, axis=0, keepdims=True)
        m_ref[h : h + 1, :] = m1
        r = pl.ds(h * HEAD_WIDTH, HEAD_WIDTH)
        acc_ref[r, :] = acc_ref[r, :] * a + tn(vals, p.astype(BF))


def attend_end(o_ref, lse_ref, m_ref, l_ref, acc_ref):
    lse_ref[...] = m_ref[...] + jnp.log(l_ref[...])
    inv = 1.0 / l_ref[...]
    for h in range(QUERY_HEADS):
        r = pl.ds(h * HEAD_WIDTH, HEAD_WIDTH)
        acc_ref[r, :] = acc_ref[r, :] * inv[h : h + 1, :]
    o_ref[...] = acc_ref[...].T.astype(o_ref.dtype)


def attend(span, q, kv, pos, block):
    rows = pos.shape[1]
    return pl.pallas_call(
        functools.partial(attend_kernel, block),
        out_shape=(
            jax.ShapeDtypeStruct((rows, QUERY_WIDTH), BF),
            jax.ShapeDtypeStruct((QUERY_HEADS, rows), F32),
        ),
        in_specs=[SM, VM, VM, VM],
        out_specs=(VM, VM),
        scratch_shapes=[
            pltpu.VMEM((QUERY_HEADS, rows), F32),
            pltpu.VMEM((QUERY_HEADS, rows), F32),
            pltpu.VMEM((QUERY_WIDTH, rows), F32),
        ],
        compiler_params=params(),
    )(span, q, kv, pos)


def attend_back_block(j, block, q_ref, do_ref, kv_ref, pos_ref, lse_ref, dl_ref, dkv_ref, acc_ref):
    rows = pos_ref.shape[1]
    start = pl.multiple_of(j * block, block)
    ok = visible(start, block, pos_ref)
    at = pl.ds(start, block)
    dks, dvs = [], []
    for g in range(KEY_VALUE_HEADS):
        keys = kv_ref[at, pl.ds(g * HEAD_WIDTH, HEAD_WIDTH)]
        vals = kv_ref[at, pl.ds(KEY_WIDTH + g * HEAD_WIDTH, HEAD_WIDTH)]
        dk = dv = None
        for h in range(4 * g, 4 * g + 4):
            q = q_ref[pl.ds(h * rows, rows), :]
            do = do_ref[pl.ds(h * rows, rows), :]
            p = jnp.where(ok, jnp.exp(nt(keys, q) - lse_ref[h : h + 1, :]), 0.0)
            ds = (p * (nt(vals, do) - dl_ref[h : h + 1, :])).astype(BF)
            r = pl.ds(h * HEAD_WIDTH, HEAD_WIDTH)
            acc_ref[r, :] += tn(keys, ds)
            a, b = nn(ds, q), nn(p.astype(BF), do)
            dk = a if dk is None else dk + a
            dv = b if dv is None else dv + b
        dks.append(dk)
        dvs.append(dv)
    dkv_ref[at, :] = jnp.concatenate(dks + dvs, axis=1).astype(BF)


def two(left, right, lanes):
    return jnp.where(lanes < MP, left, right)


def pair_columns(ref, p, lanes):
    return two(ref[:, 2 * p : 2 * p + 1], ref[:, 2 * p + 1 : 2 * p + 2], lanes)


def mixer_kernel(
    xe, mk, cw, cb, cum_t, cum, dt_t, we_t, skip, doc_c, doc_r, pre, xo, mix, so, xw, bias
):
    rows = pre.shape[0]
    for i in range(XBC // 256):
        sl = pl.ds(i * 256, 256)
        acc = jnp.broadcast_to(cb[:, sl], (rows, 256))
        for j in range(CONV):
            acc = acc + cw[j : j + 1, sl] * (xe[pl.ds(5 + j, rows), sl] * mk[:, j : j + 1])
        pre[:, sl] = acc.astype(BF)
        act = acc * jax.nn.sigmoid(acc)
        xo[:, sl] = act.astype(BF)
        if i < INNER // 256:
            mix[:, sl] = skip[:, sl] * act
    b_rows, c_rows = xo[:, pl.ds(INNER, NS)], xo[:, pl.ds(INNER + NS, NS)]
    cross = nt(c_rows, b_rows)
    t_at = lax.broadcasted_iota(jnp.int32, (rows, rows), 0)
    s_at = lax.broadcasted_iota(jnp.int32, (rows, rows), 1)
    bias[...] = jnp.where((doc_c[...] == doc_r[...]) & (s_at <= t_at), 0.0, large_negative)
    lanes = lax.broadcasted_iota(jnp.int32, (rows, 2 * MP), 1)
    for p in range(MH // 2):
        sl = pl.ds(p * 2 * MP, 2 * MP)
        xd = xo[:, sl].astype(F32) * pair_columns(dt_t, p, lanes)
        xw[:, sl] = (xd * pair_columns(we_t, p, lanes)).astype(BF)
        xb = xd.astype(BF)
        outs = []
        for h in (2 * p, 2 * p + 1):
            low = jnp.exp(jnp.minimum(cum_t[:, h : h + 1] - cum[h : h + 1, :], bias[...]))
            outs.append(nn((low * cross).astype(BF), xb))
        mix[:, sl] = mix[:, sl] + two(outs[0], outs[1], lanes)
    so[...] = tn(b_rows, xw[...]).astype(BF)


def mixer(xe, mk, cw, cb, cum_t, cum, dt_t, we_t, skip, doc_c, doc_r):
    rows = mk.shape[0]
    return pl.pallas_call(
        mixer_kernel,
        out_shape=(
            jax.ShapeDtypeStruct((rows, XBC), BF),
            jax.ShapeDtypeStruct((rows, XBC), BF),
            jax.ShapeDtypeStruct((rows, INNER), F32),
            jax.ShapeDtypeStruct((NS, INNER), BF),
        ),
        in_specs=[VM] * 11,
        out_specs=(VM,) * 4,
        scratch_shapes=[pltpu.VMEM((rows, INNER), BF), pltpu.VMEM((rows, rows), F32)],
        compiler_params=params(),
    )(xe, mk, cw, cb, cum_t, cum, dt_t, we_t, skip, doc_c, doc_r)


def spread_heads():
    head = lax.broadcasted_iota(jnp.int32, (MH, INNER), 0)
    lane = lax.broadcasted_iota(jnp.int32, (MH, INNER), 1)
    return (lane // MP == head).astype(F32)


def exact(a, b, dims):
    return lax.dot_general(
        a, b, (dims, ((), ())), precision=lax.Precision.HIGHEST, preferred_element_type=F32
    )


def wide(columns, spread_mat):
    return exact(columns, spread_mat, ((1,), (0,)))


def gate_kernel(mix, xo, state, din_t, gate, gain, att, mixed, branch):
    rows = mix.shape[0]
    spread_mat = spread_heads()

    @pl.loop(0, rows // 64)
    def _(i):
        r = pl.ds(pl.multiple_of(i * 64, 64), 64)
        carried = nn(xo[r, pl.ds(INNER + NS, NS)], state[...])
        m = mix[r, :] + carried * wide(din_t[r, :], spread_mat)
        mixed[r, :] = m.astype(BF)
        gv = gate[r, :]
        gated = m * (gv * jax.nn.sigmoid(gv))
        factor = lax.rsqrt(jnp.mean(gated * gated, axis=1, keepdims=True) + norm_eps)
        branch[r, pl.ds(0, QUERY_WIDTH)] = att[r, :]
        branch[r, pl.ds(QUERY_WIDTH, INNER)] = (gated * factor * gain[...]).astype(BF)


def gate_out(mix, xo, state, din_t, gate, gain, att):
    rows = mix.shape[0]
    return pl.pallas_call(
        gate_kernel,
        out_shape=(
            jax.ShapeDtypeStruct((rows, INNER), BF),
            jax.ShapeDtypeStruct((rows, MIXOUT), BF),
        ),
        in_specs=[VM] * 7,
        out_specs=(VM,) * 2,
        compiler_params=params(),
    )(mix, xo, state, din_t, gate, gain, att)


GATE_AT = QUERY_WIDTH + 2 * KEY_WIDTH
XBC_AT = GATE_AT + INNER


def gate_back_rows(i, grad, mixed, gate, gain, din_t, spread_mat, dm, dproj, dgain, dinc):
    r = pl.ds(pl.multiple_of(i * 64, 64), 64)
    m, gv, gr = mixed[r, :].astype(F32), gate[r, :], grad[r, pl.ds(QUERY_WIDTH, INNER)]
    sig = jax.nn.sigmoid(gv)
    sil = gv * sig
    gated = m * sil
    factor = lax.rsqrt(jnp.mean(gated * gated, axis=1, keepdims=True) + norm_eps)
    w = gr * gain[...]
    dg = factor * (w - gated * factor * factor * jnp.mean(w * gated, axis=1, keepdims=True))
    dgain[...] += jnp.sum(gr * gated * factor, axis=0, keepdims=True)
    dproj[r, pl.ds(GATE_AT, INNER)] = (dg * m * (sig * (1.0 + gv * (1.0 - sig)))).astype(BF)
    d = dg * sil
    dm[r, :] = d.astype(BF)
    dinc[r, :] = (d * wide(din_t[r, :], spread_mat)).astype(BF)


def mixer_back_steps(
    xe, mk, cw, cum_t, cum, dt_t, we_t, skip, doc_c, doc_r, pre, xo, dm, dc_in, ds, dpre, dcw, dskip, xw, bias
):
    rows = pre.shape[0]
    here = pl.ds(0, rows)
    b_rows, c_rows = xo[:, pl.ds(INNER, NS)], xo[:, pl.ds(INNER + NS, NS)]
    cross = nt(b_rows, c_rows)
    s_at = lax.broadcasted_iota(jnp.int32, (rows, rows), 0)
    t_at = lax.broadcasted_iota(jnp.int32, (rows, rows), 1)
    bias[...] = jnp.where((doc_c[...] == doc_r[...]) & (s_at <= t_at), 0.0, large_negative)
    lanes = lax.broadcasted_iota(jnp.int32, (rows, 2 * MP), 1)

    def slope(sl):
        v = pre[:, sl].astype(F32)
        sig = jax.nn.sigmoid(v)
        return sig * (1.0 + v * (1.0 - sig))

    dcross = jnp.zeros((rows, rows), F32)
    for p in range(MH // 2):
        sl = pl.ds(p * 2 * MP, 2 * MP)
        xv = xo[:, sl].astype(F32)
        dt2, we2 = pair_columns(dt_t, p, lanes), pair_columns(we_t, p, lanes)
        xd = xv * dt2
        xw[:, sl] = (xd * we2).astype(BF)
        g = dm[:, sl]
        outs = []
        for k in (0, 1):
            h = 2 * p + k
            low = jnp.exp(jnp.minimum(cum[h : h + 1, :] - cum_t[:, h : h + 1], bias[...]))
            outs.append(nn((low * cross).astype(BF), g))
            part = jnp.where((lanes < MP) == (k == 0), xd, 0.0).astype(BF)
            dcross = dcross + nt(part, g) * low
        dxd = two(outs[0], outs[1], lanes) + we2 * nn(b_rows, ds[:, sl])
        gf = g.astype(F32)
        dskip[:, sl] = jnp.sum(gf * xv, axis=0, keepdims=True)
        dpre[here, sl] = (dxd * dt2 + skip[:, sl] * gf) * slope(sl)
        if p % 4 == 3:
            yield
    db16 = dcross.astype(BF)
    slb, slc = pl.ds(INNER, NS), pl.ds(INNER + NS, NS)
    dpre[here, slb] = (nn(db16, c_rows) + nt(xw[...], ds[...])) * slope(slb)
    dpre[here, slc] = (tn(db16, b_rows) + dc_in[...]) * slope(slc)
    yield
    for i in range(XBC // 256):
        sl = pl.ds(i * 256, 256)
        d = dpre[here, sl]
        for j in range(CONV):
            dcw[j : j + 1, sl] = jnp.sum(
                d * (xe[pl.ds(5 + j, rows), sl] * mk[:, j : j + 1]), axis=0, keepdims=True
            )
        dcw[CONV : CONV + 1, sl] = jnp.sum(d, axis=0, keepdims=True)


def back_kernel(planes, count, block, *refs):
    lefts, rights, refs = refs[:count], refs[count : 2 * count], refs[2 * count :]
    if count:
        branch = rights[2]
    else:
        branch, refs = refs[0], refs[1:]
    (
        grad, mixed, gate, gain, din_t, xo, state, q_in, kv, pos, lse, cos_w, sin_w, decays,
        xe, mk, mk_next, cw, cum_t, cum, dt_t, we_t, skip, doc_c, doc_r, pre,
    ) = refs[:26]
    refs = refs[26:]
    if count:
        scattered, refs = refs[0], refs[1:]
    dproj, dgain, dcw, dskip = refs[:4]
    (
        dm, dinc, dc, dstate, dsnew, flat, qh, doh, dl, acc, dkv, dkv_own, dpre, edge, bias, esem
    ) = refs[4:20]
    refs = refs[20:]
    relay_refs, refs = refs[:6], refs[6:]
    fold_refs, refs = refs[:10], refs[10:]
    pc = Place(planes)
    n = 4 * planes
    rows = mixed.shape[0]
    greet_row(pc, count > 0)
    side = (
        scatter_steps(pc, tuple(zip(lefts, rights)), scattered, refs) if count else iter(())
    )

    def pump():
        next(side, None)

    pump()
    spread_mat = spread_heads()
    dgain[...] = jnp.zeros_like(dgain)
    pl.loop(0, rows // 64)(
        lambda i: gate_back_rows(i, grad, mixed, gate, gain, din_t, spread_mat, dm, dproj, dgain, dinc)
    )
    ds0 = tn(xo[:, pl.ds(INNER + NS, NS)], dinc[...]).astype(BF)
    dc[...] = nt(dinc[...], state[...])
    dstate[...] = ds0.reshape(dstate.shape)
    states = relay_steps(pc, True, dstate, decays, dsnew, relay_refs)
    next(states)
    for _ in range(planes):
        pump()
    split_heads(q_in, qh, jnp.asarray(HEAD_WIDTH**-0.5, BF))
    go = grad[:, pl.ds(0, QUERY_WIDTH)].astype(BF)
    head = lax.broadcasted_iota(jnp.int32, (QUERY_HEADS, QUERY_WIDTH), 0)
    lane = lax.broadcasted_iota(jnp.int32, (QUERY_HEADS, QUERY_WIDTH), 1)
    for h in range(QUERY_HEADS):
        doh[pl.ds(h * rows, rows), :] = go[:, h * HEAD_WIDTH : (h + 1) * HEAD_WIDTH]
    dl[...] = exact(
        (lane // HEAD_WIDTH == head).astype(F32),
        go.astype(F32) * branch[:, pl.ds(0, QUERY_WIDTH)].astype(F32),
        ((1,), (1,)),
    )
    acc[...] = jnp.zeros_like(acc)
    total = kv.shape[0] // block
    seen = (pc.ctx * rows + rows + block - 1) // block
    parts = 4
    each = total // parts

    @pl.loop(seen, (pc.z + 1) * 4 * rows // block)
    def _(j):
        dkv[pl.ds(pl.multiple_of(j * block, block), block), :] = jnp.zeros((block, 2 * KEY_WIDTH), BF)

    for k in range(parts):
        lo = each * k
        pl.loop(jnp.minimum(lo, seen), jnp.minimum(lo + each, seen))(
            lambda j: attend_back_block(j, block, qh, doh, kv, pos, lse, dl, dkv, acc)
        )
        pump()
        if k == 1:
            next(states)
    folds = fold_steps(
        pc, lambda s: dkv.at[pl.ds(pl.multiple_of(s * rows, rows), rows), :], dkv_own, fold_refs
    )
    next(folds)
    for t in range(QUERY_WIDTH // 128):
        dq = acc[pl.ds(t * 128, 128), :].T * (HEAD_WIDTH**-0.5)
        dproj[:, pl.ds(t * 128, 128)] = rotate(dq, cos_w, sin_w).astype(BF)
    next(states)
    flat[...] = dsnew[...].reshape(flat.shape)
    next(folds)
    mixing = mixer_back_steps(
        xe, mk, cw, cum_t, cum, dt_t, we_t, skip, doc_c, doc_r, pre, xo, dm, dc, flat, dpre, dcw, dskip, dinc, bias
    )
    next(mixing)
    next(folds)
    pump()
    next(mixing)
    pump()
    next(mixing)
    next(folds)
    pump()
    next(mixing)
    prior = rcopy(pc, dpre.at[pl.ds(0, 8), :], edge, esem.at[0], esem.at[1], (lax.rem(pc.ctx + n - 1, n), pc.y))
    pl.when(pc.ctx > 0)(lambda: prior.start())
    for _ in mixing:
        pass
    pump()
    for _ in folds:
        pass
    dproj[:, pl.ds(QUERY_WIDTH, KEY_WIDTH)] = rotate(dkv_own[:, pl.ds(0, KEY_WIDTH)], cos_w, sin_w).astype(BF)
    dproj[:, pl.ds(QUERY_WIDTH + KEY_WIDTH, KEY_WIDTH)] = dkv_own[:, pl.ds(KEY_WIDTH, KEY_WIDTH)].astype(BF)
    pl.when(pc.ctx < n - 1)(lambda: prior.wait_recv())

    @pl.when(pc.ctx == n - 1)
    def _():
        edge[...] = jnp.zeros_like(edge)

    dpre[pl.ds(rows, 8), :] = edge[...]
    for i in range(XBC // 256):
        sl = pl.ds(i * 256, 256)
        total_grad = jnp.zeros((rows, 256), F32)
        for j in range(CONV):
            total_grad = total_grad + cw[j : j + 1, sl] * (
                dpre[pl.ds(CONV - 1 - j, rows), sl] * mk_next[:, j : j + 1]
            )
        dproj[:, pl.ds(XBC_AT + i * 256, 256)] = total_grad.astype(BF)
    for _ in states:
        pass
    pl.when(pc.ctx > 0)(lambda: prior.wait_send())
    for _ in side:
        pass


def back(planes, lefts, rights, args, block, collective):
    count = len(lefts)
    n = 4 * planes
    rows = args[-1].shape[0]
    keys = n * rows
    outs = [
        jax.ShapeDtypeStruct((rows, MIXIN), BF),
        jax.ShapeDtypeStruct((1, INNER), F32),
        jax.ShapeDtypeStruct((CONV + 1, XBC), F32),
        jax.ShapeDtypeStruct((1, INNER), F32),
    ]
    scratch = [
        pltpu.VMEM((rows, INNER), BF),
        pltpu.VMEM((rows, INNER), BF),
        pltpu.VMEM((rows, NS), F32),
        pltpu.VMEM((n, NS // n, INNER), BF),
        pltpu.VMEM((n, NS // n, INNER), BF),
        pltpu.VMEM((NS, INNER), BF),
        pltpu.VMEM((QUERY_HEADS * rows, HEAD_WIDTH), BF),
        pltpu.VMEM((QUERY_HEADS * rows, HEAD_WIDTH), BF),
        pltpu.VMEM((QUERY_HEADS, rows), F32),
        pltpu.VMEM((QUERY_WIDTH, rows), F32),
        pltpu.VMEM((keys, 2 * KEY_WIDTH), BF),
        pltpu.VMEM((rows, 2 * KEY_WIDTH), F32),
        pltpu.VMEM((rows + 8, XBC), F32),
        pltpu.VMEM((8, XBC), F32),
        pltpu.VMEM((rows, rows), F32),
        DMA((2,)),
    ]
    scratch += relay_scratch(planes) + fold_scratch(planes, rows, 2 * KEY_WIDTH)
    if count:
        widths = [r.shape[1] for r in rights]
        each = lefts[0].shape[1] // n
        outs = [jax.ShapeDtypeStruct((each, sum(widths)), F32)] + outs
        scratch += scatter_scratch(planes, each, widths)
    return pl.pallas_call(
        functools.partial(back_kernel, planes, count, block),
        out_shape=tuple(outs),
        in_specs=[VM] * (2 * count + len(args)),
        out_specs=(VM,) * len(outs),
        scratch_shapes=scratch,
        compiler_params=params(collective),
    )(*lefts, *rights, *args)


def last_kernel(planes, left, dproj, w_ref, tok, scale, gain, dres, small, scattered, dhid, totals, dn, *scratch):
    pc = Place(planes)
    peers = plane_peers(pc)
    bar = pltpu.get_barrier_semaphore()
    for d in [pc.near(k) for k in "cxy"] + peers:
        pl.semaphore_signal(bar, inc=1, device_id=d, device_id_type=MESH)
    pl.semaphore_wait(bar, 3 + len(peers))
    rows = dproj.shape[0]
    side = scatter_steps(pc, ((left, dproj),), scattered, scratch[6:])
    next(side)
    for i in range(D // 256):
        dn[:, pl.ds(i * 256, 256)] = nt(dproj[...], w_ref[pl.ds(i * 256, 256), :])
        if i == 0:
            next(side)
    for _ in range(planes - 1):
        next(side)
    totals[...] = small[...]
    for i in range(rows // 64):
        r = pl.ds(i * 64, 64)
        v, g, f = tok[r, :].astype(F32), dn[r, :], scale[r, :]
        w = g * gain[...]
        dhid[r, :] = dres[r, :] + f * (w - v * f * f * jnp.mean(w * v, axis=1, keepdims=True))
        part = jnp.sum(g * v * f, axis=0, keepdims=True)
        for t in range(D // 128):
            totals[t : t + 1, :] = totals[t : t + 1, :] + part[:, t * 128 : (t + 1) * 128]
    sums = total_steps(pc, totals, scratch[:6])
    next(sums)
    for _ in range(3):
        next(side)
        next(sums)
    for _ in side:
        next(sums, None)
    for _ in sums:
        pass


def last(planes, left, dproj, w, tok, scale, gain, dres, small, collective):
    rows = dproj.shape[0]
    each = left.shape[1] // (4 * planes)
    return pl.pallas_call(
        functools.partial(last_kernel, planes),
        out_shape=(
            jax.ShapeDtypeStruct((each, MIXIN), F32),
            jax.ShapeDtypeStruct((rows, D), F32),
            jax.ShapeDtypeStruct((SMALL_ROWS, 128), F32),
        ),
        in_specs=[VM] * 8,
        out_specs=(VM,) * 3,
        scratch_shapes=[pltpu.VMEM((rows, D), F32)]
        + total_scratch(planes)
        + scatter_scratch(planes, each, [MIXIN]),
        compiler_params=params(collective),
    )(left, dproj, w, tok, scale, gain, dres, small)


def doc_layout(lengths, token_positions):
    starts = jnp.cumsum(lengths) - lengths
    inside = token_positions[:, None] >= starts[None, :]
    document_index = jnp.sum(inside.astype(jnp.int32), axis=1) - 1
    begins = jnp.max(jnp.where(inside, starts[None, :], 0), axis=1)
    return (document_index, token_positions - begins)


def rope_tables(rel_pos):
    half_dim = HEAD_WIDTH // 2
    inv_freq = rope_base ** (-2.0 * jnp.arange(half_dim, dtype=jnp.float32) / HEAD_WIDTH)
    angles = rel_pos.astype(jnp.float32)[:, None] * inv_freq[None, :]
    return (jnp.cos(angles), jnp.sin(angles))


def apply_rotary(values, cosine_table, sine_table):
    half_dim = values.shape[-1] // 2
    lower_half = values[..., :half_dim]
    upper_half = values[..., half_dim:]
    cos_rows = cosine_table[:, None, :]
    sin_rows = sine_table[:, None, :]
    return jnp.concatenate(
        [
            lower_half * cos_rows - upper_half * sin_rows,
            upper_half * cos_rows + lower_half * sin_rows,
        ],
        axis=-1,
    )


def inverse_rotary(grads, cosine_table, sine_table):
    half_dim = grads.shape[-1] // 2
    lower_half = grads[..., :half_dim]
    upper_half = grads[..., half_dim:]
    cos_rows = cosine_table[:, None, :]
    sin_rows = sine_table[:, None, :]
    return jnp.concatenate(
        [
            lower_half * cos_rows + upper_half * sin_rows,
            upper_half * cos_rows - lower_half * sin_rows,
        ],
        axis=-1,
    )


def split_small(vector):
    widths = (D, D, INNER, CONV * XBC, XBC, MH)
    pieces = []
    offset = 0
    for span_width in widths:
        pieces.append(vector[offset : offset + span_width])
        offset += span_width
    return (pieces[0], pieces[1], pieces[2], pieces[3].reshape(CONV, XBC), pieces[4], pieces[5])


def norm_backward(grad_normed, values, factor, gain_vals):
    weighted = grad_normed * gain_vals
    grad_values = factor * (
        weighted - values * factor * factor * jnp.mean(weighted * values, axis=1, keepdims=True)
    )
    grad_gain = jnp.sum(grad_normed * values * factor, axis=0)
    return (grad_values, grad_gain)


def adamw_step(param_vals, grad_vals, first_vals, second_vals, weight_decay):
    first_new = beta_one * first_vals + (1.0 - beta_one) * grad_vals
    second_new = beta_two * second_vals + (1.0 - beta_two) * grad_vals * grad_vals
    update = (
        first_new
        / (1.0 - beta_one**STEP)
        / (jnp.sqrt(second_new / (1.0 - beta_two**STEP)) + adam_eps)
    )
    return (param_vals - learn_rate * (update + weight_decay * param_vals), first_new, second_new)


def adam_direction(grad_vals, first_vals, second_vals):
    first_new = beta_one * first_vals + (1.0 - beta_one) * grad_vals
    second_new = beta_two * second_vals + (1.0 - beta_two) * grad_vals * grad_vals
    update = (
        first_new
        / (1.0 - beta_one**STEP)
        / (jnp.sqrt(second_new / (1.0 - beta_two**STEP)) + adam_eps)
    )
    return (update, first_new, second_new)


def by_head(rows):
    tokens = rows.shape[0]
    return (
        rows.reshape(tokens, QUERY_HEADS, HEAD_WIDTH)
        .transpose(1, 0, 2)
        .reshape(QUERY_HEADS * tokens, HEAD_WIDTH)
    )


def shards(
    planes,
    hidden,
    out_grad,
    decay_log,
    doc_lengths,
    weights,
    first_moment,
    second_moment,
    small_params,
    small_first,
    small_second,
):
    local_rows = hidden.shape[1]
    count = 4 * planes
    ctx_index = lax.axis_index("ctx")
    first_pos = ctx_index * local_rows
    scale_qk = HEAD_WIDTH ** (-0.5)
    contract_last = (((1,), (1,)), ((), ()))
    gain_one, gain_two, gate_gain, conv_w, conv_bias, skip_gain = split_small(small_params)
    lengths = doc_lengths[0]
    token_positions = first_pos + jnp.arange(local_rows, dtype=jnp.int32)
    near_positions = first_pos + jnp.arange(-(CONV - 1), local_rows + CONV - 1, dtype=jnp.int32)
    near_doc = doc_layout(lengths, near_positions)[0]
    document_index, rel_pos = doc_layout(lengths, token_positions)
    doc_before = near_doc[CONV - 2]
    is_start = document_index != near_doc[CONV - 2 : CONV - 2 + local_rows]
    cosine_table, sine_table = rope_tables(rel_pos)
    begins = token_positions - rel_pos
    pos = jnp.stack([token_positions, begins])
    block = 512
    span = jnp.stack([jnp.min(begins) // block, (first_pos + local_rows - 1) // block + 1])

    tok_f = hidden[0].astype(jnp.float32)
    scale_one = lax.rsqrt(jnp.mean(tok_f * tok_f, axis=1, keepdims=True) + norm_eps)
    normed_one = (tok_f * scale_one * gain_one).astype(jnp.bfloat16)
    own_b = weights.astype(jnp.bfloat16)
    mixer_w = gather_rows(own_b[:, : MIXIN + MIXOUT], planes, 0).reshape(D, MIXIN + MIXOUT)
    mlp_w = lax.all_gather(own_b[:, MIXIN + MIXOUT :], ("ctx", "fsdp"), axis=0, tiled=True)
    projected = jnp.dot(normed_one, mixer_w[:, :MIXIN], preferred_element_type=jnp.float32)
    query_rows = apply_rotary(
        projected[:, :QUERY_WIDTH].reshape(local_rows, QUERY_HEADS, HEAD_WIDTH),
        cosine_table,
        sine_table,
    ).astype(jnp.bfloat16)
    key_rows = apply_rotary(
        projected[:, QUERY_WIDTH : QUERY_WIDTH + KEY_WIDTH].reshape(
            local_rows, KEY_VALUE_HEADS, HEAD_WIDTH
        ),
        cosine_table,
        sine_table,
    ).reshape(local_rows, KEY_WIDTH)
    kv_rows = jnp.concatenate(
        [key_rows, projected[:, QUERY_WIDTH + KEY_WIDTH : QUERY_WIDTH + 2 * KEY_WIDTH]], axis=1
    ).astype(jnp.bfloat16)
    gate_in = projected[:, QUERY_WIDTH + 2 * KEY_WIDTH : QUERY_WIDTH + 2 * KEY_WIDTH + INNER]
    xbc_b = projected[:, QUERY_WIDTH + 2 * KEY_WIDTH + INNER :].astype(jnp.bfloat16)
    query_heads = by_head(query_rows.reshape(local_rows, QUERY_WIDTH) * jnp.bfloat16(scale_qk))

    log_decay = decay_log[0]
    cum = jnp.cumsum(log_decay, axis=1)
    steps_in = jnp.where(is_start[None, :], 1.0, jnp.sqrt(-jnp.expm1(2.0 * log_decay)))
    decay_in = jnp.where((document_index == doc_before)[None, :], jnp.exp(cum), 0.0)
    same_end = (document_index == document_index[-1])[None, :]
    to_end = jnp.where(same_end, jnp.exp(jnp.minimum(cum[:, -1:] - cum, 0.0)), 0.0)
    cum_t, dt_t, we_t, din_t = cum.T, steps_in.T, to_end.T, decay_in.T
    own_decay = jnp.zeros((8, 128), jnp.float32).at[0, :MH].set(decay_in[:, -1])

    kv_all, edge_in, decays = spread(planes, kv_rows, xbc_b[local_rows - 16 :], own_decay, 1)
    decays = jnp.repeat(decays[:, 0, :MH], MP, axis=1)
    kv_flat = kv_all.reshape(count * local_rows, 2 * KEY_WIDTH)

    same_doc = jnp.stack(
        [near_doc[j : j + local_rows] == document_index for j in range(CONV)], axis=1
    ).astype(jnp.float32)
    xe = jnp.concatenate(
        [
            jnp.zeros((9 - CONV, XBC), jnp.float32),
            edge_in[17 - CONV :].astype(jnp.float32),
            xbc_b.astype(jnp.float32),
        ],
        axis=0,
    )
    skip_wide = jnp.repeat(skip_gain, MP)[None, :]
    doc_c, doc_r = document_index[:, None], document_index[None, :]
    pre, xo, mix_local, state_out = mixer(
        xe, same_doc, conv_w, conv_bias[None, :], cum_t, cum, dt_t, we_t, skip_wide, doc_c, doc_r
    )
    state_in = relay(planes, False, state_out, decays, 2)
    attended, log_sums = attend(span, query_heads, kv_flat, pos, block)
    mixed, branch = gate_out(
        mix_local, xo, state_in, din_t, gate_in, gate_gain[None, :], attended
    )

    resid_one = tok_f + lax.dot_general(
        branch, mixer_w[:, MIXIN:], contract_last, preferred_element_type=jnp.float32
    )
    scale_two = lax.rsqrt(jnp.mean(resid_one * resid_one, axis=1, keepdims=True) + norm_eps)
    normed_two = (resid_one * scale_two * gain_two).astype(jnp.bfloat16)
    gate_up = jnp.dot(normed_two, mlp_w[:, : 2 * FF], preferred_element_type=jnp.float32)
    gate_part = gate_up[:, :FF]
    up_part = gate_up[:, FF:]
    sigma_gate = jax.nn.sigmoid(gate_part)
    silu_gate = gate_part * sigma_gate
    hidden_mid = (silu_gate * up_part).astype(jnp.bfloat16)
    block_out = resid_one + lax.dot_general(
        hidden_mid, mlp_w[:, 2 * FF :], contract_last, preferred_element_type=jnp.float32
    )
    out_hidden = block_out.astype(jnp.bfloat16)[None]
    grad_out = out_grad[0]
    grad_mid = jnp.dot(grad_out, mlp_w[:, 2 * FF :], preferred_element_type=jnp.float32)
    silu_slope = sigma_gate * (1.0 + gate_part * (1.0 - sigma_gate))
    grad_gate_up = jnp.concatenate(
        [grad_mid * up_part * silu_slope, grad_mid * silu_gate], axis=1
    ).astype(jnp.bfloat16)
    grad_normed_two = lax.dot_general(
        grad_gate_up, mlp_w[:, : 2 * FF], contract_last, preferred_element_type=jnp.float32
    )
    grad_norm_two, grad_gain_two = norm_backward(grad_normed_two, resid_one, scale_two, gain_two)
    grad_resid_one = grad_out.astype(jnp.float32) + grad_norm_two
    grad_resid_b = grad_resid_one.astype(jnp.bfloat16)

    grad_branch = jnp.dot(grad_resid_b, mixer_w[:, MIXIN:], preferred_element_type=jnp.float32)
    same_next = jnp.stack(
        [
            near_doc[2 * (CONV - 1) - j : 2 * (CONV - 1) - j + local_rows] == document_index
            for j in range(CONV)
        ],
        axis=1,
    ).astype(jnp.float32)
    cos_wide = jnp.tile(cosine_table, (1, 4))
    sin_back = jnp.tile(jnp.concatenate([sine_table, -sine_table], axis=1), (1, 2))
    lefts = [by_core(v, planes) for v in (normed_two, grad_out, grad_resid_b)]
    rights = [grad_gate_up, hidden_mid, branch]
    args = (
        grad_branch, mixed, gate_in, gate_gain[None, :], din_t, xo, state_in,
        query_rows.reshape(local_rows, QUERY_WIDTH), kv_flat, pos, log_sums, cos_wide, sin_back, decays,
        xe, same_doc, same_next, conv_w, cum_t, cum, dt_t, we_t, skip_wide, doc_c, doc_r, pre,
    )
    if planes <= 4:
        early, grad_proj, gate_gain_grads, conv_grads, skip_grads = back(
            planes, lefts, rights, args, block, 3
        )
    else:
        early = scatter_rows(planes, lefts, rights, 4)
        grad_proj, gate_gain_grads, conv_grads, skip_grads = back(planes, [], [], (branch,) + args, block, 3)
    small_local = jnp.concatenate(
        [
            jnp.zeros((D,), jnp.float32),
            grad_gain_two,
            gate_gain_grads[0],
            conv_grads.reshape(-1),
            jnp.sum(skip_grads.reshape(MH, MP), axis=1),
        ]
    )
    size = small_local.shape[0]
    padded = jnp.pad(small_local, (0, SMALL_ROWS * 128 - size)).reshape(SMALL_ROWS, 128)
    mixin_grads, grad_hidden, totals = last(
        planes, by_core(normed_one, planes), grad_proj, mixer_w[:, :MIXIN], hidden[0], scale_one,
        gain_one[None, :], grad_resid_one, padded, 5,
    )
    grad_hidden = grad_hidden[None]
    small_grads = totals.reshape(-1)[:size]
    grad_weights = jnp.concatenate(
        [mixin_grads, early[:, 3 * FF :], early[:, : 3 * FF]], axis=1
    )
    new_weights, new_first, new_second = adamw_step(
        weights, grad_weights, first_moment, second_moment, decay_rate
    )
    small_step, small_first_new, small_second_new = adam_direction(
        small_grads, small_first, small_second
    )
    return (
        out_hidden,
        grad_hidden,
        grad_weights,
        new_weights,
        new_first,
        new_second,
        small_grads,
        small_step,
        small_first_new,
        small_second_new,
    )


def solution(mesh):
    placed = (
        P("fsdp", "ctx", None),
        P("fsdp", "ctx", None),
        P("fsdp", None, "ctx"),
        P("fsdp", None),
        P(("ctx", "fsdp"), None),
        P(("ctx", "fsdp"), None),
        P(("ctx", "fsdp"), None),
        P(),
        P(),
        P(),
    )
    return jax.shard_map(
        functools.partial(shards, mesh.shape["ctx"] // 4),
        mesh=mesh,
        in_specs=placed,
        out_specs=(
            P("fsdp", "ctx", None),
            P("fsdp", "ctx", None),
            P(("ctx", "fsdp"), None),
            P(("ctx", "fsdp"), None),
            P(("ctx", "fsdp"), None),
            P(("ctx", "fsdp"), None),
            P(),
            P(),
            P(),
            P(),
        ),
        check_vma=False,
    )
```

```python
import functools
import math

import jax
import jax.numpy as jnp
from jax import lax
from jax.experimental import pallas as pl
from jax.experimental.pallas import tpu as pltpu
from jax.sharding import PartitionSpec as P

D = 1024
QUERY_HEADS = 8
KEY_VALUE_HEADS = 2
HEAD_WIDTH = 64
MH = 24
MP = 64
NS = 128
FF = 2048
CONV = 4
STEP = 3
QUERY_WIDTH = 512
KEY_WIDTH = 128
INNER = 1536
XBC = 1792
MIXIN = 4096
MIXOUT = 2048
SMALL_ROWS = 104
TOKENS = 256
PIECE = 512

norm_eps = 1e-05
rope_base = 100000000000.0
large_negative = -1e30
learn_rate = 0.02
beta_one = 0.9
beta_two = 0.95
adam_eps = 1e-08
decay_rate = 0.1

MESH = pl.DeviceIdType.MESH
BF = jnp.bfloat16
F32 = jnp.float32
VM = pl.BlockSpec(memory_space=pltpu.VMEM)
SM = pl.BlockSpec(memory_space=pltpu.SMEM)
HB = pl.BlockSpec(memory_space=pl.ANY)
DMA = pltpu.SemaphoreType.DMA


def params(collective=None):
    if collective is None:
        return pltpu.CompilerParams(vmem_limit_bytes=62 * 2**20)
    return pltpu.CompilerParams(
        collective_id=collective, has_side_effects=True, vmem_limit_bytes=62 * 2**20
    )


def nt(a, b):
    return lax.dot_general(a, b, (((1,), (1,)), ((), ())), preferred_element_type=F32)


def tn(a, b):
    return lax.dot_general(a, b, (((0,), (0,)), ((), ())), preferred_element_type=F32)


def nn(a, b):
    return lax.dot_general(a, b, (((1,), (0,)), ((), ())), preferred_element_type=F32)


class Place:
    def __init__(self, planes):
        ctx = lax.axis_index("ctx")
        self.ctx = ctx
        self.Z, self.z, self.x, self.c = planes, ctx // 4, (ctx // 2) % 2, ctx % 2
        self.y = lax.axis_index("fsdp")
        self.up, self.down = self.z + 1 < planes, self.z > 0

    def shard(self, z, x, y, c):
        return ((z * 2 + x) * 2 + c) * 2 + y

    def spot(self, z, x, c):
        return (z * 2 + x) * 2 + c

    def dev(self, z, x, y, c):
        return ((z * 2 + x) * 2 + c, y)

    def near(self, d):
        z, x, y, c = self.z, self.x, self.y, self.c
        return {
            "x": self.dev(z, 1 - x, y, c),
            "y": self.dev(z, x, 1 - y, c),
            "c": self.dev(z, x, y, 1 - c),
            "u": self.dev(z + 1, x, y, c),
            "d": self.dev(z - 1, x, y, c),
        }[d]

    def zord(self, k):
        if k == self.Z - 1:
            return self.z
        low = self.Z - 1 - k
        z = self.z
        return jnp.where(
            2 * z < self.Z, jnp.where(low > z, low, low - 1), jnp.where(k < z, k, k + 1)
        )


def greet(pc, dims="xyc", chain=True):
    bar = pltpu.get_barrier_semaphore()

    def sig(d):
        pl.semaphore_signal(bar, inc=1, device_id=pc.near(d), device_id_type=MESH)

    for d in dims:
        sig(d)
    if chain:
        pl.when(pc.up)(lambda: sig("u"))
        pl.when(pc.down)(lambda: sig("d"))
    peers = len(dims)
    if chain:
        peers = peers + pc.up.astype(jnp.int32) + pc.down.astype(jnp.int32)
    pl.semaphore_wait(bar, peers)


def greet_row(pc, across=False):
    bar = pltpu.get_barrier_semaphore()
    n = 4 * pc.Z

    @pl.loop(1, n)
    def _(d):
        pl.semaphore_signal(
            bar, inc=1, device_id=(lax.rem(pc.ctx + d, n), pc.y), device_id_type=MESH
        )

    if across:
        pl.semaphore_signal(bar, inc=1, device_id=pc.near("y"), device_id_type=MESH)
    pl.semaphore_wait(bar, n - 1 + int(across))


def rcopy(pc, src, dst, ssem, rsem, d):
    return pltpu.make_async_remote_copy(
        src_ref=src,
        dst_ref=dst,
        send_sem=ssem,
        recv_sem=rsem,
        device_id=pc.near(d) if isinstance(d, str) else d,
        device_id_type=MESH,
    )


def add_into(dst, parts, width=512):
    columns = dst.shape[-1]
    step = width if columns % width == 0 else (256 if columns % 256 == 0 else 128)

    @pl.loop(0, columns // step)
    def _(i):
        sl = pl.ds(pl.multiple_of(i * step, step), step)
        total = parts[0][:, sl].astype(F32)
        for r in parts[1:]:
            total = total + r[:, sl].astype(F32)
        dst[:, sl] = total.astype(dst.dtype)


def thirds(columns):
    h = columns * 25 // 64 // 128 * 128
    return columns - 2 * h, h


def gather_scratch(planes):
    return [
        DMA((2, planes, 2)),
        DMA((2, planes)),
        DMA((2, planes, 2)),
        DMA((2, planes, 4)),
        DMA((2, planes, 8)),
        DMA((2, planes)),
        DMA((2 + planes,)),
        DMA((4 + 2 * planes,)),
        DMA,
    ]


def gather_steps(pc, w_ref, out_ref, scratch):
    zs, xs, ys, cs, rs, tz, tc, tr, loc = scratch
    Z, z, x, y, c = pc.Z, pc.z, pc.x, pc.y, pc.c
    w, h = thirds(w_ref.shape[-1])

    def cols(p):
        return pl.ds(0, w) if p == 2 else pl.ds(w + p * h, h)

    def spot(q):
        return (x if q < 2 else 1 - x), (y if q % 2 == 0 else 1 - y)

    def cp(p, zz, q, sem, d, own=False, core=None):
        xx, yy = spot(q)
        dst = out_ref.at[zz, xx, c, yy, :, cols(p)]
        return rcopy(pc, w_ref.at[:, cols(p)] if own else dst, dst, sem, rs.at[p, zz, core if core is not None else q], d)

    def along(p, zz, up, own=False):
        return cp(p, zz, 0, zs.at[p, zz, int(up)], "u" if up else "d", own, 0)

    def first(p, zz, own=False):
        return cp(p, zz, 0, xs.at[p, zz], "x" if p == 0 else "y", own, 2 if p == 0 else 1)

    def second(p, zz, q, own=False):
        if p == 0:
            return cp(p, zz, 2 * q, ys.at[p, zz, q], "y", own, 2 * q + 1)
        return cp(p, zz, q, ys.at[p, zz, q], "x", own, 2 + q)

    def core(p, zz, q, own=False):
        return cp(p, zz, q, cs.at[p, zz, q], "c", own, 4 + q)

    def arrived(p, zz, q):
        rcopy(
            pc, w_ref.at[:, cols(p)], out_ref.at[0, 0, 0, 0, :, cols(p)], loc, rs.at[p, zz, q], "c"
        ).wait_recv()

    def t_x():
        return rcopy(
            pc, w_ref.at[:, cols(2)], out_ref.at[z, x, c, y, :, cols(2)], tc.at[0], tr.at[0], "x"
        )

    def t_y():
        v = out_ref.at[z, :, c, y, :, cols(2)]
        return rcopy(pc, v, v, tc.at[1], tr.at[1], "y")

    def t_z(zz, up):
        v = out_ref.at[zz, :, c, :, :, cols(2)]
        return rcopy(pc, v, v, tz.at[int(up), zz], tr.at[4 + zz], "u" if up else "d")

    def t_c(zz):
        v = out_ref.at[zz, :, c, :, :, cols(2)]
        return rcopy(pc, v, v, tc.at[2 + zz], tr.at[4 + Z + zz], "c")

    keep = pltpu.make_async_copy(w_ref, out_ref.at[z, x, c, y], loc)
    keep.start()
    t_x().start()
    for p in (0, 1):
        pl.when(pc.up)(lambda: along(p, z, True, True).start())
        pl.when(pc.down)(lambda: along(p, z, False, True).start())
        first(p, z, True).start()
    for p in (0, 1):
        second(p, z, 0, True).start()
        core(p, z, 0, True).start()
    yield False
    keep.wait()
    t_x().wait_recv()
    t_y().start()
    for d in range(1, Z):
        for p in (0, 1):

            def onward(zz, up, more):
                arrived(p, zz, 0)
                pl.when(more)(lambda: along(p, zz, up).start())
                first(p, zz).start()
                second(p, zz, 0).start()
                core(p, zz, 0).start()

            pl.when(z - d >= 0)(lambda: onward(z - d, True, pc.up))
            pl.when(z + d < Z)(lambda: onward(z + d, False, pc.down))
        if d == 1:
            t_y().wait_recv()
            pl.when(pc.up)(lambda: t_z(z, True).start())
            pl.when(pc.down)(lambda: t_z(z, False).start())
            t_c(z).start()
        yield False

    def hop(d):
        def onward(zz, up, more):
            t_z(zz, up).wait_recv()
            pl.when(more)(lambda: t_z(zz, up).start())
            t_c(zz).start()

        pl.when(z - d >= 0)(lambda: onward(z - d, True, pc.up))
        pl.when(z + d < Z)(lambda: onward(z + d, False, pc.down))

    near = [lax.rem(z + k, Z) for k in range(Z)]
    for k, zz in enumerate(near):
        for p in (0, 1):
            q = 2 if p == 0 else 1
            arrived(p, zz, q)
            second(p, zz, 1).start()
            core(p, zz, q).start()
        if k > 0:
            hop(k)
        yield False
    for i in (0, 1):
        for k, zz in enumerate(near):
            for p in (0, 1):
                q = (1 if i == 0 else 3) if p == 0 else (2 if i == 0 else 3)
                arrived(p, zz, q)
                core(p, zz, q).start()
            yield i == 1 and k == Z - 1
    for zz in near:
        for p in (0, 1):
            for q in range(4):
                arrived(p, zz, 4 + q)
        t_c(zz).wait_recv()
        yield True
    t_x().wait_send()
    t_y().wait_send()
    for zz in range(Z):
        for p in (0, 1):
            pl.when(pc.up & (zz <= z))(lambda: along(p, zz, True).wait_send())
            pl.when(pc.down & (zz >= z))(lambda: along(p, zz, False).wait_send())
            first(p, zz).wait_send()
            for q in (0, 1):
                second(p, zz, q).wait_send()
            for q in range(4):
                core(p, zz, q).wait_send()
        pl.when(pc.up & (zz <= z))(lambda: t_z(zz, True).wait_send())
        pl.when(pc.down & (zz >= z))(lambda: t_z(zz, False).wait_send())
        t_c(zz).wait_send()


def spread_scratch(planes):
    n = 4 * planes
    return [DMA((planes,)), DMA((planes,)), DMA((planes, 2)), DMA((n,)), DMA((n,)), DMA((n,)), DMA((3,))]


def spread_steps(pc, kv_ref, edge_ref, dec_ref, all_ref, got_ref, decs_ref, scratch):
    us, xs, cs, rs, ds, dr, one = scratch
    Z, z, x, c = pc.Z, pc.z, pc.x, pc.c
    n = 4 * Z
    me = pc.ctx

    def cp(zz, xx, sem, d, own=False):
        s = pc.spot(zz, xx, c)
        return rcopy(pc, kv_ref if own else all_ref.at[s], all_ref.at[s], sem, rs.at[s], d)

    def arrived(s):
        rcopy(pc, kv_ref, all_ref.at[s], one.at[0], rs.at[s], "c").wait_recv()

    def decay_copy(d):
        return rcopy(pc, dec_ref, decs_ref.at[me], ds.at[d], dr.at[d], (lax.rem(me + d, n), pc.y))

    edge = rcopy(pc, edge_ref, got_ref, one.at[1], one.at[2], (lax.rem(me + 1, n), pc.y))
    keep = pltpu.make_async_copy(kv_ref, all_ref.at[me], one.at[0])
    pl.when(me < n - 1)(lambda: edge.start())
    keep.start()
    pl.when(pc.up)(lambda: cp(z, x, us.at[z], "u", True).start())
    cp(z, x, xs.at[z], "x", True).start()
    cp(z, x, cs.at[z, 0], "c", True).start()
    decs_ref[me] = dec_ref[...]
    pl.loop(1, n)(lambda d: decay_copy(d).start())
    yield
    pl.when(me > 0)(lambda: edge.wait_recv())

    @pl.when(me == 0)
    def _():
        got_ref[...] = jnp.zeros_like(got_ref)

    yield
    for d in range(1, Z):

        @pl.when(z - d >= 0)
        def _():
            zz = z - d
            arrived(pc.spot(zz, x, c))
            pl.when(pc.up)(lambda: cp(zz, x, us.at[zz], "u").start())
            cp(zz, x, xs.at[zz], "x").start()
            cp(zz, x, cs.at[zz, 0], "c").start()

        yield
    for d in range(Z):

        @pl.when(z - d >= 0)
        def _():
            arrived(pc.spot(z - d, 1 - x, c))
            cp(z - d, 1 - x, cs.at[z - d, 1], "c").start()

    yield
    for d in range(Z):

        @pl.when(z - d >= 0)
        def _():
            for xx in (x, 1 - x):
                arrived(pc.spot(z - d, xx, 1 - c))

    keep.wait()
    pl.loop(1, n)(lambda d: decay_copy(d).wait_recv())
    yield
    for zz in range(Z):

        @pl.when(zz <= z)
        def _():
            pl.when(pc.up)(lambda: cp(zz, x, us.at[zz], "u").wait_send())
            cp(zz, x, xs.at[zz], "x").wait_send()
            cp(zz, x, cs.at[zz, 0], "c").wait_send()
            cp(zz, 1 - x, cs.at[zz, 1], "c").wait_send()

    pl.when(me < n - 1)(lambda: edge.wait_send())
    pl.loop(1, n)(lambda d: decay_copy(d).wait_send())


def scatter_scratch(planes, rows, widths):
    columns = sum(widths)
    w, h = columns // 4, columns // 8 * 3
    half = 4 * planes * rows
    return [
        pltpu.VMEM((planes, 2, 2, rows, columns), BF),
        pltpu.VMEM((2, planes, 2, rows, h), BF),
        pltpu.VMEM((2, planes, rows, h), BF),
        pltpu.VMEM((2, planes + 1, rows, h), BF),
        pltpu.VMEM((planes + 1, 2, 2, rows, w), BF),
        pltpu.VMEM((3, rows, w), BF),
        pltpu.VMEM((len(widths), half, TOKENS), BF),
        pltpu.VMEM((TOKENS, columns), BF),
        DMA((len(widths),)),
        DMA((len(widths),)),
        DMA((columns // PIECE,)),
        DMA((columns // PIECE,)),
        DMA((2, planes, 2)),
        DMA((2, planes, 2)),
        DMA((2, planes)),
        DMA((2, planes)),
        DMA((3, planes)),
        DMA((3, planes + 1)),
        DMA((3,)),
        DMA((3,)),
    ]


def scatter_steps(pc, pairs, out_ref, scratch):
    g, r2, r3, rz, rw, rt, la, rb, as_, ar, bs, br, s2, q2, s3, q3, sz, qz, st, qt = scratch
    Z, z, x, y, c = pc.Z, pc.z, pc.x, pc.y, pc.c
    rows = g.shape[3]
    w = g.shape[-1] // 4
    h = g.shape[-1] // 8 * 3
    depth = 4 * rows

    def cols(p):
        return pl.ds(0, w) if p == 2 else pl.ds(w + p * h, h)

    pieces = []
    base = 0
    for i, (left, right) in enumerate(pairs):
        for at in range(0, right.shape[1], PIECE):
            pieces.append((i, at, base + at))
        base += right.shape[1]

    def acopy(i):
        return rcopy(pc, pairs[i][0].at[1 - c], la.at[i], as_.at[i], ar.at[i], "c")

    def bcopy(k):
        i, at, to = pieces[k]
        return rcopy(
            pc, pairs[i][1].at[:, pl.ds(at, PIECE)], rb.at[:, pl.ds(to, PIECE)], bs.at[k], br.at[k], "c"
        )

    def make(zz, k, first):
        i, at, to = pieces[k]
        if first:
            if at == 0:
                acopy(i).wait_recv()
            bcopy(k).wait_recv()
        here = pl.ds(pl.multiple_of(zz * depth, depth), depth)
        mine, theirs = pairs[i][0][c, here, :], la[i, here, :]
        for t in range(0, PIECE, 512):
            tile = nn(mine, pairs[i][1][:, pl.ds(at + t, 512)]) + nn(theirs, rb[:, pl.ds(to + t, 512)])
            g[zz, :, :, :, pl.ds(to + t, 512)] = tile.reshape(2, 2, rows, 512).astype(BF)

    def copy2(p, zz, j):
        xx, yy = (x if j == 0 else 1 - x, 1 - y) if p == 0 else (1 - x, y if j == 0 else 1 - y)
        return rcopy(
            pc, g.at[zz, xx, yy, :, cols(p)], r2.at[p, zz, j], s2.at[p, zz, j], q2.at[p, zz, j],
            "y" if p == 0 else "x",
        )

    def copy3(p, zz):
        xx, yy = (1 - x, y) if p == 0 else (x, 1 - y)
        return rcopy(
            pc, g.at[zz, xx, yy, :, cols(p)], r3.at[p, zz], s3.at[p, zz], q3.at[p, zz],
            "x" if p == 0 else "y",
        )

    def views(p, zz, slot):
        if p == 2:
            return g.at[zz, :, :, :, cols(p)], rw.at[slot]
        return g.at[zz, x, y, :, cols(p)], rz.at[p, slot]

    def sendz(p, zz, up):
        slot = jnp.where(zz == z + 1, Z, zz) if up else zz
        src, dst = views(p, zz, slot)
        return rcopy(pc, src, dst, sz.at[p, zz], qz.at[p, slot], "u" if up else "d")

    def gotz(p, slot):
        src, dst = views(p, 0, slot)
        rcopy(pc, src, dst, sz.at[p, 0], qz.at[p, slot], "c").wait_recv()

    def add_plane(zz, slots):
        for xx in (0, 1):
            for yy in (0, 1):
                a = g.at[zz, xx, yy, :, cols(2)]
                add_into(a, [a] + [rw.at[k, xx, yy] for k in slots])

    def at_time(t, f):
        below, above = t - (Z - 1 - z), Z - 1 - (t - z)
        pl.when((below >= 0) & (below < z))(lambda: f(below, False, pc.up))
        pl.when((above > z) & (above < Z))(lambda: f(above, True, pc.down))

    def chain_first(zz, up, more):
        @pl.when(more)
        def _():
            gotz(2, zz)
            add_plane(zz, [zz])

        sendz(2, zz, up).start()

    def tail(k):
        if k < 2:
            return rcopy(pc, g.at[z, k, 1 - y, :, cols(2)], rt.at[k], st.at[k], qt.at[k], "y")
        return rcopy(pc, g.at[z, 1 - x, y, :, cols(2)], rt.at[2], st.at[2], qt.at[2], "x")

    for i in range(len(pairs)):
        acopy(i).start()
        for k in range(len(pieces)):
            if pieces[k][0] == i:
                bcopy(k).start()
    yield
    ends = {w + h: 0, w + 2 * h: 1}
    for k in range(Z + 1):
        if k < Z:
            zz = pc.zord(k)
            for n in range(len(pieces)):
                make(zz, n, k == 0)
                end = pieces[n][2] + PIECE
                if end == w and k == 0 and Z > 1:
                    at_time(0, chain_first)
                if end in ends:
                    copy2(ends[end], zz, 1).start()
            yield
        if k > 0:
            zz = pc.zord(k - 1)
            for p in (0, 1):
                copy2(p, zz, 1).wait_recv()
                a = g.at[(zz,) + ((1 - x, y) if p == 0 else (x, 1 - y)) + (slice(None), cols(p))]
                add_into(a, [a, r2.at[p, zz, 1]])
                copy3(p, zz).start()
            for p in (0, 1):
                copy2(p, zz, 0).start()
            if 0 < k - 1 < Z - 1:
                at_time(k - 1, chain_first)
            yield

    def own(p, zz):
        copy2(p, zz, 0).wait_recv()
        copy3(p, zz).wait_recv()
        a = g.at[zz, x, y, :, cols(p)]
        return a, [a, r2.at[p, zz, 0], r3.at[p, zz]]

    def chain(p, zz, up, more):
        a, parts = own(p, zz)

        @pl.when(more)
        def _():
            gotz(p, zz)
            add_into(a, parts + [rz.at[p, zz]])

        @pl.when(jnp.logical_not(more))
        def _():
            add_into(a, parts)

        sendz(p, zz, up).start()

    def gather_plane(slot):
        gotz(2, slot)
        add_plane(z, [slot])

    pl.when(pc.up)(lambda: gather_plane(z))
    pl.when(pc.down)(lambda: gather_plane(Z))
    for k in (0, 1):
        tail(k).start()
    yield
    for t in range(Z - 1):
        for p in (0, 1):
            at_time(t, functools.partial(chain, p))
        if t == 0:
            for k in (0, 1):
                tail(k).wait_recv()
                a = g.at[z, k, y, :, cols(2)]
                add_into(a, [a, rt.at[k]])
            tail(2).start()
        yield
    tail(2).wait_recv()
    add_into(out_ref.at[:, cols(2)], [g.at[z, x, y, :, cols(2)], rt.at[2]])
    for p in (0, 1):
        a, parts = own(p, z)
        o = out_ref.at[:, cols(p)]
        add_into(o, parts)

        def last(slot):
            gotz(p, slot)
            add_into(o, [o, rz.at[p, slot]])

        pl.when(pc.up)(lambda: last(z))
        pl.when(pc.down)(lambda: last(Z))
        yield
    for i in range(len(pairs)):
        acopy(i).wait_send()
    for k in range(len(pieces)):
        bcopy(k).wait_send()
    for k in range(3):
        tail(k).wait_send()
    for zz in range(Z):
        for p in (0, 1):
            for j in (0, 1):
                copy2(p, zz, j).wait_send()
            copy3(p, zz).wait_send()
        for p in (0, 1, 2):
            pl.when(zz < z)(lambda: sendz(p, zz, False).wait_send())
            pl.when(zz > z)(lambda: sendz(p, zz, True).wait_send())


def scatter_kernel(planes, count, *refs):
    pc = Place(planes)
    greet(pc)
    pairs = tuple(zip(refs[:count], refs[count : 2 * count]))
    for _ in scatter_steps(pc, pairs, refs[2 * count], refs[2 * count + 1 :]):
        pass


def scatter_rows(planes, lefts, rights, collective):
    rows = lefts[0].shape[1] // (4 * planes)
    widths = [r.shape[1] for r in rights]
    return pl.pallas_call(
        functools.partial(scatter_kernel, planes, len(lefts)),
        out_shape=jax.ShapeDtypeStruct((rows, sum(widths)), F32),
        in_specs=[VM] * (2 * len(lefts)),
        out_specs=VM,
        scratch_shapes=scatter_scratch(planes, rows, widths),
        compiler_params=params(collective),
    )(*lefts, *rights)


def by_core(rows, planes):
    tokens = rows.shape[0]
    each = D // (8 * planes)
    cut = rows.T.reshape(2 * planes, 2, 2 * each, tokens)
    return cut.transpose(1, 0, 2, 3).reshape(2, D // 2, tokens)


def fold_scratch(planes, rows, columns):
    return [
        pltpu.VMEM((planes, 2, rows, columns), BF),
        pltpu.VMEM((planes, rows, columns), BF),
        pltpu.VMEM((planes, rows, columns), BF),
        pltpu.VMEM((planes, 2, rows, columns), BF),
        DMA((planes, 2)),
        DMA((planes, 2)),
        DMA((planes,)),
        DMA((planes,)),
        DMA((planes,)),
        DMA((planes,)),
    ]


def fold_steps(pc, block, out_ref, scratch):
    rc, rx, rz, acc, cs, cr, xs, xr, zs, zr = scratch
    Z, z, x, c = pc.Z, pc.z, pc.x, pc.c

    def ccopy(zz, q):
        xx = x if q == 0 else 1 - x
        return rcopy(pc, block(pc.spot(zz, xx, 1 - c)), rc.at[zz, q], cs.at[zz, q], cr.at[zz, q], "c")

    def xcopy(zz):
        return rcopy(pc, acc.at[zz, 1], rx.at[zz], xs.at[zz], xr.at[zz], "x")

    def zcopy(zz):
        return rcopy(pc, acc.at[zz, 0], rz.at[zz], zs.at[zz], zr.at[zz], "d")

    def each(f):
        for zz in range(Z):
            pl.when(zz <= z)(functools.partial(f, zz))

    def a(zz):
        ccopy(zz, 1).start()
        ccopy(zz, 0).start()

    def b(zz):
        ccopy(zz, 1).wait_recv()
        add_into(acc.at[zz, 1], [block(pc.spot(zz, 1 - x, c)), rc.at[zz, 1]], 128)
        xcopy(zz).start()

    def m(zz):
        ccopy(zz, 0).wait_recv()
        add_into(acc.at[zz, 0], [block(pc.spot(zz, x, c)), rc.at[zz, 0]], 128)

    def e(zz):
        xcopy(zz).wait_recv()

        def finish(parts):
            @pl.when(zz < z)
            def _():
                add_into(acc.at[zz, 0], parts, 128)
                zcopy(zz).start()

            pl.when(zz == z)(lambda: add_into(out_ref, parts, 128))

        @pl.when(pc.up)
        def _():
            zcopy(zz).wait_recv()
            finish([acc.at[zz, 0], rx.at[zz], rz.at[zz]])

        pl.when(jnp.logical_not(pc.up))(lambda: finish([acc.at[zz, 0], rx.at[zz]]))

    def w(zz):
        ccopy(zz, 1).wait_send()
        ccopy(zz, 0).wait_send()
        xcopy(zz).wait_send()
        pl.when(zz < z)(lambda: zcopy(zz).wait_send())

    for f in (a, b, m, e):
        each(f)
        yield
    each(w)


def relay_scratch(planes):
    n = 4 * planes
    piece = pltpu.VMEM((n, NS // n, INNER), BF)
    return [piece, piece, DMA((n,)), DMA((n,)), DMA((n,)), DMA((n,))]


def relay_steps(pc, reverse, s_ref, dec_ref, out_ref, scratch):
    got, part, ss, sr, bs, br = scratch
    n = 4 * pc.Z
    me = pc.ctx

    def to(d):
        return lax.rem(me + d, n)

    def there(d):
        return rcopy(pc, s_ref.at[to(d)], got.at[me], ss.at[d], sr.at[d], (to(d), pc.y))

    def back(d):
        return rcopy(pc, part.at[to(d)], out_ref.at[me], bs.at[d], br.at[d], (to(d), pc.y))

    pl.loop(1, n)(lambda d: there(d).start())
    got[me] = s_ref[me]
    yield
    pl.loop(1, n)(lambda d: there(d).wait_recv())
    total = jnp.zeros(got.shape[1:], F32)
    for k in range(n):
        j = n - 1 - k if reverse else k
        part[j] = total.astype(BF)
        total = total * dec_ref[pl.ds(j, 1), :] + got[j].astype(F32)
    pl.loop(1, n)(lambda d: back(d).start())
    out_ref[me] = part[me]
    yield
    pl.loop(1, n)(lambda d: back(d).wait_recv())
    yield

    @pl.loop(1, n)
    def _(d):
        there(d).wait_send()
        back(d).wait_send()


def total_scratch(planes):
    shape = (SMALL_ROWS, 128)
    return [
        pltpu.VMEM((6,) + shape, F32),
        pltpu.VMEM((planes,) + shape, F32),
        DMA((3,)),
        DMA((3,)),
        DMA((planes,)),
        DMA((planes,)),
    ]


def plane_peers(pc):
    return [pc.dev(lax.rem(pc.z + d, pc.Z), pc.x, pc.y, pc.c) for d in range(1, pc.Z)]


def total_steps(pc, out_ref, scratch):
    rx, rz, ss, sr, zs, zr = scratch
    Z, z = pc.Z, pc.z
    for i, d in enumerate("cxy"):
        rx[2 * i] = out_ref[...]
        cp = rcopy(pc, rx.at[2 * i], rx.at[2 * i + 1], ss.at[i], sr.at[i], d)
        cp.start()
        yield
        cp.wait()
        out_ref[...] = out_ref[...] + rx[2 * i + 1]
    rz[z] = out_ref[...]
    copies = [rcopy(pc, rz.at[z], rz.at[z], zs.at[d], zr.at[d], to) for d, to in enumerate(plane_peers(pc))]
    for cp in copies:
        cp.start()
    yield
    for cp in copies:
        cp.wait()
    total = rz[0]
    for k in range(1, Z):
        total = total + rz[k]
    out_ref[...] = total


def visible(start, block, pos_ref):
    kpos = start + lax.broadcasted_iota(jnp.int32, (block, pos_ref.shape[1]), 0)
    return (kpos <= pos_ref[0:1, :]) & (kpos >= pos_ref[1:2, :])


def split_heads(src, dst, scale=None):
    rows = src.shape[0]
    for h in range(QUERY_HEADS):
        v = src[:, pl.ds(h * HEAD_WIDTH, HEAD_WIDTH)]
        dst[pl.ds(h * rows, rows), :] = v if scale is None else v * scale


def swap_halves(v):
    width = v.shape[1]
    lane = lax.broadcasted_iota(jnp.int32, v.shape, 1)
    low = lax.rem(lane, HEAD_WIDTH) < HEAD_WIDTH // 2
    ahead = pltpu.roll(v, width - HEAD_WIDTH // 2, 1)
    behind = pltpu.roll(v, HEAD_WIDTH // 2, 1)
    return jnp.where(low, ahead, behind)


def rotate(v, cos_ref, sin_ref, sign=1.0):
    return v * cos_ref[...] + swap_halves(v) * (sign * sin_ref[...])


def attend_block(j, block, q_ref, kv, pos_ref, m_ref, l_ref, acc_ref):
    rows = pos_ref.shape[1]
    start = pl.multiple_of(j * block, block)
    ok = visible(start, block, pos_ref)
    for h in range(QUERY_HEADS):
        g = h // (QUERY_HEADS // KEY_VALUE_HEADS)
        keys = kv[:, g * HEAD_WIDTH : (g + 1) * HEAD_WIDTH]
        vals = kv[:, KEY_WIDTH + g * HEAD_WIDTH : KEY_WIDTH + (g + 1) * HEAD_WIDTH]
        s = jnp.where(ok, nt(keys, q_ref[pl.ds(h * rows, rows), :]), large_negative)
        m0 = m_ref[h : h + 1, :]
        m1 = jnp.maximum(m0, jnp.max(s, axis=0, keepdims=True))
        p = jnp.where(ok, jnp.exp(s - m1), 0.0)
        a = jnp.exp(m0 - m1)
        l_ref[h : h + 1, :] = l_ref[h : h + 1, :] * a + jnp.sum(p, axis=0, keepdims=True)
        m_ref[h : h + 1, :] = m1
        r = pl.ds(h * HEAD_WIDTH, HEAD_WIDTH)
        acc_ref[r, :] = acc_ref[r, :] * a + tn(vals, p.astype(BF))


def attend_end(o_ref, lse_ref, m_ref, l_ref, acc_ref):
    lse_ref[...] = m_ref[...] + jnp.log(l_ref[...])
    inv = 1.0 / l_ref[...]
    for h in range(QUERY_HEADS):
        r = pl.ds(h * HEAD_WIDTH, HEAD_WIDTH)
        acc_ref[r, :] = acc_ref[r, :] * inv[h : h + 1, :]
    o_ref[...] = acc_ref[...].T.astype(o_ref.dtype)


def attend_back_block(j, block, q_ref, do_ref, kv_ref, pos_ref, lse_ref, dl_ref, dkv_ref, acc_ref):
    rows = pos_ref.shape[1]
    start = pl.multiple_of(j * block, block)
    ok = visible(start, block, pos_ref)
    at = pl.ds(start, block)
    dks, dvs = [], []
    for g in range(KEY_VALUE_HEADS):
        keys = kv_ref[at, pl.ds(g * HEAD_WIDTH, HEAD_WIDTH)]
        vals = kv_ref[at, pl.ds(KEY_WIDTH + g * HEAD_WIDTH, HEAD_WIDTH)]
        dk = dv = None
        for h in range(4 * g, 4 * g + 4):
            q = q_ref[pl.ds(h * rows, rows), :]
            do = do_ref[pl.ds(h * rows, rows), :]
            p = jnp.where(ok, jnp.exp(nt(keys, q) - lse_ref[h : h + 1, :]), 0.0)
            ds = (p * (nt(vals, do) - dl_ref[h : h + 1, :])).astype(BF)
            r = pl.ds(h * HEAD_WIDTH, HEAD_WIDTH)
            acc_ref[r, :] += tn(keys, ds)
            a, b = nn(ds, q), nn(p.astype(BF), do)
            dk = a if dk is None else dk + a
            dv = b if dv is None else dv + b
        dks.append(dk)
        dvs.append(dv)
    dkv_ref[at, :] = jnp.concatenate(dks + dvs, axis=1).astype(BF)


def two(left, right, lanes):
    return jnp.where(lanes < MP, left, right)


def pair_columns(ref, p, lanes):
    return two(ref[:, 2 * p : 2 * p + 1], ref[:, 2 * p + 1 : 2 * p + 2], lanes)


def mixer_steps(
    xe, mk, cw, cb, cum_t, cum, dt_t, we_t, skip, doc_c, doc_r, pre, xo, mix, so, xw, bias
):
    rows = pre.shape[0]
    for i in range(XBC // 256):
        sl = pl.ds(i * 256, 256)
        acc = jnp.broadcast_to(cb[:, sl], (rows, 256))
        for j in range(CONV):
            acc = acc + cw[j : j + 1, sl] * (xe[pl.ds(5 + j, rows), sl] * mk[:, j : j + 1])
        pre[:, sl] = acc.astype(BF)
        act = acc * jax.nn.sigmoid(acc)
        xo[:, sl] = act.astype(BF)
        if i < INNER // 256:
            mix[:, sl] = skip[:, sl] * act
        if i == 3:
            yield
    yield
    b_rows, c_rows = xo[:, pl.ds(INNER, NS)], xo[:, pl.ds(INNER + NS, NS)]
    cross = nt(c_rows, b_rows)
    t_at = lax.broadcasted_iota(jnp.int32, (rows, rows), 0)
    s_at = lax.broadcasted_iota(jnp.int32, (rows, rows), 1)
    bias[...] = jnp.where((doc_c[...] == doc_r[...]) & (s_at <= t_at), 0.0, large_negative)
    lanes = lax.broadcasted_iota(jnp.int32, (rows, 2 * MP), 1)
    for p in range(MH // 2):
        sl = pl.ds(p * 2 * MP, 2 * MP)
        xd = xo[:, sl].astype(F32) * pair_columns(dt_t, p, lanes)
        xw[:, sl] = (xd * pair_columns(we_t, p, lanes)).astype(BF)
        xb = xd.astype(BF)
        outs = []
        for h in (2 * p, 2 * p + 1):
            low = jnp.exp(jnp.minimum(cum_t[:, h : h + 1] - cum[h : h + 1, :], bias[...]))
            outs.append(nn((low * cross).astype(BF), xb))
        mix[:, sl] = mix[:, sl] + two(outs[0], outs[1], lanes)
        if p % 3 == 2:
            yield
    so[...] = tn(b_rows, xw[...]).astype(BF).reshape(so.shape)


def spread_heads():
    head = lax.broadcasted_iota(jnp.int32, (MH, INNER), 0)
    lane = lax.broadcasted_iota(jnp.int32, (MH, INNER), 1)
    return (lane // MP == head).astype(F32)


def exact(a, b, dims):
    return lax.dot_general(
        a, b, (dims, ((), ())), precision=lax.Precision.HIGHEST, preferred_element_type=F32
    )


def wide(columns, spread_mat):
    return exact(columns, spread_mat, ((1,), (0,)))


def gate_kernel(planes, lens, mix, xo, state_in, ldec, gate, small, att, mixed, branch, gain, state, din_t):
    rows = mix.shape[0]
    spread_mat = spread_heads()
    unpack(small, "gate", gain)
    state[...] = state_in[...].reshape(state.shape)
    first = Place(planes).ctx * rows
    a = lax.broadcasted_iota(jnp.int32, (rows, rows), 0)
    b = lax.broadcasted_iota(jnp.int32, (rows, rows), 1)
    docs = doc_of(first + lax.broadcasted_iota(jnp.int32, (rows, 1), 0), lens)
    before = doc_of(jnp.full((1, 1), first - 1, jnp.int32), lens)
    ct = exact((b <= a).astype(F32), ldec[...], ((1,), (1,)))
    din_t[...] = jnp.where(docs == before, jnp.exp(ct), 0.0)

    @pl.loop(0, rows // 64)
    def _(i):
        r = pl.ds(pl.multiple_of(i * 64, 64), 64)
        carried = nn(xo[r, pl.ds(INNER + NS, NS)], state[...])
        m = mix[r, :] + carried * wide(din_t[r, :], spread_mat)
        mixed[r, :] = m.astype(BF)
        gv = gate[r, :]
        gated = m * (gv * jax.nn.sigmoid(gv))
        factor = lax.rsqrt(jnp.mean(gated * gated, axis=1, keepdims=True) + norm_eps)
        branch[r, pl.ds(0, QUERY_WIDTH)] = att[r, :]
        branch[r, pl.ds(QUERY_WIDTH, INNER)] = (gated * factor * gain[...]).astype(BF)


def gate_out(planes, lens, mix, xo, state, ldec, gate, small, att):
    rows = mix.shape[0]
    return pl.pallas_call(
        functools.partial(gate_kernel, planes),
        out_shape=(
            jax.ShapeDtypeStruct((rows, INNER), BF),
            jax.ShapeDtypeStruct((rows, MIXOUT), BF),
        ),
        in_specs=[SM] + [VM] * 7,
        out_specs=(VM,) * 2,
        scratch_shapes=[
            pltpu.VMEM((1, INNER), F32),
            pltpu.VMEM((NS, INNER), BF),
            pltpu.VMEM((rows, MH), F32),
        ],
        compiler_params=params(),
    )(lens, mix, xo, state, ldec, gate, small, att)


def doc_of(pos, lens):
    start = 0
    found = jnp.full_like(pos, -1)
    for d in range(lens.shape[1]):
        found = found + (pos >= start).astype(jnp.int32)
        start = start + lens[0, d]
    return found


def begin_of(pos, lens):
    start = 0
    found = jnp.zeros_like(pos)
    for d in range(lens.shape[1]):
        found = jnp.maximum(found, jnp.where(pos >= start, start, 0))
        start = start + lens[0, d]
    return found


def table_scratch(rows):
    return [
        pltpu.VMEM((2, rows), jnp.int32),
        pltpu.VMEM((rows, 8), F32),
        pltpu.VMEM((rows, 1), jnp.int32),
        pltpu.VMEM((1, rows), jnp.int32),
        pltpu.VMEM((MH, rows), F32),
        pltpu.VMEM((rows, MH), F32),
        pltpu.VMEM((rows, MH), F32),
        pltpu.VMEM((rows, MH), F32),
        pltpu.VMEM((rows, MH), F32),
    ]


def make_tables(pc, lens, ldec, root_t, tables):
    pos, same, doc_c, doc_r, cum, cum_t, dt_t, we_t, din_t = tables
    rows = ldec.shape[1]
    first = pc.ctx * rows
    at_c = first + lax.broadcasted_iota(jnp.int32, (rows, 1), 0)
    at_r = first + lax.broadcasted_iota(jnp.int32, (1, rows), 1)
    pos[0:1, :] = at_r
    pos[1:2, :] = begin_of(at_r, lens)
    dc = doc_of(at_c, lens)
    doc_c[...] = dc
    doc_r[...] = doc_of(at_r, lens)
    for j in range(CONV):
        same[:, j : j + 1] = (doc_of(at_c - (CONV - 1) + j, lens) == dc).astype(F32)
        same[:, CONV + j : CONV + j + 1] = (doc_of(at_c + (CONV - 1) - j, lens) == dc).astype(F32)
    a = lax.broadcasted_iota(jnp.int32, (rows, rows), 0)
    b = lax.broadcasted_iota(jnp.int32, (rows, rows), 1)
    cum[...] = exact(ldec[...], (a <= b).astype(F32), ((1,), (0,)))
    ct = exact((b <= a).astype(F32), ldec[...], ((1,), (1,)))
    cum_t[...] = ct
    fresh = doc_of(at_c - 1, lens) != dc
    dt_t[...] = jnp.where(fresh, 1.0, root_t[...])
    before = doc_of(jnp.full((1, 1), first - 1, jnp.int32), lens)
    end = doc_of(jnp.full((1, 1), first + rows - 1, jnp.int32), lens)
    din_t[...] = jnp.where(dc == before, jnp.exp(ct), 0.0)
    we_t[...] = jnp.where(dc == end, jnp.exp(jnp.minimum(ct[rows - 1 : rows, :] - ct, 0.0)), 0.0)


SMALL_AT = {"one": (0, 8), "two": (8, 8), "gate": (16, 12), "bias": (84, 14), "skip": (98, 1)}


def unpack(small, name, dst, row=0):
    at, tiles = SMALL_AT[name] if isinstance(name, str) else name
    for i in range(tiles):
        dst[row : row + 1, pl.ds(i * 128, 128)] = small[at + i : at + i + 1, :]


def unpack_conv(small, dst):
    for j in range(CONV):
        unpack(small, (28 + 14 * j, 14), dst, j)


def wide_skip(small, spread_mat, dst):
    dst[...] = wide(jnp.broadcast_to(small[98:99, 0:MH], (8, MH)), spread_mat)[0:1, :]


GATE_AT = QUERY_WIDTH + 2 * KEY_WIDTH
XBC_AT = GATE_AT + INNER
FIRST = QUERY_WIDTH + 2 * KEY_WIDTH + XBC


def front_kernel(
    planes, block, lens, hid, w1, w2, cos_w, sin_w, ldec, root_t, small,
    normed, scale, g1, g2, q_out, kv_all, xe, decays, pre, xo, mix, state_in, att, lse,
    kv_own, edge_out, edge_in, dec_own, decs, dec_rows, gains, conv_w, conv_b, skip, so, qh, m_ref, l_ref,
    acc, xw, bias, *refs,
):
    tables, refs = refs[:9], refs[9:]
    pos, same, doc_c, doc_r, cum, cum_t, dt_t, we_t, din_t = tables
    first_refs, refs = refs[:9], refs[9:]
    rest_refs, refs = refs[:9], refs[9:]
    spread_refs, refs = refs[:7], refs[7:]
    relay_refs = refs[:6]
    pc = Place(planes)
    n = 4 * planes
    rows = hid.shape[0]
    greet_row(pc, True)
    gather = gather_steps(pc, w1, g1, first_refs)
    rest = gather_steps(pc, w2, g2, rest_refs)
    next(gather)

    def pump(count=1):
        for _ in range(count):
            next(rest, None)

    unpack(small, "one", gains)
    unpack(small, "bias", conv_b)
    unpack_conv(small, conv_w)
    spread_mat = spread_heads()
    wide_skip(small, spread_mat, skip)
    for i in range(rows // 64):
        r = pl.ds(i * 64, 64)
        v = hid[r, :].astype(F32)
        f = lax.rsqrt(jnp.mean(v * v, axis=1, keepdims=True) + norm_eps)
        scale[r, :] = f
        normed[r, :] = (v * f * gains[...]).astype(BF)
    next(gather)
    make_tables(pc, lens, ldec, root_t, tables)
    dec_own[...] = jnp.zeros_like(dec_own)
    dec_own[0:1, 0:MH] = din_t[rows - 1 : rows, :]
    begun = False
    for tail in gather:
        if tail and not begun:
            begun = True
            pump()

    def project(at, width):
        return nn(normed[...], g1[:, :, :, :, :, pl.ds(at, width)].reshape(D, width))

    base = GATE_AT
    for i in range(XBC // 256):
        sl = pl.ds(i * 256, 256)
        xb = project(base + i * 256, 256).astype(BF)
        xe[pl.ds(8, rows), sl] = xb.astype(F32)
        edge_out[:, sl] = xb[rows - 16 :, :]
    kv = project(QUERY_WIDTH, 2 * KEY_WIDTH)
    kv_own[:, pl.ds(0, KEY_WIDTH)] = rotate(kv[:, :KEY_WIDTH], cos_w, sin_w).astype(BF)
    kv_own[:, pl.ds(KEY_WIDTH, KEY_WIDTH)] = kv[:, KEY_WIDTH:].astype(BF)
    spreads = spread_steps(pc, kv_own, edge_out, dec_own, kv_all, edge_in, decs, spread_refs)
    next(spreads)
    for i in range(QUERY_WIDTH // 256):
        qv = project(i * 256, 256)
        for t in (0, 1):
            q_out[:, pl.ds(i * 256 + t * 128, 128)] = rotate(
                qv[:, t * 128 : (t + 1) * 128], cos_w, sin_w
            ).astype(BF)
    split_heads(q_out, qh, jnp.asarray(HEAD_WIDTH**-0.5, BF))
    next(spreads)
    xe[pl.ds(0, 8), :] = edge_in[pl.ds(8, 8), :].astype(F32)
    pump()
    next(spreads)
    mixing = mixer_steps(
        xe, same, conv_w, conv_b, cum_t, cum, dt_t, we_t, skip, doc_c, doc_r, pre, xo, mix, so, xw, bias
    )
    for _ in mixing:
        next(spreads, None)
        pump()
    for k in range(n):
        dec_rows[k : k + 1, :] = decs[k, 0:1, :]
    decays[...] = wide(dec_rows[:, 0:MH], spread_mat)
    states = relay_steps(pc, False, so, decays, state_in, relay_refs)
    next(states)
    m_ref[...] = jnp.full_like(m_ref, large_negative)
    l_ref[...] = jnp.zeros_like(l_ref)
    acc[...] = jnp.zeros_like(acc)
    seen = (pc.ctx * rows + rows + block - 1) // block
    per = block // rows
    parts = 8
    each = n // per // parts

    def keys_at(j):
        return kv_all[pl.ds(j * per, per), :, :].reshape(block, 2 * KEY_WIDTH)

    for k in range(parts):
        lo = each * k

        @pl.loop(jnp.minimum(lo, seen), jnp.minimum(lo + each, seen))
        def _(j):
            attend_block(j, block, qh, keys_at(j), pos, m_ref, l_ref, acc)

        pump(2)
        if k in (3, 6):
            next(states)
    attend_end(att, lse, m_ref, l_ref, acc)
    for _ in spreads:
        pass
    for _ in rest:
        pass
    for _ in states:
        pass


def front(planes, lens, hid, w1, w2, cos_w, sin_w, ldec, root_t, small, block, collective):
    n = 4 * planes
    rows = hid.shape[0]
    each = w1.shape[0]
    sds = jax.ShapeDtypeStruct
    return pl.pallas_call(
        functools.partial(front_kernel, planes, block),
        out_shape=(
            sds((rows, D), BF),
            sds((rows, 1), F32),
            sds((planes, 2, 2, 2, each, w1.shape[1]), BF),
            sds((planes, 2, 2, 2, each, w2.shape[1]), BF),
            sds((rows, QUERY_WIDTH), BF),
            sds((n, rows, 2 * KEY_WIDTH), BF),
            sds((rows + 8, XBC), F32),
            sds((n, INNER), F32),
            sds((rows, XBC), BF),
            sds((rows, XBC), BF),
            sds((rows, INNER), F32),
            sds((n, NS // n, INNER), BF),
            sds((rows, QUERY_WIDTH), BF),
            sds((QUERY_HEADS, rows), F32),
        ),
        in_specs=[SM, VM, VM, HB] + [VM] * 5,
        out_specs=(VM, VM, VM, HB) + (VM,) * 10,
        scratch_shapes=[
            pltpu.VMEM((rows, 2 * KEY_WIDTH), BF),
            pltpu.VMEM((16, XBC), BF),
            pltpu.VMEM((16, XBC), BF),
            pltpu.VMEM((8, 128), F32),
            pltpu.VMEM((n, 8, 128), F32),
            pltpu.VMEM((n, 128), F32),
            pltpu.VMEM((1, D), F32),
            pltpu.VMEM((CONV, XBC), F32),
            pltpu.VMEM((1, XBC), F32),
            pltpu.VMEM((1, INNER), F32),
            pltpu.VMEM((n, NS // n, INNER), BF),
            pltpu.VMEM((QUERY_HEADS * rows, HEAD_WIDTH), BF),
            pltpu.VMEM((QUERY_HEADS, rows), F32),
            pltpu.VMEM((QUERY_HEADS, rows), F32),
            pltpu.VMEM((QUERY_WIDTH, rows), F32),
            pltpu.VMEM((rows, INNER), BF),
            pltpu.VMEM((rows, rows), F32),
        ]
        + table_scratch(rows)
        + gather_scratch(planes)
        + gather_scratch(planes)
        + spread_scratch(planes)
        + relay_scratch(planes),
        compiler_params=params(collective),
    )(lens, hid, w1, w2, cos_w, sin_w, ldec, root_t, small)


def gate_back_rows(i, grad, mixed, gate, gain, din_t, spread_mat, dm, dproj, dgain, dinc):
    r = pl.ds(pl.multiple_of(i * 64, 64), 64)
    m, gv, gr = mixed[r, :].astype(F32), gate[r, :], grad[r, pl.ds(QUERY_WIDTH, INNER)]
    sig = jax.nn.sigmoid(gv)
    sil = gv * sig
    gated = m * sil
    factor = lax.rsqrt(jnp.mean(gated * gated, axis=1, keepdims=True) + norm_eps)
    w = gr * gain[...]
    dg = factor * (w - gated * factor * factor * jnp.mean(w * gated, axis=1, keepdims=True))
    dgain[...] += jnp.sum(gr * gated * factor, axis=0, keepdims=True)
    dproj[r, pl.ds(GATE_AT, INNER)] = (dg * m * (sig * (1.0 + gv * (1.0 - sig)))).astype(BF)
    d = dg * sil
    dm[r, :] = d.astype(BF)
    dinc[r, :] = (d * wide(din_t[r, :], spread_mat)).astype(BF)


def mixer_back_steps(
    xe, mk, cw, cum_t, cum, dt_t, we_t, skip, doc_c, doc_r, pre, xo, dm, dc_in, ds, dpre, dcw, dskip, xw, bias
):
    rows = pre.shape[0]
    here = pl.ds(0, rows)
    b_rows, c_rows = xo[:, pl.ds(INNER, NS)], xo[:, pl.ds(INNER + NS, NS)]
    cross = nt(b_rows, c_rows)
    s_at = lax.broadcasted_iota(jnp.int32, (rows, rows), 0)
    t_at = lax.broadcasted_iota(jnp.int32, (rows, rows), 1)
    bias[...] = jnp.where((doc_c[...] == doc_r[...]) & (s_at <= t_at), 0.0, large_negative)
    lanes = lax.broadcasted_iota(jnp.int32, (rows, 2 * MP), 1)

    def slope(sl):
        v = pre[:, sl].astype(F32)
        sig = jax.nn.sigmoid(v)
        return sig * (1.0 + v * (1.0 - sig))

    dcross = jnp.zeros((rows, rows), F32)
    for p in range(MH // 2):
        sl = pl.ds(p * 2 * MP, 2 * MP)
        xv = xo[:, sl].astype(F32)
        dt2, we2 = pair_columns(dt_t, p, lanes), pair_columns(we_t, p, lanes)
        xd = xv * dt2
        xw[:, sl] = (xd * we2).astype(BF)
        g = dm[:, sl]
        outs = []
        for k in (0, 1):
            h = 2 * p + k
            low = jnp.exp(jnp.minimum(cum[h : h + 1, :] - cum_t[:, h : h + 1], bias[...]))
            outs.append(nn((low * cross).astype(BF), g))
            part = jnp.where((lanes < MP) == (k == 0), xd, 0.0).astype(BF)
            dcross = dcross + nt(part, g) * low
        dxd = two(outs[0], outs[1], lanes) + we2 * nn(b_rows, ds[:, sl])
        gf = g.astype(F32)
        dskip[:, sl] = jnp.sum(gf * xv, axis=0, keepdims=True)
        dpre[here, sl] = (dxd * dt2 + skip[:, sl] * gf) * slope(sl)
        if p % 4 == 3:
            yield
    db16 = dcross.astype(BF)
    slb, slc = pl.ds(INNER, NS), pl.ds(INNER + NS, NS)
    dpre[here, slb] = (nn(db16, c_rows) + nt(xw[...], ds[...])) * slope(slb)
    dpre[here, slc] = (tn(db16, b_rows) + dc_in[...]) * slope(slc)
    yield
    for i in range(XBC // 256):
        sl = pl.ds(i * 256, 256)
        d = dpre[here, sl]
        for j in range(CONV):
            dcw[j : j + 1, sl] = jnp.sum(
                d * (xe[pl.ds(5 + j, rows), sl] * mk[:, j : j + 1]), axis=0, keepdims=True
            )
        dcw[CONV : CONV + 1, sl] = jnp.sum(d, axis=0, keepdims=True)


def back_kernel(planes, count, block, *refs):
    lefts, rights, refs = refs[:count], refs[count : 2 * count], refs[2 * count :]
    if count:
        branch = rights[2]
    else:
        branch, refs = refs[0], refs[1:]
    (
        lens, grad, mixed, gate, xo, state_in, q_in, kv, lse, cos_w, sin_w, decays, xe, ldec, root_t, small, pre,
    ) = refs[:17]
    refs = refs[17:]
    if count:
        scattered, refs = refs[0], refs[1:]
    dproj, dgain, dcw, dskip = refs[:4]
    (
        dm, dinc, dc, dstate, dsnew, flat, qh, doh, dl, acc, dkv, dkv_own, dpre, edge, bias, esem
    ) = refs[4:20]
    gain, cw, skip, state = refs[20:24]
    tables, refs = refs[24:33], refs[33:]
    pos, same, doc_c, doc_r, cum, cum_t, dt_t, we_t, din_t = tables
    relay_refs, refs = refs[:6], refs[6:]
    fold_refs, refs = refs[:10], refs[10:]
    pc = Place(planes)
    n = 4 * planes
    rows = mixed.shape[0]
    greet_row(pc, count > 0)
    side = (
        scatter_steps(pc, tuple(zip(lefts, rights)), scattered, refs) if count else iter(())
    )

    def pump():
        next(side, None)

    pump()
    spread_mat = spread_heads()
    unpack(small, "gate", gain)
    unpack_conv(small, cw)
    wide_skip(small, spread_mat, skip)
    make_tables(pc, lens, ldec, root_t, tables)
    state[...] = state_in[...].reshape(state.shape)
    dgain[...] = jnp.zeros_like(dgain)
    pl.loop(0, rows // 64)(
        lambda i: gate_back_rows(i, grad, mixed, gate, gain, din_t, spread_mat, dm, dproj, dgain, dinc)
    )
    ds0 = tn(xo[:, pl.ds(INNER + NS, NS)], dinc[...]).astype(BF)
    dc[...] = nt(dinc[...], state[...])
    dstate[...] = ds0.reshape(dstate.shape)
    states = relay_steps(pc, True, dstate, decays, dsnew, relay_refs)
    next(states)
    for _ in range(planes):
        pump()
    split_heads(q_in, qh, jnp.asarray(HEAD_WIDTH**-0.5, BF))
    go = grad[:, pl.ds(0, QUERY_WIDTH)].astype(BF)
    head = lax.broadcasted_iota(jnp.int32, (QUERY_HEADS, QUERY_WIDTH), 0)
    lane = lax.broadcasted_iota(jnp.int32, (QUERY_HEADS, QUERY_WIDTH), 1)
    for h in range(QUERY_HEADS):
        doh[pl.ds(h * rows, rows), :] = go[:, h * HEAD_WIDTH : (h + 1) * HEAD_WIDTH]
    dl[...] = exact(
        (lane // HEAD_WIDTH == head).astype(F32),
        go.astype(F32) * branch[:, pl.ds(0, QUERY_WIDTH)].astype(F32),
        ((1,), (1,)),
    )
    acc[...] = jnp.zeros_like(acc)
    total = kv.shape[0] // block
    seen = (pc.ctx * rows + rows + block - 1) // block
    parts = 4
    each = total // parts

    @pl.loop(seen, (pc.z + 1) * 4 * rows // block)
    def _(j):
        dkv[pl.ds(pl.multiple_of(j * block, block), block), :] = jnp.zeros((block, 2 * KEY_WIDTH), BF)

    for k in range(parts):
        lo = each * k
        pl.loop(jnp.minimum(lo, seen), jnp.minimum(lo + each, seen))(
            lambda j: attend_back_block(j, block, qh, doh, kv, pos, lse, dl, dkv, acc)
        )
        pump()
        if k == 1:
            next(states)
    folds = fold_steps(
        pc, lambda s: dkv.at[pl.ds(pl.multiple_of(s * rows, rows), rows), :], dkv_own, fold_refs
    )
    next(folds)
    for t in range(QUERY_WIDTH // 128):
        dq = acc[pl.ds(t * 128, 128), :].T * (HEAD_WIDTH**-0.5)
        dproj[:, pl.ds(t * 128, 128)] = rotate(dq, cos_w, sin_w, -1.0).astype(BF)
    next(states)
    flat[...] = dsnew[...].reshape(flat.shape)
    next(folds)
    mixing = mixer_back_steps(
        xe, same, cw, cum_t, cum, dt_t, we_t, skip, doc_c, doc_r, pre, xo, dm, dc, flat, dpre, dcw, dskip, dinc, bias
    )
    next(mixing)
    next(folds)
    pump()
    next(mixing)
    pump()
    next(mixing)
    next(folds)
    pump()
    next(mixing)
    prior = rcopy(pc, dpre.at[pl.ds(0, 8), :], edge, esem.at[0], esem.at[1], (lax.rem(pc.ctx + n - 1, n), pc.y))
    pl.when(pc.ctx > 0)(lambda: prior.start())
    for _ in mixing:
        pass
    pump()
    for _ in folds:
        pass
    dproj[:, pl.ds(QUERY_WIDTH, KEY_WIDTH)] = rotate(dkv_own[:, pl.ds(0, KEY_WIDTH)], cos_w, sin_w, -1.0).astype(BF)
    dproj[:, pl.ds(QUERY_WIDTH + KEY_WIDTH, KEY_WIDTH)] = dkv_own[:, pl.ds(KEY_WIDTH, KEY_WIDTH)].astype(BF)
    pl.when(pc.ctx < n - 1)(lambda: prior.wait_recv())

    @pl.when(pc.ctx == n - 1)
    def _():
        edge[...] = jnp.zeros_like(edge)

    dpre[pl.ds(rows, 8), :] = edge[...]
    for i in range(XBC // 256):
        sl = pl.ds(i * 256, 256)
        total_grad = jnp.zeros((rows, 256), F32)
        for j in range(CONV):
            total_grad = total_grad + cw[j : j + 1, sl] * (
                dpre[pl.ds(CONV - 1 - j, rows), sl] * same[:, CONV + j : CONV + j + 1]
            )
        dproj[:, pl.ds(XBC_AT + i * 256, 256)] = total_grad.astype(BF)
    for _ in states:
        pass
    pl.when(pc.ctx > 0)(lambda: prior.wait_send())
    for _ in side:
        pass


def back(planes, lefts, rights, args, block, collective):
    count = len(lefts)
    n = 4 * planes
    rows = args[-1].shape[0]
    keys = n * rows
    outs = [
        jax.ShapeDtypeStruct((rows, MIXIN), BF),
        jax.ShapeDtypeStruct((1, INNER), F32),
        jax.ShapeDtypeStruct((CONV + 1, XBC), F32),
        jax.ShapeDtypeStruct((1, INNER), F32),
    ]
    scratch = [
        pltpu.VMEM((rows, INNER), BF),
        pltpu.VMEM((rows, INNER), BF),
        pltpu.VMEM((rows, NS), F32),
        pltpu.VMEM((n, NS // n, INNER), BF),
        pltpu.VMEM((n, NS // n, INNER), BF),
        pltpu.VMEM((NS, INNER), BF),
        pltpu.VMEM((QUERY_HEADS * rows, HEAD_WIDTH), BF),
        pltpu.VMEM((QUERY_HEADS * rows, HEAD_WIDTH), BF),
        pltpu.VMEM((QUERY_HEADS, rows), F32),
        pltpu.VMEM((QUERY_WIDTH, rows), F32),
        pltpu.VMEM((keys, 2 * KEY_WIDTH), BF),
        pltpu.VMEM((rows, 2 * KEY_WIDTH), F32),
        pltpu.VMEM((rows + 8, XBC), F32),
        pltpu.VMEM((8, XBC), F32),
        pltpu.VMEM((rows, rows), F32),
        DMA((2,)),
        pltpu.VMEM((1, INNER), F32),
        pltpu.VMEM((CONV, XBC), F32),
        pltpu.VMEM((1, INNER), F32),
        pltpu.VMEM((NS, INNER), BF),
    ]
    scratch += table_scratch(rows)
    scratch += relay_scratch(planes) + fold_scratch(planes, rows, 2 * KEY_WIDTH)
    if count:
        widths = [r.shape[1] for r in rights]
        each = lefts[0].shape[1] // n
        outs = [jax.ShapeDtypeStruct((each, sum(widths)), F32)] + outs
        scratch += scatter_scratch(planes, each, widths)
    return pl.pallas_call(
        functools.partial(back_kernel, planes, count, block),
        out_shape=tuple(outs),
        in_specs=[VM] * (2 * count + (not count)) + [SM] + [VM] * (len(args) - 2 + bool(count)),
        out_specs=(VM,) * len(outs),
        scratch_shapes=scratch,
        compiler_params=params(collective),
    )(*lefts, *rights, *args)


def last_kernel(
    planes, left, dproj, w1, w2, tok, scale, packed, dres, small, scattered, dhid, totals, dn, wg, wsem, gain, *scratch
):
    pc = Place(planes)
    peers = plane_peers(pc)
    bar = pltpu.get_barrier_semaphore()
    for d in [pc.near(k) for k in "cxy"] + peers:
        pl.semaphore_signal(bar, inc=1, device_id=d, device_id_type=MESH)
    pl.semaphore_wait(bar, 3 + len(peers))
    rows = dproj.shape[0]
    fetch = pltpu.make_async_copy(w2.at[:, :, :, :, :, pl.ds(0, INNER)], wg, wsem)
    fetch.start()
    side = scatter_steps(pc, ((left, dproj),), scattered, scratch[6:])
    next(side)
    unpack(packed, "one", gain)
    fetch.wait()
    next(side)
    part = planes // 4
    for i in range(4):
        at = pl.ds(i * part, part)
        a, b = w1[at].reshape(D // 4, FIRST), wg[at].reshape(D // 4, INNER)
        dn[:, pl.ds(i * 256, 256)] = (
            nt(dproj[:, pl.ds(0, GATE_AT)], a[:, :GATE_AT])
            + nt(dproj[:, pl.ds(GATE_AT, INNER)], b)
            + nt(dproj[:, pl.ds(XBC_AT, XBC)], a[:, GATE_AT:])
        )
        if i > 0:
            next(side)
    totals[...] = small[...]
    for i in range(rows // 64):
        r = pl.ds(i * 64, 64)
        v, g, f = tok[r, :].astype(F32), dn[r, :], scale[r, :]
        w = g * gain[...]
        dhid[r, :] = dres[r, :] + f * (w - v * f * f * jnp.mean(w * v, axis=1, keepdims=True))
        part = jnp.sum(g * v * f, axis=0, keepdims=True)
        for t in range(D // 128):
            totals[t : t + 1, :] = totals[t : t + 1, :] + part[:, t * 128 : (t + 1) * 128]
    sums = total_steps(pc, totals, scratch[:6])
    next(sums)
    for _ in range(3):
        next(side)
        next(sums)
    for _ in side:
        next(sums, None)
    for _ in sums:
        pass


def last(planes, left, dproj, w1, w2, tok, scale, packed, dres, small, collective):
    rows = dproj.shape[0]
    each = left.shape[1] // (4 * planes)
    return pl.pallas_call(
        functools.partial(last_kernel, planes),
        out_shape=(
            jax.ShapeDtypeStruct((each, MIXIN), F32),
            jax.ShapeDtypeStruct((rows, D), F32),
            jax.ShapeDtypeStruct((SMALL_ROWS, 128), F32),
        ),
        in_specs=[VM] * 3 + [HB] + [VM] * 5,
        out_specs=(VM,) * 3,
        scratch_shapes=[
            pltpu.VMEM((rows, D), F32),
            pltpu.VMEM(w2.shape[:-1] + (INNER,), BF),
            DMA,
            pltpu.VMEM((1, D), F32),
        ]
        + total_scratch(planes)
        + scatter_scratch(planes, each, [MIXIN]),
        compiler_params=params(collective),
    )(left, dproj, w1, w2, tok, scale, packed, dres, small)


def doc_layout(lengths, token_positions):
    starts = jnp.cumsum(lengths) - lengths
    inside = token_positions[:, None] >= starts[None, :]
    document_index = jnp.sum(inside.astype(jnp.int32), axis=1) - 1
    begins = jnp.max(jnp.where(inside, starts[None, :], 0), axis=1)
    return (document_index, token_positions - begins)


def rope_tables(rel_pos):
    half_dim = HEAD_WIDTH // 2
    inv_freq = rope_base ** (-2.0 * jnp.arange(half_dim, dtype=jnp.float32) / HEAD_WIDTH)
    angles = rel_pos.astype(jnp.float32)[:, None] * inv_freq[None, :]
    return (jnp.cos(angles), jnp.sin(angles))


def norm_backward(grad_normed, values, factor, gain_vals):
    weighted = grad_normed * gain_vals
    grad_values = factor * (
        weighted - values * factor * factor * jnp.mean(weighted * values, axis=1, keepdims=True)
    )
    grad_gain = jnp.sum(grad_normed * values * factor, axis=0)
    return (grad_values, grad_gain)


def adamw_step(param_vals, grad_vals, first_vals, second_vals, weight_decay):
    first_new = beta_one * first_vals + (1.0 - beta_one) * grad_vals
    second_new = beta_two * second_vals + (1.0 - beta_two) * grad_vals * grad_vals
    update = (
        first_new
        / (1.0 - beta_one**STEP)
        / (jnp.sqrt(second_new / (1.0 - beta_two**STEP)) + adam_eps)
    )
    return (param_vals - learn_rate * (update + weight_decay * param_vals), first_new, second_new)


def adam_direction(grad_vals, first_vals, second_vals):
    first_new = beta_one * first_vals + (1.0 - beta_one) * grad_vals
    second_new = beta_two * second_vals + (1.0 - beta_two) * grad_vals * grad_vals
    update = (
        first_new
        / (1.0 - beta_one**STEP)
        / (jnp.sqrt(second_new / (1.0 - beta_two**STEP)) + adam_eps)
    )
    return (update, first_new, second_new)


def shards(
    planes,
    hidden,
    out_grad,
    decay_log,
    doc_lengths,
    weights,
    first_moment,
    second_moment,
    small_params,
    small_first,
    small_second,
):
    local_rows = hidden.shape[1]
    count = 4 * planes
    ctx_index = lax.axis_index("ctx")
    first_pos = ctx_index * local_rows
    contract_last = (((1,), (1,)), ((), ()))
    lengths = doc_lengths[0]
    token_positions = first_pos + jnp.arange(local_rows, dtype=jnp.int32)
    cosine_table, sine_table = rope_tables(doc_layout(lengths, token_positions)[1])
    cos_wide = jnp.tile(cosine_table, (1, 4))
    sin_wide = jnp.tile(jnp.concatenate([-sine_table, sine_table], axis=1), (1, 2))
    size = small_params.shape[0]
    packed = jnp.pad(small_params, (0, SMALL_ROWS * 128 - size)).reshape(SMALL_ROWS, 128)
    log_decay = decay_log[0]
    root_t = jnp.sqrt(-jnp.expm1(2.0 * log_decay)).T
    block = 512
    own_b = weights.astype(jnp.bfloat16)
    own_first = jnp.concatenate([own_b[:, :GATE_AT], own_b[:, XBC_AT:MIXIN]], axis=1)
    own_rest = jnp.concatenate([own_b[:, GATE_AT:XBC_AT], own_b[:, MIXIN:]], axis=1)
    (
        normed_one, scale_one, first_w, rest_w, query_rows, kv_all, xe, decays, pre, xo, mix_local,
        state_in, attended, log_sums,
    ) = front(
        planes, doc_lengths, hidden[0], own_first, own_rest, cos_wide, sin_wide, log_decay, root_t,
        packed, block, 0,
    )
    rest_flat = rest_w.reshape(D, rest_w.shape[-1])
    mixout_w = rest_flat[:, INNER : INNER + MIXOUT]
    mlp_w = rest_flat[:, INNER + MIXOUT :]
    gate_in = jnp.dot(normed_one, rest_flat[:, :INNER], preferred_element_type=jnp.float32)
    mixed, branch = gate_out(
        planes, doc_lengths, mix_local, xo, state_in, log_decay, gate_in, packed, attended
    )

    tok_f = hidden[0].astype(jnp.float32)
    gain_two = small_params[D : 2 * D]
    resid_one = tok_f + lax.dot_general(
        branch, mixout_w, contract_last, preferred_element_type=jnp.float32
    )
    scale_two = lax.rsqrt(jnp.mean(resid_one * resid_one, axis=1, keepdims=True) + norm_eps)
    normed_two = (resid_one * scale_two * gain_two).astype(jnp.bfloat16)
    gate_up = jnp.dot(normed_two, mlp_w[:, : 2 * FF], preferred_element_type=jnp.float32)
    gate_part = gate_up[:, :FF]
    up_part = gate_up[:, FF:]
    sigma_gate = jax.nn.sigmoid(gate_part)
    silu_gate = gate_part * sigma_gate
    hidden_mid = (silu_gate * up_part).astype(jnp.bfloat16)
    block_out = resid_one + lax.dot_general(
        hidden_mid, mlp_w[:, 2 * FF :], contract_last, preferred_element_type=jnp.float32
    )
    out_hidden = block_out.astype(jnp.bfloat16)[None]
    grad_out = out_grad[0]
    grad_mid = jnp.dot(grad_out, mlp_w[:, 2 * FF :], preferred_element_type=jnp.float32)
    silu_slope = sigma_gate * (1.0 + gate_part * (1.0 - sigma_gate))
    grad_gate_up = jnp.concatenate(
        [grad_mid * up_part * silu_slope, grad_mid * silu_gate], axis=1
    ).astype(jnp.bfloat16)
    grad_normed_two = lax.dot_general(
        grad_gate_up, mlp_w[:, : 2 * FF], contract_last, preferred_element_type=jnp.float32
    )
    grad_norm_two, grad_gain_two = norm_backward(grad_normed_two, resid_one, scale_two, gain_two)
    grad_resid_one = grad_out.astype(jnp.float32) + grad_norm_two
    grad_resid_b = grad_resid_one.astype(jnp.bfloat16)

    grad_branch = jnp.dot(grad_resid_b, mixout_w, preferred_element_type=jnp.float32)
    lefts = [by_core(v, planes) for v in (normed_two, grad_out, grad_resid_b)]
    rights = [grad_gate_up, hidden_mid, branch]
    args = (
        doc_lengths, grad_branch, mixed, gate_in, xo, state_in, query_rows,
        kv_all.reshape(count * local_rows, 2 * KEY_WIDTH), log_sums, cos_wide, sin_wide, decays,
        xe, log_decay, root_t, packed, pre,
    )
    if planes <= 4:
        early, grad_proj, gate_gain_grads, conv_grads, skip_grads = back(
            planes, lefts, rights, args, block, 3
        )
    else:
        early = scatter_rows(planes, lefts, rights, 4)
        grad_proj, gate_gain_grads, conv_grads, skip_grads = back(planes, [], [], (branch,) + args, block, 3)
    small_local = jnp.concatenate(
        [
            jnp.zeros((D,), jnp.float32),
            grad_gain_two,
            gate_gain_grads[0],
            conv_grads.reshape(-1),
            jnp.sum(skip_grads.reshape(MH, MP), axis=1),
        ]
    )
    padded = jnp.pad(small_local, (0, SMALL_ROWS * 128 - size)).reshape(SMALL_ROWS, 128)
    mixin_grads, grad_hidden, totals = last(
        planes, by_core(normed_one, planes), grad_proj, first_w, rest_w, hidden[0], scale_one,
        packed, grad_resid_one, padded, 5,
    )
    grad_hidden = grad_hidden[None]
    small_grads = totals.reshape(-1)[:size]
    grad_weights = jnp.concatenate(
        [mixin_grads, early[:, 3 * FF :], early[:, : 3 * FF]], axis=1
    )
    new_weights, new_first, new_second = adamw_step(
        weights, grad_weights, first_moment, second_moment, decay_rate
    )
    small_step, small_first_new, small_second_new = adam_direction(
        small_grads, small_first, small_second
    )
    return (
        out_hidden,
        grad_hidden,
        grad_weights,
        new_weights,
        new_first,
        new_second,
        small_grads,
        small_step,
        small_first_new,
        small_second_new,
    )


def solution(mesh):
    placed = (
        P("fsdp", "ctx", None),
        P("fsdp", "ctx", None),
        P("fsdp", None, "ctx"),
        P("fsdp", None),
        P(("ctx", "fsdp"), None),
        P(("ctx", "fsdp"), None),
        P(("ctx", "fsdp"), None),
        P(),
        P(),
        P(),
    )
    return jax.shard_map(
        functools.partial(shards, mesh.shape["ctx"] // 4),
        mesh=mesh,
        in_specs=placed,
        out_specs=(
            P("fsdp", "ctx", None),
            P("fsdp", "ctx", None),
            P(("ctx", "fsdp"), None),
            P(("ctx", "fsdp"), None),
            P(("ctx", "fsdp"), None),
            P(("ctx", "fsdp"), None),
            P(),
            P(),
            P(),
            P(),
        ),
        check_vma=False,
    )
```

```python
import functools
import math

import jax
import jax.numpy as jnp
from jax import lax
from jax.experimental import pallas as pl
from jax.experimental.pallas import tpu as pltpu
from jax.sharding import PartitionSpec as P

D = 1024
QUERY_HEADS = 8
KEY_VALUE_HEADS = 2
HEAD_WIDTH = 64
MH = 24
MP = 64
NS = 128
FF = 2048
CONV = 4
STEP = 3
QUERY_WIDTH = 512
KEY_WIDTH = 128
INNER = 1536
XBC = 1792
MIXIN = 4096
MIXOUT = 2048
SMALL_ROWS = 104
TOKENS = 256
PIECE = 256

norm_eps = 1e-05
rope_base = 100000000000.0
large_negative = -1e30
learn_rate = 0.02
beta_one = 0.9
beta_two = 0.95
adam_eps = 1e-08
decay_rate = 0.1

MESH = pl.DeviceIdType.MESH
BF = jnp.bfloat16
F32 = jnp.float32
VM = pl.BlockSpec(memory_space=pltpu.VMEM)
SM = pl.BlockSpec(memory_space=pltpu.SMEM)
HB = pl.BlockSpec(memory_space=pl.ANY)
DMA = pltpu.SemaphoreType.DMA


def params(collective=None):
    if collective is None:
        return pltpu.CompilerParams(vmem_limit_bytes=62 * 2**20)
    return pltpu.CompilerParams(
        collective_id=collective, has_side_effects=True, vmem_limit_bytes=62 * 2**20
    )


def nt(a, b):
    return lax.dot_general(a, b, (((1,), (1,)), ((), ())), preferred_element_type=F32)


def tn(a, b):
    return lax.dot_general(a, b, (((0,), (0,)), ((), ())), preferred_element_type=F32)


def nn(a, b):
    return lax.dot_general(a, b, (((1,), (0,)), ((), ())), preferred_element_type=F32)


class Place:
    def __init__(self, planes):
        ctx = lax.axis_index("ctx")
        self.ctx = ctx
        self.Z, self.z, self.x, self.c = planes, ctx // 4, (ctx // 2) % 2, ctx % 2
        self.y = lax.axis_index("fsdp")
        self.up, self.down = self.z + 1 < planes, self.z > 0

    def shard(self, z, x, y, c):
        return ((z * 2 + x) * 2 + c) * 2 + y

    def spot(self, z, x, c):
        return (z * 2 + x) * 2 + c

    def dev(self, z, x, y, c):
        return ((z * 2 + x) * 2 + c, y)

    def near(self, d):
        z, x, y, c = self.z, self.x, self.y, self.c
        return {
            "x": self.dev(z, 1 - x, y, c),
            "y": self.dev(z, x, 1 - y, c),
            "c": self.dev(z, x, y, 1 - c),
            "u": self.dev(z + 1, x, y, c),
            "d": self.dev(z - 1, x, y, c),
        }[d]

    def zord(self, k):
        if k == self.Z - 1:
            return self.z
        low = self.Z - 1 - k
        z = self.z
        return jnp.where(
            2 * z < self.Z, jnp.where(low > z, low, low - 1), jnp.where(k < z, k, k + 1)
        )


def greet(pc, dims="xyc", chain=True):
    bar = pltpu.get_barrier_semaphore()

    def sig(d):
        pl.semaphore_signal(bar, inc=1, device_id=pc.near(d), device_id_type=MESH)

    for d in dims:
        sig(d)
    if chain:
        pl.when(pc.up)(lambda: sig("u"))
        pl.when(pc.down)(lambda: sig("d"))
    peers = len(dims)
    if chain:
        peers = peers + pc.up.astype(jnp.int32) + pc.down.astype(jnp.int32)
    pl.semaphore_wait(bar, peers)


def greet_row(pc, across=False):
    bar = pltpu.get_barrier_semaphore()
    n = 4 * pc.Z

    @pl.loop(1, n)
    def _(d):
        pl.semaphore_signal(
            bar, inc=1, device_id=(lax.rem(pc.ctx + d, n), pc.y), device_id_type=MESH
        )

    if across:
        pl.semaphore_signal(bar, inc=1, device_id=pc.near("y"), device_id_type=MESH)
    pl.semaphore_wait(bar, n - 1 + int(across))


def rcopy(pc, src, dst, ssem, rsem, d):
    return pltpu.make_async_remote_copy(
        src_ref=src,
        dst_ref=dst,
        send_sem=ssem,
        recv_sem=rsem,
        device_id=pc.near(d) if isinstance(d, str) else d,
        device_id_type=MESH,
    )


def add_into(dst, parts, width=512):
    columns = dst.shape[-1]
    step = width if columns % width == 0 else (256 if columns % 256 == 0 else 128)

    @pl.loop(0, columns // step)
    def _(i):
        sl = pl.ds(pl.multiple_of(i * step, step), step)
        total = parts[0][:, sl].astype(F32)
        for r in parts[1:]:
            total = total + r[:, sl].astype(F32)
        dst[:, sl] = total.astype(dst.dtype)


def plane_peers(pc):
    return [pc.dev(lax.rem(pc.z + d, pc.Z), pc.x, pc.y, pc.c) for d in range(1, pc.Z)]


def greet_planes(pc):
    bar = pltpu.get_barrier_semaphore()
    peers = [pc.near(d) for d in "xyc"] + plane_peers(pc)
    for d in peers:
        pl.semaphore_signal(bar, inc=1, device_id=d, device_id_type=MESH)
    pl.semaphore_wait(bar, len(peers))


EVEN = (25, 25, 64)
REST = (35, 19, 64)


def split(columns, shares, unit):
    a, b = (columns * s // shares[2] // unit * unit for s in shares[:2])
    return a, b, columns - a - b


def part_columns(widths, p):
    a, b, w = widths
    return pl.ds((w, w + a, 0)[p], widths[p])


def gather_scratch(planes):
    return [
        DMA((2, planes, 2)),
        DMA((2, planes)),
        DMA((2, planes, 2)),
        DMA((2, planes, 4)),
        DMA((2, planes, 8)),
        DMA((2, planes)),
        DMA((2 + planes,)),
        DMA((4 + 2 * planes,)),
        DMA,
    ]


def gather_steps(pc, w_ref, out_ref, scratch, shares):
    zs, xs, ys, cs, rs, tz, tc, tr, loc = scratch
    Z, z, x, y, c = pc.Z, pc.z, pc.x, pc.y, pc.c
    widths = split(w_ref.shape[-1], shares, 128)

    def cols(p):
        return part_columns(widths, p)

    def spot(q):
        return (x if q < 2 else 1 - x), (y if q % 2 == 0 else 1 - y)

    def cp(p, zz, q, sem, d, own=False, core=None):
        xx, yy = spot(q)
        dst = out_ref.at[zz, xx, c, yy, :, cols(p)]
        return rcopy(pc, w_ref.at[:, cols(p)] if own else dst, dst, sem, rs.at[p, zz, core if core is not None else q], d)

    def along(p, zz, up, own=False):
        return cp(p, zz, 0, zs.at[p, zz, int(up)], "u" if up else "d", own, 0)

    def first(p, zz, own=False):
        return cp(p, zz, 0, xs.at[p, zz], "x" if p == 0 else "y", own, 2 if p == 0 else 1)

    def second(p, zz, q, own=False):
        if p == 0:
            return cp(p, zz, 2 * q, ys.at[p, zz, q], "y", own, 2 * q + 1)
        return cp(p, zz, q, ys.at[p, zz, q], "x", own, 2 + q)

    def core(p, zz, q, own=False):
        return cp(p, zz, q, cs.at[p, zz, q], "c", own, 4 + q)

    def arrived(p, zz, q):
        rcopy(
            pc, w_ref.at[:, cols(p)], out_ref.at[0, 0, 0, 0, :, cols(p)], loc, rs.at[p, zz, q], "c"
        ).wait_recv()

    def t_x():
        return rcopy(
            pc, w_ref.at[:, cols(2)], out_ref.at[z, x, c, y, :, cols(2)], tc.at[0], tr.at[0], "x"
        )

    def t_y():
        v = out_ref.at[z, :, c, y, :, cols(2)]
        return rcopy(pc, v, v, tc.at[1], tr.at[1], "y")

    def t_z(zz, up):
        v = out_ref.at[zz, :, c, :, :, cols(2)]
        return rcopy(pc, v, v, tz.at[int(up), zz], tr.at[4 + zz], "u" if up else "d")

    def t_c(zz):
        v = out_ref.at[zz, :, c, :, :, cols(2)]
        return rcopy(pc, v, v, tc.at[2 + zz], tr.at[4 + Z + zz], "c")

    keep = pltpu.make_async_copy(w_ref, out_ref.at[z, x, c, y], loc)
    keep.start()
    t_x().start()
    for p in (0, 1):
        pl.when(pc.up)(lambda: along(p, z, True, True).start())
        pl.when(pc.down)(lambda: along(p, z, False, True).start())
        first(p, z, True).start()
    for p in (0, 1):
        second(p, z, 0, True).start()
        core(p, z, 0, True).start()
    yield False
    keep.wait()
    t_x().wait_recv()
    t_y().start()
    for d in range(1, Z):
        for p in (0, 1):

            def onward(zz, up, more):
                arrived(p, zz, 0)
                pl.when(more)(lambda: along(p, zz, up).start())
                first(p, zz).start()
                second(p, zz, 0).start()
                core(p, zz, 0).start()

            pl.when(z - d >= 0)(lambda: onward(z - d, True, pc.up))
            pl.when(z + d < Z)(lambda: onward(z + d, False, pc.down))
        if d == 1:
            t_y().wait_recv()
            pl.when(pc.up)(lambda: t_z(z, True).start())
            pl.when(pc.down)(lambda: t_z(z, False).start())
            t_c(z).start()
        yield False

    def hop(d):
        def onward(zz, up, more):
            t_z(zz, up).wait_recv()
            pl.when(more)(lambda: t_z(zz, up).start())
            t_c(zz).start()

        pl.when(z - d >= 0)(lambda: onward(z - d, True, pc.up))
        pl.when(z + d < Z)(lambda: onward(z + d, False, pc.down))

    near = [lax.rem(z + k, Z) for k in range(Z)]
    for k, zz in enumerate(near):
        for p in (0, 1):
            q = 2 if p == 0 else 1
            arrived(p, zz, q)
            second(p, zz, 1).start()
            core(p, zz, q).start()
        if k > 0:
            hop(k)
        yield False
    for i in (0, 1):
        for k, zz in enumerate(near):
            for p in (0, 1):
                q = (1 if i == 0 else 3) if p == 0 else (2 if i == 0 else 3)
                arrived(p, zz, q)
                core(p, zz, q).start()
            yield i == 1 and k == Z - 1
    for zz in near:
        for p in (0, 1):
            for q in range(4):
                arrived(p, zz, 4 + q)
        t_c(zz).wait_recv()
        yield True
    t_x().wait_send()
    t_y().wait_send()
    for zz in range(Z):
        for p in (0, 1):
            pl.when(pc.up & (zz <= z))(lambda: along(p, zz, True).wait_send())
            pl.when(pc.down & (zz >= z))(lambda: along(p, zz, False).wait_send())
            first(p, zz).wait_send()
            for q in (0, 1):
                second(p, zz, q).wait_send()
            for q in range(4):
                core(p, zz, q).wait_send()
        pl.when(pc.up & (zz <= z))(lambda: t_z(zz, True).wait_send())
        pl.when(pc.down & (zz >= z))(lambda: t_z(zz, False).wait_send())
        t_c(zz).wait_send()


def spread_scratch(planes):
    n = 4 * planes
    return [DMA((planes,)), DMA((planes,)), DMA((planes, 2)), DMA((n,)), DMA((n,)), DMA((n,)), DMA((3,))]


def spread_steps(pc, kv_ref, edge_ref, dec_ref, all_ref, got_ref, decs_ref, scratch):
    us, xs, cs, rs, ds, dr, one = scratch
    Z, z, x, c = pc.Z, pc.z, pc.x, pc.c
    n = 4 * Z
    me = pc.ctx

    def cp(zz, xx, sem, d, own=False):
        s = pc.spot(zz, xx, c)
        return rcopy(pc, kv_ref if own else all_ref.at[s], all_ref.at[s], sem, rs.at[s], d)

    def arrived(s):
        rcopy(pc, kv_ref, all_ref.at[s], one.at[0], rs.at[s], "c").wait_recv()

    def decay_copy(d):
        return rcopy(pc, dec_ref, decs_ref.at[me], ds.at[d], dr.at[d], (lax.rem(me + d, n), pc.y))

    edge = rcopy(pc, edge_ref, got_ref, one.at[1], one.at[2], (lax.rem(me + 1, n), pc.y))
    keep = pltpu.make_async_copy(kv_ref, all_ref.at[me], one.at[0])
    pl.when(me < n - 1)(lambda: edge.start())
    keep.start()
    pl.when(pc.up)(lambda: cp(z, x, us.at[z], "u", True).start())
    cp(z, x, xs.at[z], "x", True).start()
    cp(z, x, cs.at[z, 0], "c", True).start()
    decs_ref[me] = dec_ref[...]
    pl.loop(1, n)(lambda d: decay_copy(d).start())
    yield
    pl.when(me > 0)(lambda: edge.wait_recv())

    @pl.when(me == 0)
    def _():
        got_ref[...] = jnp.zeros_like(got_ref)

    yield
    for d in range(1, Z):

        @pl.when(z - d >= 0)
        def _():
            zz = z - d
            arrived(pc.spot(zz, x, c))
            pl.when(pc.up)(lambda: cp(zz, x, us.at[zz], "u").start())
            cp(zz, x, xs.at[zz], "x").start()
            cp(zz, x, cs.at[zz, 0], "c").start()

        yield
    for d in range(Z):

        @pl.when(z - d >= 0)
        def _():
            arrived(pc.spot(z - d, 1 - x, c))
            cp(z - d, 1 - x, cs.at[z - d, 1], "c").start()

    yield
    for d in range(Z):

        @pl.when(z - d >= 0)
        def _():
            for xx in (x, 1 - x):
                arrived(pc.spot(z - d, xx, 1 - c))

    keep.wait()
    pl.loop(1, n)(lambda d: decay_copy(d).wait_recv())
    yield
    for zz in range(Z):

        @pl.when(zz <= z)
        def _():
            pl.when(pc.up)(lambda: cp(zz, x, us.at[zz], "u").wait_send())
            cp(zz, x, xs.at[zz], "x").wait_send()
            cp(zz, x, cs.at[zz, 0], "c").wait_send()
            cp(zz, 1 - x, cs.at[zz, 1], "c").wait_send()

    pl.when(me < n - 1)(lambda: edge.wait_send())
    pl.loop(1, n)(lambda d: decay_copy(d).wait_send())


LAST = (7, 7, 16)
EARLY = (21, 9, 32)


def scatter_scratch(planes, rows, widths, shares):
    columns = sum(widths)
    a, b, w = split(columns, shares, PIECE)
    half = 4 * planes * rows
    return [
        pltpu.VMEM((planes, 2, 2, rows, columns), BF),
        pltpu.VMEM((planes, 2, rows, a + b), BF),
        pltpu.VMEM((planes, rows, a + b), BF),
        pltpu.VMEM((planes, rows, a + b), BF),
        pltpu.VMEM((planes + 1, 2, 2, rows, w), BF),
        pltpu.VMEM((3, rows, w), BF),
        pltpu.VMEM((len(widths), half, TOKENS), BF),
        pltpu.VMEM((TOKENS, columns), BF),
        DMA((len(widths),)),
        DMA((len(widths),)),
        DMA((columns // PIECE,)),
        DMA((columns // PIECE,)),
        DMA((2, planes, 2)),
        DMA((2, planes, 2)),
        DMA((2, planes)),
        DMA((2, planes)),
        DMA((3, planes)),
        DMA((3, planes + 1)),
        DMA((3,)),
        DMA((3,)),
    ]


def scatter_steps(pc, pairs, out_ref, scratch, shares):
    g, r2, r3, rz, rw, rt, la, rb, as_, ar, bs, br, s2, q2, s3, q3, sz, qz, st, qt = scratch
    Z, z, x, y, c = pc.Z, pc.z, pc.x, pc.y, pc.c
    rows = g.shape[3]
    widths = split(g.shape[-1], shares, PIECE)
    w = widths[2]
    depth = 4 * rows

    def cols(p):
        return part_columns(widths, p)

    def got(p):
        return pl.ds(p * widths[0], widths[p])

    pieces = []
    base = 0
    for i, (left, right) in enumerate(pairs):
        for at in range(0, right.shape[1], PIECE):
            pieces.append((i, at, base + at))
        base += right.shape[1]

    def acopy(i):
        return rcopy(pc, pairs[i][0].at[1 - c], la.at[i], as_.at[i], ar.at[i], "c")

    def bcopy(k):
        i, at, to = pieces[k]
        return rcopy(
            pc, pairs[i][1].at[:, pl.ds(at, PIECE)], rb.at[:, pl.ds(to, PIECE)], bs.at[k], br.at[k], "c"
        )

    def make(zz, k, first):
        i, at, to = pieces[k]
        if first:
            if at == 0:
                acopy(i).wait_recv()
            bcopy(k).wait_recv()
        here = pl.ds(pl.multiple_of(zz * depth, depth), depth)
        mine, theirs = pairs[i][0][c, here, :], la[i, here, :]
        tile = nn(mine, pairs[i][1][:, pl.ds(at, PIECE)]) + nn(theirs, rb[:, pl.ds(to, PIECE)])
        g[zz, :, :, :, pl.ds(to, PIECE)] = tile.reshape(2, 2, rows, PIECE).astype(BF)

    def copy2(p, zz, j):
        xx, yy = (x if j == 0 else 1 - x, 1 - y) if p == 0 else (1 - x, y if j == 0 else 1 - y)
        return rcopy(
            pc, g.at[zz, xx, yy, :, cols(p)], r2.at[zz, j, :, got(p)], s2.at[p, zz, j], q2.at[p, zz, j],
            "y" if p == 0 else "x",
        )

    def copy3(p, zz):
        xx, yy = (1 - x, y) if p == 0 else (x, 1 - y)
        return rcopy(
            pc, g.at[zz, xx, yy, :, cols(p)], r3.at[zz, :, got(p)], s3.at[p, zz], q3.at[p, zz],
            "x" if p == 0 else "y",
        )

    def sendz(p, zz):
        return rcopy(
            pc, g.at[zz, x, y, :, cols(p)], rz.at[z, :, got(p)], sz.at[p, zz], qz.at[p, z], pc.dev(zz, x, y, c)
        )

    def gotz(p, zz):
        rcopy(pc, g.at[0, x, y, :, cols(p)], rz.at[zz, :, got(p)], sz.at[p, 0], qz.at[p, zz], "c").wait_recv()

    def send_plane(zz, up):
        slot = jnp.where(zz == z + 1, Z, zz) if up else zz
        return rcopy(
            pc, g.at[zz, :, :, :, cols(2)], rw.at[slot], sz.at[2, zz], qz.at[2, slot], "u" if up else "d"
        )

    def got_plane(slot):
        rcopy(
            pc, g.at[0, :, :, :, cols(2)], rw.at[slot], sz.at[2, 0], qz.at[2, slot], "c"
        ).wait_recv()

    def add_plane(zz, slots):
        for xx in (0, 1):
            for yy in (0, 1):
                a = g.at[zz, xx, yy, :, cols(2)]
                add_into(a, [a] + [rw.at[k, xx, yy] for k in slots])

    def at_time(t, f):
        below, above = t - (Z - 1 - z), Z - 1 - (t - z)
        pl.when((below >= 0) & (below < z))(lambda: f(below, False, pc.up))
        pl.when((above > z) & (above < Z))(lambda: f(above, True, pc.down))

    def chain_first(zz, up, more):
        @pl.when(more)
        def _():
            got_plane(zz)
            add_plane(zz, [zz])

        send_plane(zz, up).start()

    def tail(k):
        if k < 2:
            return rcopy(pc, g.at[z, k, 1 - y, :, cols(2)], rt.at[k], st.at[k], qt.at[k], "y")
        return rcopy(pc, g.at[z, 1 - x, y, :, cols(2)], rt.at[2], st.at[2], qt.at[2], "x")

    for i in range(len(pairs)):
        acopy(i).start()
        for k in range(len(pieces)):
            if pieces[k][0] == i:
                bcopy(k).start()
    yield
    ends = {w + widths[0]: 0, w + widths[0] + widths[1]: 1}

    def own(p, zz):
        copy2(p, zz, 0).wait_recv()
        copy3(p, zz).wait_recv()
        a = g.at[zz, x, y, :, cols(p)]
        return a, [a, r2.at[zz, 0, :, got(p)], r3.at[zz, :, got(p)]]

    def gather_plane(slot):
        got_plane(slot)
        add_plane(z, [slot])

    for k in range(Z + 2):
        if k < Z:
            zz = pc.zord(k)
            for n in range(len(pieces)):
                make(zz, n, k == 0)
                end = pieces[n][2] + PIECE
                if end == w and k == 0 and Z > 1:
                    at_time(0, chain_first)
                if end in ends:
                    copy2(ends[end], zz, 1).start()
                if n == len(pieces) // 2:
                    yield
            yield
        if 0 < k <= Z:
            zz = pc.zord(k - 1)
            for p in (0, 1):
                copy2(p, zz, 1).wait_recv()
                a = g.at[(zz,) + ((1 - x, y) if p == 0 else (x, 1 - y)) + (slice(None), cols(p))]
                add_into(a, [a, r2.at[zz, 1, :, got(p)]])
                copy3(p, zz).start()
            for p in (0, 1):
                copy2(p, zz, 0).start()
            if 0 < k - 1 < Z - 1:
                at_time(k - 1, chain_first)
            yield
        if 1 < k <= Z:
            zz = pc.zord(k - 2)
            for p in (0, 1):
                a, parts = own(p, zz)
                add_into(a, parts)
                sendz(p, zz).start()
            yield
    pl.when(pc.up)(lambda: gather_plane(z))
    pl.when(pc.down)(lambda: gather_plane(Z))
    for k in (0, 1):
        tail(k).start()
    yield
    finals = []
    for p in (0, 1):
        finals.append(own(p, z)[1])
    for k in (0, 1):
        tail(k).wait_recv()
        a = g.at[z, k, y, :, cols(2)]
        add_into(a, [a, rt.at[k]])
    tail(2).start()
    yield
    for p in (0, 1):
        for d in range(1, Z):
            slot = lax.rem(z + d, Z)
            gotz(p, slot)
            finals[p].append(rz.at[slot, :, got(p)])
        add_into(out_ref.at[:, cols(p)], finals[p])
        yield
    tail(2).wait_recv()
    add_into(out_ref.at[:, cols(2)], [g.at[z, x, y, :, cols(2)], rt.at[2]])
    for i in range(len(pairs)):
        acopy(i).wait_send()
    for k in range(len(pieces)):
        bcopy(k).wait_send()
    for k in range(3):
        tail(k).wait_send()
    for zz in range(Z):
        for p in (0, 1):
            for j in (0, 1):
                copy2(p, zz, j).wait_send()
            copy3(p, zz).wait_send()
            pl.when(zz != z)(lambda: sendz(p, zz).wait_send())
        pl.when(zz < z)(lambda: send_plane(zz, False).wait_send())
        pl.when(zz > z)(lambda: send_plane(zz, True).wait_send())


def scatter_kernel(planes, count, *refs):
    pc = Place(planes)
    greet_planes(pc)
    pairs = tuple(zip(refs[:count], refs[count : 2 * count]))
    for _ in scatter_steps(pc, pairs, refs[2 * count], refs[2 * count + 1 :], EARLY):
        pass


def scatter_rows(planes, lefts, rights, collective):
    rows = lefts[0].shape[1] // (4 * planes)
    widths = [r.shape[1] for r in rights]
    return pl.pallas_call(
        functools.partial(scatter_kernel, planes, len(lefts)),
        out_shape=jax.ShapeDtypeStruct((rows, sum(widths)), F32),
        in_specs=[VM] * (2 * len(lefts)),
        out_specs=VM,
        scratch_shapes=scatter_scratch(planes, rows, widths, EARLY),
        compiler_params=params(collective),
    )(*lefts, *rights)


def by_core(rows, planes):
    tokens = rows.shape[0]
    each = D // (8 * planes)
    cut = rows.T.reshape(2 * planes, 2, 2 * each, tokens)
    return cut.transpose(1, 0, 2, 3).reshape(2, D // 2, tokens)


def fold_scratch(planes, rows, columns):
    return [
        pltpu.VMEM((planes, 2, rows, columns), BF),
        pltpu.VMEM((planes, rows, columns), BF),
        pltpu.VMEM((planes, rows, columns), BF),
        pltpu.VMEM((planes, 2, rows, columns), BF),
        DMA((planes, 2)),
        DMA((planes, 2)),
        DMA((planes,)),
        DMA((planes,)),
        DMA((planes,)),
        DMA((planes,)),
    ]


def fold_steps(pc, block, out_ref, scratch):
    rc, rx, rz, acc, cs, cr, xs, xr, zs, zr = scratch
    Z, z, x, c = pc.Z, pc.z, pc.x, pc.c

    def ccopy(zz, q):
        xx = x if q == 0 else 1 - x
        return rcopy(pc, block(pc.spot(zz, xx, 1 - c)), rc.at[zz, q], cs.at[zz, q], cr.at[zz, q], "c")

    def xcopy(zz):
        return rcopy(pc, acc.at[zz, 1], rx.at[zz], xs.at[zz], xr.at[zz], "x")

    def zcopy(zz):
        return rcopy(pc, acc.at[zz, 0], rz.at[zz], zs.at[zz], zr.at[zz], "d")

    def each(f):
        for zz in range(Z):
            pl.when(zz <= z)(functools.partial(f, zz))

    def a(zz):
        ccopy(zz, 1).start()
        ccopy(zz, 0).start()

    def b(zz):
        ccopy(zz, 1).wait_recv()
        add_into(acc.at[zz, 1], [block(pc.spot(zz, 1 - x, c)), rc.at[zz, 1]], 128)
        xcopy(zz).start()

    def m(zz):
        ccopy(zz, 0).wait_recv()
        add_into(acc.at[zz, 0], [block(pc.spot(zz, x, c)), rc.at[zz, 0]], 128)

    def e(zz):
        xcopy(zz).wait_recv()

        def finish(parts):
            @pl.when(zz < z)
            def _():
                add_into(acc.at[zz, 0], parts, 128)
                zcopy(zz).start()

            pl.when(zz == z)(lambda: add_into(out_ref, parts, 128))

        @pl.when(pc.up)
        def _():
            zcopy(zz).wait_recv()
            finish([acc.at[zz, 0], rx.at[zz], rz.at[zz]])

        pl.when(jnp.logical_not(pc.up))(lambda: finish([acc.at[zz, 0], rx.at[zz]]))

    def w(zz):
        ccopy(zz, 1).wait_send()
        ccopy(zz, 0).wait_send()
        xcopy(zz).wait_send()
        pl.when(zz < z)(lambda: zcopy(zz).wait_send())

    for f in (a, b, m, e):
        each(f)
        yield
    each(w)


def relay_scratch(planes):
    n = 4 * planes
    piece = pltpu.VMEM((n, NS // n, INNER), BF)
    return [piece, piece, DMA((n,)), DMA((n,)), DMA((n,)), DMA((n,))]


def relay_steps(pc, reverse, s_ref, dec_ref, out_ref, scratch):
    got, part, ss, sr, bs, br = scratch
    n = 4 * pc.Z
    me = pc.ctx

    def to(d):
        return lax.rem(me + d, n)

    def there(d):
        return rcopy(pc, s_ref.at[to(d)], got.at[me], ss.at[d], sr.at[d], (to(d), pc.y))

    def back(d):
        return rcopy(pc, part.at[to(d)], out_ref.at[me], bs.at[d], br.at[d], (to(d), pc.y))

    pl.loop(1, n)(lambda d: there(d).start())
    got[me] = s_ref[me]
    yield
    pl.loop(1, n)(lambda d: there(d).wait_recv())
    total = jnp.zeros(got.shape[1:], F32)
    for k in range(n):
        j = n - 1 - k if reverse else k
        part[j] = total.astype(BF)
        total = total * dec_ref[pl.ds(j, 1), :] + got[j].astype(F32)
    pl.loop(1, n)(lambda d: back(d).start())
    out_ref[me] = part[me]
    yield
    pl.loop(1, n)(lambda d: back(d).wait_recv())
    yield

    @pl.loop(1, n)
    def _(d):
        there(d).wait_send()
        back(d).wait_send()


def total_scratch(planes):
    shape = (SMALL_ROWS, 128)
    return [
        pltpu.VMEM((6,) + shape, F32),
        pltpu.VMEM((planes,) + shape, F32),
        DMA((3,)),
        DMA((3,)),
        DMA((planes,)),
        DMA((planes,)),
    ]


def total_steps(pc, out_ref, scratch):
    rx, rz, ss, sr, zs, zr = scratch
    Z, z = pc.Z, pc.z
    for i, d in enumerate("cxy"):
        rx[2 * i] = out_ref[...]
        cp = rcopy(pc, rx.at[2 * i], rx.at[2 * i + 1], ss.at[i], sr.at[i], d)
        cp.start()
        yield
        cp.wait()
        out_ref[...] = out_ref[...] + rx[2 * i + 1]
    rz[z] = out_ref[...]
    copies = [rcopy(pc, rz.at[z], rz.at[z], zs.at[d], zr.at[d], to) for d, to in enumerate(plane_peers(pc))]
    for cp in copies:
        cp.start()
    yield
    for cp in copies:
        cp.wait()
    total = rz[0]
    for k in range(1, Z):
        total = total + rz[k]
    out_ref[...] = total


def visible(start, block, pos_ref):
    kpos = start + lax.broadcasted_iota(jnp.int32, (block, pos_ref.shape[1]), 0)
    return (kpos <= pos_ref[0:1, :]) & (kpos >= pos_ref[1:2, :])


def split_heads(src, dst, scale=None):
    rows = src.shape[0]
    for h in range(QUERY_HEADS):
        v = src[:, pl.ds(h * HEAD_WIDTH, HEAD_WIDTH)]
        dst[pl.ds(h * rows, rows), :] = v if scale is None else v * scale


def swap_halves(v):
    width = v.shape[1]
    lane = lax.broadcasted_iota(jnp.int32, v.shape, 1)
    low = lax.rem(lane, HEAD_WIDTH) < HEAD_WIDTH // 2
    ahead = pltpu.roll(v, width - HEAD_WIDTH // 2, 1)
    behind = pltpu.roll(v, HEAD_WIDTH // 2, 1)
    return jnp.where(low, ahead, behind)


def rotate(v, cos_ref, sin_ref, sign=1.0):
    return v * cos_ref[...] + swap_halves(v) * (sign * sin_ref[...])


def attend_block(j, block, q_ref, kv, pos_ref, m_ref, l_ref, acc_ref, heads):
    rows = pos_ref.shape[1]
    start = pl.multiple_of(j * block, block)
    ok = visible(start, block, pos_ref)
    for h in heads:
        g = h // (QUERY_HEADS // KEY_VALUE_HEADS)
        keys = kv[:, g * HEAD_WIDTH : (g + 1) * HEAD_WIDTH]
        vals = kv[:, KEY_WIDTH + g * HEAD_WIDTH : KEY_WIDTH + (g + 1) * HEAD_WIDTH]
        s = jnp.where(ok, nt(keys, q_ref[pl.ds(h * rows, rows), :]), large_negative)
        m0 = m_ref[h : h + 1, :]
        m1 = jnp.maximum(m0, jnp.max(s, axis=0, keepdims=True))
        p = jnp.where(ok, jnp.exp(s - m1), 0.0)
        a = jnp.exp(m0 - m1)
        l_ref[h : h + 1, :] = l_ref[h : h + 1, :] * a + jnp.sum(p, axis=0, keepdims=True)
        m_ref[h : h + 1, :] = m1
        r = pl.ds(h * HEAD_WIDTH, HEAD_WIDTH)
        acc_ref[r, :] = acc_ref[r, :] * a + tn(vals, p.astype(BF))


def attend_end(o_ref, lse_ref, m_ref, l_ref, acc_ref):
    lse_ref[...] = m_ref[...] + jnp.log(l_ref[...])
    inv = 1.0 / l_ref[...]
    for h in range(QUERY_HEADS):
        r = pl.ds(h * HEAD_WIDTH, HEAD_WIDTH)
        acc_ref[r, :] = acc_ref[r, :] * inv[h : h + 1, :]
    o_ref[...] = acc_ref[...].T.astype(o_ref.dtype)


def attend_back_block(j, g, block, q_ref, do_ref, kv_ref, pos_ref, lse_ref, dl_ref, dkv_ref, acc_ref):
    rows = pos_ref.shape[1]
    start = pl.multiple_of(j * block, block)
    ok = visible(start, block, pos_ref)
    at = pl.ds(start, block)
    keys = kv_ref[at, pl.ds(g * HEAD_WIDTH, HEAD_WIDTH)]
    vals = kv_ref[at, pl.ds(KEY_WIDTH + g * HEAD_WIDTH, HEAD_WIDTH)]
    dk = dv = None
    for h in range(4 * g, 4 * g + 4):
        q = q_ref[pl.ds(h * rows, rows), :]
        do = do_ref[pl.ds(h * rows, rows), :]
        p = jnp.where(ok, jnp.exp(nt(keys, q) - lse_ref[h : h + 1, :]), 0.0)
        ds = (p * (nt(vals, do) - dl_ref[h : h + 1, :])).astype(BF)
        r = pl.ds(h * HEAD_WIDTH, HEAD_WIDTH)
        acc_ref[r, :] += tn(keys, ds)
        a, b = nn(ds, q), nn(p.astype(BF), do)
        dk = a if dk is None else dk + a
        dv = b if dv is None else dv + b
    dkv_ref[at, pl.ds(g * HEAD_WIDTH, HEAD_WIDTH)] = dk.astype(BF)
    dkv_ref[at, pl.ds(KEY_WIDTH + g * HEAD_WIDTH, HEAD_WIDTH)] = dv.astype(BF)


def two(left, right, lanes):
    return jnp.where(lanes < MP, left, right)


def pair_columns(ref, p, lanes):
    return two(ref[:, 2 * p : 2 * p + 1], ref[:, 2 * p + 1 : 2 * p + 2], lanes)


def mixer_steps(
    xe, mk, cw, cb, cum_t, cum, dt_t, we_t, skip, doc_c, doc_r, pre, xo, mix, so, xw, bias
):
    rows = pre.shape[0]
    for i in range(XBC // 256):
        sl = pl.ds(i * 256, 256)
        acc = jnp.broadcast_to(cb[:, sl], (rows, 256))
        for j in range(CONV):
            acc = acc + cw[j : j + 1, sl] * (xe[pl.ds(5 + j, rows), sl] * mk[:, j : j + 1])
        pre[:, sl] = acc.astype(BF)
        act = acc * jax.nn.sigmoid(acc)
        xo[:, sl] = act.astype(BF)
        if i < INNER // 256:
            mix[:, sl] = skip[:, sl] * act
        if i == 3:
            yield
    yield
    b_rows, c_rows = xo[:, pl.ds(INNER, NS)], xo[:, pl.ds(INNER + NS, NS)]
    cross = nt(c_rows, b_rows)
    t_at = lax.broadcasted_iota(jnp.int32, (rows, rows), 0)
    s_at = lax.broadcasted_iota(jnp.int32, (rows, rows), 1)
    bias[...] = jnp.where((doc_c[...] == doc_r[...]) & (s_at <= t_at), 0.0, large_negative)
    lanes = lax.broadcasted_iota(jnp.int32, (rows, 2 * MP), 1)
    for p in range(MH // 2):
        sl = pl.ds(p * 2 * MP, 2 * MP)
        xd = xo[:, sl].astype(F32) * pair_columns(dt_t, p, lanes)
        xw[:, sl] = (xd * pair_columns(we_t, p, lanes)).astype(BF)
        xb = xd.astype(BF)
        outs = []
        for h in (2 * p, 2 * p + 1):
            low = jnp.exp(jnp.minimum(cum_t[:, h : h + 1] - cum[h : h + 1, :], bias[...]))
            outs.append(nn((low * cross).astype(BF), xb))
        mix[:, sl] = mix[:, sl] + two(outs[0], outs[1], lanes)
        if p % 3 == 2:
            yield
    so[...] = tn(b_rows, xw[...]).astype(BF).reshape(so.shape)


def spread_heads():
    head = lax.broadcasted_iota(jnp.int32, (MH, INNER), 0)
    lane = lax.broadcasted_iota(jnp.int32, (MH, INNER), 1)
    return (lane // MP == head).astype(F32)


def exact(a, b, dims):
    return lax.dot_general(
        a, b, (dims, ((), ())), precision=lax.Precision.HIGHEST, preferred_element_type=F32
    )


def wide(columns, spread_mat):
    return exact(columns, spread_mat, ((1,), (0,)))


def gate_kernel(planes, lens, mix, xo, state_in, ldec, gate, small, att, mixed, branch, gain, state, din_t):
    rows = mix.shape[0]
    spread_mat = spread_heads()
    unpack(small, "gate", gain)
    state[...] = state_in[...].reshape(state.shape)
    first = Place(planes).ctx * rows
    a = lax.broadcasted_iota(jnp.int32, (rows, rows), 0)
    b = lax.broadcasted_iota(jnp.int32, (rows, rows), 1)
    docs = doc_of(first + lax.broadcasted_iota(jnp.int32, (rows, 1), 0), lens)
    before = doc_of(jnp.full((1, 1), first - 1, jnp.int32), lens)
    ct = exact((b <= a).astype(F32), ldec[...], ((1,), (1,)))
    din_t[...] = jnp.where(docs == before, jnp.exp(ct), 0.0)

    @pl.loop(0, rows // 64)
    def _(i):
        r = pl.ds(pl.multiple_of(i * 64, 64), 64)
        carried = nn(xo[r, pl.ds(INNER + NS, NS)], state[...])
        m = mix[r, :] + carried * wide(din_t[r, :], spread_mat)
        mixed[r, :] = m.astype(BF)
        gv = gate[r, :]
        gated = m * (gv * jax.nn.sigmoid(gv))
        factor = lax.rsqrt(jnp.mean(gated * gated, axis=1, keepdims=True) + norm_eps)
        branch[r, pl.ds(0, QUERY_WIDTH)] = att[r, :]
        branch[r, pl.ds(QUERY_WIDTH, INNER)] = (gated * factor * gain[...]).astype(BF)


def gate_out(planes, lens, mix, xo, state, ldec, gate, small, att):
    rows = mix.shape[0]
    return pl.pallas_call(
        functools.partial(gate_kernel, planes),
        out_shape=(
            jax.ShapeDtypeStruct((rows, INNER), BF),
            jax.ShapeDtypeStruct((rows, MIXOUT), BF),
        ),
        in_specs=[SM] + [VM] * 7,
        out_specs=(VM,) * 2,
        scratch_shapes=[
            pltpu.VMEM((1, INNER), F32),
            pltpu.VMEM((NS, INNER), BF),
            pltpu.VMEM((rows, MH), F32),
        ],
        compiler_params=params(),
    )(lens, mix, xo, state, ldec, gate, small, att)


def doc_of(pos, lens):
    start = 0
    found = jnp.full_like(pos, -1)
    for d in range(lens.shape[1]):
        found = found + (pos >= start).astype(jnp.int32)
        start = start + lens[0, d]
    return found


def begin_of(pos, lens):
    start = 0
    found = jnp.zeros_like(pos)
    for d in range(lens.shape[1]):
        found = jnp.maximum(found, jnp.where(pos >= start, start, 0))
        start = start + lens[0, d]
    return found


def table_scratch(rows):
    return [
        pltpu.VMEM((2, rows), jnp.int32),
        pltpu.VMEM((rows, 8), F32),
        pltpu.VMEM((rows, 1), jnp.int32),
        pltpu.VMEM((1, rows), jnp.int32),
        pltpu.VMEM((MH, rows), F32),
        pltpu.VMEM((rows, MH), F32),
        pltpu.VMEM((rows, MH), F32),
        pltpu.VMEM((rows, MH), F32),
        pltpu.VMEM((rows, MH), F32),
    ]


def make_tables(pc, lens, ldec, root_t, tables):
    pos, same, doc_c, doc_r, cum, cum_t, dt_t, we_t, din_t = tables
    rows = ldec.shape[1]
    first = pc.ctx * rows
    at_c = first + lax.broadcasted_iota(jnp.int32, (rows, 1), 0)
    at_r = first + lax.broadcasted_iota(jnp.int32, (1, rows), 1)
    pos[0:1, :] = at_r
    pos[1:2, :] = begin_of(at_r, lens)
    dc = doc_of(at_c, lens)
    doc_c[...] = dc
    doc_r[...] = doc_of(at_r, lens)
    for j in range(CONV):
        same[:, j : j + 1] = (doc_of(at_c - (CONV - 1) + j, lens) == dc).astype(F32)
        same[:, CONV + j : CONV + j + 1] = (doc_of(at_c + (CONV - 1) - j, lens) == dc).astype(F32)
    a = lax.broadcasted_iota(jnp.int32, (rows, rows), 0)
    b = lax.broadcasted_iota(jnp.int32, (rows, rows), 1)
    cum[...] = exact(ldec[...], (a <= b).astype(F32), ((1,), (0,)))
    ct = exact((b <= a).astype(F32), ldec[...], ((1,), (1,)))
    cum_t[...] = ct
    fresh = doc_of(at_c - 1, lens) != dc
    dt_t[...] = jnp.where(fresh, 1.0, root_t[...])
    before = doc_of(jnp.full((1, 1), first - 1, jnp.int32), lens)
    end = doc_of(jnp.full((1, 1), first + rows - 1, jnp.int32), lens)
    din_t[...] = jnp.where(dc == before, jnp.exp(ct), 0.0)
    we_t[...] = jnp.where(dc == end, jnp.exp(jnp.minimum(ct[rows - 1 : rows, :] - ct, 0.0)), 0.0)


SMALL_AT = {"one": (0, 8), "two": (8, 8), "gate": (16, 12), "bias": (84, 14), "skip": (98, 1)}


def unpack(small, name, dst, row=0):
    at, tiles = SMALL_AT[name] if isinstance(name, str) else name
    for i in range(tiles):
        dst[row : row + 1, pl.ds(i * 128, 128)] = small[at + i : at + i + 1, :]


def unpack_conv(small, dst):
    for j in range(CONV):
        unpack(small, (28 + 14 * j, 14), dst, j)


def wide_skip(small, spread_mat, dst):
    dst[...] = wide(jnp.broadcast_to(small[98:99, 0:MH], (8, MH)), spread_mat)[0:1, :]


GATE_AT = QUERY_WIDTH + 2 * KEY_WIDTH
XBC_AT = GATE_AT + INNER
FIRST = QUERY_WIDTH + 2 * KEY_WIDTH + XBC


def front_kernel(
    planes, block, lens, hid, w1, w2, cos_w, sin_w, ldec, root_t, small,
    normed, scale, g1, g2, q_out, kv_all, xe, decays, pre, xo, mix, state_in, att, lse,
    kv_own, edge_out, edge_in, dec_own, decs, dec_rows, gains, conv_w, conv_b, skip, so, qh, m_ref, l_ref,
    acc, xw, bias, *refs,
):
    tables, refs = refs[:9], refs[9:]
    pos, same, doc_c, doc_r, cum, cum_t, dt_t, we_t, din_t = tables
    first_refs, refs = refs[:9], refs[9:]
    rest_refs, refs = refs[:9], refs[9:]
    spread_refs, refs = refs[:7], refs[7:]
    relay_refs = refs[:6]
    pc = Place(planes)
    n = 4 * planes
    rows = hid.shape[0]
    greet_row(pc, True)
    gather = gather_steps(pc, w1, g1, first_refs, EVEN)
    rest = gather_steps(pc, w2, g2, rest_refs, REST)
    next(gather)

    def pump(count=1):
        for _ in range(count):
            next(rest, None)

    unpack(small, "one", gains)
    unpack(small, "bias", conv_b)
    unpack_conv(small, conv_w)
    spread_mat = spread_heads()
    wide_skip(small, spread_mat, skip)
    for i in range(rows // 64):
        r = pl.ds(i * 64, 64)
        v = hid[r, :].astype(F32)
        f = lax.rsqrt(jnp.mean(v * v, axis=1, keepdims=True) + norm_eps)
        scale[r, :] = f
        normed[r, :] = (v * f * gains[...]).astype(BF)
        next(gather)
    make_tables(pc, lens, ldec, root_t, tables)
    dec_own[...] = jnp.zeros_like(dec_own)
    dec_own[0:1, 0:MH] = din_t[rows - 1 : rows, :]
    for k, _ in enumerate(gather):
        if k == planes:
            pump()

    def project(at, width):
        return nn(normed[...], g1[:, :, :, :, :, pl.ds(at, width)].reshape(D, width))

    base = GATE_AT
    for i in range(XBC // 256):
        sl = pl.ds(i * 256, 256)
        xb = project(base + i * 256, 256).astype(BF)
        xe[pl.ds(8, rows), sl] = xb.astype(F32)
        edge_out[:, sl] = xb[rows - 16 :, :]
    kv = project(QUERY_WIDTH, 2 * KEY_WIDTH)
    kv_own[:, pl.ds(0, KEY_WIDTH)] = rotate(kv[:, :KEY_WIDTH], cos_w, sin_w).astype(BF)
    kv_own[:, pl.ds(KEY_WIDTH, KEY_WIDTH)] = kv[:, KEY_WIDTH:].astype(BF)
    spreads = spread_steps(pc, kv_own, edge_out, dec_own, kv_all, edge_in, decs, spread_refs)
    next(spreads)
    for i in range(QUERY_WIDTH // 256):
        qv = project(i * 256, 256)
        for t in (0, 1):
            q_out[:, pl.ds(i * 256 + t * 128, 128)] = rotate(
                qv[:, t * 128 : (t + 1) * 128], cos_w, sin_w
            ).astype(BF)
    split_heads(q_out, qh, jnp.asarray(HEAD_WIDTH**-0.5, BF))
    next(spreads)
    xe[pl.ds(0, 8), :] = edge_in[pl.ds(8, 8), :].astype(F32)
    pump()
    next(spreads)
    mixing = mixer_steps(
        xe, same, conv_w, conv_b, cum_t, cum, dt_t, we_t, skip, doc_c, doc_r, pre, xo, mix, so, xw, bias
    )
    for _ in mixing:
        next(spreads, None)
        pump()
    for k in range(n):
        dec_rows[k : k + 1, :] = decs[k, 0:1, :]
    decays[...] = wide(dec_rows[:, 0:MH], spread_mat)
    states = relay_steps(pc, False, so, decays, state_in, relay_refs)
    next(states)
    m_ref[...] = jnp.full_like(m_ref, large_negative)
    l_ref[...] = jnp.zeros_like(l_ref)
    acc[...] = jnp.zeros_like(acc)
    seen = (pc.ctx * rows + rows + block - 1) // block
    per = block // rows
    parts = 8
    each = n // per // parts

    def keys_at(j):
        return kv_all[pl.ds(j * per, per), :, :].reshape(block, 2 * KEY_WIDTH)

    for k in range(parts):
        lo = each * k

        @pl.loop(jnp.minimum(lo, seen), jnp.minimum(lo + each, seen))
        def _(j):
            attend_block(j, block, qh, keys_at(j), pos, m_ref, l_ref, acc, range(QUERY_HEADS))

        pump(2)
        if k in (3, 6):
            next(states)
    attend_end(att, lse, m_ref, l_ref, acc)
    for _ in spreads:
        pass
    for _ in rest:
        pass
    for _ in states:
        pass


def front(planes, lens, hid, w1, w2, cos_w, sin_w, ldec, root_t, small, block, collective):
    n = 4 * planes
    rows = hid.shape[0]
    each = w1.shape[0]
    sds = jax.ShapeDtypeStruct
    return pl.pallas_call(
        functools.partial(front_kernel, planes, block),
        out_shape=(
            sds((rows, D), BF),
            sds((rows, 1), F32),
            sds((planes, 2, 2, 2, each, w1.shape[1]), BF),
            sds((planes, 2, 2, 2, each, w2.shape[1]), BF),
            sds((rows, QUERY_WIDTH), BF),
            sds((n, rows, 2 * KEY_WIDTH), BF),
            sds((rows + 8, XBC), F32),
            sds((n, INNER), F32),
            sds((rows, XBC), BF),
            sds((rows, XBC), BF),
            sds((rows, INNER), F32),
            sds((n, NS // n, INNER), BF),
            sds((rows, QUERY_WIDTH), BF),
            sds((QUERY_HEADS, rows), F32),
        ),
        in_specs=[SM, VM, VM, HB] + [VM] * 5,
        out_specs=(VM, VM, VM, HB) + (VM,) * 10,
        scratch_shapes=[
            pltpu.VMEM((rows, 2 * KEY_WIDTH), BF),
            pltpu.VMEM((16, XBC), BF),
            pltpu.VMEM((16, XBC), BF),
            pltpu.VMEM((8, 128), F32),
            pltpu.VMEM((n, 8, 128), F32),
            pltpu.VMEM((n, 128), F32),
            pltpu.VMEM((1, D), F32),
            pltpu.VMEM((CONV, XBC), F32),
            pltpu.VMEM((1, XBC), F32),
            pltpu.VMEM((1, INNER), F32),
            pltpu.VMEM((n, NS // n, INNER), BF),
            pltpu.VMEM((QUERY_HEADS * rows, HEAD_WIDTH), BF),
            pltpu.VMEM((QUERY_HEADS, rows), F32),
            pltpu.VMEM((QUERY_HEADS, rows), F32),
            pltpu.VMEM((QUERY_WIDTH, rows), F32),
            pltpu.VMEM((rows, INNER), BF),
            pltpu.VMEM((rows, rows), F32),
        ]
        + table_scratch(rows)
        + gather_scratch(planes)
        + gather_scratch(planes)
        + spread_scratch(planes)
        + relay_scratch(planes),
        compiler_params=params(collective),
    )(lens, hid, w1, w2, cos_w, sin_w, ldec, root_t, small)


def gate_back_rows(i, grad, mixed, gate, gain, din_t, spread_mat, dm, dproj, dgain, dinc):
    r = pl.ds(pl.multiple_of(i * 64, 64), 64)
    m, gv, gr = mixed[r, :].astype(F32), gate[r, :], grad[r, pl.ds(QUERY_WIDTH, INNER)]
    sig = jax.nn.sigmoid(gv)
    sil = gv * sig
    gated = m * sil
    factor = lax.rsqrt(jnp.mean(gated * gated, axis=1, keepdims=True) + norm_eps)
    w = gr * gain[...]
    dg = factor * (w - gated * factor * factor * jnp.mean(w * gated, axis=1, keepdims=True))
    dgain[...] += jnp.sum(gr * gated * factor, axis=0, keepdims=True)
    dproj[r, pl.ds(GATE_AT, INNER)] = (dg * m * (sig * (1.0 + gv * (1.0 - sig)))).astype(BF)
    d = dg * sil
    dm[r, :] = d.astype(BF)
    dinc[r, :] = (d * wide(din_t[r, :], spread_mat)).astype(BF)


def mixer_back_steps(
    xe, mk, cw, cum_t, cum, dt_t, we_t, skip, doc_c, doc_r, pre, xo, dm, dc_in, ds, dpre, dcw, dskip, xw, bias
):
    rows = pre.shape[0]
    here = pl.ds(0, rows)
    b_rows, c_rows = xo[:, pl.ds(INNER, NS)], xo[:, pl.ds(INNER + NS, NS)]
    cross = nt(b_rows, c_rows)
    s_at = lax.broadcasted_iota(jnp.int32, (rows, rows), 0)
    t_at = lax.broadcasted_iota(jnp.int32, (rows, rows), 1)
    bias[...] = jnp.where((doc_c[...] == doc_r[...]) & (s_at <= t_at), 0.0, large_negative)
    lanes = lax.broadcasted_iota(jnp.int32, (rows, 2 * MP), 1)

    def slope(sl):
        v = pre[:, sl].astype(F32)
        sig = jax.nn.sigmoid(v)
        return sig * (1.0 + v * (1.0 - sig))

    dcross = jnp.zeros((rows, rows), F32)
    for p in range(MH // 2):
        sl = pl.ds(p * 2 * MP, 2 * MP)
        xv = xo[:, sl].astype(F32)
        dt2, we2 = pair_columns(dt_t, p, lanes), pair_columns(we_t, p, lanes)
        xd = xv * dt2
        xw[:, sl] = (xd * we2).astype(BF)
        g = dm[:, sl]
        outs = []
        for k in (0, 1):
            h = 2 * p + k
            low = jnp.exp(jnp.minimum(cum[h : h + 1, :] - cum_t[:, h : h + 1], bias[...]))
            outs.append(nn((low * cross).astype(BF), g))
            part = jnp.where((lanes < MP) == (k == 0), xd, 0.0).astype(BF)
            dcross = dcross + nt(part, g) * low
        dxd = two(outs[0], outs[1], lanes) + we2 * nn(b_rows, ds[:, sl])
        gf = g.astype(F32)
        dskip[:, sl] = jnp.sum(gf * xv, axis=0, keepdims=True)
        dpre[here, sl] = (dxd * dt2 + skip[:, sl] * gf) * slope(sl)
        if p % 4 == 3:
            yield
    db16 = dcross.astype(BF)
    slb, slc = pl.ds(INNER, NS), pl.ds(INNER + NS, NS)
    dpre[here, slb] = (nn(db16, c_rows) + nt(xw[...], ds[...])) * slope(slb)
    dpre[here, slc] = (tn(db16, b_rows) + dc_in[...]) * slope(slc)
    yield
    for i in range(XBC // 256):
        sl = pl.ds(i * 256, 256)
        d = dpre[here, sl]
        for j in range(CONV):
            dcw[j : j + 1, sl] = jnp.sum(
                d * (xe[pl.ds(5 + j, rows), sl] * mk[:, j : j + 1]), axis=0, keepdims=True
            )
        dcw[CONV : CONV + 1, sl] = jnp.sum(d, axis=0, keepdims=True)


def back_kernel(planes, count, block, *refs):
    lefts, rights, refs = refs[:count], refs[count : 2 * count], refs[2 * count :]
    if count:
        branch = rights[2]
    else:
        branch, refs = refs[0], refs[1:]
    (
        lens, grad, mixed, gate, xo, state_in, q_in, kv, lse, cos_w, sin_w, decays, xe, ldec, root_t, small, pre,
    ) = refs[:17]
    refs = refs[17:]
    if count:
        scattered, refs = refs[0], refs[1:]
    dproj, dgain, dcw, dskip = refs[:4]
    (
        dm, dinc, dc, dstate, dsnew, flat, qh, doh, dl, acc, dkv, dkv_own, dpre, edge, bias, esem
    ) = refs[4:20]
    gain, cw, skip, state = refs[20:24]
    tables, refs = refs[24:33], refs[33:]
    pos, same, doc_c, doc_r, cum, cum_t, dt_t, we_t, din_t = tables
    relay_refs, refs = refs[:6], refs[6:]
    fold_refs, refs = refs[:10], refs[10:]
    pc = Place(planes)
    n = 4 * planes
    rows = mixed.shape[0]
    greet_row(pc, count > 0)
    side = (
        scatter_steps(pc, tuple(zip(lefts, rights)), scattered, refs, EARLY) if count else iter(())
    )

    def pump():
        next(side, None)

    pump()
    spread_mat = spread_heads()
    unpack(small, "gate", gain)
    unpack_conv(small, cw)
    wide_skip(small, spread_mat, skip)
    make_tables(pc, lens, ldec, root_t, tables)
    state[...] = state_in[...].reshape(state.shape)
    dgain[...] = jnp.zeros_like(dgain)
    pl.loop(0, rows // 64)(
        lambda i: gate_back_rows(i, grad, mixed, gate, gain, din_t, spread_mat, dm, dproj, dgain, dinc)
    )
    ds0 = tn(xo[:, pl.ds(INNER + NS, NS)], dinc[...]).astype(BF)
    dc[...] = nt(dinc[...], state[...])
    dstate[...] = ds0.reshape(dstate.shape)
    states = relay_steps(pc, True, dstate, decays, dsnew, relay_refs)
    next(states)
    for _ in range(4):
        pump()
    split_heads(q_in, qh, jnp.asarray(HEAD_WIDTH**-0.5, BF))
    go = grad[:, pl.ds(0, QUERY_WIDTH)].astype(BF)
    head = lax.broadcasted_iota(jnp.int32, (QUERY_HEADS, QUERY_WIDTH), 0)
    lane = lax.broadcasted_iota(jnp.int32, (QUERY_HEADS, QUERY_WIDTH), 1)
    for h in range(QUERY_HEADS):
        doh[pl.ds(h * rows, rows), :] = go[:, h * HEAD_WIDTH : (h + 1) * HEAD_WIDTH]
    dl[...] = exact(
        (lane // HEAD_WIDTH == head).astype(F32),
        go.astype(F32) * branch[:, pl.ds(0, QUERY_WIDTH)].astype(F32),
        ((1,), (1,)),
    )
    acc[...] = jnp.zeros_like(acc)
    total = kv.shape[0] // block
    seen = (pc.ctx * rows + rows + block - 1) // block
    parts = 8
    each = total // parts

    @pl.loop(seen, (pc.z + 1) * 4 * rows // block)
    def _(j):
        dkv[pl.ds(pl.multiple_of(j * block, block), block), :] = jnp.zeros((block, 2 * KEY_WIDTH), BF)

    for k in range(parts):
        lo = each * k
        for g in range(KEY_VALUE_HEADS):
            pl.loop(jnp.minimum(lo, seen), jnp.minimum(lo + each, seen))(
                lambda j: attend_back_block(j, g, block, qh, doh, kv, pos, lse, dl, dkv, acc)
            )
            if g == 1:
                pump()
        if k == 3:
            next(states)
    folds = fold_steps(
        pc, lambda s: dkv.at[pl.ds(pl.multiple_of(s * rows, rows), rows), :], dkv_own, fold_refs
    )
    next(folds)
    for t in range(QUERY_WIDTH // 128):
        dq = acc[pl.ds(t * 128, 128), :].T * (HEAD_WIDTH**-0.5)
        dproj[:, pl.ds(t * 128, 128)] = rotate(dq, cos_w, sin_w, -1.0).astype(BF)
    next(states)
    flat[...] = dsnew[...].reshape(flat.shape)
    next(folds)
    mixing = mixer_back_steps(
        xe, same, cw, cum_t, cum, dt_t, we_t, skip, doc_c, doc_r, pre, xo, dm, dc, flat, dpre, dcw, dskip, dinc, bias
    )
    next(mixing)
    next(folds)
    pump()
    next(mixing)
    pump()
    next(mixing)
    next(folds)
    pump()
    next(mixing)
    prior = rcopy(pc, dpre.at[pl.ds(0, 8), :], edge, esem.at[0], esem.at[1], (lax.rem(pc.ctx + n - 1, n), pc.y))
    pl.when(pc.ctx > 0)(lambda: prior.start())
    for _ in mixing:
        pass
    pump()
    for _ in folds:
        pass
    dproj[:, pl.ds(QUERY_WIDTH, KEY_WIDTH)] = rotate(dkv_own[:, pl.ds(0, KEY_WIDTH)], cos_w, sin_w, -1.0).astype(BF)
    dproj[:, pl.ds(QUERY_WIDTH + KEY_WIDTH, KEY_WIDTH)] = dkv_own[:, pl.ds(KEY_WIDTH, KEY_WIDTH)].astype(BF)
    pl.when(pc.ctx < n - 1)(lambda: prior.wait_recv())

    @pl.when(pc.ctx == n - 1)
    def _():
        edge[...] = jnp.zeros_like(edge)

    dpre[pl.ds(rows, 8), :] = edge[...]
    for i in range(XBC // 256):
        sl = pl.ds(i * 256, 256)
        total_grad = jnp.zeros((rows, 256), F32)
        for j in range(CONV):
            total_grad = total_grad + cw[j : j + 1, sl] * (
                dpre[pl.ds(CONV - 1 - j, rows), sl] * same[:, CONV + j : CONV + j + 1]
            )
        dproj[:, pl.ds(XBC_AT + i * 256, 256)] = total_grad.astype(BF)
    for _ in states:
        pass
    pl.when(pc.ctx > 0)(lambda: prior.wait_send())
    for _ in side:
        pass


def back(planes, lefts, rights, args, block, collective):
    count = len(lefts)
    n = 4 * planes
    rows = args[-1].shape[0]
    keys = n * rows
    outs = [
        jax.ShapeDtypeStruct((rows, MIXIN), BF),
        jax.ShapeDtypeStruct((1, INNER), F32),
        jax.ShapeDtypeStruct((CONV + 1, XBC), F32),
        jax.ShapeDtypeStruct((1, INNER), F32),
    ]
    scratch = [
        pltpu.VMEM((rows, INNER), BF),
        pltpu.VMEM((rows, INNER), BF),
        pltpu.VMEM((rows, NS), F32),
        pltpu.VMEM((n, NS // n, INNER), BF),
        pltpu.VMEM((n, NS // n, INNER), BF),
        pltpu.VMEM((NS, INNER), BF),
        pltpu.VMEM((QUERY_HEADS * rows, HEAD_WIDTH), BF),
        pltpu.VMEM((QUERY_HEADS * rows, HEAD_WIDTH), BF),
        pltpu.VMEM((QUERY_HEADS, rows), F32),
        pltpu.VMEM((QUERY_WIDTH, rows), F32),
        pltpu.VMEM((keys, 2 * KEY_WIDTH), BF),
        pltpu.VMEM((rows, 2 * KEY_WIDTH), F32),
        pltpu.VMEM((rows + 8, XBC), F32),
        pltpu.VMEM((8, XBC), F32),
        pltpu.VMEM((rows, rows), F32),
        DMA((2,)),
        pltpu.VMEM((1, INNER), F32),
        pltpu.VMEM((CONV, XBC), F32),
        pltpu.VMEM((1, INNER), F32),
        pltpu.VMEM((NS, INNER), BF),
    ]
    scratch += table_scratch(rows)
    scratch += relay_scratch(planes) + fold_scratch(planes, rows, 2 * KEY_WIDTH)
    if count:
        widths = [r.shape[1] for r in rights]
        each = lefts[0].shape[1] // n
        outs = [jax.ShapeDtypeStruct((each, sum(widths)), F32)] + outs
        scratch += scatter_scratch(planes, each, widths, EARLY)
    return pl.pallas_call(
        functools.partial(back_kernel, planes, count, block),
        out_shape=tuple(outs),
        in_specs=[VM] * (2 * count + (not count)) + [SM] + [VM] * (len(args) - 2 + bool(count)),
        out_specs=(VM,) * len(outs),
        scratch_shapes=scratch,
        compiler_params=params(collective),
    )(*lefts, *rights, *args)


def last_kernel(
    planes, left, dproj, w1, w2, tok, scale, packed, dres, small, scattered, dhid, totals, dn, wg, wsem, gain, *scratch
):
    pc = Place(planes)
    greet_planes(pc)
    rows = dproj.shape[0]
    fetch = pltpu.make_async_copy(w2.at[:, :, :, :, :, pl.ds(0, INNER)], wg, wsem)
    fetch.start()
    side = scatter_steps(pc, ((left, dproj),), scattered, scratch[6:], LAST)
    next(side)
    unpack(packed, "one", gain)
    fetch.wait()
    next(side)
    part = planes // 4
    for i in range(4):
        at = pl.ds(i * part, part)
        a, b = w1[at].reshape(D // 4, FIRST), wg[at].reshape(D // 4, INNER)
        dn[:, pl.ds(i * 256, 256)] = (
            nt(dproj[:, pl.ds(0, GATE_AT)], a[:, :GATE_AT])
            + nt(dproj[:, pl.ds(GATE_AT, INNER)], b)
            + nt(dproj[:, pl.ds(XBC_AT, XBC)], a[:, GATE_AT:])
        )
        next(side)
        next(side)
    totals[...] = small[...]
    for i in range(rows // 64):
        r = pl.ds(i * 64, 64)
        v, g, f = tok[r, :].astype(F32), dn[r, :], scale[r, :]
        w = g * gain[...]
        dhid[r, :] = dres[r, :] + f * (w - v * f * f * jnp.mean(w * v, axis=1, keepdims=True))
        part = jnp.sum(g * v * f, axis=0, keepdims=True)
        for t in range(D // 128):
            totals[t : t + 1, :] = totals[t : t + 1, :] + part[:, t * 128 : (t + 1) * 128]
    sums = total_steps(pc, totals, scratch[:6])
    next(sums)
    for _ in side:
        next(sums, None)
    for _ in sums:
        pass


def last(planes, left, dproj, w1, w2, tok, scale, packed, dres, small, collective):
    rows = dproj.shape[0]
    each = left.shape[1] // (4 * planes)
    return pl.pallas_call(
        functools.partial(last_kernel, planes),
        out_shape=(
            jax.ShapeDtypeStruct((each, MIXIN), F32),
            jax.ShapeDtypeStruct((rows, D), F32),
            jax.ShapeDtypeStruct((SMALL_ROWS, 128), F32),
        ),
        in_specs=[VM] * 3 + [HB] + [VM] * 5,
        out_specs=(VM,) * 3,
        scratch_shapes=[
            pltpu.VMEM((rows, D), F32),
            pltpu.VMEM(w2.shape[:-1] + (INNER,), BF),
            DMA,
            pltpu.VMEM((1, D), F32),
        ]
        + total_scratch(planes)
        + scatter_scratch(planes, each, [MIXIN], LAST),
        compiler_params=params(collective),
    )(left, dproj, w1, w2, tok, scale, packed, dres, small)


def doc_layout(lengths, token_positions):
    starts = jnp.cumsum(lengths) - lengths
    inside = token_positions[:, None] >= starts[None, :]
    document_index = jnp.sum(inside.astype(jnp.int32), axis=1) - 1
    begins = jnp.max(jnp.where(inside, starts[None, :], 0), axis=1)
    return (document_index, token_positions - begins)


def rope_tables(rel_pos):
    half_dim = HEAD_WIDTH // 2
    inv_freq = rope_base ** (-2.0 * jnp.arange(half_dim, dtype=jnp.float32) / HEAD_WIDTH)
    angles = rel_pos.astype(jnp.float32)[:, None] * inv_freq[None, :]
    return (jnp.cos(angles), jnp.sin(angles))


def norm_backward(grad_normed, values, factor, gain_vals):
    weighted = grad_normed * gain_vals
    grad_values = factor * (
        weighted - values * factor * factor * jnp.mean(weighted * values, axis=1, keepdims=True)
    )
    grad_gain = jnp.sum(grad_normed * values * factor, axis=0)
    return (grad_values, grad_gain)


def adamw_step(param_vals, grad_vals, first_vals, second_vals, weight_decay):
    first_new = beta_one * first_vals + (1.0 - beta_one) * grad_vals
    second_new = beta_two * second_vals + (1.0 - beta_two) * grad_vals * grad_vals
    update = (
        first_new
        / (1.0 - beta_one**STEP)
        / (jnp.sqrt(second_new / (1.0 - beta_two**STEP)) + adam_eps)
    )
    return (param_vals - learn_rate * (update + weight_decay * param_vals), first_new, second_new)


def adam_direction(grad_vals, first_vals, second_vals):
    first_new = beta_one * first_vals + (1.0 - beta_one) * grad_vals
    second_new = beta_two * second_vals + (1.0 - beta_two) * grad_vals * grad_vals
    update = (
        first_new
        / (1.0 - beta_one**STEP)
        / (jnp.sqrt(second_new / (1.0 - beta_two**STEP)) + adam_eps)
    )
    return (update, first_new, second_new)


def shards(
    planes,
    hidden,
    out_grad,
    decay_log,
    doc_lengths,
    weights,
    first_moment,
    second_moment,
    small_params,
    small_first,
    small_second,
):
    local_rows = hidden.shape[1]
    count = 4 * planes
    ctx_index = lax.axis_index("ctx")
    first_pos = ctx_index * local_rows
    contract_last = (((1,), (1,)), ((), ()))
    lengths = doc_lengths[0]
    token_positions = first_pos + jnp.arange(local_rows, dtype=jnp.int32)
    cosine_table, sine_table = rope_tables(doc_layout(lengths, token_positions)[1])
    cos_wide = jnp.tile(cosine_table, (1, 4))
    sin_wide = jnp.tile(jnp.concatenate([-sine_table, sine_table], axis=1), (1, 2))
    size = small_params.shape[0]
    packed = jnp.pad(small_params, (0, SMALL_ROWS * 128 - size)).reshape(SMALL_ROWS, 128)
    log_decay = decay_log[0]
    root_t = jnp.sqrt(-jnp.expm1(2.0 * log_decay)).T
    block = 512
    own_b = weights.astype(jnp.bfloat16)
    own_first = jnp.concatenate([own_b[:, :GATE_AT], own_b[:, XBC_AT:MIXIN]], axis=1)
    own_rest = jnp.concatenate([own_b[:, GATE_AT:XBC_AT], own_b[:, MIXIN:]], axis=1)
    (
        normed_one, scale_one, first_w, rest_w, query_rows, kv_all, xe, decays, pre, xo, mix_local,
        state_in, attended, log_sums,
    ) = front(
        planes, doc_lengths, hidden[0], own_first, own_rest, cos_wide, sin_wide, log_decay, root_t,
        packed, block, 0,
    )
    rest_flat = rest_w.reshape(D, rest_w.shape[-1])
    mixout_w = rest_flat[:, INNER : INNER + MIXOUT]
    mlp_w = rest_flat[:, INNER + MIXOUT :]
    gate_in = jnp.dot(normed_one, rest_flat[:, :INNER], preferred_element_type=jnp.float32)
    mixed, branch = gate_out(
        planes, doc_lengths, mix_local, xo, state_in, log_decay, gate_in, packed, attended
    )

    tok_f = hidden[0].astype(jnp.float32)
    gain_two = small_params[D : 2 * D]
    resid_one = tok_f + lax.dot_general(
        branch, mixout_w, contract_last, preferred_element_type=jnp.float32
    )
    scale_two = lax.rsqrt(jnp.mean(resid_one * resid_one, axis=1, keepdims=True) + norm_eps)
    normed_two = (resid_one * scale_two * gain_two).astype(jnp.bfloat16)
    gate_up = jnp.dot(normed_two, mlp_w[:, : 2 * FF], preferred_element_type=jnp.float32)
    gate_part = gate_up[:, :FF]
    up_part = gate_up[:, FF:]
    sigma_gate = jax.nn.sigmoid(gate_part)
    silu_gate = gate_part * sigma_gate
    hidden_mid = (silu_gate * up_part).astype(jnp.bfloat16)
    block_out = resid_one + lax.dot_general(
        hidden_mid, mlp_w[:, 2 * FF :], contract_last, preferred_element_type=jnp.float32
    )
    out_hidden = block_out.astype(jnp.bfloat16)[None]
    grad_out = out_grad[0]
    grad_mid = jnp.dot(grad_out, mlp_w[:, 2 * FF :], preferred_element_type=jnp.float32)
    silu_slope = sigma_gate * (1.0 + gate_part * (1.0 - sigma_gate))
    grad_gate_up = jnp.concatenate(
        [grad_mid * up_part * silu_slope, grad_mid * silu_gate], axis=1
    ).astype(jnp.bfloat16)
    grad_normed_two = lax.dot_general(
        grad_gate_up, mlp_w[:, : 2 * FF], contract_last, preferred_element_type=jnp.float32
    )
    grad_norm_two, grad_gain_two = norm_backward(grad_normed_two, resid_one, scale_two, gain_two)
    grad_resid_one = grad_out.astype(jnp.float32) + grad_norm_two
    grad_resid_b = grad_resid_one.astype(jnp.bfloat16)

    grad_branch = jnp.dot(grad_resid_b, mixout_w, preferred_element_type=jnp.float32)
    lefts = [by_core(v, planes) for v in (normed_two, grad_out, grad_resid_b)]
    rights = [grad_gate_up, hidden_mid, branch]
    args = (
        doc_lengths, grad_branch, mixed, gate_in, xo, state_in, query_rows,
        kv_all.reshape(count * local_rows, 2 * KEY_WIDTH), log_sums, cos_wide, sin_wide, decays,
        xe, log_decay, root_t, packed, pre,
    )
    if planes <= 4:
        early, grad_proj, gate_gain_grads, conv_grads, skip_grads = back(
            planes, lefts, rights, args, block, 3
        )
    else:
        early = scatter_rows(planes, lefts, rights, 4)
        grad_proj, gate_gain_grads, conv_grads, skip_grads = back(planes, [], [], (branch,) + args, block, 3)
    small_local = jnp.concatenate(
        [
            jnp.zeros((D,), jnp.float32),
            grad_gain_two,
            gate_gain_grads[0],
            conv_grads.reshape(-1),
            jnp.sum(skip_grads.reshape(MH, MP), axis=1),
        ]
    )
    padded = jnp.pad(small_local, (0, SMALL_ROWS * 128 - size)).reshape(SMALL_ROWS, 128)
    mixin_grads, grad_hidden, totals = last(
        planes, by_core(normed_one, planes), grad_proj, first_w, rest_w, hidden[0], scale_one,
        packed, grad_resid_one, padded, 5,
    )
    grad_hidden = grad_hidden[None]
    small_grads = totals.reshape(-1)[:size]
    grad_weights = jnp.concatenate(
        [mixin_grads, early[:, 3 * FF :], early[:, : 3 * FF]], axis=1
    )
    new_weights, new_first, new_second = adamw_step(
        weights, grad_weights, first_moment, second_moment, decay_rate
    )
    small_step, small_first_new, small_second_new = adam_direction(
        small_grads, small_first, small_second
    )
    return (
        out_hidden,
        grad_hidden,
        grad_weights,
        new_weights,
        new_first,
        new_second,
        small_grads,
        small_step,
        small_first_new,
        small_second_new,
    )


def solution(mesh):
    placed = (
        P("fsdp", "ctx", None),
        P("fsdp", "ctx", None),
        P("fsdp", None, "ctx"),
        P("fsdp", None),
        P(("ctx", "fsdp"), None),
        P(("ctx", "fsdp"), None),
        P(("ctx", "fsdp"), None),
        P(),
        P(),
        P(),
    )
    return jax.shard_map(
        functools.partial(shards, mesh.shape["ctx"] // 4),
        mesh=mesh,
        in_specs=placed,
        out_specs=(
            P("fsdp", "ctx", None),
            P("fsdp", "ctx", None),
            P(("ctx", "fsdp"), None),
            P(("ctx", "fsdp"), None),
            P(("ctx", "fsdp"), None),
            P(("ctx", "fsdp"), None),
            P(),
            P(),
            P(),
            P(),
        ),
        check_vma=False,
    )
```

```python
import functools
import math

import jax
import jax.numpy as jnp
from jax import lax
from jax.experimental import pallas as pl
from jax.experimental.pallas import tpu as pltpu
from jax.sharding import PartitionSpec as P

D = 1024
QUERY_HEADS = 8
KEY_VALUE_HEADS = 2
HEAD_WIDTH = 64
MH = 24
MP = 64
NS = 128
FF = 2048
CONV = 4
STEP = 3
QUERY_WIDTH = 512
KEY_WIDTH = 128
INNER = 1536
XBC = 1792
MIXIN = 4096
MIXOUT = 2048
SMALL_ROWS = 104
TOKENS = 256
PIECE = 256

norm_eps = 1e-05
rope_base = 100000000000.0
large_negative = -1e30
learn_rate = 0.02
beta_one = 0.9
beta_two = 0.95
adam_eps = 1e-08
decay_rate = 0.1

MESH = pl.DeviceIdType.MESH
BF = jnp.bfloat16
F32 = jnp.float32
VM = pl.BlockSpec(memory_space=pltpu.VMEM)
SM = pl.BlockSpec(memory_space=pltpu.SMEM)
HB = pl.BlockSpec(memory_space=pl.ANY)
DMA = pltpu.SemaphoreType.DMA


def params(collective=None):
    if collective is None:
        return pltpu.CompilerParams(vmem_limit_bytes=62 * 2**20)
    return pltpu.CompilerParams(
        collective_id=collective, has_side_effects=True, vmem_limit_bytes=62 * 2**20
    )


def nt(a, b):
    return lax.dot_general(a, b, (((1,), (1,)), ((), ())), preferred_element_type=F32)


def tn(a, b):
    return lax.dot_general(a, b, (((0,), (0,)), ((), ())), preferred_element_type=F32)


def nn(a, b):
    return lax.dot_general(a, b, (((1,), (0,)), ((), ())), preferred_element_type=F32)


class Place:
    def __init__(self, planes):
        ctx = lax.axis_index("ctx")
        self.ctx = ctx
        self.Z, self.z, self.x, self.c = planes, ctx // 4, (ctx // 2) % 2, ctx % 2
        self.y = lax.axis_index("fsdp")
        self.up, self.down = self.z + 1 < planes, self.z > 0

    def shard(self, z, x, y, c):
        return ((z * 2 + x) * 2 + c) * 2 + y

    def spot(self, z, x, c):
        return (z * 2 + x) * 2 + c

    def dev(self, z, x, y, c):
        return ((z * 2 + x) * 2 + c, y)

    def near(self, d):
        z, x, y, c = self.z, self.x, self.y, self.c
        return {
            "x": self.dev(z, 1 - x, y, c),
            "y": self.dev(z, x, 1 - y, c),
            "c": self.dev(z, x, y, 1 - c),
            "u": self.dev(z + 1, x, y, c),
            "d": self.dev(z - 1, x, y, c),
        }[d]

    def zord(self, k):
        if k == self.Z - 1:
            return self.z
        low = self.Z - 1 - k
        z = self.z
        return jnp.where(
            2 * z < self.Z, jnp.where(low > z, low, low - 1), jnp.where(k < z, k, k + 1)
        )


def greet(pc, dims="xyc", chain=True):
    bar = pltpu.get_barrier_semaphore()

    def sig(d):
        pl.semaphore_signal(bar, inc=1, device_id=pc.near(d), device_id_type=MESH)

    for d in dims:
        sig(d)
    if chain:
        pl.when(pc.up)(lambda: sig("u"))
        pl.when(pc.down)(lambda: sig("d"))
    peers = len(dims)
    if chain:
        peers = peers + pc.up.astype(jnp.int32) + pc.down.astype(jnp.int32)
    pl.semaphore_wait(bar, peers)


def greet_row(pc, across=False):
    bar = pltpu.get_barrier_semaphore()
    n = 4 * pc.Z

    @pl.loop(1, n)
    def _(d):
        pl.semaphore_signal(
            bar, inc=1, device_id=(lax.rem(pc.ctx + d, n), pc.y), device_id_type=MESH
        )

    if across:
        pl.semaphore_signal(bar, inc=1, device_id=pc.near("y"), device_id_type=MESH)
    pl.semaphore_wait(bar, n - 1 + int(across))


def rcopy(pc, src, dst, ssem, rsem, d):
    return pltpu.make_async_remote_copy(
        src_ref=src,
        dst_ref=dst,
        send_sem=ssem,
        recv_sem=rsem,
        device_id=pc.near(d) if isinstance(d, str) else d,
        device_id_type=MESH,
    )


def add_into(dst, parts, width=512):
    columns = dst.shape[-1]
    step = width if columns % width == 0 else (256 if columns % 256 == 0 else 128)

    @pl.loop(0, columns // step)
    def _(i):
        sl = pl.ds(pl.multiple_of(i * step, step), step)
        total = parts[0][:, sl].astype(F32)
        for r in parts[1:]:
            total = total + r[:, sl].astype(F32)
        dst[:, sl] = total.astype(dst.dtype)


def plane_peers(pc):
    return [pc.dev(lax.rem(pc.z + d, pc.Z), pc.x, pc.y, pc.c) for d in range(1, pc.Z)]


def greet_planes(pc):
    bar = pltpu.get_barrier_semaphore()
    peers = [pc.near(d) for d in "xyc"] + plane_peers(pc)
    for d in peers:
        pl.semaphore_signal(bar, inc=1, device_id=d, device_id_type=MESH)
    pl.semaphore_wait(bar, len(peers))


EVEN = (25, 25, 64)
REST = (35, 19, 64)


def split(columns, shares, unit):
    a, b = (columns * s // shares[2] // unit * unit for s in shares[:2])
    return a, b, columns - a - b


def part_columns(widths, p):
    a, b, w = widths
    return pl.ds((w, w + a, 0)[p], widths[p])


def gather_scratch(planes):
    return [
        DMA((2, planes, 2)),
        DMA((2, planes)),
        DMA((2, planes, 2)),
        DMA((2, planes, 4)),
        DMA((2, planes, 8)),
        DMA((2, planes)),
        DMA((2 + planes,)),
        DMA((4 + 2 * planes,)),
        DMA,
    ]


def gather_steps(pc, w_ref, out_ref, scratch, shares):
    zs, xs, ys, cs, rs, tz, tc, tr, loc = scratch
    Z, z, x, y, c = pc.Z, pc.z, pc.x, pc.y, pc.c
    widths = split(w_ref.shape[-1], shares, 128)

    def cols(p):
        return part_columns(widths, p)

    def spot(q):
        return (x if q < 2 else 1 - x), (y if q % 2 == 0 else 1 - y)

    def cp(p, zz, q, sem, d, own=False, core=None):
        xx, yy = spot(q)
        dst = out_ref.at[zz, xx, c, yy, :, cols(p)]
        return rcopy(pc, w_ref.at[:, cols(p)] if own else dst, dst, sem, rs.at[p, zz, core if core is not None else q], d)

    def along(p, zz, up, own=False):
        return cp(p, zz, 0, zs.at[p, zz, int(up)], "u" if up else "d", own, 0)

    def first(p, zz, own=False):
        return cp(p, zz, 0, xs.at[p, zz], "x" if p == 0 else "y", own, 2 if p == 0 else 1)

    def second(p, zz, q, own=False):
        if p == 0:
            return cp(p, zz, 2 * q, ys.at[p, zz, q], "y", own, 2 * q + 1)
        return cp(p, zz, q, ys.at[p, zz, q], "x", own, 2 + q)

    def core(p, zz, q, own=False):
        return cp(p, zz, q, cs.at[p, zz, q], "c", own, 4 + q)

    def arrived(p, zz, q):
        rcopy(
            pc, w_ref.at[:, cols(p)], out_ref.at[0, 0, 0, 0, :, cols(p)], loc, rs.at[p, zz, q], "c"
        ).wait_recv()

    def t_x():
        return rcopy(
            pc, w_ref.at[:, cols(2)], out_ref.at[z, x, c, y, :, cols(2)], tc.at[0], tr.at[0], "x"
        )

    def t_y():
        v = out_ref.at[z, :, c, y, :, cols(2)]
        return rcopy(pc, v, v, tc.at[1], tr.at[1], "y")

    def t_z(zz, up):
        v = out_ref.at[zz, :, c, :, :, cols(2)]
        return rcopy(pc, v, v, tz.at[int(up), zz], tr.at[4 + zz], "u" if up else "d")

    def t_c(zz):
        v = out_ref.at[zz, :, c, :, :, cols(2)]
        return rcopy(pc, v, v, tc.at[2 + zz], tr.at[4 + Z + zz], "c")

    keep = pltpu.make_async_copy(w_ref, out_ref.at[z, x, c, y], loc)
    keep.start()
    t_x().start()
    for p in (0, 1):
        pl.when(pc.up)(lambda: along(p, z, True, True).start())
        pl.when(pc.down)(lambda: along(p, z, False, True).start())
        first(p, z, True).start()
    for p in (0, 1):
        second(p, z, 0, True).start()
        core(p, z, 0, True).start()
    yield False
    keep.wait()
    t_x().wait_recv()
    t_y().start()
    for d in range(1, Z):
        for p in (0, 1):

            def onward(zz, up, more):
                arrived(p, zz, 0)
                pl.when(more)(lambda: along(p, zz, up).start())
                first(p, zz).start()
                second(p, zz, 0).start()
                core(p, zz, 0).start()

            pl.when(z - d >= 0)(lambda: onward(z - d, True, pc.up))
            pl.when(z + d < Z)(lambda: onward(z + d, False, pc.down))
        if d == 1:
            t_y().wait_recv()
            pl.when(pc.up)(lambda: t_z(z, True).start())
            pl.when(pc.down)(lambda: t_z(z, False).start())
            t_c(z).start()
        yield False

    def hop(d):
        def onward(zz, up, more):
            t_z(zz, up).wait_recv()
            pl.when(more)(lambda: t_z(zz, up).start())
            t_c(zz).start()

        pl.when(z - d >= 0)(lambda: onward(z - d, True, pc.up))
        pl.when(z + d < Z)(lambda: onward(z + d, False, pc.down))

    near = [lax.rem(z + k, Z) for k in range(Z)]
    for k, zz in enumerate(near):
        for p in (0, 1):
            q = 2 if p == 0 else 1
            arrived(p, zz, q)
            second(p, zz, 1).start()
            core(p, zz, q).start()
        if k > 0:
            hop(k)
        yield False
    for i in (0, 1):
        for k, zz in enumerate(near):
            for p in (0, 1):
                q = (1 if i == 0 else 3) if p == 0 else (2 if i == 0 else 3)
                arrived(p, zz, q)
                core(p, zz, q).start()
            yield i == 1 and k == Z - 1
    for zz in near:
        for p in (0, 1):
            for q in range(4):
                arrived(p, zz, 4 + q)
        t_c(zz).wait_recv()
        yield True
    t_x().wait_send()
    t_y().wait_send()
    for zz in range(Z):
        for p in (0, 1):
            pl.when(pc.up & (zz <= z))(lambda: along(p, zz, True).wait_send())
            pl.when(pc.down & (zz >= z))(lambda: along(p, zz, False).wait_send())
            first(p, zz).wait_send()
            for q in (0, 1):
                second(p, zz, q).wait_send()
            for q in range(4):
                core(p, zz, q).wait_send()
        pl.when(pc.up & (zz <= z))(lambda: t_z(zz, True).wait_send())
        pl.when(pc.down & (zz >= z))(lambda: t_z(zz, False).wait_send())
        t_c(zz).wait_send()


def spread_scratch(planes):
    n = 4 * planes
    return [DMA((planes,)), DMA((planes,)), DMA((planes, 2)), DMA((n,)), DMA((n,)), DMA((n,)), DMA((3,))]


def spread_steps(pc, kv_ref, edge_ref, dec_ref, all_ref, got_ref, decs_ref, scratch):
    us, xs, cs, rs, ds, dr, one = scratch
    Z, z, x, c = pc.Z, pc.z, pc.x, pc.c
    n = 4 * Z
    me = pc.ctx

    def cp(zz, xx, sem, d, own=False):
        s = pc.spot(zz, xx, c)
        return rcopy(pc, kv_ref if own else all_ref.at[s], all_ref.at[s], sem, rs.at[s], d)

    def arrived(s):
        rcopy(pc, kv_ref, all_ref.at[s], one.at[0], rs.at[s], "c").wait_recv()

    def decay_copy(d):
        return rcopy(pc, dec_ref, decs_ref.at[me], ds.at[d], dr.at[d], (lax.rem(me + d, n), pc.y))

    edge = rcopy(pc, edge_ref, got_ref, one.at[1], one.at[2], (lax.rem(me + 1, n), pc.y))
    keep = pltpu.make_async_copy(kv_ref, all_ref.at[me], one.at[0])
    pl.when(me < n - 1)(lambda: edge.start())
    keep.start()
    pl.when(pc.up)(lambda: cp(z, x, us.at[z], "u", True).start())
    cp(z, x, xs.at[z], "x", True).start()
    cp(z, x, cs.at[z, 0], "c", True).start()
    decs_ref[me] = dec_ref[...]
    pl.loop(1, n)(lambda d: decay_copy(d).start())
    yield
    pl.when(me > 0)(lambda: edge.wait_recv())

    @pl.when(me == 0)
    def _():
        got_ref[...] = jnp.zeros_like(got_ref)

    yield
    for d in range(1, Z):

        @pl.when(z - d >= 0)
        def _():
            zz = z - d
            arrived(pc.spot(zz, x, c))
            pl.when(pc.up)(lambda: cp(zz, x, us.at[zz], "u").start())
            cp(zz, x, xs.at[zz], "x").start()
            cp(zz, x, cs.at[zz, 0], "c").start()

        yield
    for d in range(Z):

        @pl.when(z - d >= 0)
        def _():
            arrived(pc.spot(z - d, 1 - x, c))
            cp(z - d, 1 - x, cs.at[z - d, 1], "c").start()

    yield
    for d in range(Z):

        @pl.when(z - d >= 0)
        def _():
            for xx in (x, 1 - x):
                arrived(pc.spot(z - d, xx, 1 - c))

    keep.wait()
    pl.loop(1, n)(lambda d: decay_copy(d).wait_recv())
    yield
    for zz in range(Z):

        @pl.when(zz <= z)
        def _():
            pl.when(pc.up)(lambda: cp(zz, x, us.at[zz], "u").wait_send())
            cp(zz, x, xs.at[zz], "x").wait_send()
            cp(zz, x, cs.at[zz, 0], "c").wait_send()
            cp(zz, 1 - x, cs.at[zz, 1], "c").wait_send()

    pl.when(me < n - 1)(lambda: edge.wait_send())
    pl.loop(1, n)(lambda d: decay_copy(d).wait_send())


LAST = (7, 7, 16)
EARLY = (6, 6, 16)
STEP_PIECE = 512


def scatter_scratch(planes, rows, widths, shares):
    columns = sum(widths)
    a, b, w = split(columns, shares, PIECE)
    half = 4 * planes * rows
    return [
        pltpu.VMEM((planes, 2, 2, rows, columns), BF),
        pltpu.VMEM((planes, 2, rows, a + b), BF),
        pltpu.VMEM((planes, rows, a + b), BF),
        pltpu.VMEM((planes, rows, a + b), BF),
        pltpu.VMEM((planes + 1, 2, 2, rows, w), BF),
        pltpu.VMEM((3, rows, w), BF),
        pltpu.VMEM((len(widths), half, TOKENS), BF),
        pltpu.VMEM((TOKENS, columns), BF),
        DMA((len(widths),)),
        DMA((len(widths),)),
        DMA((columns // PIECE,)),
        DMA((columns // PIECE,)),
        DMA((2, planes, 2)),
        DMA((2, planes, 2)),
        DMA((2, planes)),
        DMA((2, planes)),
        DMA((3, planes)),
        DMA((3, planes + 1)),
        DMA((3,)),
        DMA((3,)),
    ]


def scatter_steps(pc, pairs, out_ref, scratch, shares):
    g, r2, r3, rz, rw, rt, la, rb, as_, ar, bs, br, s2, q2, s3, q3, sz, qz, st, qt = scratch
    Z, z, x, y, c = pc.Z, pc.z, pc.x, pc.y, pc.c
    rows = g.shape[3]
    widths = split(g.shape[-1], shares, PIECE)
    w = widths[2]
    depth = 4 * rows

    def cols(p):
        return part_columns(widths, p)

    def got(p):
        return pl.ds(p * widths[0], widths[p])

    pieces = []
    base = 0
    for i, (left, right) in enumerate(pairs):
        for at in range(0, right.shape[1], PIECE):
            pieces.append((i, at, base + at))
        base += right.shape[1]

    def acopy(i):
        return rcopy(pc, pairs[i][0].at[1 - c], la.at[i], as_.at[i], ar.at[i], "c")

    def bcopy(k):
        i, at, to = pieces[k]
        return rcopy(
            pc, pairs[i][1].at[:, pl.ds(at, PIECE)], rb.at[:, pl.ds(to, PIECE)], bs.at[k], br.at[k], "c"
        )

    def make(zz, k, first):
        i, at, to = pieces[k]
        if first:
            if at == 0:
                acopy(i).wait_recv()
            bcopy(k).wait_recv()
        here = pl.ds(pl.multiple_of(zz * depth, depth), depth)
        mine, theirs = pairs[i][0][c, here, :], la[i, here, :]
        tile = nn(mine, pairs[i][1][:, pl.ds(at, PIECE)]) + nn(theirs, rb[:, pl.ds(to, PIECE)])
        g[zz, :, :, :, pl.ds(to, PIECE)] = tile.reshape(2, 2, rows, PIECE).astype(BF)

    def copy2(p, zz, j):
        xx, yy = (x if j == 0 else 1 - x, 1 - y) if p == 0 else (1 - x, y if j == 0 else 1 - y)
        return rcopy(
            pc, g.at[zz, xx, yy, :, cols(p)], r2.at[zz, j, :, got(p)], s2.at[p, zz, j], q2.at[p, zz, j],
            "y" if p == 0 else "x",
        )

    def copy3(p, zz):
        xx, yy = (1 - x, y) if p == 0 else (x, 1 - y)
        return rcopy(
            pc, g.at[zz, xx, yy, :, cols(p)], r3.at[zz, :, got(p)], s3.at[p, zz], q3.at[p, zz],
            "x" if p == 0 else "y",
        )

    def sendz(p, zz):
        return rcopy(
            pc, g.at[zz, x, y, :, cols(p)], rz.at[z, :, got(p)], sz.at[p, zz], qz.at[p, z], pc.dev(zz, x, y, c)
        )

    def gotz(p, zz):
        rcopy(pc, g.at[0, x, y, :, cols(p)], rz.at[zz, :, got(p)], sz.at[p, 0], qz.at[p, zz], "c").wait_recv()

    def send_plane(zz, up):
        slot = jnp.where(zz == z + 1, Z, zz) if up else zz
        return rcopy(
            pc, g.at[zz, :, :, :, cols(2)], rw.at[slot], sz.at[2, zz], qz.at[2, slot], "u" if up else "d"
        )

    def got_plane(slot):
        rcopy(
            pc, g.at[0, :, :, :, cols(2)], rw.at[slot], sz.at[2, 0], qz.at[2, slot], "c"
        ).wait_recv()

    def add_plane(zz, slots):
        for xx in (0, 1):
            for yy in (0, 1):
                a = g.at[zz, xx, yy, :, cols(2)]
                add_into(a, [a] + [rw.at[k, xx, yy] for k in slots])

    def at_time(t, f):
        below, above = t - (Z - 1 - z), Z - 1 - (t - z)
        pl.when((below >= 0) & (below < z))(lambda: f(below, False, pc.up))
        pl.when((above > z) & (above < Z))(lambda: f(above, True, pc.down))

    def chain_first(zz, up, more):
        @pl.when(more)
        def _():
            got_plane(zz)
            add_plane(zz, [zz])

        send_plane(zz, up).start()

    def tail(k):
        if k < 2:
            return rcopy(pc, g.at[z, k, 1 - y, :, cols(2)], rt.at[k], st.at[k], qt.at[k], "y")
        return rcopy(pc, g.at[z, 1 - x, y, :, cols(2)], rt.at[2], st.at[2], qt.at[2], "x")

    for i in range(len(pairs)):
        acopy(i).start()
        for k in range(len(pieces)):
            if pieces[k][0] == i:
                bcopy(k).start()
    yield
    ends = {w + widths[0]: 0, w + widths[0] + widths[1]: 1}

    def own(p, zz):
        copy2(p, zz, 0).wait_recv()
        copy3(p, zz).wait_recv()
        a = g.at[zz, x, y, :, cols(p)]
        return a, [a, r2.at[zz, 0, :, got(p)], r3.at[zz, :, got(p)]]

    def gather_plane(slot):
        got_plane(slot)
        add_plane(z, [slot])

    for k in range(Z + 2):
        if k < Z:
            zz = pc.zord(k)
            for n in range(len(pieces)):
                make(zz, n, k == 0)
                end = pieces[n][2] + PIECE
                if end == w and k == 0 and Z > 1:
                    at_time(0, chain_first)
                if end in ends:
                    copy2(ends[end], zz, 1).start()
                if n == len(pieces) // 2:
                    yield
            yield
        if 0 < k <= Z:
            zz = pc.zord(k - 1)
            for p in (0, 1):
                copy2(p, zz, 1).wait_recv()
                a = g.at[(zz,) + ((1 - x, y) if p == 0 else (x, 1 - y)) + (slice(None), cols(p))]
                add_into(a, [a, r2.at[zz, 1, :, got(p)]])
                copy3(p, zz).start()
            for p in (0, 1):
                copy2(p, zz, 0).start()
            if 0 < k - 1 < Z - 1:
                at_time(k - 1, chain_first)
            yield
        if 1 < k <= Z:
            zz = pc.zord(k - 2)
            for p in (0, 1):
                a, parts = own(p, zz)
                add_into(a, parts)
                sendz(p, zz).start()
            yield
    pl.when(pc.up)(lambda: gather_plane(z))
    pl.when(pc.down)(lambda: gather_plane(Z))
    for k in (0, 1):
        tail(k).start()
    yield
    finals = []
    for p in (0, 1):
        finals.append(own(p, z)[1])
    for k in (0, 1):
        tail(k).wait_recv()
        a = g.at[z, k, y, :, cols(2)]
        add_into(a, [a, rt.at[k]])
    tail(2).start()
    yield
    for p in (0, 1):
        for d in range(1, Z):
            slot = lax.rem(z + d, Z)
            gotz(p, slot)
            finals[p].append(rz.at[slot, :, got(p)])
        add_into(out_ref.at[:, cols(p)], finals[p])
        yield
    tail(2).wait_recv()
    add_into(out_ref.at[:, cols(2)], [g.at[z, x, y, :, cols(2)], rt.at[2]])
    for i in range(len(pairs)):
        acopy(i).wait_send()
    for k in range(len(pieces)):
        bcopy(k).wait_send()
    for k in range(3):
        tail(k).wait_send()
    for zz in range(Z):
        for p in (0, 1):
            for j in (0, 1):
                copy2(p, zz, j).wait_send()
            copy3(p, zz).wait_send()
            pl.when(zz != z)(lambda: sendz(p, zz).wait_send())
        pl.when(zz < z)(lambda: send_plane(zz, False).wait_send())
        pl.when(zz > z)(lambda: send_plane(zz, True).wait_send())


def woven_scratch(planes, rows, widths):
    columns = sum(widths)
    a, b, w = split(columns, EARLY, STEP_PIECE)
    half = 4 * planes * rows
    return [
        pltpu.VMEM((planes, 2, 2, rows, columns), BF),
        pltpu.VMEM((planes, 2, rows, a + b), BF),
        pltpu.VMEM((planes, rows, a + b), BF),
        pltpu.VMEM((planes + 1, rows, a + b), BF),
        pltpu.VMEM((planes + 1, 2, 2, rows, w), BF),
        pltpu.VMEM((3, rows, w), BF),
        pltpu.VMEM((len(widths), half, TOKENS), BF),
        pltpu.VMEM((TOKENS, columns), BF),
        DMA((len(widths),)),
        DMA((len(widths),)),
        DMA((columns // STEP_PIECE,)),
        DMA((columns // STEP_PIECE,)),
        DMA((2, planes, 2)),
        DMA((2, planes, 2)),
        DMA((2, planes)),
        DMA((2, planes)),
        DMA((3, planes)),
        DMA((3, planes + 1)),
        DMA((3,)),
        DMA((3,)),
    ]


def woven_steps(pc, pairs, out_ref, scratch):
    g, r2, r3, rz, rw, rt, la, rb, as_, ar, bs, br, s2, q2, s3, q3, sz, qz, st, qt = scratch
    Z, z, x, y, c = pc.Z, pc.z, pc.x, pc.y, pc.c
    rows = g.shape[3]
    widths = split(g.shape[-1], EARLY, STEP_PIECE)
    w = widths[2]
    depth = 4 * rows

    def cols(p):
        return part_columns(widths, p)

    def got(p):
        return pl.ds(p * widths[0], widths[p])

    pieces = []
    base = 0
    for i, (left, right) in enumerate(pairs):
        for at in range(0, right.shape[1], STEP_PIECE):
            pieces.append((i, at, base + at))
        base += right.shape[1]

    def acopy(i):
        return rcopy(pc, pairs[i][0].at[1 - c], la.at[i], as_.at[i], ar.at[i], "c")

    def bcopy(k):
        i, at, to = pieces[k]
        return rcopy(
            pc, pairs[i][1].at[:, pl.ds(at, STEP_PIECE)], rb.at[:, pl.ds(to, STEP_PIECE)], bs.at[k], br.at[k], "c"
        )

    def make(zz, k, first):
        i, at, to = pieces[k]
        if first:
            if at == 0:
                acopy(i).wait_recv()
            bcopy(k).wait_recv()
        here = pl.ds(pl.multiple_of(zz * depth, depth), depth)
        mine, theirs = pairs[i][0][c, here, :], la[i, here, :]
        for t in range(0, STEP_PIECE, 512):
            tile = nn(mine, pairs[i][1][:, pl.ds(at + t, 512)]) + nn(theirs, rb[:, pl.ds(to + t, 512)])
            g[zz, :, :, :, pl.ds(to + t, 512)] = tile.reshape(2, 2, rows, 512).astype(BF)

    def copy2(p, zz, j):
        xx, yy = (x if j == 0 else 1 - x, 1 - y) if p == 0 else (1 - x, y if j == 0 else 1 - y)
        return rcopy(
            pc, g.at[zz, xx, yy, :, cols(p)], r2.at[zz, j, :, got(p)], s2.at[p, zz, j], q2.at[p, zz, j],
            "y" if p == 0 else "x",
        )

    def copy3(p, zz):
        xx, yy = (1 - x, y) if p == 0 else (x, 1 - y)
        return rcopy(
            pc, g.at[zz, xx, yy, :, cols(p)], r3.at[zz, :, got(p)], s3.at[p, zz], q3.at[p, zz],
            "x" if p == 0 else "y",
        )

    def views(p, zz, slot):
        if p == 2:
            return g.at[zz, :, :, :, cols(p)], rw.at[slot]
        return g.at[zz, x, y, :, cols(p)], rz.at[slot, :, got(p)]

    def sendz(p, zz, up):
        slot = jnp.where(zz == z + 1, Z, zz) if up else zz
        src, dst = views(p, zz, slot)
        return rcopy(pc, src, dst, sz.at[p, zz], qz.at[p, slot], "u" if up else "d")

    def gotz(p, slot):
        src, dst = views(p, 0, slot)
        rcopy(pc, src, dst, sz.at[p, 0], qz.at[p, slot], "c").wait_recv()

    def add_plane(zz, slots):
        for xx in (0, 1):
            for yy in (0, 1):
                a = g.at[zz, xx, yy, :, cols(2)]
                add_into(a, [a] + [rw.at[k, xx, yy] for k in slots])

    def at_time(t, f):
        below, above = t - (Z - 1 - z), Z - 1 - (t - z)
        pl.when((below >= 0) & (below < z))(lambda: f(below, False, pc.up))
        pl.when((above > z) & (above < Z))(lambda: f(above, True, pc.down))

    def chain_first(zz, up, more):
        @pl.when(more)
        def _():
            gotz(2, zz)
            add_plane(zz, [zz])

        sendz(2, zz, up).start()

    def tail(k):
        if k < 2:
            return rcopy(pc, g.at[z, k, 1 - y, :, cols(2)], rt.at[k], st.at[k], qt.at[k], "y")
        return rcopy(pc, g.at[z, 1 - x, y, :, cols(2)], rt.at[2], st.at[2], qt.at[2], "x")

    for i in range(len(pairs)):
        acopy(i).start()
        for k in range(len(pieces)):
            if pieces[k][0] == i:
                bcopy(k).start()
    yield
    ends = {w + widths[0]: 0, w + widths[0] + widths[1]: 1}
    for k in range(Z + 1):
        if k < Z:
            zz = pc.zord(k)
            for n in range(len(pieces)):
                make(zz, n, k == 0)
                end = pieces[n][2] + STEP_PIECE
                if end == w and k == 0 and Z > 1:
                    at_time(0, chain_first)
                if end in ends:
                    copy2(ends[end], zz, 1).start()
            yield
        if k > 0:
            zz = pc.zord(k - 1)
            for p in (0, 1):
                copy2(p, zz, 1).wait_recv()
                a = g.at[(zz,) + ((1 - x, y) if p == 0 else (x, 1 - y)) + (slice(None), cols(p))]
                add_into(a, [a, r2.at[zz, 1, :, got(p)]])
                copy3(p, zz).start()
            for p in (0, 1):
                copy2(p, zz, 0).start()
            if 0 < k - 1 < Z - 1:
                at_time(k - 1, chain_first)
            yield

    def own(p, zz):
        copy2(p, zz, 0).wait_recv()
        copy3(p, zz).wait_recv()
        a = g.at[zz, x, y, :, cols(p)]
        return a, [a, r2.at[zz, 0, :, got(p)], r3.at[zz, :, got(p)]]

    def chain(p, zz, up, more):
        a, parts = own(p, zz)

        @pl.when(more)
        def _():
            gotz(p, zz)
            add_into(a, parts + [rz.at[zz, :, got(p)]])

        @pl.when(jnp.logical_not(more))
        def _():
            add_into(a, parts)

        sendz(p, zz, up).start()

    def gather_plane(slot):
        gotz(2, slot)
        add_plane(z, [slot])

    pl.when(pc.up)(lambda: gather_plane(z))
    pl.when(pc.down)(lambda: gather_plane(Z))
    for k in (0, 1):
        tail(k).start()
    yield
    for t in range(Z - 1):
        for p in (0, 1):
            at_time(t, functools.partial(chain, p))
        if t == 0:
            for k in (0, 1):
                tail(k).wait_recv()
                a = g.at[z, k, y, :, cols(2)]
                add_into(a, [a, rt.at[k]])
            tail(2).start()
        yield
    tail(2).wait_recv()
    add_into(out_ref.at[:, cols(2)], [g.at[z, x, y, :, cols(2)], rt.at[2]])
    for p in (0, 1):
        a, parts = own(p, z)
        o = out_ref.at[:, cols(p)]
        add_into(o, parts)

        def last(slot):
            gotz(p, slot)
            add_into(o, [o, rz.at[slot, :, got(p)]])

        pl.when(pc.up)(lambda: last(z))
        pl.when(pc.down)(lambda: last(Z))
        yield
    for i in range(len(pairs)):
        acopy(i).wait_send()
    for k in range(len(pieces)):
        bcopy(k).wait_send()
    for k in range(3):
        tail(k).wait_send()
    for zz in range(Z):
        for p in (0, 1):
            for j in (0, 1):
                copy2(p, zz, j).wait_send()
            copy3(p, zz).wait_send()
        for p in (0, 1, 2):
            pl.when(zz < z)(lambda: sendz(p, zz, False).wait_send())
            pl.when(zz > z)(lambda: sendz(p, zz, True).wait_send())


def scatter_kernel(planes, count, *refs):
    pc = Place(planes)
    greet_planes(pc)
    pairs = tuple(zip(refs[:count], refs[count : 2 * count]))
    for _ in scatter_steps(pc, pairs, refs[2 * count], refs[2 * count + 1 :], LAST):
        pass


def scatter_rows(planes, lefts, rights, collective):
    rows = lefts[0].shape[1] // (4 * planes)
    widths = [r.shape[1] for r in rights]
    return pl.pallas_call(
        functools.partial(scatter_kernel, planes, len(lefts)),
        out_shape=jax.ShapeDtypeStruct((rows, sum(widths)), F32),
        in_specs=[VM] * (2 * len(lefts)),
        out_specs=VM,
        scratch_shapes=scatter_scratch(planes, rows, widths, LAST),
        compiler_params=params(collective),
    )(*lefts, *rights)


def by_core(rows, planes):
    tokens = rows.shape[0]
    each = D // (8 * planes)
    cut = rows.T.reshape(2 * planes, 2, 2 * each, tokens)
    return cut.transpose(1, 0, 2, 3).reshape(2, D // 2, tokens)


def fold_scratch(planes, rows, columns):
    return [
        pltpu.VMEM((planes, 2, rows, columns), BF),
        pltpu.VMEM((planes, rows, columns), BF),
        pltpu.VMEM((planes, rows, columns), BF),
        pltpu.VMEM((planes, 2, rows, columns), BF),
        DMA((planes, 2)),
        DMA((planes, 2)),
        DMA((planes,)),
        DMA((planes,)),
        DMA((planes,)),
        DMA((planes,)),
    ]


def fold_steps(pc, block, out_ref, scratch):
    rc, rx, rz, acc, cs, cr, xs, xr, zs, zr = scratch
    Z, z, x, c = pc.Z, pc.z, pc.x, pc.c

    def ccopy(zz, q):
        xx = x if q == 0 else 1 - x
        return rcopy(pc, block(pc.spot(zz, xx, 1 - c)), rc.at[zz, q], cs.at[zz, q], cr.at[zz, q], "c")

    def xcopy(zz):
        return rcopy(pc, acc.at[zz, 1], rx.at[zz], xs.at[zz], xr.at[zz], "x")

    def zcopy(zz):
        return rcopy(pc, acc.at[zz, 0], rz.at[zz], zs.at[zz], zr.at[zz], "d")

    def each(f):
        for zz in range(Z):
            pl.when(zz <= z)(functools.partial(f, zz))

    def a(zz):
        ccopy(zz, 1).start()
        ccopy(zz, 0).start()

    def b(zz):
        ccopy(zz, 1).wait_recv()
        add_into(acc.at[zz, 1], [block(pc.spot(zz, 1 - x, c)), rc.at[zz, 1]], 128)
        xcopy(zz).start()

    def m(zz):
        ccopy(zz, 0).wait_recv()
        add_into(acc.at[zz, 0], [block(pc.spot(zz, x, c)), rc.at[zz, 0]], 128)

    def e(zz):
        xcopy(zz).wait_recv()

        def finish(parts):
            @pl.when(zz < z)
            def _():
                add_into(acc.at[zz, 0], parts, 128)
                zcopy(zz).start()

            pl.when(zz == z)(lambda: add_into(out_ref, parts, 128))

        @pl.when(pc.up)
        def _():
            zcopy(zz).wait_recv()
            finish([acc.at[zz, 0], rx.at[zz], rz.at[zz]])

        pl.when(jnp.logical_not(pc.up))(lambda: finish([acc.at[zz, 0], rx.at[zz]]))

    def w(zz):
        ccopy(zz, 1).wait_send()
        ccopy(zz, 0).wait_send()
        xcopy(zz).wait_send()
        pl.when(zz < z)(lambda: zcopy(zz).wait_send())

    for f in (a, b, m, e):
        each(f)
        yield
    each(w)


def relay_scratch(planes):
    n = 4 * planes
    piece = pltpu.VMEM((n, NS // n, INNER), BF)
    return [piece, piece, DMA((n,)), DMA((n,)), DMA((n,)), DMA((n,))]


def relay_steps(pc, reverse, s_ref, dec_ref, out_ref, scratch):
    got, part, ss, sr, bs, br = scratch
    n = 4 * pc.Z
    me = pc.ctx

    def to(d):
        return lax.rem(me + d, n)

    def there(d):
        return rcopy(pc, s_ref.at[to(d)], got.at[me], ss.at[d], sr.at[d], (to(d), pc.y))

    def back(d):
        return rcopy(pc, part.at[to(d)], out_ref.at[me], bs.at[d], br.at[d], (to(d), pc.y))

    pl.loop(1, n)(lambda d: there(d).start())
    got[me] = s_ref[me]
    yield
    pl.loop(1, n)(lambda d: there(d).wait_recv())
    total = jnp.zeros(got.shape[1:], F32)
    for k in range(n):
        j = n - 1 - k if reverse else k
        part[j] = total.astype(BF)
        total = total * dec_ref[pl.ds(j, 1), :] + got[j].astype(F32)
    pl.loop(1, n)(lambda d: back(d).start())
    out_ref[me] = part[me]
    yield
    pl.loop(1, n)(lambda d: back(d).wait_recv())
    yield

    @pl.loop(1, n)
    def _(d):
        there(d).wait_send()
        back(d).wait_send()


def total_scratch(planes):
    shape = (SMALL_ROWS, 128)
    return [
        pltpu.VMEM((6,) + shape, F32),
        pltpu.VMEM((planes,) + shape, F32),
        DMA((3,)),
        DMA((3,)),
        DMA((planes,)),
        DMA((planes,)),
    ]


def total_steps(pc, out_ref, scratch):
    rx, rz, ss, sr, zs, zr = scratch
    Z, z = pc.Z, pc.z
    for i, d in enumerate("cxy"):
        rx[2 * i] = out_ref[...]
        cp = rcopy(pc, rx.at[2 * i], rx.at[2 * i + 1], ss.at[i], sr.at[i], d)
        cp.start()
        yield
        cp.wait()
        out_ref[...] = out_ref[...] + rx[2 * i + 1]
    rz[z] = out_ref[...]
    copies = [rcopy(pc, rz.at[z], rz.at[z], zs.at[d], zr.at[d], to) for d, to in enumerate(plane_peers(pc))]
    for cp in copies:
        cp.start()
    yield
    for cp in copies:
        cp.wait()
    total = rz[0]
    for k in range(1, Z):
        total = total + rz[k]
    out_ref[...] = total


def visible(start, block, pos_ref):
    kpos = start + lax.broadcasted_iota(jnp.int32, (block, pos_ref.shape[1]), 0)
    return (kpos <= pos_ref[0:1, :]) & (kpos >= pos_ref[1:2, :])


def split_heads(src, dst, scale=None):
    rows = src.shape[0]
    for h in range(QUERY_HEADS):
        v = src[:, pl.ds(h * HEAD_WIDTH, HEAD_WIDTH)]
        dst[pl.ds(h * rows, rows), :] = v if scale is None else v * scale


def swap_halves(v):
    width = v.shape[1]
    lane = lax.broadcasted_iota(jnp.int32, v.shape, 1)
    low = lax.rem(lane, HEAD_WIDTH) < HEAD_WIDTH // 2
    ahead = pltpu.roll(v, width - HEAD_WIDTH // 2, 1)
    behind = pltpu.roll(v, HEAD_WIDTH // 2, 1)
    return jnp.where(low, ahead, behind)


def rotate(v, cos_ref, sin_ref, sign=1.0):
    return v * cos_ref[...] + swap_halves(v) * (sign * sin_ref[...])


def attend_block(j, block, q_ref, kv, pos_ref, m_ref, l_ref, acc_ref, heads):
    rows = pos_ref.shape[1]
    start = pl.multiple_of(j * block, block)
    ok = visible(start, block, pos_ref)
    for h in heads:
        g = h // (QUERY_HEADS // KEY_VALUE_HEADS)
        keys = kv[:, g * HEAD_WIDTH : (g + 1) * HEAD_WIDTH]
        vals = kv[:, KEY_WIDTH + g * HEAD_WIDTH : KEY_WIDTH + (g + 1) * HEAD_WIDTH]
        s = jnp.where(ok, nt(keys, q_ref[pl.ds(h * rows, rows), :]), large_negative)
        m0 = m_ref[h : h + 1, :]
        m1 = jnp.maximum(m0, jnp.max(s, axis=0, keepdims=True))
        p = jnp.where(ok, jnp.exp(s - m1), 0.0)
        a = jnp.exp(m0 - m1)
        l_ref[h : h + 1, :] = l_ref[h : h + 1, :] * a + jnp.sum(p, axis=0, keepdims=True)
        m_ref[h : h + 1, :] = m1
        r = pl.ds(h * HEAD_WIDTH, HEAD_WIDTH)
        acc_ref[r, :] = acc_ref[r, :] * a + tn(vals, p.astype(BF))


def attend_end(o_ref, lse_ref, m_ref, l_ref, acc_ref):
    lse_ref[...] = m_ref[...] + jnp.log(l_ref[...])
    inv = 1.0 / l_ref[...]
    for h in range(QUERY_HEADS):
        r = pl.ds(h * HEAD_WIDTH, HEAD_WIDTH)
        acc_ref[r, :] = acc_ref[r, :] * inv[h : h + 1, :]
    o_ref[...] = acc_ref[...].T.astype(o_ref.dtype)


def attend_back_block(j, g, block, q_ref, do_ref, kv_ref, pos_ref, lse_ref, dl_ref, dkv_ref, acc_ref):
    rows = pos_ref.shape[1]
    start = pl.multiple_of(j * block, block)
    ok = visible(start, block, pos_ref)
    at = pl.ds(start, block)
    keys = kv_ref[at, pl.ds(g * HEAD_WIDTH, HEAD_WIDTH)]
    vals = kv_ref[at, pl.ds(KEY_WIDTH + g * HEAD_WIDTH, HEAD_WIDTH)]
    dk = dv = None
    for h in range(4 * g, 4 * g + 4):
        q = q_ref[pl.ds(h * rows, rows), :]
        do = do_ref[pl.ds(h * rows, rows), :]
        p = jnp.where(ok, jnp.exp(nt(keys, q) - lse_ref[h : h + 1, :]), 0.0)
        ds = (p * (nt(vals, do) - dl_ref[h : h + 1, :])).astype(BF)
        r = pl.ds(h * HEAD_WIDTH, HEAD_WIDTH)
        acc_ref[r, :] += tn(keys, ds)
        a, b = nn(ds, q), nn(p.astype(BF), do)
        dk = a if dk is None else dk + a
        dv = b if dv is None else dv + b
    dkv_ref[at, pl.ds(g * HEAD_WIDTH, HEAD_WIDTH)] = dk.astype(BF)
    dkv_ref[at, pl.ds(KEY_WIDTH + g * HEAD_WIDTH, HEAD_WIDTH)] = dv.astype(BF)


def two(left, right, lanes):
    return jnp.where(lanes < MP, left, right)


def pair_columns(ref, p, lanes):
    return two(ref[:, 2 * p : 2 * p + 1], ref[:, 2 * p + 1 : 2 * p + 2], lanes)


def mixer_steps(
    xe, mk, cw, cb, cum_t, cum, dt_t, we_t, skip, doc_c, doc_r, pre, xo, mix, so, xw, bias
):
    rows = pre.shape[0]
    for i in range(XBC // 256):
        sl = pl.ds(i * 256, 256)
        acc = jnp.broadcast_to(cb[:, sl], (rows, 256))
        for j in range(CONV):
            acc = acc + cw[j : j + 1, sl] * (xe[pl.ds(5 + j, rows), sl] * mk[:, j : j + 1])
        pre[:, sl] = acc.astype(BF)
        act = acc * jax.nn.sigmoid(acc)
        xo[:, sl] = act.astype(BF)
        if i < INNER // 256:
            mix[:, sl] = skip[:, sl] * act
        if i == 3:
            yield
    yield
    b_rows, c_rows = xo[:, pl.ds(INNER, NS)], xo[:, pl.ds(INNER + NS, NS)]
    cross = nt(c_rows, b_rows)
    t_at = lax.broadcasted_iota(jnp.int32, (rows, rows), 0)
    s_at = lax.broadcasted_iota(jnp.int32, (rows, rows), 1)
    bias[...] = jnp.where((doc_c[...] == doc_r[...]) & (s_at <= t_at), 0.0, large_negative)
    lanes = lax.broadcasted_iota(jnp.int32, (rows, 2 * MP), 1)
    for p in range(MH // 2):
        sl = pl.ds(p * 2 * MP, 2 * MP)
        xd = xo[:, sl].astype(F32) * pair_columns(dt_t, p, lanes)
        xw[:, sl] = (xd * pair_columns(we_t, p, lanes)).astype(BF)
        xb = xd.astype(BF)
        outs = []
        for h in (2 * p, 2 * p + 1):
            low = jnp.exp(jnp.minimum(cum_t[:, h : h + 1] - cum[h : h + 1, :], bias[...]))
            outs.append(nn((low * cross).astype(BF), xb))
        mix[:, sl] = mix[:, sl] + two(outs[0], outs[1], lanes)
        if p % 3 == 2:
            yield
    so[...] = tn(b_rows, xw[...]).astype(BF).reshape(so.shape)


def spread_heads():
    head = lax.broadcasted_iota(jnp.int32, (MH, INNER), 0)
    lane = lax.broadcasted_iota(jnp.int32, (MH, INNER), 1)
    return (lane // MP == head).astype(F32)


def exact(a, b, dims):
    return lax.dot_general(
        a, b, (dims, ((), ())), precision=lax.Precision.HIGHEST, preferred_element_type=F32
    )


def wide(columns, spread_mat):
    return exact(columns, spread_mat, ((1,), (0,)))


def gate_kernel(planes, lens, mix, xo, state_in, ldec, gate, small, att, mixed, branch, gain, state, din_t):
    rows = mix.shape[0]
    spread_mat = spread_heads()
    unpack(small, "gate", gain)
    state[...] = state_in[...].reshape(state.shape)
    first = Place(planes).ctx * rows
    a = lax.broadcasted_iota(jnp.int32, (rows, rows), 0)
    b = lax.broadcasted_iota(jnp.int32, (rows, rows), 1)
    docs = doc_of(first + lax.broadcasted_iota(jnp.int32, (rows, 1), 0), lens)
    before = doc_of(jnp.full((1, 1), first - 1, jnp.int32), lens)
    ct = exact((b <= a).astype(F32), ldec[...], ((1,), (1,)))
    din_t[...] = jnp.where(docs == before, jnp.exp(ct), 0.0)

    @pl.loop(0, rows // 64)
    def _(i):
        r = pl.ds(pl.multiple_of(i * 64, 64), 64)
        carried = nn(xo[r, pl.ds(INNER + NS, NS)], state[...])
        m = mix[r, :] + carried * wide(din_t[r, :], spread_mat)
        mixed[r, :] = m.astype(BF)
        gv = gate[r, :]
        gated = m * (gv * jax.nn.sigmoid(gv))
        factor = lax.rsqrt(jnp.mean(gated * gated, axis=1, keepdims=True) + norm_eps)
        branch[r, pl.ds(0, QUERY_WIDTH)] = att[r, :]
        branch[r, pl.ds(QUERY_WIDTH, INNER)] = (gated * factor * gain[...]).astype(BF)


def gate_out(planes, lens, mix, xo, state, ldec, gate, small, att):
    rows = mix.shape[0]
    return pl.pallas_call(
        functools.partial(gate_kernel, planes),
        out_shape=(
            jax.ShapeDtypeStruct((rows, INNER), BF),
            jax.ShapeDtypeStruct((rows, MIXOUT), BF),
        ),
        in_specs=[SM] + [VM] * 7,
        out_specs=(VM,) * 2,
        scratch_shapes=[
            pltpu.VMEM((1, INNER), F32),
            pltpu.VMEM((NS, INNER), BF),
            pltpu.VMEM((rows, MH), F32),
        ],
        compiler_params=params(),
    )(lens, mix, xo, state, ldec, gate, small, att)


def doc_of(pos, lens):
    start = 0
    found = jnp.full_like(pos, -1)
    for d in range(lens.shape[1]):
        found = found + (pos >= start).astype(jnp.int32)
        start = start + lens[0, d]
    return found


def begin_of(pos, lens):
    start = 0
    found = jnp.zeros_like(pos)
    for d in range(lens.shape[1]):
        found = jnp.maximum(found, jnp.where(pos >= start, start, 0))
        start = start + lens[0, d]
    return found


def table_scratch(rows):
    return [
        pltpu.VMEM((2, rows), jnp.int32),
        pltpu.VMEM((rows, 8), F32),
        pltpu.VMEM((rows, 1), jnp.int32),
        pltpu.VMEM((1, rows), jnp.int32),
        pltpu.VMEM((MH, rows), F32),
        pltpu.VMEM((rows, MH), F32),
        pltpu.VMEM((rows, MH), F32),
        pltpu.VMEM((rows, MH), F32),
        pltpu.VMEM((rows, MH), F32),
    ]


def make_tables(pc, lens, ldec, root_t, tables):
    pos, same, doc_c, doc_r, cum, cum_t, dt_t, we_t, din_t = tables
    rows = ldec.shape[1]
    first = pc.ctx * rows
    at_c = first + lax.broadcasted_iota(jnp.int32, (rows, 1), 0)
    at_r = first + lax.broadcasted_iota(jnp.int32, (1, rows), 1)
    pos[0:1, :] = at_r
    pos[1:2, :] = begin_of(at_r, lens)
    dc = doc_of(at_c, lens)
    doc_c[...] = dc
    doc_r[...] = doc_of(at_r, lens)
    for j in range(CONV):
        same[:, j : j + 1] = (doc_of(at_c - (CONV - 1) + j, lens) == dc).astype(F32)
        same[:, CONV + j : CONV + j + 1] = (doc_of(at_c + (CONV - 1) - j, lens) == dc).astype(F32)
    a = lax.broadcasted_iota(jnp.int32, (rows, rows), 0)
    b = lax.broadcasted_iota(jnp.int32, (rows, rows), 1)
    cum[...] = exact(ldec[...], (a <= b).astype(F32), ((1,), (0,)))
    ct = exact((b <= a).astype(F32), ldec[...], ((1,), (1,)))
    cum_t[...] = ct
    fresh = doc_of(at_c - 1, lens) != dc
    dt_t[...] = jnp.where(fresh, 1.0, root_t[...])
    before = doc_of(jnp.full((1, 1), first - 1, jnp.int32), lens)
    end = doc_of(jnp.full((1, 1), first + rows - 1, jnp.int32), lens)
    din_t[...] = jnp.where(dc == before, jnp.exp(ct), 0.0)
    we_t[...] = jnp.where(dc == end, jnp.exp(jnp.minimum(ct[rows - 1 : rows, :] - ct, 0.0)), 0.0)


SMALL_AT = {"one": (0, 8), "two": (8, 8), "gate": (16, 12), "bias": (84, 14), "skip": (98, 1)}


def unpack(small, name, dst, row=0):
    at, tiles = SMALL_AT[name] if isinstance(name, str) else name
    for i in range(tiles):
        dst[row : row + 1, pl.ds(i * 128, 128)] = small[at + i : at + i + 1, :]


def unpack_conv(small, dst):
    for j in range(CONV):
        unpack(small, (28 + 14 * j, 14), dst, j)


def wide_skip(small, spread_mat, dst):
    dst[...] = wide(jnp.broadcast_to(small[98:99, 0:MH], (8, MH)), spread_mat)[0:1, :]


GATE_AT = QUERY_WIDTH + 2 * KEY_WIDTH
XBC_AT = GATE_AT + INNER
FIRST = QUERY_WIDTH + 2 * KEY_WIDTH + XBC


def front_kernel(
    planes, block, lens, hid, w1, w2, cos_w, sin_w, ldec, root_t, small,
    normed, scale, g1, g2, q_out, kv_all, xe, decays, pre, xo, mix, state_in, att, lse,
    kv_own, edge_out, edge_in, dec_own, decs, dec_rows, gains, conv_w, conv_b, skip, so, qh, m_ref, l_ref,
    acc, xw, bias, *refs,
):
    tables, refs = refs[:9], refs[9:]
    pos, same, doc_c, doc_r, cum, cum_t, dt_t, we_t, din_t = tables
    first_refs, refs = refs[:9], refs[9:]
    rest_refs, refs = refs[:9], refs[9:]
    spread_refs, refs = refs[:7], refs[7:]
    relay_refs = refs[:6]
    pc = Place(planes)
    n = 4 * planes
    rows = hid.shape[0]
    greet_row(pc, True)
    gather = gather_steps(pc, w1, g1, first_refs, EVEN)
    rest = gather_steps(pc, w2, g2, rest_refs, REST)
    next(gather)

    def pump(count=1):
        for _ in range(count):
            next(rest, None)

    unpack(small, "one", gains)
    unpack(small, "bias", conv_b)
    unpack_conv(small, conv_w)
    spread_mat = spread_heads()
    wide_skip(small, spread_mat, skip)
    for i in range(rows // 64):
        r = pl.ds(i * 64, 64)
        v = hid[r, :].astype(F32)
        f = lax.rsqrt(jnp.mean(v * v, axis=1, keepdims=True) + norm_eps)
        scale[r, :] = f
        normed[r, :] = (v * f * gains[...]).astype(BF)
        next(gather)
    make_tables(pc, lens, ldec, root_t, tables)
    dec_own[...] = jnp.zeros_like(dec_own)
    dec_own[0:1, 0:MH] = din_t[rows - 1 : rows, :]
    for k, _ in enumerate(gather):
        if k == planes:
            pump()

    def project(at, width):
        return nn(normed[...], g1[:, :, :, :, :, pl.ds(at, width)].reshape(D, width))

    base = GATE_AT
    for i in range(XBC // 256):
        sl = pl.ds(i * 256, 256)
        xb = project(base + i * 256, 256).astype(BF)
        xe[pl.ds(8, rows), sl] = xb.astype(F32)
        edge_out[:, sl] = xb[rows - 16 :, :]
    kv = project(QUERY_WIDTH, 2 * KEY_WIDTH)
    kv_own[:, pl.ds(0, KEY_WIDTH)] = rotate(kv[:, :KEY_WIDTH], cos_w, sin_w).astype(BF)
    kv_own[:, pl.ds(KEY_WIDTH, KEY_WIDTH)] = kv[:, KEY_WIDTH:].astype(BF)
    spreads = spread_steps(pc, kv_own, edge_out, dec_own, kv_all, edge_in, decs, spread_refs)
    next(spreads)
    for i in range(QUERY_WIDTH // 256):
        qv = project(i * 256, 256)
        for t in (0, 1):
            q_out[:, pl.ds(i * 256 + t * 128, 128)] = rotate(
                qv[:, t * 128 : (t + 1) * 128], cos_w, sin_w
            ).astype(BF)
    split_heads(q_out, qh, jnp.asarray(HEAD_WIDTH**-0.5, BF))
    next(spreads)
    xe[pl.ds(0, 8), :] = edge_in[pl.ds(8, 8), :].astype(F32)
    pump()
    next(spreads)
    mixing = mixer_steps(
        xe, same, conv_w, conv_b, cum_t, cum, dt_t, we_t, skip, doc_c, doc_r, pre, xo, mix, so, xw, bias
    )
    for _ in mixing:
        next(spreads, None)
        pump()
    for k in range(n):
        dec_rows[k : k + 1, :] = decs[k, 0:1, :]
    decays[...] = wide(dec_rows[:, 0:MH], spread_mat)
    states = relay_steps(pc, False, so, decays, state_in, relay_refs)
    next(states)
    m_ref[...] = jnp.full_like(m_ref, large_negative)
    l_ref[...] = jnp.zeros_like(l_ref)
    acc[...] = jnp.zeros_like(acc)
    seen = (pc.ctx * rows + rows + block - 1) // block
    per = block // rows
    parts = 8
    each = n // per // parts

    def keys_at(j):
        return kv_all[pl.ds(j * per, per), :, :].reshape(block, 2 * KEY_WIDTH)

    for k in range(parts):
        lo = each * k

        @pl.loop(jnp.minimum(lo, seen), jnp.minimum(lo + each, seen))
        def _(j):
            attend_block(j, block, qh, keys_at(j), pos, m_ref, l_ref, acc, range(QUERY_HEADS))

        pump(2)
        if k in (3, 6):
            next(states)
    attend_end(att, lse, m_ref, l_ref, acc)
    for _ in spreads:
        pass
    for _ in rest:
        pass
    for _ in states:
        pass


def front(planes, lens, hid, w1, w2, cos_w, sin_w, ldec, root_t, small, block, collective):
    n = 4 * planes
    rows = hid.shape[0]
    each = w1.shape[0]
    sds = jax.ShapeDtypeStruct
    return pl.pallas_call(
        functools.partial(front_kernel, planes, block),
        out_shape=(
            sds((rows, D), BF),
            sds((rows, 1), F32),
            sds((planes, 2, 2, 2, each, w1.shape[1]), BF),
            sds((planes, 2, 2, 2, each, w2.shape[1]), BF),
            sds((rows, QUERY_WIDTH), BF),
            sds((n, rows, 2 * KEY_WIDTH), BF),
            sds((rows + 8, XBC), F32),
            sds((n, INNER), F32),
            sds((rows, XBC), BF),
            sds((rows, XBC), BF),
            sds((rows, INNER), F32),
            sds((n, NS // n, INNER), BF),
            sds((rows, QUERY_WIDTH), BF),
            sds((QUERY_HEADS, rows), F32),
        ),
        in_specs=[SM, VM, VM, HB] + [VM] * 5,
        out_specs=(VM, VM, VM, HB) + (VM,) * 10,
        scratch_shapes=[
            pltpu.VMEM((rows, 2 * KEY_WIDTH), BF),
            pltpu.VMEM((16, XBC), BF),
            pltpu.VMEM((16, XBC), BF),
            pltpu.VMEM((8, 128), F32),
            pltpu.VMEM((n, 8, 128), F32),
            pltpu.VMEM((n, 128), F32),
            pltpu.VMEM((1, D), F32),
            pltpu.VMEM((CONV, XBC), F32),
            pltpu.VMEM((1, XBC), F32),
            pltpu.VMEM((1, INNER), F32),
            pltpu.VMEM((n, NS // n, INNER), BF),
            pltpu.VMEM((QUERY_HEADS * rows, HEAD_WIDTH), BF),
            pltpu.VMEM((QUERY_HEADS, rows), F32),
            pltpu.VMEM((QUERY_HEADS, rows), F32),
            pltpu.VMEM((QUERY_WIDTH, rows), F32),
            pltpu.VMEM((rows, INNER), BF),
            pltpu.VMEM((rows, rows), F32),
        ]
        + table_scratch(rows)
        + gather_scratch(planes)
        + gather_scratch(planes)
        + spread_scratch(planes)
        + relay_scratch(planes),
        compiler_params=params(collective),
    )(lens, hid, w1, w2, cos_w, sin_w, ldec, root_t, small)


def gate_back_rows(i, grad, mixed, gate, gain, din_t, spread_mat, dm, dproj, dgain, dinc):
    r = pl.ds(pl.multiple_of(i * 64, 64), 64)
    m, gv, gr = mixed[r, :].astype(F32), gate[r, :], grad[r, pl.ds(QUERY_WIDTH, INNER)]
    sig = jax.nn.sigmoid(gv)
    sil = gv * sig
    gated = m * sil
    factor = lax.rsqrt(jnp.mean(gated * gated, axis=1, keepdims=True) + norm_eps)
    w = gr * gain[...]
    dg = factor * (w - gated * factor * factor * jnp.mean(w * gated, axis=1, keepdims=True))
    dgain[...] += jnp.sum(gr * gated * factor, axis=0, keepdims=True)
    dproj[r, pl.ds(GATE_AT, INNER)] = (dg * m * (sig * (1.0 + gv * (1.0 - sig)))).astype(BF)
    d = dg * sil
    dm[r, :] = d.astype(BF)
    dinc[r, :] = (d * wide(din_t[r, :], spread_mat)).astype(BF)


def mixer_back_steps(
    xe, mk, cw, cum_t, cum, dt_t, we_t, skip, doc_c, doc_r, pre, xo, dm, dc_in, ds, dpre, dcw, dskip, xw, bias
):
    rows = pre.shape[0]
    here = pl.ds(0, rows)
    b_rows, c_rows = xo[:, pl.ds(INNER, NS)], xo[:, pl.ds(INNER + NS, NS)]
    cross = nt(b_rows, c_rows)
    s_at = lax.broadcasted_iota(jnp.int32, (rows, rows), 0)
    t_at = lax.broadcasted_iota(jnp.int32, (rows, rows), 1)
    bias[...] = jnp.where((doc_c[...] == doc_r[...]) & (s_at <= t_at), 0.0, large_negative)
    lanes = lax.broadcasted_iota(jnp.int32, (rows, 2 * MP), 1)

    def slope(sl):
        v = pre[:, sl].astype(F32)
        sig = jax.nn.sigmoid(v)
        return sig * (1.0 + v * (1.0 - sig))

    dcross = jnp.zeros((rows, rows), F32)
    for p in range(MH // 2):
        sl = pl.ds(p * 2 * MP, 2 * MP)
        xv = xo[:, sl].astype(F32)
        dt2, we2 = pair_columns(dt_t, p, lanes), pair_columns(we_t, p, lanes)
        xd = xv * dt2
        xw[:, sl] = (xd * we2).astype(BF)
        g = dm[:, sl]
        outs = []
        for k in (0, 1):
            h = 2 * p + k
            low = jnp.exp(jnp.minimum(cum[h : h + 1, :] - cum_t[:, h : h + 1], bias[...]))
            outs.append(nn((low * cross).astype(BF), g))
            part = jnp.where((lanes < MP) == (k == 0), xd, 0.0).astype(BF)
            dcross = dcross + nt(part, g) * low
        dxd = two(outs[0], outs[1], lanes) + we2 * nn(b_rows, ds[:, sl])
        gf = g.astype(F32)
        dskip[:, sl] = jnp.sum(gf * xv, axis=0, keepdims=True)
        dpre[here, sl] = (dxd * dt2 + skip[:, sl] * gf) * slope(sl)
        if p % 4 == 3:
            yield
    db16 = dcross.astype(BF)
    slb, slc = pl.ds(INNER, NS), pl.ds(INNER + NS, NS)
    dpre[here, slb] = (nn(db16, c_rows) + nt(xw[...], ds[...])) * slope(slb)
    dpre[here, slc] = (tn(db16, b_rows) + dc_in[...]) * slope(slc)
    yield
    for i in range(XBC // 256):
        sl = pl.ds(i * 256, 256)
        d = dpre[here, sl]
        for j in range(CONV):
            dcw[j : j + 1, sl] = jnp.sum(
                d * (xe[pl.ds(5 + j, rows), sl] * mk[:, j : j + 1]), axis=0, keepdims=True
            )
        dcw[CONV : CONV + 1, sl] = jnp.sum(d, axis=0, keepdims=True)


def back_kernel(planes, count, block, *refs):
    lefts, rights, refs = refs[:count], refs[count : 2 * count], refs[2 * count :]
    if count:
        branch = rights[2]
    else:
        branch, refs = refs[0], refs[1:]
    (
        lens, grad, mixed, gate, xo, state_in, q_in, kv, lse, cos_w, sin_w, decays, xe, ldec, root_t, small, pre,
    ) = refs[:17]
    refs = refs[17:]
    if count:
        scattered, refs = refs[0], refs[1:]
    dproj, dgain, dcw, dskip = refs[:4]
    (
        dm, dinc, dc, dstate, dsnew, flat, qh, doh, dl, acc, dkv, dkv_own, dpre, edge, bias, esem
    ) = refs[4:20]
    gain, cw, skip, state = refs[20:24]
    tables, refs = refs[24:33], refs[33:]
    pos, same, doc_c, doc_r, cum, cum_t, dt_t, we_t, din_t = tables
    relay_refs, refs = refs[:6], refs[6:]
    fold_refs, refs = refs[:10], refs[10:]
    pc = Place(planes)
    n = 4 * planes
    rows = mixed.shape[0]
    greet_row(pc, count > 0)
    side = (
        woven_steps(pc, tuple(zip(lefts, rights)), scattered, refs) if count else iter(())
    )

    def pump():
        next(side, None)

    pump()
    spread_mat = spread_heads()
    unpack(small, "gate", gain)
    unpack_conv(small, cw)
    wide_skip(small, spread_mat, skip)
    make_tables(pc, lens, ldec, root_t, tables)
    state[...] = state_in[...].reshape(state.shape)
    dgain[...] = jnp.zeros_like(dgain)
    pl.loop(0, rows // 64)(
        lambda i: gate_back_rows(i, grad, mixed, gate, gain, din_t, spread_mat, dm, dproj, dgain, dinc)
    )
    ds0 = tn(xo[:, pl.ds(INNER + NS, NS)], dinc[...]).astype(BF)
    dc[...] = nt(dinc[...], state[...])
    dstate[...] = ds0.reshape(dstate.shape)
    states = relay_steps(pc, True, dstate, decays, dsnew, relay_refs)
    next(states)
    for _ in range(planes):
        pump()
    split_heads(q_in, qh, jnp.asarray(HEAD_WIDTH**-0.5, BF))
    go = grad[:, pl.ds(0, QUERY_WIDTH)].astype(BF)
    head = lax.broadcasted_iota(jnp.int32, (QUERY_HEADS, QUERY_WIDTH), 0)
    lane = lax.broadcasted_iota(jnp.int32, (QUERY_HEADS, QUERY_WIDTH), 1)
    for h in range(QUERY_HEADS):
        doh[pl.ds(h * rows, rows), :] = go[:, h * HEAD_WIDTH : (h + 1) * HEAD_WIDTH]
    dl[...] = exact(
        (lane // HEAD_WIDTH == head).astype(F32),
        go.astype(F32) * branch[:, pl.ds(0, QUERY_WIDTH)].astype(F32),
        ((1,), (1,)),
    )
    acc[...] = jnp.zeros_like(acc)
    total = kv.shape[0] // block
    seen = (pc.ctx * rows + rows + block - 1) // block
    parts = 4
    each = total // parts

    @pl.loop(seen, (pc.z + 1) * 4 * rows // block)
    def _(j):
        dkv[pl.ds(pl.multiple_of(j * block, block), block), :] = jnp.zeros((block, 2 * KEY_WIDTH), BF)

    for k in range(parts):
        lo = each * k

        @pl.loop(jnp.minimum(lo, seen), jnp.minimum(lo + each, seen))
        def _(j):
            for g in range(KEY_VALUE_HEADS):
                attend_back_block(j, g, block, qh, doh, kv, pos, lse, dl, dkv, acc)

        pump()
        if k == 1:
            next(states)
    folds = fold_steps(
        pc, lambda s: dkv.at[pl.ds(pl.multiple_of(s * rows, rows), rows), :], dkv_own, fold_refs
    )
    next(folds)
    for t in range(QUERY_WIDTH // 128):
        dq = acc[pl.ds(t * 128, 128), :].T * (HEAD_WIDTH**-0.5)
        dproj[:, pl.ds(t * 128, 128)] = rotate(dq, cos_w, sin_w, -1.0).astype(BF)
    next(states)
    flat[...] = dsnew[...].reshape(flat.shape)
    next(folds)
    mixing = mixer_back_steps(
        xe, same, cw, cum_t, cum, dt_t, we_t, skip, doc_c, doc_r, pre, xo, dm, dc, flat, dpre, dcw, dskip, dinc, bias
    )
    next(mixing)
    next(folds)
    pump()
    next(mixing)
    pump()
    next(mixing)
    next(folds)
    pump()
    next(mixing)
    prior = rcopy(pc, dpre.at[pl.ds(0, 8), :], edge, esem.at[0], esem.at[1], (lax.rem(pc.ctx + n - 1, n), pc.y))
    pl.when(pc.ctx > 0)(lambda: prior.start())
    for _ in mixing:
        pass
    pump()
    for _ in folds:
        pass
    dproj[:, pl.ds(QUERY_WIDTH, KEY_WIDTH)] = rotate(dkv_own[:, pl.ds(0, KEY_WIDTH)], cos_w, sin_w, -1.0).astype(BF)
    dproj[:, pl.ds(QUERY_WIDTH + KEY_WIDTH, KEY_WIDTH)] = dkv_own[:, pl.ds(KEY_WIDTH, KEY_WIDTH)].astype(BF)
    pl.when(pc.ctx < n - 1)(lambda: prior.wait_recv())

    @pl.when(pc.ctx == n - 1)
    def _():
        edge[...] = jnp.zeros_like(edge)

    dpre[pl.ds(rows, 8), :] = edge[...]
    for i in range(XBC // 256):
        sl = pl.ds(i * 256, 256)
        total_grad = jnp.zeros((rows, 256), F32)
        for j in range(CONV):
            total_grad = total_grad + cw[j : j + 1, sl] * (
                dpre[pl.ds(CONV - 1 - j, rows), sl] * same[:, CONV + j : CONV + j + 1]
            )
        dproj[:, pl.ds(XBC_AT + i * 256, 256)] = total_grad.astype(BF)
    for _ in states:
        pass
    pl.when(pc.ctx > 0)(lambda: prior.wait_send())
    for _ in side:
        pass


def back(planes, lefts, rights, args, block, collective):
    count = len(lefts)
    n = 4 * planes
    rows = args[-1].shape[0]
    keys = n * rows
    outs = [
        jax.ShapeDtypeStruct((rows, MIXIN), BF),
        jax.ShapeDtypeStruct((1, INNER), F32),
        jax.ShapeDtypeStruct((CONV + 1, XBC), F32),
        jax.ShapeDtypeStruct((1, INNER), F32),
    ]
    scratch = [
        pltpu.VMEM((rows, INNER), BF),
        pltpu.VMEM((rows, INNER), BF),
        pltpu.VMEM((rows, NS), F32),
        pltpu.VMEM((n, NS // n, INNER), BF),
        pltpu.VMEM((n, NS // n, INNER), BF),
        pltpu.VMEM((NS, INNER), BF),
        pltpu.VMEM((QUERY_HEADS * rows, HEAD_WIDTH), BF),
        pltpu.VMEM((QUERY_HEADS * rows, HEAD_WIDTH), BF),
        pltpu.VMEM((QUERY_HEADS, rows), F32),
        pltpu.VMEM((QUERY_WIDTH, rows), F32),
        pltpu.VMEM((keys, 2 * KEY_WIDTH), BF),
        pltpu.VMEM((rows, 2 * KEY_WIDTH), F32),
        pltpu.VMEM((rows + 8, XBC), F32),
        pltpu.VMEM((8, XBC), F32),
        pltpu.VMEM((rows, rows), F32),
        DMA((2,)),
        pltpu.VMEM((1, INNER), F32),
        pltpu.VMEM((CONV, XBC), F32),
        pltpu.VMEM((1, INNER), F32),
        pltpu.VMEM((NS, INNER), BF),
    ]
    scratch += table_scratch(rows)
    scratch += relay_scratch(planes) + fold_scratch(planes, rows, 2 * KEY_WIDTH)
    if count:
        widths = [r.shape[1] for r in rights]
        each = lefts[0].shape[1] // n
        outs = [jax.ShapeDtypeStruct((each, sum(widths)), F32)] + outs
        scratch += woven_scratch(planes, each, widths)
    return pl.pallas_call(
        functools.partial(back_kernel, planes, count, block),
        out_shape=tuple(outs),
        in_specs=[VM] * (2 * count + (not count)) + [SM] + [VM] * (len(args) - 2 + bool(count)),
        out_specs=(VM,) * len(outs),
        scratch_shapes=scratch,
        compiler_params=params(collective),
    )(*lefts, *rights, *args)


def last_kernel(
    planes, left, dproj, w1, w2, tok, scale, packed, dres, small, scattered, dhid, totals, dn, wg, wsem, gain, *scratch
):
    pc = Place(planes)
    greet_planes(pc)
    rows = dproj.shape[0]
    fetch = pltpu.make_async_copy(w2.at[:, :, :, :, :, pl.ds(0, INNER)], wg, wsem)
    fetch.start()
    side = scatter_steps(pc, ((left, dproj),), scattered, scratch[6:], LAST)
    next(side)
    unpack(packed, "one", gain)
    fetch.wait()
    next(side)
    part = planes // 4
    for i in range(4):
        at = pl.ds(i * part, part)
        a, b = w1[at].reshape(D // 4, FIRST), wg[at].reshape(D // 4, INNER)
        dn[:, pl.ds(i * 256, 256)] = (
            nt(dproj[:, pl.ds(0, GATE_AT)], a[:, :GATE_AT])
            + nt(dproj[:, pl.ds(GATE_AT, INNER)], b)
            + nt(dproj[:, pl.ds(XBC_AT, XBC)], a[:, GATE_AT:])
        )
        next(side)
        next(side)
    totals[...] = small[...]
    for i in range(rows // 64):
        r = pl.ds(i * 64, 64)
        v, g, f = tok[r, :].astype(F32), dn[r, :], scale[r, :]
        w = g * gain[...]
        dhid[r, :] = dres[r, :] + f * (w - v * f * f * jnp.mean(w * v, axis=1, keepdims=True))
        part = jnp.sum(g * v * f, axis=0, keepdims=True)
        for t in range(D // 128):
            totals[t : t + 1, :] = totals[t : t + 1, :] + part[:, t * 128 : (t + 1) * 128]
    sums = total_steps(pc, totals, scratch[:6])
    next(sums)
    for _ in side:
        next(sums, None)
    for _ in sums:
        pass


def last(planes, left, dproj, w1, w2, tok, scale, packed, dres, small, collective):
    rows = dproj.shape[0]
    each = left.shape[1] // (4 * planes)
    return pl.pallas_call(
        functools.partial(last_kernel, planes),
        out_shape=(
            jax.ShapeDtypeStruct((each, MIXIN), F32),
            jax.ShapeDtypeStruct((rows, D), F32),
            jax.ShapeDtypeStruct((SMALL_ROWS, 128), F32),
        ),
        in_specs=[VM] * 3 + [HB] + [VM] * 5,
        out_specs=(VM,) * 3,
        scratch_shapes=[
            pltpu.VMEM((rows, D), F32),
            pltpu.VMEM(w2.shape[:-1] + (INNER,), BF),
            DMA,
            pltpu.VMEM((1, D), F32),
        ]
        + total_scratch(planes)
        + scatter_scratch(planes, each, [MIXIN], LAST),
        compiler_params=params(collective),
    )(left, dproj, w1, w2, tok, scale, packed, dres, small)


def doc_layout(lengths, token_positions):
    starts = jnp.cumsum(lengths) - lengths
    inside = token_positions[:, None] >= starts[None, :]
    document_index = jnp.sum(inside.astype(jnp.int32), axis=1) - 1
    begins = jnp.max(jnp.where(inside, starts[None, :], 0), axis=1)
    return (document_index, token_positions - begins)


def rope_tables(rel_pos):
    half_dim = HEAD_WIDTH // 2
    inv_freq = rope_base ** (-2.0 * jnp.arange(half_dim, dtype=jnp.float32) / HEAD_WIDTH)
    angles = rel_pos.astype(jnp.float32)[:, None] * inv_freq[None, :]
    return (jnp.cos(angles), jnp.sin(angles))


def norm_backward(grad_normed, values, factor, gain_vals):
    weighted = grad_normed * gain_vals
    grad_values = factor * (
        weighted - values * factor * factor * jnp.mean(weighted * values, axis=1, keepdims=True)
    )
    grad_gain = jnp.sum(grad_normed * values * factor, axis=0)
    return (grad_values, grad_gain)


def adamw_step(param_vals, grad_vals, first_vals, second_vals, weight_decay):
    first_new = beta_one * first_vals + (1.0 - beta_one) * grad_vals
    second_new = beta_two * second_vals + (1.0 - beta_two) * grad_vals * grad_vals
    update = (
        first_new
        / (1.0 - beta_one**STEP)
        / (jnp.sqrt(second_new / (1.0 - beta_two**STEP)) + adam_eps)
    )
    return (param_vals - learn_rate * (update + weight_decay * param_vals), first_new, second_new)


def adam_direction(grad_vals, first_vals, second_vals):
    first_new = beta_one * first_vals + (1.0 - beta_one) * grad_vals
    second_new = beta_two * second_vals + (1.0 - beta_two) * grad_vals * grad_vals
    update = (
        first_new
        / (1.0 - beta_one**STEP)
        / (jnp.sqrt(second_new / (1.0 - beta_two**STEP)) + adam_eps)
    )
    return (update, first_new, second_new)


def shards(
    planes,
    hidden,
    out_grad,
    decay_log,
    doc_lengths,
    weights,
    first_moment,
    second_moment,
    small_params,
    small_first,
    small_second,
):
    local_rows = hidden.shape[1]
    count = 4 * planes
    ctx_index = lax.axis_index("ctx")
    first_pos = ctx_index * local_rows
    contract_last = (((1,), (1,)), ((), ()))
    lengths = doc_lengths[0]
    token_positions = first_pos + jnp.arange(local_rows, dtype=jnp.int32)
    cosine_table, sine_table = rope_tables(doc_layout(lengths, token_positions)[1])
    cos_wide = jnp.tile(cosine_table, (1, 4))
    sin_wide = jnp.tile(jnp.concatenate([-sine_table, sine_table], axis=1), (1, 2))
    size = small_params.shape[0]
    packed = jnp.pad(small_params, (0, SMALL_ROWS * 128 - size)).reshape(SMALL_ROWS, 128)
    log_decay = decay_log[0]
    root_t = jnp.sqrt(-jnp.expm1(2.0 * log_decay)).T
    block = 512
    own_b = weights.astype(jnp.bfloat16)
    own_first = jnp.concatenate([own_b[:, :GATE_AT], own_b[:, XBC_AT:MIXIN]], axis=1)
    own_rest = jnp.concatenate([own_b[:, GATE_AT:XBC_AT], own_b[:, MIXIN:]], axis=1)
    (
        normed_one, scale_one, first_w, rest_w, query_rows, kv_all, xe, decays, pre, xo, mix_local,
        state_in, attended, log_sums,
    ) = front(
        planes, doc_lengths, hidden[0], own_first, own_rest, cos_wide, sin_wide, log_decay, root_t,
        packed, block, 0,
    )
    rest_flat = rest_w.reshape(D, rest_w.shape[-1])
    mixout_w = rest_flat[:, INNER : INNER + MIXOUT]
    mlp_w = rest_flat[:, INNER + MIXOUT :]
    gate_in = jnp.dot(normed_one, rest_flat[:, :INNER], preferred_element_type=jnp.float32)
    mixed, branch = gate_out(
        planes, doc_lengths, mix_local, xo, state_in, log_decay, gate_in, packed, attended
    )

    tok_f = hidden[0].astype(jnp.float32)
    gain_two = small_params[D : 2 * D]
    resid_one = tok_f + lax.dot_general(
        branch, mixout_w, contract_last, preferred_element_type=jnp.float32
    )
    scale_two = lax.rsqrt(jnp.mean(resid_one * resid_one, axis=1, keepdims=True) + norm_eps)
    normed_two = (resid_one * scale_two * gain_two).astype(jnp.bfloat16)
    gate_up = jnp.dot(normed_two, mlp_w[:, : 2 * FF], preferred_element_type=jnp.float32)
    gate_part = gate_up[:, :FF]
    up_part = gate_up[:, FF:]
    sigma_gate = jax.nn.sigmoid(gate_part)
    silu_gate = gate_part * sigma_gate
    hidden_mid = (silu_gate * up_part).astype(jnp.bfloat16)
    block_out = resid_one + lax.dot_general(
        hidden_mid, mlp_w[:, 2 * FF :], contract_last, preferred_element_type=jnp.float32
    )
    out_hidden = block_out.astype(jnp.bfloat16)[None]
    grad_out = out_grad[0]
    grad_mid = jnp.dot(grad_out, mlp_w[:, 2 * FF :], preferred_element_type=jnp.float32)
    silu_slope = sigma_gate * (1.0 + gate_part * (1.0 - sigma_gate))
    grad_gate_up = jnp.concatenate(
        [grad_mid * up_part * silu_slope, grad_mid * silu_gate], axis=1
    ).astype(jnp.bfloat16)
    grad_normed_two = lax.dot_general(
        grad_gate_up, mlp_w[:, : 2 * FF], contract_last, preferred_element_type=jnp.float32
    )
    grad_norm_two, grad_gain_two = norm_backward(grad_normed_two, resid_one, scale_two, gain_two)
    grad_resid_one = grad_out.astype(jnp.float32) + grad_norm_two
    grad_resid_b = grad_resid_one.astype(jnp.bfloat16)

    grad_branch = jnp.dot(grad_resid_b, mixout_w, preferred_element_type=jnp.float32)
    lefts = [by_core(v, planes) for v in (normed_two, grad_out, grad_resid_b)]
    rights = [grad_gate_up, hidden_mid, branch]
    args = (
        doc_lengths, grad_branch, mixed, gate_in, xo, state_in, query_rows,
        kv_all.reshape(count * local_rows, 2 * KEY_WIDTH), log_sums, cos_wide, sin_wide, decays,
        xe, log_decay, root_t, packed, pre,
    )
    if planes <= 4:
        early, grad_proj, gate_gain_grads, conv_grads, skip_grads = back(
            planes, lefts, rights, args, block, 3
        )
    else:
        early = scatter_rows(planes, lefts, rights, 4)
        grad_proj, gate_gain_grads, conv_grads, skip_grads = back(planes, [], [], (branch,) + args, block, 3)
    small_local = jnp.concatenate(
        [
            jnp.zeros((D,), jnp.float32),
            grad_gain_two,
            gate_gain_grads[0],
            conv_grads.reshape(-1),
            jnp.sum(skip_grads.reshape(MH, MP), axis=1),
        ]
    )
    padded = jnp.pad(small_local, (0, SMALL_ROWS * 128 - size)).reshape(SMALL_ROWS, 128)
    mixin_grads, grad_hidden, totals = last(
        planes, by_core(normed_one, planes), grad_proj, first_w, rest_w, hidden[0], scale_one,
        packed, grad_resid_one, padded, 5,
    )
    grad_hidden = grad_hidden[None]
    small_grads = totals.reshape(-1)[:size]
    grad_weights = jnp.concatenate(
        [mixin_grads, early[:, 3 * FF :], early[:, : 3 * FF]], axis=1
    )
    new_weights, new_first, new_second = adamw_step(
        weights, grad_weights, first_moment, second_moment, decay_rate
    )
    small_step, small_first_new, small_second_new = adam_direction(
        small_grads, small_first, small_second
    )
    return (
        out_hidden,
        grad_hidden,
        grad_weights,
        new_weights,
        new_first,
        new_second,
        small_grads,
        small_step,
        small_first_new,
        small_second_new,
    )


def solution(mesh):
    placed = (
        P("fsdp", "ctx", None),
        P("fsdp", "ctx", None),
        P("fsdp", None, "ctx"),
        P("fsdp", None),
        P(("ctx", "fsdp"), None),
        P(("ctx", "fsdp"), None),
        P(("ctx", "fsdp"), None),
        P(),
        P(),
        P(),
    )
    return jax.shard_map(
        functools.partial(shards, mesh.shape["ctx"] // 4),
        mesh=mesh,
        in_specs=placed,
        out_specs=(
            P("fsdp", "ctx", None),
            P("fsdp", "ctx", None),
            P(("ctx", "fsdp"), None),
            P(("ctx", "fsdp"), None),
            P(("ctx", "fsdp"), None),
            P(("ctx", "fsdp"), None),
            P(),
            P(),
            P(),
            P(),
        ),
        check_vma=False,
    )
```

```python
import functools
import math

import jax
import jax.numpy as jnp
from jax import lax
from jax.experimental import pallas as pl
from jax.experimental.pallas import tpu as pltpu
from jax.sharding import PartitionSpec as P

D = 1024
QUERY_HEADS = 8
KEY_VALUE_HEADS = 2
HEAD_WIDTH = 64
MH = 24
MP = 64
NS = 128
FF = 2048
CONV = 4
STEP = 3
QUERY_WIDTH = 512
KEY_WIDTH = 128
INNER = 1536
XBC = 1792
MIXIN = 4096
MIXOUT = 2048
SMALL_ROWS = 104
TOKENS = 256
PIECE = 256

norm_eps = 1e-05
rope_base = 100000000000.0
large_negative = -1e30
learn_rate = 0.02
beta_one = 0.9
beta_two = 0.95
adam_eps = 1e-08
decay_rate = 0.1

MESH = pl.DeviceIdType.MESH
BF = jnp.bfloat16
F32 = jnp.float32
VM = pl.BlockSpec(memory_space=pltpu.VMEM)
SM = pl.BlockSpec(memory_space=pltpu.SMEM)
HB = pl.BlockSpec(memory_space=pl.ANY)
DMA = pltpu.SemaphoreType.DMA


def params(collective=None):
    if collective is None:
        return pltpu.CompilerParams(vmem_limit_bytes=62 * 2**20)
    return pltpu.CompilerParams(
        collective_id=collective, has_side_effects=True, vmem_limit_bytes=62 * 2**20
    )


def nt(a, b):
    return lax.dot_general(a, b, (((1,), (1,)), ((), ())), preferred_element_type=F32)


def tn(a, b):
    return lax.dot_general(a, b, (((0,), (0,)), ((), ())), preferred_element_type=F32)


def nn(a, b):
    return lax.dot_general(a, b, (((1,), (0,)), ((), ())), preferred_element_type=F32)


class Place:
    def __init__(self, planes):
        ctx = lax.axis_index("ctx")
        self.ctx = ctx
        self.Z, self.z, self.x, self.c = planes, ctx // 4, (ctx // 2) % 2, ctx % 2
        self.y = lax.axis_index("fsdp")
        self.up, self.down = self.z + 1 < planes, self.z > 0

    def shard(self, z, x, y, c):
        return ((z * 2 + x) * 2 + c) * 2 + y

    def spot(self, z, x, c):
        return (z * 2 + x) * 2 + c

    def dev(self, z, x, y, c):
        return ((z * 2 + x) * 2 + c, y)

    def near(self, d):
        z, x, y, c = self.z, self.x, self.y, self.c
        return {
            "x": self.dev(z, 1 - x, y, c),
            "y": self.dev(z, x, 1 - y, c),
            "c": self.dev(z, x, y, 1 - c),
            "u": self.dev(z + 1, x, y, c),
            "d": self.dev(z - 1, x, y, c),
        }[d]

    def zord(self, k):
        if k == self.Z - 1:
            return self.z
        low = self.Z - 1 - k
        z = self.z
        return jnp.where(
            2 * z < self.Z, jnp.where(low > z, low, low - 1), jnp.where(k < z, k, k + 1)
        )


def greet(pc, dims="xyc", chain=True):
    bar = pltpu.get_barrier_semaphore()

    def sig(d):
        pl.semaphore_signal(bar, inc=1, device_id=pc.near(d), device_id_type=MESH)

    for d in dims:
        sig(d)
    if chain:
        pl.when(pc.up)(lambda: sig("u"))
        pl.when(pc.down)(lambda: sig("d"))
    peers = len(dims)
    if chain:
        peers = peers + pc.up.astype(jnp.int32) + pc.down.astype(jnp.int32)
    pl.semaphore_wait(bar, peers)


def greet_row(pc, across=False):
    bar = pltpu.get_barrier_semaphore()
    n = 4 * pc.Z

    @pl.loop(1, n)
    def _(d):
        pl.semaphore_signal(
            bar, inc=1, device_id=(lax.rem(pc.ctx + d, n), pc.y), device_id_type=MESH
        )

    if across:
        pl.semaphore_signal(bar, inc=1, device_id=pc.near("y"), device_id_type=MESH)
    pl.semaphore_wait(bar, n - 1 + int(across))


def rcopy(pc, src, dst, ssem, rsem, d):
    return pltpu.make_async_remote_copy(
        src_ref=src,
        dst_ref=dst,
        send_sem=ssem,
        recv_sem=rsem,
        device_id=pc.near(d) if isinstance(d, str) else d,
        device_id_type=MESH,
    )


def add_into(dst, parts, width=512):
    columns = dst.shape[-1]
    step = width if columns % width == 0 else (256 if columns % 256 == 0 else 128)

    @pl.loop(0, columns // step)
    def _(i):
        sl = pl.ds(pl.multiple_of(i * step, step), step)
        total = parts[0][:, sl].astype(F32)
        for r in parts[1:]:
            total = total + r[:, sl].astype(F32)
        dst[:, sl] = total.astype(dst.dtype)


def plane_peers(pc):
    return [pc.dev(lax.rem(pc.z + d, pc.Z), pc.x, pc.y, pc.c) for d in range(1, pc.Z)]


def greet_planes(pc):
    bar = pltpu.get_barrier_semaphore()
    peers = [pc.near(d) for d in "xyc"] + plane_peers(pc)
    for d in peers:
        pl.semaphore_signal(bar, inc=1, device_id=d, device_id_type=MESH)
    pl.semaphore_wait(bar, len(peers))


EVEN = (25, 25, 64)
REST = (35, 19, 64)


def split(columns, shares, unit):
    a, b = (columns * s // shares[2] // unit * unit for s in shares[:2])
    return a, b, columns - a - b


def part_columns(widths, p):
    a, b, w = widths
    return pl.ds((w, w + a, 0)[p], widths[p])


def gather_scratch(planes):
    return [
        DMA((2, planes, 2)),
        DMA((2, planes)),
        DMA((2, planes, 2)),
        DMA((2, planes, 4)),
        DMA((2, planes, 8)),
        DMA((2, planes)),
        DMA((2 + planes,)),
        DMA((4 + 2 * planes,)),
        DMA,
    ]


def gather_steps(pc, w_ref, out_ref, scratch, shares):
    zs, xs, ys, cs, rs, tz, tc, tr, loc = scratch
    Z, z, x, y, c = pc.Z, pc.z, pc.x, pc.y, pc.c
    widths = split(w_ref.shape[-1], shares, 128)

    def cols(p):
        return part_columns(widths, p)

    def spot(q):
        return (x if q < 2 else 1 - x), (y if q % 2 == 0 else 1 - y)

    def cp(p, zz, q, sem, d, own=False, core=None):
        xx, yy = spot(q)
        dst = out_ref.at[zz, xx, c, yy, :, cols(p)]
        return rcopy(pc, w_ref.at[:, cols(p)] if own else dst, dst, sem, rs.at[p, zz, core if core is not None else q], d)

    def along(p, zz, up, own=False):
        return cp(p, zz, 0, zs.at[p, zz, int(up)], "u" if up else "d", own, 0)

    def first(p, zz, own=False):
        return cp(p, zz, 0, xs.at[p, zz], "x" if p == 0 else "y", own, 2 if p == 0 else 1)

    def second(p, zz, q, own=False):
        if p == 0:
            return cp(p, zz, 2 * q, ys.at[p, zz, q], "y", own, 2 * q + 1)
        return cp(p, zz, q, ys.at[p, zz, q], "x", own, 2 + q)

    def core(p, zz, q, own=False):
        return cp(p, zz, q, cs.at[p, zz, q], "c", own, 4 + q)

    def arrived(p, zz, q):
        rcopy(
            pc, w_ref.at[:, cols(p)], out_ref.at[0, 0, 0, 0, :, cols(p)], loc, rs.at[p, zz, q], "c"
        ).wait_recv()

    def t_x():
        return rcopy(
            pc, w_ref.at[:, cols(2)], out_ref.at[z, x, c, y, :, cols(2)], tc.at[0], tr.at[0], "x"
        )

    def t_y():
        v = out_ref.at[z, :, c, y, :, cols(2)]
        return rcopy(pc, v, v, tc.at[1], tr.at[1], "y")

    def t_z(zz, up):
        v = out_ref.at[zz, :, c, :, :, cols(2)]
        return rcopy(pc, v, v, tz.at[int(up), zz], tr.at[4 + zz], "u" if up else "d")

    def t_c(zz):
        v = out_ref.at[zz, :, c, :, :, cols(2)]
        return rcopy(pc, v, v, tc.at[2 + zz], tr.at[4 + Z + zz], "c")

    keep = pltpu.make_async_copy(w_ref, out_ref.at[z, x, c, y], loc)
    keep.start()
    t_x().start()
    for p in (0, 1):
        pl.when(pc.up)(lambda: along(p, z, True, True).start())
        pl.when(pc.down)(lambda: along(p, z, False, True).start())
        first(p, z, True).start()
    for p in (0, 1):
        second(p, z, 0, True).start()
        core(p, z, 0, True).start()
    yield False
    keep.wait()
    t_x().wait_recv()
    t_y().start()
    for d in range(1, Z):
        for p in (0, 1):

            def onward(zz, up, more):
                arrived(p, zz, 0)
                pl.when(more)(lambda: along(p, zz, up).start())
                first(p, zz).start()
                second(p, zz, 0).start()
                core(p, zz, 0).start()

            pl.when(z - d >= 0)(lambda: onward(z - d, True, pc.up))
            pl.when(z + d < Z)(lambda: onward(z + d, False, pc.down))
        if d == 1:
            t_y().wait_recv()
            pl.when(pc.up)(lambda: t_z(z, True).start())
            pl.when(pc.down)(lambda: t_z(z, False).start())
            t_c(z).start()
        yield False

    def hop(d):
        def onward(zz, up, more):
            t_z(zz, up).wait_recv()
            pl.when(more)(lambda: t_z(zz, up).start())
            t_c(zz).start()

        pl.when(z - d >= 0)(lambda: onward(z - d, True, pc.up))
        pl.when(z + d < Z)(lambda: onward(z + d, False, pc.down))

    near = [lax.rem(z + k, Z) for k in range(Z)]
    for k, zz in enumerate(near):
        for p in (0, 1):
            q = 2 if p == 0 else 1
            arrived(p, zz, q)
            second(p, zz, 1).start()
            core(p, zz, q).start()
        if k > 0:
            hop(k)
        yield False
    for i in (0, 1):
        for k, zz in enumerate(near):
            for p in (0, 1):
                q = (1 if i == 0 else 3) if p == 0 else (2 if i == 0 else 3)
                arrived(p, zz, q)
                core(p, zz, q).start()
            yield i == 1 and k == Z - 1
    for zz in near:
        for p in (0, 1):
            for q in range(4):
                arrived(p, zz, 4 + q)
        t_c(zz).wait_recv()
        yield True
    t_x().wait_send()
    t_y().wait_send()
    for zz in range(Z):
        for p in (0, 1):
            pl.when(pc.up & (zz <= z))(lambda: along(p, zz, True).wait_send())
            pl.when(pc.down & (zz >= z))(lambda: along(p, zz, False).wait_send())
            first(p, zz).wait_send()
            for q in (0, 1):
                second(p, zz, q).wait_send()
            for q in range(4):
                core(p, zz, q).wait_send()
        pl.when(pc.up & (zz <= z))(lambda: t_z(zz, True).wait_send())
        pl.when(pc.down & (zz >= z))(lambda: t_z(zz, False).wait_send())
        t_c(zz).wait_send()


def spread_scratch(planes):
    n = 4 * planes
    return [DMA((planes,)), DMA((planes,)), DMA((planes, 2)), DMA((n,)), DMA((n,)), DMA((n,)), DMA((3,))]


def spread_steps(pc, kv_ref, edge_ref, dec_ref, all_ref, got_ref, decs_ref, scratch):
    us, xs, cs, rs, ds, dr, one = scratch
    Z, z, x, c = pc.Z, pc.z, pc.x, pc.c
    n = 4 * Z
    me = pc.ctx

    def cp(zz, xx, sem, d, own=False):
        s = pc.spot(zz, xx, c)
        return rcopy(pc, kv_ref if own else all_ref.at[s], all_ref.at[s], sem, rs.at[s], d)

    def arrived(s):
        rcopy(pc, kv_ref, all_ref.at[s], one.at[0], rs.at[s], "c").wait_recv()

    def decay_copy(d):
        return rcopy(pc, dec_ref, decs_ref.at[me], ds.at[d], dr.at[d], (lax.rem(me + d, n), pc.y))

    edge = rcopy(pc, edge_ref, got_ref, one.at[1], one.at[2], (lax.rem(me + 1, n), pc.y))
    keep = pltpu.make_async_copy(kv_ref, all_ref.at[me], one.at[0])
    pl.when(me < n - 1)(lambda: edge.start())
    keep.start()
    pl.when(pc.up)(lambda: cp(z, x, us.at[z], "u", True).start())
    cp(z, x, xs.at[z], "x", True).start()
    cp(z, x, cs.at[z, 0], "c", True).start()
    decs_ref[me] = dec_ref[...]
    pl.loop(1, n)(lambda d: decay_copy(d).start())
    yield
    pl.when(me > 0)(lambda: edge.wait_recv())

    @pl.when(me == 0)
    def _():
        got_ref[...] = jnp.zeros_like(got_ref)

    yield
    for d in range(1, Z):

        @pl.when(z - d >= 0)
        def _():
            zz = z - d
            arrived(pc.spot(zz, x, c))
            pl.when(pc.up)(lambda: cp(zz, x, us.at[zz], "u").start())
            cp(zz, x, xs.at[zz], "x").start()
            cp(zz, x, cs.at[zz, 0], "c").start()

        yield
    for d in range(Z):

        @pl.when(z - d >= 0)
        def _():
            arrived(pc.spot(z - d, 1 - x, c))
            cp(z - d, 1 - x, cs.at[z - d, 1], "c").start()

    yield
    for d in range(Z):

        @pl.when(z - d >= 0)
        def _():
            for xx in (x, 1 - x):
                arrived(pc.spot(z - d, xx, 1 - c))

    keep.wait()
    pl.loop(1, n)(lambda d: decay_copy(d).wait_recv())
    yield
    for zz in range(Z):

        @pl.when(zz <= z)
        def _():
            pl.when(pc.up)(lambda: cp(zz, x, us.at[zz], "u").wait_send())
            cp(zz, x, xs.at[zz], "x").wait_send()
            cp(zz, x, cs.at[zz, 0], "c").wait_send()
            cp(zz, 1 - x, cs.at[zz, 1], "c").wait_send()

    pl.when(me < n - 1)(lambda: edge.wait_send())
    pl.loop(1, n)(lambda d: decay_copy(d).wait_send())


LAST = (7, 7, 16)
EARLY = (6, 6, 16)
STEP_PIECE = 512


def scatter_scratch(planes, rows, widths, shares):
    columns = sum(widths)
    a, b, w = split(columns, shares, PIECE)
    half = 4 * planes * rows
    return [
        pltpu.VMEM((planes, 2, 2, rows, columns), BF),
        pltpu.VMEM((planes, 2, rows, a + b), BF),
        pltpu.VMEM((planes, rows, a + b), BF),
        pltpu.VMEM((planes, rows, a + b), BF),
        pltpu.VMEM((planes + 1, 2, 2, rows, w), BF),
        pltpu.VMEM((3, rows, w), BF),
        pltpu.VMEM((len(widths), half, TOKENS), BF),
        pltpu.VMEM((TOKENS, columns), BF),
        DMA((len(widths),)),
        DMA((len(widths),)),
        DMA((columns // PIECE,)),
        DMA((columns // PIECE,)),
        DMA((2, planes, 2)),
        DMA((2, planes, 2)),
        DMA((2, planes)),
        DMA((2, planes)),
        DMA((3, planes)),
        DMA((3, planes + 1)),
        DMA((3,)),
        DMA((3,)),
    ]


def scatter_steps(pc, pairs, out_ref, scratch, shares):
    g, r2, r3, rz, rw, rt, la, rb, as_, ar, bs, br, s2, q2, s3, q3, sz, qz, st, qt = scratch
    Z, z, x, y, c = pc.Z, pc.z, pc.x, pc.y, pc.c
    rows = g.shape[3]
    widths = split(g.shape[-1], shares, PIECE)
    w = widths[2]
    depth = 4 * rows

    def cols(p):
        return part_columns(widths, p)

    def got(p):
        return pl.ds(p * widths[0], widths[p])

    pieces = []
    base = 0
    for i, (left, right) in enumerate(pairs):
        for at in range(0, right.shape[1], PIECE):
            pieces.append((i, at, base + at))
        base += right.shape[1]

    def acopy(i):
        return rcopy(pc, pairs[i][0].at[1 - c], la.at[i], as_.at[i], ar.at[i], "c")

    def bcopy(k):
        i, at, to = pieces[k]
        return rcopy(
            pc, pairs[i][1].at[:, pl.ds(at, PIECE)], rb.at[:, pl.ds(to, PIECE)], bs.at[k], br.at[k], "c"
        )

    def make(zz, k, first):
        i, at, to = pieces[k]
        if first:
            if at == 0:
                acopy(i).wait_recv()
            bcopy(k).wait_recv()
        here = pl.ds(pl.multiple_of(zz * depth, depth), depth)
        mine, theirs = pairs[i][0][c, here, :], la[i, here, :]
        tile = nn(mine, pairs[i][1][:, pl.ds(at, PIECE)]) + nn(theirs, rb[:, pl.ds(to, PIECE)])
        g[zz, :, :, :, pl.ds(to, PIECE)] = tile.reshape(2, 2, rows, PIECE).astype(BF)

    def copy2(p, zz, j):
        xx, yy = (x if j == 0 else 1 - x, 1 - y) if p == 0 else (1 - x, y if j == 0 else 1 - y)
        return rcopy(
            pc, g.at[zz, xx, yy, :, cols(p)], r2.at[zz, j, :, got(p)], s2.at[p, zz, j], q2.at[p, zz, j],
            "y" if p == 0 else "x",
        )

    def copy3(p, zz):
        xx, yy = (1 - x, y) if p == 0 else (x, 1 - y)
        return rcopy(
            pc, g.at[zz, xx, yy, :, cols(p)], r3.at[zz, :, got(p)], s3.at[p, zz], q3.at[p, zz],
            "x" if p == 0 else "y",
        )

    def sendz(p, zz):
        return rcopy(
            pc, g.at[zz, x, y, :, cols(p)], rz.at[z, :, got(p)], sz.at[p, zz], qz.at[p, z], pc.dev(zz, x, y, c)
        )

    def gotz(p, zz):
        rcopy(pc, g.at[0, x, y, :, cols(p)], rz.at[zz, :, got(p)], sz.at[p, 0], qz.at[p, zz], "c").wait_recv()

    def send_plane(zz, up):
        slot = jnp.where(zz == z + 1, Z, zz) if up else zz
        return rcopy(
            pc, g.at[zz, :, :, :, cols(2)], rw.at[slot], sz.at[2, zz], qz.at[2, slot], "u" if up else "d"
        )

    def got_plane(slot):
        rcopy(
            pc, g.at[0, :, :, :, cols(2)], rw.at[slot], sz.at[2, 0], qz.at[2, slot], "c"
        ).wait_recv()

    def add_plane(zz, slots):
        for xx in (0, 1):
            for yy in (0, 1):
                a = g.at[zz, xx, yy, :, cols(2)]
                add_into(a, [a] + [rw.at[k, xx, yy] for k in slots])

    def at_time(t, f):
        below, above = t - (Z - 1 - z), Z - 1 - (t - z)
        pl.when((below >= 0) & (below < z))(lambda: f(below, False, pc.up))
        pl.when((above > z) & (above < Z))(lambda: f(above, True, pc.down))

    def chain_first(zz, up, more):
        @pl.when(more)
        def _():
            got_plane(zz)
            add_plane(zz, [zz])

        send_plane(zz, up).start()

    def tail(k):
        if k < 2:
            return rcopy(pc, g.at[z, k, 1 - y, :, cols(2)], rt.at[k], st.at[k], qt.at[k], "y")
        return rcopy(pc, g.at[z, 1 - x, y, :, cols(2)], rt.at[2], st.at[2], qt.at[2], "x")

    for i in range(len(pairs)):
        acopy(i).start()
        for k in range(len(pieces)):
            if pieces[k][0] == i:
                bcopy(k).start()
    yield
    ends = {w + widths[0]: 0, w + widths[0] + widths[1]: 1}

    def own(p, zz):
        copy2(p, zz, 0).wait_recv()
        copy3(p, zz).wait_recv()
        a = g.at[zz, x, y, :, cols(p)]
        return a, [a, r2.at[zz, 0, :, got(p)], r3.at[zz, :, got(p)]]

    def gather_plane(slot):
        got_plane(slot)
        add_plane(z, [slot])

    for k in range(Z + 2):
        if k < Z:
            zz = pc.zord(k)
            for n in range(len(pieces)):
                make(zz, n, k == 0)
                end = pieces[n][2] + PIECE
                if end == w and k == 0 and Z > 1:
                    at_time(0, chain_first)
                if end in ends:
                    copy2(ends[end], zz, 1).start()
                if n == len(pieces) // 2:
                    yield
            yield
        if 0 < k <= Z:
            zz = pc.zord(k - 1)
            for p in (0, 1):
                copy2(p, zz, 1).wait_recv()
                a = g.at[(zz,) + ((1 - x, y) if p == 0 else (x, 1 - y)) + (slice(None), cols(p))]
                add_into(a, [a, r2.at[zz, 1, :, got(p)]])
                copy3(p, zz).start()
            for p in (0, 1):
                copy2(p, zz, 0).start()
            if 0 < k - 1 < Z - 1:
                at_time(k - 1, chain_first)
            yield
        if 1 < k <= Z:
            zz = pc.zord(k - 2)
            for p in (0, 1):
                a, parts = own(p, zz)
                add_into(a, parts)
                sendz(p, zz).start()
            yield
    pl.when(pc.up)(lambda: gather_plane(z))
    pl.when(pc.down)(lambda: gather_plane(Z))
    for k in (0, 1):
        tail(k).start()
    yield
    finals = []
    for p in (0, 1):
        finals.append(own(p, z)[1])
    for k in (0, 1):
        tail(k).wait_recv()
        a = g.at[z, k, y, :, cols(2)]
        add_into(a, [a, rt.at[k]])
    tail(2).start()
    yield
    for p in (0, 1):
        for d in range(1, Z):
            slot = lax.rem(z + d, Z)
            gotz(p, slot)
            finals[p].append(rz.at[slot, :, got(p)])
        add_into(out_ref.at[:, cols(p)], finals[p])
        yield
    tail(2).wait_recv()
    add_into(out_ref.at[:, cols(2)], [g.at[z, x, y, :, cols(2)], rt.at[2]])
    for i in range(len(pairs)):
        acopy(i).wait_send()
    for k in range(len(pieces)):
        bcopy(k).wait_send()
    for k in range(3):
        tail(k).wait_send()
    for zz in range(Z):
        for p in (0, 1):
            for j in (0, 1):
                copy2(p, zz, j).wait_send()
            copy3(p, zz).wait_send()
            pl.when(zz != z)(lambda: sendz(p, zz).wait_send())
        pl.when(zz < z)(lambda: send_plane(zz, False).wait_send())
        pl.when(zz > z)(lambda: send_plane(zz, True).wait_send())


def woven_scratch(planes, rows, widths):
    columns = sum(widths)
    a, b, w = split(columns, EARLY, STEP_PIECE)
    half = 4 * planes * rows
    return [
        pltpu.VMEM((planes, 2, 2, rows, columns), BF),
        pltpu.VMEM((planes, 2, rows, a + b), BF),
        pltpu.VMEM((planes, rows, a + b), BF),
        pltpu.VMEM((planes + 1, rows, a + b), BF),
        pltpu.VMEM((planes + 1, 2, 2, rows, w), BF),
        pltpu.VMEM((3, rows, w), BF),
        pltpu.VMEM((len(widths), half, TOKENS), BF),
        pltpu.VMEM((TOKENS, columns), BF),
        DMA((len(widths),)),
        DMA((len(widths),)),
        DMA((columns // STEP_PIECE,)),
        DMA((columns // STEP_PIECE,)),
        DMA((2, planes, 2)),
        DMA((2, planes, 2)),
        DMA((2, planes)),
        DMA((2, planes)),
        DMA((3, planes)),
        DMA((3, planes + 1)),
        DMA((3,)),
        DMA((3,)),
    ]


def woven_steps(pc, pairs, out_ref, scratch):
    g, r2, r3, rz, rw, rt, la, rb, as_, ar, bs, br, s2, q2, s3, q3, sz, qz, st, qt = scratch
    Z, z, x, y, c = pc.Z, pc.z, pc.x, pc.y, pc.c
    rows = g.shape[3]
    widths = split(g.shape[-1], EARLY, STEP_PIECE)
    w = widths[2]
    depth = 4 * rows

    def cols(p):
        return part_columns(widths, p)

    def got(p):
        return pl.ds(p * widths[0], widths[p])

    pieces = []
    base = 0
    for i, (left, right) in enumerate(pairs):
        for at in range(0, right.shape[1], STEP_PIECE):
            pieces.append((i, at, base + at))
        base += right.shape[1]

    def acopy(i):
        return rcopy(pc, pairs[i][0].at[1 - c], la.at[i], as_.at[i], ar.at[i], "c")

    def bcopy(k):
        i, at, to = pieces[k]
        return rcopy(
            pc, pairs[i][1].at[:, pl.ds(at, STEP_PIECE)], rb.at[:, pl.ds(to, STEP_PIECE)], bs.at[k], br.at[k], "c"
        )

    def make(zz, k, first):
        i, at, to = pieces[k]
        if first:
            if at == 0:
                acopy(i).wait_recv()
            bcopy(k).wait_recv()
        here = pl.ds(pl.multiple_of(zz * depth, depth), depth)
        mine, theirs = pairs[i][0][c, here, :], la[i, here, :]
        for t in range(0, STEP_PIECE, 512):
            tile = nn(mine, pairs[i][1][:, pl.ds(at + t, 512)]) + nn(theirs, rb[:, pl.ds(to + t, 512)])
            g[zz, :, :, :, pl.ds(to + t, 512)] = tile.reshape(2, 2, rows, 512).astype(BF)

    def copy2(p, zz, j):
        xx, yy = (x if j == 0 else 1 - x, 1 - y) if p == 0 else (1 - x, y if j == 0 else 1 - y)
        return rcopy(
            pc, g.at[zz, xx, yy, :, cols(p)], r2.at[zz, j, :, got(p)], s2.at[p, zz, j], q2.at[p, zz, j],
            "y" if p == 0 else "x",
        )

    def copy3(p, zz):
        xx, yy = (1 - x, y) if p == 0 else (x, 1 - y)
        return rcopy(
            pc, g.at[zz, xx, yy, :, cols(p)], r3.at[zz, :, got(p)], s3.at[p, zz], q3.at[p, zz],
            "x" if p == 0 else "y",
        )

    def views(p, zz, slot):
        if p == 2:
            return g.at[zz, :, :, :, cols(p)], rw.at[slot]
        return g.at[zz, x, y, :, cols(p)], rz.at[slot, :, got(p)]

    def sendz(p, zz, up):
        slot = jnp.where(zz == z + 1, Z, zz) if up else zz
        src, dst = views(p, zz, slot)
        return rcopy(pc, src, dst, sz.at[p, zz], qz.at[p, slot], "u" if up else "d")

    def gotz(p, slot):
        src, dst = views(p, 0, slot)
        rcopy(pc, src, dst, sz.at[p, 0], qz.at[p, slot], "c").wait_recv()

    def add_plane(zz, slots):
        for xx in (0, 1):
            for yy in (0, 1):
                a = g.at[zz, xx, yy, :, cols(2)]
                add_into(a, [a] + [rw.at[k, xx, yy] for k in slots])

    def at_time(t, f):
        below, above = t - (Z - 1 - z), Z - 1 - (t - z)
        pl.when((below >= 0) & (below < z))(lambda: f(below, False, pc.up))
        pl.when((above > z) & (above < Z))(lambda: f(above, True, pc.down))

    def chain_first(zz, up, more):
        @pl.when(more)
        def _():
            gotz(2, zz)
            add_plane(zz, [zz])

        sendz(2, zz, up).start()

    def tail(k):
        if k < 2:
            return rcopy(pc, g.at[z, k, 1 - y, :, cols(2)], rt.at[k], st.at[k], qt.at[k], "y")
        return rcopy(pc, g.at[z, 1 - x, y, :, cols(2)], rt.at[2], st.at[2], qt.at[2], "x")

    for i in range(len(pairs)):
        acopy(i).start()
        for k in range(len(pieces)):
            if pieces[k][0] == i:
                bcopy(k).start()
    yield
    ends = {w + widths[0]: 0, w + widths[0] + widths[1]: 1}
    for k in range(Z + 1):
        if k < Z:
            zz = pc.zord(k)
            for n in range(len(pieces)):
                make(zz, n, k == 0)
                end = pieces[n][2] + STEP_PIECE
                if end == w and k == 0 and Z > 1:
                    at_time(0, chain_first)
                if end in ends:
                    copy2(ends[end], zz, 1).start()
            yield
        if k > 0:
            zz = pc.zord(k - 1)
            for p in (0, 1):
                copy2(p, zz, 1).wait_recv()
                a = g.at[(zz,) + ((1 - x, y) if p == 0 else (x, 1 - y)) + (slice(None), cols(p))]
                add_into(a, [a, r2.at[zz, 1, :, got(p)]])
                copy3(p, zz).start()
            for p in (0, 1):
                copy2(p, zz, 0).start()
            if 0 < k - 1 < Z - 1:
                at_time(k - 1, chain_first)
            yield

    def own(p, zz):
        copy2(p, zz, 0).wait_recv()
        copy3(p, zz).wait_recv()
        a = g.at[zz, x, y, :, cols(p)]
        return a, [a, r2.at[zz, 0, :, got(p)], r3.at[zz, :, got(p)]]

    def chain(p, zz, up, more):
        a, parts = own(p, zz)

        @pl.when(more)
        def _():
            gotz(p, zz)
            add_into(a, parts + [rz.at[zz, :, got(p)]])

        @pl.when(jnp.logical_not(more))
        def _():
            add_into(a, parts)

        sendz(p, zz, up).start()

    def gather_plane(slot):
        gotz(2, slot)
        add_plane(z, [slot])

    pl.when(pc.up)(lambda: gather_plane(z))
    pl.when(pc.down)(lambda: gather_plane(Z))
    for k in (0, 1):
        tail(k).start()
    yield
    for t in range(Z - 1):
        for p in (0, 1):
            at_time(t, functools.partial(chain, p))
        if t == 0:
            for k in (0, 1):
                tail(k).wait_recv()
                a = g.at[z, k, y, :, cols(2)]
                add_into(a, [a, rt.at[k]])
            tail(2).start()
        yield
    tail(2).wait_recv()
    add_into(out_ref.at[:, cols(2)], [g.at[z, x, y, :, cols(2)], rt.at[2]])
    for p in (0, 1):
        a, parts = own(p, z)
        o = out_ref.at[:, cols(p)]
        add_into(o, parts)

        def last(slot):
            gotz(p, slot)
            add_into(o, [o, rz.at[slot, :, got(p)]])

        pl.when(pc.up)(lambda: last(z))
        pl.when(pc.down)(lambda: last(Z))
        yield
    for i in range(len(pairs)):
        acopy(i).wait_send()
    for k in range(len(pieces)):
        bcopy(k).wait_send()
    for k in range(3):
        tail(k).wait_send()
    for zz in range(Z):
        for p in (0, 1):
            for j in (0, 1):
                copy2(p, zz, j).wait_send()
            copy3(p, zz).wait_send()
        for p in (0, 1, 2):
            pl.when(zz < z)(lambda: sendz(p, zz, False).wait_send())
            pl.when(zz > z)(lambda: sendz(p, zz, True).wait_send())


def scatter_kernel(planes, count, *refs):
    pc = Place(planes)
    greet_planes(pc)
    pairs = tuple(zip(refs[:count], refs[count : 2 * count]))
    for _ in scatter_steps(pc, pairs, refs[2 * count], refs[2 * count + 1 :], LAST):
        pass


def scatter_rows(planes, lefts, rights, collective):
    rows = lefts[0].shape[1] // (4 * planes)
    widths = [r.shape[1] for r in rights]
    return pl.pallas_call(
        functools.partial(scatter_kernel, planes, len(lefts)),
        out_shape=jax.ShapeDtypeStruct((rows, sum(widths)), F32),
        in_specs=[VM] * (2 * len(lefts)),
        out_specs=VM,
        scratch_shapes=scatter_scratch(planes, rows, widths, LAST),
        compiler_params=params(collective),
    )(*lefts, *rights)


def by_core(rows, planes):
    tokens = rows.shape[0]
    each = D // (8 * planes)
    cut = rows.T.reshape(2 * planes, 2, 2 * each, tokens)
    return cut.transpose(1, 0, 2, 3).reshape(2, D // 2, tokens)


def fold_scratch(planes, rows, columns):
    return [
        pltpu.VMEM((planes, 2, rows, columns), BF),
        pltpu.VMEM((planes, rows, columns), BF),
        pltpu.VMEM((planes, rows, columns), BF),
        pltpu.VMEM((planes, 2, rows, columns), BF),
        DMA((planes, 2)),
        DMA((planes, 2)),
        DMA((planes,)),
        DMA((planes,)),
        DMA((planes,)),
        DMA((planes,)),
    ]


def fold_steps(pc, block, out_ref, scratch):
    rc, rx, rz, acc, cs, cr, xs, xr, zs, zr = scratch
    Z, z, x, c = pc.Z, pc.z, pc.x, pc.c

    def ccopy(zz, q):
        xx = x if q == 0 else 1 - x
        return rcopy(pc, block(pc.spot(zz, xx, 1 - c)), rc.at[zz, q], cs.at[zz, q], cr.at[zz, q], "c")

    def xcopy(zz):
        return rcopy(pc, acc.at[zz, 1], rx.at[zz], xs.at[zz], xr.at[zz], "x")

    def zcopy(zz):
        return rcopy(pc, acc.at[zz, 0], rz.at[zz], zs.at[zz], zr.at[zz], "d")

    def each(f):
        for zz in range(Z):
            pl.when(zz <= z)(functools.partial(f, zz))

    def a(zz):
        ccopy(zz, 1).start()
        ccopy(zz, 0).start()

    def b(zz):
        ccopy(zz, 1).wait_recv()
        add_into(acc.at[zz, 1], [block(pc.spot(zz, 1 - x, c)), rc.at[zz, 1]], 128)
        xcopy(zz).start()

    def m(zz):
        ccopy(zz, 0).wait_recv()
        add_into(acc.at[zz, 0], [block(pc.spot(zz, x, c)), rc.at[zz, 0]], 128)

    def e(zz):
        xcopy(zz).wait_recv()

        def finish(parts):
            @pl.when(zz < z)
            def _():
                add_into(acc.at[zz, 0], parts, 128)
                zcopy(zz).start()

            pl.when(zz == z)(lambda: add_into(out_ref, parts, 128))

        @pl.when(pc.up)
        def _():
            zcopy(zz).wait_recv()
            finish([acc.at[zz, 0], rx.at[zz], rz.at[zz]])

        pl.when(jnp.logical_not(pc.up))(lambda: finish([acc.at[zz, 0], rx.at[zz]]))

    def w(zz):
        ccopy(zz, 1).wait_send()
        ccopy(zz, 0).wait_send()
        xcopy(zz).wait_send()
        pl.when(zz < z)(lambda: zcopy(zz).wait_send())

    for f in (a, b, m, e):
        each(f)
        yield
    each(w)


def relay_scratch(planes):
    n = 4 * planes
    piece = pltpu.VMEM((n, NS // n, INNER), BF)
    return [piece, piece, DMA((n,)), DMA((n,)), DMA((n,)), DMA((n,))]


def relay_steps(pc, reverse, s_ref, dec_ref, out_ref, scratch):
    got, part, ss, sr, bs, br = scratch
    n = 4 * pc.Z
    me = pc.ctx

    def to(d):
        return lax.rem(me + d, n)

    def there(d):
        return rcopy(pc, s_ref.at[to(d)], got.at[me], ss.at[d], sr.at[d], (to(d), pc.y))

    def back(d):
        return rcopy(pc, part.at[to(d)], out_ref.at[me], bs.at[d], br.at[d], (to(d), pc.y))

    pl.loop(1, n)(lambda d: there(d).start())
    got[me] = s_ref[me]
    yield
    pl.loop(1, n)(lambda d: there(d).wait_recv())
    total = jnp.zeros(got.shape[1:], F32)
    for k in range(n):
        j = n - 1 - k if reverse else k
        part[j] = total.astype(BF)
        total = total * dec_ref[pl.ds(j, 1), :] + got[j].astype(F32)
    pl.loop(1, n)(lambda d: back(d).start())
    out_ref[me] = part[me]
    yield
    pl.loop(1, n)(lambda d: back(d).wait_recv())
    yield

    @pl.loop(1, n)
    def _(d):
        there(d).wait_send()
        back(d).wait_send()


def total_scratch(planes):
    shape = (SMALL_ROWS, 128)
    return [
        pltpu.VMEM((6,) + shape, F32),
        pltpu.VMEM((planes,) + shape, F32),
        DMA((3,)),
        DMA((3,)),
        DMA((planes,)),
        DMA((planes,)),
    ]


def total_steps(pc, out_ref, scratch):
    rx, rz, ss, sr, zs, zr = scratch
    Z, z = pc.Z, pc.z
    for i, d in enumerate("cxy"):
        rx[2 * i] = out_ref[...]
        cp = rcopy(pc, rx.at[2 * i], rx.at[2 * i + 1], ss.at[i], sr.at[i], d)
        cp.start()
        yield
        cp.wait()
        out_ref[...] = out_ref[...] + rx[2 * i + 1]
    rz[z] = out_ref[...]
    copies = [rcopy(pc, rz.at[z], rz.at[z], zs.at[d], zr.at[d], to) for d, to in enumerate(plane_peers(pc))]
    for cp in copies:
        cp.start()
    yield
    for cp in copies:
        cp.wait()
    total = rz[0]
    for k in range(1, Z):
        total = total + rz[k]
    out_ref[...] = total


def visible(start, block, pos_ref):
    kpos = start + lax.broadcasted_iota(jnp.int32, (block, pos_ref.shape[1]), 0)
    return (kpos <= pos_ref[0:1, :]) & (kpos >= pos_ref[1:2, :])


def split_heads(src, dst, scale=None):
    rows = src.shape[0]
    for h in range(QUERY_HEADS):
        v = src[:, pl.ds(h * HEAD_WIDTH, HEAD_WIDTH)]
        dst[pl.ds(h * rows, rows), :] = v if scale is None else v * scale


def swap_halves(v):
    width = v.shape[1]
    lane = lax.broadcasted_iota(jnp.int32, v.shape, 1)
    low = lax.rem(lane, HEAD_WIDTH) < HEAD_WIDTH // 2
    ahead = pltpu.roll(v, width - HEAD_WIDTH // 2, 1)
    behind = pltpu.roll(v, HEAD_WIDTH // 2, 1)
    return jnp.where(low, ahead, behind)


def rotate(v, cos_ref, sin_ref, sign=1.0):
    return v * cos_ref[...] + swap_halves(v) * (sign * sin_ref[...])


def attend_block(j, block, q_ref, kv, pos_ref, m_ref, l_ref, acc_ref, heads):
    rows = pos_ref.shape[1]
    start = pl.multiple_of(j * block, block)
    ok = visible(start, block, pos_ref)
    for h in heads:
        g = h // (QUERY_HEADS // KEY_VALUE_HEADS)
        keys = kv[:, g * HEAD_WIDTH : (g + 1) * HEAD_WIDTH]
        vals = kv[:, KEY_WIDTH + g * HEAD_WIDTH : KEY_WIDTH + (g + 1) * HEAD_WIDTH]
        s = jnp.where(ok, nt(keys, q_ref[pl.ds(h * rows, rows), :]), 2.0 * large_negative)
        m0 = m_ref[h : h + 1, :]
        m1 = jnp.maximum(m0, jnp.max(s, axis=0, keepdims=True))
        p = jnp.exp(s - m1)
        a = jnp.exp(m0 - m1)
        l_ref[h : h + 1, :] = l_ref[h : h + 1, :] * a + jnp.sum(p, axis=0, keepdims=True)
        m_ref[h : h + 1, :] = m1
        r = pl.ds(h * HEAD_WIDTH, HEAD_WIDTH)
        acc_ref[r, :] = acc_ref[r, :] * a + tn(vals, p.astype(BF))


def attend_end(o_ref, lse_ref, m_ref, l_ref, acc_ref):
    lse_ref[...] = m_ref[...] + jnp.log(l_ref[...])
    inv = 1.0 / l_ref[...]
    for h in range(QUERY_HEADS):
        r = pl.ds(h * HEAD_WIDTH, HEAD_WIDTH)
        acc_ref[r, :] = acc_ref[r, :] * inv[h : h + 1, :]
    o_ref[...] = acc_ref[...].T.astype(o_ref.dtype)


def attend_back_block(j, g, block, q_ref, do_ref, kv_ref, pos_ref, lse_ref, dl_ref, dkv_ref, acc_ref):
    rows = pos_ref.shape[1]
    start = pl.multiple_of(j * block, block)
    ok = visible(start, block, pos_ref)
    at = pl.ds(start, block)
    keys = kv_ref[at, pl.ds(g * HEAD_WIDTH, HEAD_WIDTH)]
    vals = kv_ref[at, pl.ds(KEY_WIDTH + g * HEAD_WIDTH, HEAD_WIDTH)]
    dk = dv = None
    for h in range(4 * g, 4 * g + 4):
        q = q_ref[pl.ds(h * rows, rows), :]
        do = do_ref[pl.ds(h * rows, rows), :]
        p = jnp.where(ok, jnp.exp(nt(keys, q) - lse_ref[h : h + 1, :]), 0.0)
        ds = (p * (nt(vals, do) - dl_ref[h : h + 1, :])).astype(BF)
        r = pl.ds(h * HEAD_WIDTH, HEAD_WIDTH)
        acc_ref[r, :] += tn(keys, ds)
        a, b = nn(ds, q), nn(p.astype(BF), do)
        dk = a if dk is None else dk + a
        dv = b if dv is None else dv + b
    dkv_ref[at, pl.ds(g * HEAD_WIDTH, HEAD_WIDTH)] = dk.astype(BF)
    dkv_ref[at, pl.ds(KEY_WIDTH + g * HEAD_WIDTH, HEAD_WIDTH)] = dv.astype(BF)


def two(left, right, lanes):
    return jnp.where(lanes < MP, left, right)


def pair_columns(ref, p, lanes):
    return two(ref[:, 2 * p : 2 * p + 1], ref[:, 2 * p + 1 : 2 * p + 2], lanes)


def mixer_steps(
    xe, mk, cw, cb, cum_t, cum, dt_t, we_t, skip, doc_c, doc_r, pre, xo, mix, so, xw, bias
):
    rows = pre.shape[0]
    for i in range(XBC // 256):
        sl = pl.ds(i * 256, 256)
        acc = jnp.broadcast_to(cb[:, sl], (rows, 256))
        for j in range(CONV):
            acc = acc + cw[j : j + 1, sl] * (xe[pl.ds(5 + j, rows), sl] * mk[:, j : j + 1])
        pre[:, sl] = acc.astype(BF)
        act = acc * jax.nn.sigmoid(acc)
        xo[:, sl] = act.astype(BF)
        if i < INNER // 256:
            mix[:, sl] = skip[:, sl] * act
        if i == 3:
            yield
    yield
    b_rows, c_rows = xo[:, pl.ds(INNER, NS)], xo[:, pl.ds(INNER + NS, NS)]
    cross = nt(c_rows, b_rows)
    t_at = lax.broadcasted_iota(jnp.int32, (rows, rows), 0)
    s_at = lax.broadcasted_iota(jnp.int32, (rows, rows), 1)
    bias[...] = jnp.where((doc_c[...] == doc_r[...]) & (s_at <= t_at), 0.0, large_negative)
    lanes = lax.broadcasted_iota(jnp.int32, (rows, 2 * MP), 1)
    for p in range(MH // 2):
        sl = pl.ds(p * 2 * MP, 2 * MP)
        xd = xo[:, sl].astype(F32) * pair_columns(dt_t, p, lanes)
        xw[:, sl] = (xd * pair_columns(we_t, p, lanes)).astype(BF)
        xb = xd.astype(BF)
        outs = []
        for h in (2 * p, 2 * p + 1):
            low = jnp.exp(jnp.minimum(cum_t[:, h : h + 1] - cum[h : h + 1, :], bias[...]))
            outs.append(nn((low * cross).astype(BF), xb))
        mix[:, sl] = mix[:, sl] + two(outs[0], outs[1], lanes)
        if p % 3 == 2:
            yield
    so[...] = tn(b_rows, xw[...]).astype(BF).reshape(so.shape)


def spread_heads():
    head = lax.broadcasted_iota(jnp.int32, (MH, INNER), 0)
    lane = lax.broadcasted_iota(jnp.int32, (MH, INNER), 1)
    return (lane // MP == head).astype(F32)


def exact(a, b, dims):
    return lax.dot_general(
        a, b, (dims, ((), ())), precision=lax.Precision.HIGHEST, preferred_element_type=F32
    )


def wide(columns, spread_mat):
    return exact(columns, spread_mat, ((1,), (0,)))


def gate_kernel(planes, lens, mix, xo, state_in, ldec, gate, small, att, mixed, branch, gain, state, din_t):
    rows = mix.shape[0]
    spread_mat = spread_heads()
    unpack(small, "gate", gain)
    state[...] = state_in[...].reshape(state.shape)
    first = Place(planes).ctx * rows
    a = lax.broadcasted_iota(jnp.int32, (rows, rows), 0)
    b = lax.broadcasted_iota(jnp.int32, (rows, rows), 1)
    docs = doc_of(first + lax.broadcasted_iota(jnp.int32, (rows, 1), 0), lens)
    before = doc_of(jnp.full((1, 1), first - 1, jnp.int32), lens)
    ct = exact((b <= a).astype(F32), ldec[...], ((1,), (1,)))
    din_t[...] = jnp.where(docs == before, jnp.exp(ct), 0.0)

    @pl.loop(0, rows // 64)
    def _(i):
        r = pl.ds(pl.multiple_of(i * 64, 64), 64)
        carried = nn(xo[r, pl.ds(INNER + NS, NS)], state[...])
        m = mix[r, :] + carried * wide(din_t[r, :], spread_mat)
        mixed[r, :] = m.astype(BF)
        gv = gate[r, :]
        gated = m * (gv * jax.nn.sigmoid(gv))
        factor = lax.rsqrt(jnp.mean(gated * gated, axis=1, keepdims=True) + norm_eps)
        branch[r, pl.ds(0, QUERY_WIDTH)] = att[r, :]
        branch[r, pl.ds(QUERY_WIDTH, INNER)] = (gated * factor * gain[...]).astype(BF)


def gate_out(planes, lens, mix, xo, state, ldec, gate, small, att):
    rows = mix.shape[0]
    return pl.pallas_call(
        functools.partial(gate_kernel, planes),
        out_shape=(
            jax.ShapeDtypeStruct((rows, INNER), BF),
            jax.ShapeDtypeStruct((rows, MIXOUT), BF),
        ),
        in_specs=[SM] + [VM] * 7,
        out_specs=(VM,) * 2,
        scratch_shapes=[
            pltpu.VMEM((1, INNER), F32),
            pltpu.VMEM((NS, INNER), BF),
            pltpu.VMEM((rows, MH), F32),
        ],
        compiler_params=params(),
    )(lens, mix, xo, state, ldec, gate, small, att)


def doc_of(pos, lens):
    start = 0
    found = jnp.full_like(pos, -1)
    for d in range(lens.shape[1]):
        found = found + (pos >= start).astype(jnp.int32)
        start = start + lens[0, d]
    return found


def begin_of(pos, lens):
    start = 0
    found = jnp.zeros_like(pos)
    for d in range(lens.shape[1]):
        found = jnp.maximum(found, jnp.where(pos >= start, start, 0))
        start = start + lens[0, d]
    return found


def table_scratch(rows):
    return [
        pltpu.VMEM((2, rows), jnp.int32),
        pltpu.VMEM((rows, 8), F32),
        pltpu.VMEM((rows, 1), jnp.int32),
        pltpu.VMEM((1, rows), jnp.int32),
        pltpu.VMEM((MH, rows), F32),
        pltpu.VMEM((rows, MH), F32),
        pltpu.VMEM((rows, MH), F32),
        pltpu.VMEM((rows, MH), F32),
        pltpu.VMEM((rows, MH), F32),
    ]


def make_tables(pc, lens, ldec, root_t, tables):
    pos, same, doc_c, doc_r, cum, cum_t, dt_t, we_t, din_t = tables
    rows = ldec.shape[1]
    first = pc.ctx * rows
    at_c = first + lax.broadcasted_iota(jnp.int32, (rows, 1), 0)
    at_r = first + lax.broadcasted_iota(jnp.int32, (1, rows), 1)
    pos[0:1, :] = at_r
    pos[1:2, :] = begin_of(at_r, lens)
    dc = doc_of(at_c, lens)
    doc_c[...] = dc
    doc_r[...] = doc_of(at_r, lens)
    for j in range(CONV):
        same[:, j : j + 1] = (doc_of(at_c - (CONV - 1) + j, lens) == dc).astype(F32)
        same[:, CONV + j : CONV + j + 1] = (doc_of(at_c + (CONV - 1) - j, lens) == dc).astype(F32)
    a = lax.broadcasted_iota(jnp.int32, (rows, rows), 0)
    b = lax.broadcasted_iota(jnp.int32, (rows, rows), 1)
    cum[...] = exact(ldec[...], (a <= b).astype(F32), ((1,), (0,)))
    ct = exact((b <= a).astype(F32), ldec[...], ((1,), (1,)))
    cum_t[...] = ct
    fresh = doc_of(at_c - 1, lens) != dc
    dt_t[...] = jnp.where(fresh, 1.0, root_t[...])
    before = doc_of(jnp.full((1, 1), first - 1, jnp.int32), lens)
    end = doc_of(jnp.full((1, 1), first + rows - 1, jnp.int32), lens)
    din_t[...] = jnp.where(dc == before, jnp.exp(ct), 0.0)
    we_t[...] = jnp.where(dc == end, jnp.exp(jnp.minimum(ct[rows - 1 : rows, :] - ct, 0.0)), 0.0)


SMALL_AT = {"one": (0, 8), "two": (8, 8), "gate": (16, 12), "bias": (84, 14), "skip": (98, 1)}


def unpack(small, name, dst, row=0):
    at, tiles = SMALL_AT[name] if isinstance(name, str) else name
    for i in range(tiles):
        dst[row : row + 1, pl.ds(i * 128, 128)] = small[at + i : at + i + 1, :]


def unpack_conv(small, dst):
    for j in range(CONV):
        unpack(small, (28 + 14 * j, 14), dst, j)


def wide_skip(small, spread_mat, dst):
    dst[...] = wide(jnp.broadcast_to(small[98:99, 0:MH], (8, MH)), spread_mat)[0:1, :]


GATE_AT = QUERY_WIDTH + 2 * KEY_WIDTH
XBC_AT = GATE_AT + INNER
FIRST = QUERY_WIDTH + 2 * KEY_WIDTH + XBC


def front_kernel(
    planes, block, lens, hid, w1, w2, cos_w, sin_w, ldec, root_t, small,
    normed, scale, g1, g2, q_out, kv_all, xe, decays, pre, xo, mix, state_in, att, lse,
    kv_own, edge_out, edge_in, dec_own, decs, dec_rows, gains, conv_w, conv_b, skip, so, qh, m_ref, l_ref,
    acc, xw, bias, *refs,
):
    tables, refs = refs[:9], refs[9:]
    pos, same, doc_c, doc_r, cum, cum_t, dt_t, we_t, din_t = tables
    first_refs, refs = refs[:9], refs[9:]
    rest_refs, refs = refs[:9], refs[9:]
    spread_refs, refs = refs[:7], refs[7:]
    relay_refs = refs[:6]
    pc = Place(planes)
    n = 4 * planes
    rows = hid.shape[0]
    greet_row(pc, True)
    gather = gather_steps(pc, w1, g1, first_refs, EVEN)
    rest = gather_steps(pc, w2, g2, rest_refs, REST)
    next(gather)

    def pump(count=1):
        for _ in range(count):
            next(rest, None)

    unpack(small, "one", gains)
    unpack(small, "bias", conv_b)
    unpack_conv(small, conv_w)
    spread_mat = spread_heads()
    wide_skip(small, spread_mat, skip)
    for i in range(rows // 64):
        r = pl.ds(i * 64, 64)
        v = hid[r, :].astype(F32)
        f = lax.rsqrt(jnp.mean(v * v, axis=1, keepdims=True) + norm_eps)
        scale[r, :] = f
        normed[r, :] = (v * f * gains[...]).astype(BF)
        next(gather)
    make_tables(pc, lens, ldec, root_t, tables)
    dec_own[...] = jnp.zeros_like(dec_own)
    dec_own[0:1, 0:MH] = din_t[rows - 1 : rows, :]
    for k, _ in enumerate(gather):
        if k == planes:
            pump()

    def project(at, width):
        return nn(normed[...], g1[:, :, :, :, :, pl.ds(at, width)].reshape(D, width))

    base = GATE_AT
    for i in range(XBC // 256):
        sl = pl.ds(i * 256, 256)
        xb = project(base + i * 256, 256).astype(BF)
        xe[pl.ds(8, rows), sl] = xb.astype(F32)
        edge_out[:, sl] = xb[rows - 16 :, :]
    kv = project(QUERY_WIDTH, 2 * KEY_WIDTH)
    kv_own[:, pl.ds(0, KEY_WIDTH)] = rotate(kv[:, :KEY_WIDTH], cos_w, sin_w).astype(BF)
    kv_own[:, pl.ds(KEY_WIDTH, KEY_WIDTH)] = kv[:, KEY_WIDTH:].astype(BF)
    spreads = spread_steps(pc, kv_own, edge_out, dec_own, kv_all, edge_in, decs, spread_refs)
    next(spreads)
    for i in range(QUERY_WIDTH // 256):
        qv = project(i * 256, 256)
        for t in (0, 1):
            q_out[:, pl.ds(i * 256 + t * 128, 128)] = rotate(
                qv[:, t * 128 : (t + 1) * 128], cos_w, sin_w
            ).astype(BF)
    split_heads(q_out, qh, jnp.asarray(HEAD_WIDTH**-0.5, BF))
    next(spreads)
    xe[pl.ds(0, 8), :] = edge_in[pl.ds(8, 8), :].astype(F32)
    pump()
    next(spreads)
    mixing = mixer_steps(
        xe, same, conv_w, conv_b, cum_t, cum, dt_t, we_t, skip, doc_c, doc_r, pre, xo, mix, so, xw, bias
    )
    for _ in mixing:
        next(spreads, None)
        pump()
    for k in range(n):
        dec_rows[k : k + 1, :] = decs[k, 0:1, :]
    decays[...] = wide(dec_rows[:, 0:MH], spread_mat)
    states = relay_steps(pc, False, so, decays, state_in, relay_refs)
    next(states)
    m_ref[...] = jnp.full_like(m_ref, large_negative)
    l_ref[...] = jnp.zeros_like(l_ref)
    acc[...] = jnp.zeros_like(acc)
    seen = (pc.ctx * rows + rows + block - 1) // block
    per = block // rows
    parts = 8
    each = n // per // parts

    def keys_at(j):
        return kv_all[pl.ds(j * per, per), :, :].reshape(block, 2 * KEY_WIDTH)

    for k in range(parts):
        lo = each * k

        @pl.loop(jnp.minimum(lo, seen), jnp.minimum(lo + each, seen))
        def _(j):
            attend_block(j, block, qh, keys_at(j), pos, m_ref, l_ref, acc, range(QUERY_HEADS))

        pump(2)
        if k in (3, 6):
            next(states)
    attend_end(att, lse, m_ref, l_ref, acc)
    for _ in spreads:
        pass
    for _ in rest:
        pass
    for _ in states:
        pass


def front(planes, lens, hid, w1, w2, cos_w, sin_w, ldec, root_t, small, block, collective):
    n = 4 * planes
    rows = hid.shape[0]
    each = w1.shape[0]
    sds = jax.ShapeDtypeStruct
    return pl.pallas_call(
        functools.partial(front_kernel, planes, block),
        out_shape=(
            sds((rows, D), BF),
            sds((rows, 1), F32),
            sds((planes, 2, 2, 2, each, w1.shape[1]), BF),
            sds((planes, 2, 2, 2, each, w2.shape[1]), BF),
            sds((rows, QUERY_WIDTH), BF),
            sds((n, rows, 2 * KEY_WIDTH), BF),
            sds((rows + 8, XBC), F32),
            sds((n, INNER), F32),
            sds((rows, XBC), BF),
            sds((rows, XBC), BF),
            sds((rows, INNER), F32),
            sds((n, NS // n, INNER), BF),
            sds((rows, QUERY_WIDTH), BF),
            sds((QUERY_HEADS, rows), F32),
        ),
        in_specs=[SM, VM, VM, HB] + [VM] * 5,
        out_specs=(VM, VM, VM, HB) + (VM,) * 10,
        scratch_shapes=[
            pltpu.VMEM((rows, 2 * KEY_WIDTH), BF),
            pltpu.VMEM((16, XBC), BF),
            pltpu.VMEM((16, XBC), BF),
            pltpu.VMEM((8, 128), F32),
            pltpu.VMEM((n, 8, 128), F32),
            pltpu.VMEM((n, 128), F32),
            pltpu.VMEM((1, D), F32),
            pltpu.VMEM((CONV, XBC), F32),
            pltpu.VMEM((1, XBC), F32),
            pltpu.VMEM((1, INNER), F32),
            pltpu.VMEM((n, NS // n, INNER), BF),
            pltpu.VMEM((QUERY_HEADS * rows, HEAD_WIDTH), BF),
            pltpu.VMEM((QUERY_HEADS, rows), F32),
            pltpu.VMEM((QUERY_HEADS, rows), F32),
            pltpu.VMEM((QUERY_WIDTH, rows), F32),
            pltpu.VMEM((rows, INNER), BF),
            pltpu.VMEM((rows, rows), F32),
        ]
        + table_scratch(rows)
        + gather_scratch(planes)
        + gather_scratch(planes)
        + spread_scratch(planes)
        + relay_scratch(planes),
        compiler_params=params(collective),
    )(lens, hid, w1, w2, cos_w, sin_w, ldec, root_t, small)


def gate_back_rows(i, grad, mixed, gate, gain, din_t, spread_mat, dm, dproj, dgain, dinc):
    r = pl.ds(pl.multiple_of(i * 64, 64), 64)
    m, gv, gr = mixed[r, :].astype(F32), gate[r, :], grad[r, pl.ds(QUERY_WIDTH, INNER)]
    sig = jax.nn.sigmoid(gv)
    sil = gv * sig
    gated = m * sil
    factor = lax.rsqrt(jnp.mean(gated * gated, axis=1, keepdims=True) + norm_eps)
    w = gr * gain[...]
    dg = factor * (w - gated * factor * factor * jnp.mean(w * gated, axis=1, keepdims=True))
    dgain[...] += jnp.sum(gr * gated * factor, axis=0, keepdims=True)
    dproj[r, pl.ds(GATE_AT, INNER)] = (dg * m * (sig * (1.0 + gv * (1.0 - sig)))).astype(BF)
    d = dg * sil
    dm[r, :] = d.astype(BF)
    dinc[r, :] = (d * wide(din_t[r, :], spread_mat)).astype(BF)


def mixer_back_steps(
    xe, mk, cw, cum_t, cum, dt_t, we_t, skip, doc_c, doc_r, pre, xo, dm, dc_in, ds, dpre, dcw, dskip, xw, bias
):
    rows = pre.shape[0]
    here = pl.ds(0, rows)
    b_rows, c_rows = xo[:, pl.ds(INNER, NS)], xo[:, pl.ds(INNER + NS, NS)]
    cross = nt(b_rows, c_rows)
    s_at = lax.broadcasted_iota(jnp.int32, (rows, rows), 0)
    t_at = lax.broadcasted_iota(jnp.int32, (rows, rows), 1)
    bias[...] = jnp.where((doc_c[...] == doc_r[...]) & (s_at <= t_at), 0.0, large_negative)
    lanes = lax.broadcasted_iota(jnp.int32, (rows, 2 * MP), 1)

    def slope(sl):
        v = pre[:, sl].astype(F32)
        sig = jax.nn.sigmoid(v)
        return sig * (1.0 + v * (1.0 - sig))

    dcross = jnp.zeros((rows, rows), F32)
    for p in range(MH // 2):
        sl = pl.ds(p * 2 * MP, 2 * MP)
        xv = xo[:, sl].astype(F32)
        dt2, we2 = pair_columns(dt_t, p, lanes), pair_columns(we_t, p, lanes)
        xd = xv * dt2
        xw[:, sl] = (xd * we2).astype(BF)
        g = dm[:, sl]
        outs = []
        for k in (0, 1):
            h = 2 * p + k
            low = jnp.exp(jnp.minimum(cum[h : h + 1, :] - cum_t[:, h : h + 1], bias[...]))
            outs.append(nn((low * cross).astype(BF), g))
            part = jnp.where((lanes < MP) == (k == 0), xd, 0.0).astype(BF)
            dcross = dcross + nt(part, g) * low
        dxd = two(outs[0], outs[1], lanes) + we2 * nn(b_rows, ds[:, sl])
        gf = g.astype(F32)
        dskip[:, sl] = jnp.sum(gf * xv, axis=0, keepdims=True)
        dpre[here, sl] = (dxd * dt2 + skip[:, sl] * gf) * slope(sl)
        if p % 4 == 3:
            yield
    db16 = dcross.astype(BF)
    slb, slc = pl.ds(INNER, NS), pl.ds(INNER + NS, NS)
    dpre[here, slb] = (nn(db16, c_rows) + nt(xw[...], ds[...])) * slope(slb)
    dpre[here, slc] = (tn(db16, b_rows) + dc_in[...]) * slope(slc)
    yield
    for i in range(XBC // 256):
        sl = pl.ds(i * 256, 256)
        d = dpre[here, sl]
        for j in range(CONV):
            dcw[j : j + 1, sl] = jnp.sum(
                d * (xe[pl.ds(5 + j, rows), sl] * mk[:, j : j + 1]), axis=0, keepdims=True
            )
        dcw[CONV : CONV + 1, sl] = jnp.sum(d, axis=0, keepdims=True)


def back_kernel(planes, count, block, *refs):
    lefts, rights, refs = refs[:count], refs[count : 2 * count], refs[2 * count :]
    if count:
        branch = rights[0]
    else:
        branch, refs = refs[0], refs[1:]
    (
        lens, grad, mixed, gate, xo, state_in, q_in, kv, lse, cos_w, sin_w, decays, xe, ldec, root_t, small, pre,
    ) = refs[:17]
    refs = refs[17:]
    if count:
        scattered, refs = refs[0], refs[1:]
    dproj, dgain, dcw, dskip = refs[:4]
    (
        dm, dinc, dc, dstate, dsnew, flat, qh, doh, dl, acc, dkv, dkv_own, dpre, edge, bias, esem
    ) = refs[4:20]
    gain, cw, skip, state = refs[20:24]
    tables, refs = refs[24:33], refs[33:]
    pos, same, doc_c, doc_r, cum, cum_t, dt_t, we_t, din_t = tables
    relay_refs, refs = refs[:6], refs[6:]
    fold_refs, refs = refs[:10], refs[10:]
    pc = Place(planes)
    n = 4 * planes
    rows = mixed.shape[0]
    greet_row(pc, count > 0)
    side = (
        woven_steps(pc, tuple(zip(lefts, rights)), scattered, refs) if count else iter(())
    )

    def pump():
        next(side, None)

    pump()
    spread_mat = spread_heads()
    unpack(small, "gate", gain)
    unpack_conv(small, cw)
    wide_skip(small, spread_mat, skip)
    make_tables(pc, lens, ldec, root_t, tables)
    state[...] = state_in[...].reshape(state.shape)
    dgain[...] = jnp.zeros_like(dgain)
    pl.loop(0, rows // 64)(
        lambda i: gate_back_rows(i, grad, mixed, gate, gain, din_t, spread_mat, dm, dproj, dgain, dinc)
    )
    ds0 = tn(xo[:, pl.ds(INNER + NS, NS)], dinc[...]).astype(BF)
    dc[...] = nt(dinc[...], state[...])
    dstate[...] = ds0.reshape(dstate.shape)
    states = relay_steps(pc, True, dstate, decays, dsnew, relay_refs)
    next(states)
    for _ in range(planes):
        pump()
    split_heads(q_in, qh, jnp.asarray(HEAD_WIDTH**-0.5, BF))
    go = grad[:, pl.ds(0, QUERY_WIDTH)].astype(BF)
    head = lax.broadcasted_iota(jnp.int32, (QUERY_HEADS, QUERY_WIDTH), 0)
    lane = lax.broadcasted_iota(jnp.int32, (QUERY_HEADS, QUERY_WIDTH), 1)
    for h in range(QUERY_HEADS):
        doh[pl.ds(h * rows, rows), :] = go[:, h * HEAD_WIDTH : (h + 1) * HEAD_WIDTH]
    dl[...] = exact(
        (lane // HEAD_WIDTH == head).astype(F32),
        go.astype(F32) * branch[:, pl.ds(0, QUERY_WIDTH)].astype(F32),
        ((1,), (1,)),
    )
    acc[...] = jnp.zeros_like(acc)
    total = kv.shape[0] // block
    seen = (pc.ctx * rows + rows + block - 1) // block
    parts = 4
    each = total // parts

    @pl.loop(seen, (pc.z + 1) * 4 * rows // block)
    def _(j):
        dkv[pl.ds(pl.multiple_of(j * block, block), block), :] = jnp.zeros((block, 2 * KEY_WIDTH), BF)

    for k in range(parts):
        lo = each * k

        @pl.loop(jnp.minimum(lo, seen), jnp.minimum(lo + each, seen))
        def _(j):
            for g in range(KEY_VALUE_HEADS):
                attend_back_block(j, g, block, qh, doh, kv, pos, lse, dl, dkv, acc)

        pump()
        if k == 1:
            next(states)
    folds = fold_steps(
        pc, lambda s: dkv.at[pl.ds(pl.multiple_of(s * rows, rows), rows), :], dkv_own, fold_refs
    )
    next(folds)
    for t in range(QUERY_WIDTH // 128):
        dq = acc[pl.ds(t * 128, 128), :].T * (HEAD_WIDTH**-0.5)
        dproj[:, pl.ds(t * 128, 128)] = rotate(dq, cos_w, sin_w, -1.0).astype(BF)
    next(states)
    flat[...] = dsnew[...].reshape(flat.shape)
    next(folds)
    mixing = mixer_back_steps(
        xe, same, cw, cum_t, cum, dt_t, we_t, skip, doc_c, doc_r, pre, xo, dm, dc, flat, dpre, dcw, dskip, dinc, bias
    )
    next(mixing)
    next(folds)
    pump()
    next(mixing)
    pump()
    next(mixing)
    next(folds)
    pump()
    next(mixing)
    prior = rcopy(pc, dpre.at[pl.ds(0, 8), :], edge, esem.at[0], esem.at[1], (lax.rem(pc.ctx + n - 1, n), pc.y))
    pl.when(pc.ctx > 0)(lambda: prior.start())
    for _ in mixing:
        pass
    pump()
    for _ in folds:
        pass
    dproj[:, pl.ds(QUERY_WIDTH, KEY_WIDTH)] = rotate(dkv_own[:, pl.ds(0, KEY_WIDTH)], cos_w, sin_w, -1.0).astype(BF)
    dproj[:, pl.ds(QUERY_WIDTH + KEY_WIDTH, KEY_WIDTH)] = dkv_own[:, pl.ds(KEY_WIDTH, KEY_WIDTH)].astype(BF)
    pl.when(pc.ctx < n - 1)(lambda: prior.wait_recv())

    @pl.when(pc.ctx == n - 1)
    def _():
        edge[...] = jnp.zeros_like(edge)

    dpre[pl.ds(rows, 8), :] = edge[...]
    for i in range(XBC // 256):
        sl = pl.ds(i * 256, 256)
        total_grad = jnp.zeros((rows, 256), F32)
        for j in range(CONV):
            total_grad = total_grad + cw[j : j + 1, sl] * (
                dpre[pl.ds(CONV - 1 - j, rows), sl] * same[:, CONV + j : CONV + j + 1]
            )
        dproj[:, pl.ds(XBC_AT + i * 256, 256)] = total_grad.astype(BF)
    for _ in states:
        pass
    pl.when(pc.ctx > 0)(lambda: prior.wait_send())
    for _ in side:
        pass


def back(planes, lefts, rights, args, block, collective):
    count = len(lefts)
    n = 4 * planes
    rows = args[-1].shape[0]
    keys = n * rows
    outs = [
        jax.ShapeDtypeStruct((rows, MIXIN), BF),
        jax.ShapeDtypeStruct((1, INNER), F32),
        jax.ShapeDtypeStruct((CONV + 1, XBC), F32),
        jax.ShapeDtypeStruct((1, INNER), F32),
    ]
    scratch = [
        pltpu.VMEM((rows, INNER), BF),
        pltpu.VMEM((rows, INNER), BF),
        pltpu.VMEM((rows, NS), F32),
        pltpu.VMEM((n, NS // n, INNER), BF),
        pltpu.VMEM((n, NS // n, INNER), BF),
        pltpu.VMEM((NS, INNER), BF),
        pltpu.VMEM((QUERY_HEADS * rows, HEAD_WIDTH), BF),
        pltpu.VMEM((QUERY_HEADS * rows, HEAD_WIDTH), BF),
        pltpu.VMEM((QUERY_HEADS, rows), F32),
        pltpu.VMEM((QUERY_WIDTH, rows), F32),
        pltpu.VMEM((keys, 2 * KEY_WIDTH), BF),
        pltpu.VMEM((rows, 2 * KEY_WIDTH), F32),
        pltpu.VMEM((rows + 8, XBC), F32),
        pltpu.VMEM((8, XBC), F32),
        pltpu.VMEM((rows, rows), F32),
        DMA((2,)),
        pltpu.VMEM((1, INNER), F32),
        pltpu.VMEM((CONV, XBC), F32),
        pltpu.VMEM((1, INNER), F32),
        pltpu.VMEM((NS, INNER), BF),
    ]
    scratch += table_scratch(rows)
    scratch += relay_scratch(planes) + fold_scratch(planes, rows, 2 * KEY_WIDTH)
    if count:
        widths = [r.shape[1] for r in rights]
        each = lefts[0].shape[1] // n
        outs = [jax.ShapeDtypeStruct((each, sum(widths)), F32)] + outs
        scratch += woven_scratch(planes, each, widths)
    return pl.pallas_call(
        functools.partial(back_kernel, planes, count, block),
        out_shape=tuple(outs),
        in_specs=[VM] * (2 * count + (not count)) + [SM] + [VM] * (len(args) - 2 + bool(count)),
        out_specs=(VM,) * len(outs),
        scratch_shapes=scratch,
        compiler_params=params(collective),
    )(*lefts, *rights, *args)


def last_kernel(
    planes, left, dproj, w1, w2, tok, scale, packed, dres, small, scattered, dhid, totals, dn, wg, wsem, gain, *scratch
):
    pc = Place(planes)
    greet_planes(pc)
    rows = dproj.shape[0]
    fetch = pltpu.make_async_copy(w2.at[:, :, :, :, :, pl.ds(0, INNER)], wg, wsem)
    fetch.start()
    side = scatter_steps(pc, ((left, dproj),), scattered, scratch[6:], LAST)
    next(side)
    unpack(packed, "one", gain)
    fetch.wait()
    next(side)
    part = planes // 4
    for i in range(4):
        at = pl.ds(i * part, part)
        a, b = w1[at].reshape(D // 4, FIRST), wg[at].reshape(D // 4, INNER)
        dn[:, pl.ds(i * 256, 256)] = (
            nt(dproj[:, pl.ds(0, GATE_AT)], a[:, :GATE_AT])
            + nt(dproj[:, pl.ds(GATE_AT, INNER)], b)
            + nt(dproj[:, pl.ds(XBC_AT, XBC)], a[:, GATE_AT:])
        )
        next(side)
        next(side)
    totals[...] = small[...]
    for i in range(rows // 64):
        r = pl.ds(i * 64, 64)
        v, g, f = tok[r, :].astype(F32), dn[r, :], scale[r, :]
        w = g * gain[...]
        dhid[r, :] = dres[r, :] + f * (w - v * f * f * jnp.mean(w * v, axis=1, keepdims=True))
        part = jnp.sum(g * v * f, axis=0, keepdims=True)
        for t in range(D // 128):
            totals[t : t + 1, :] = totals[t : t + 1, :] + part[:, t * 128 : (t + 1) * 128]
    sums = total_steps(pc, totals, scratch[:6])
    next(sums)
    for _ in side:
        next(sums, None)
    for _ in sums:
        pass


def last(planes, left, dproj, w1, w2, tok, scale, packed, dres, small, collective):
    rows = dproj.shape[0]
    each = left.shape[1] // (4 * planes)
    return pl.pallas_call(
        functools.partial(last_kernel, planes),
        out_shape=(
            jax.ShapeDtypeStruct((each, MIXIN), F32),
            jax.ShapeDtypeStruct((rows, D), F32),
            jax.ShapeDtypeStruct((SMALL_ROWS, 128), F32),
        ),
        in_specs=[VM] * 3 + [HB] + [VM] * 5,
        out_specs=(VM,) * 3,
        scratch_shapes=[
            pltpu.VMEM((rows, D), F32),
            pltpu.VMEM(w2.shape[:-1] + (INNER,), BF),
            DMA,
            pltpu.VMEM((1, D), F32),
        ]
        + total_scratch(planes)
        + scatter_scratch(planes, each, [MIXIN], LAST),
        compiler_params=params(collective),
    )(left, dproj, w1, w2, tok, scale, packed, dres, small)


def doc_layout(lengths, token_positions):
    starts = jnp.cumsum(lengths) - lengths
    inside = token_positions[:, None] >= starts[None, :]
    document_index = jnp.sum(inside.astype(jnp.int32), axis=1) - 1
    begins = jnp.max(jnp.where(inside, starts[None, :], 0), axis=1)
    return (document_index, token_positions - begins)


def rope_tables(rel_pos):
    half_dim = HEAD_WIDTH // 2
    inv_freq = rope_base ** (-2.0 * jnp.arange(half_dim, dtype=jnp.float32) / HEAD_WIDTH)
    angles = rel_pos.astype(jnp.float32)[:, None] * inv_freq[None, :]
    return (jnp.cos(angles), jnp.sin(angles))


def norm_backward(grad_normed, values, factor, gain_vals):
    weighted = grad_normed * gain_vals
    grad_values = factor * (
        weighted - values * factor * factor * jnp.mean(weighted * values, axis=1, keepdims=True)
    )
    grad_gain = jnp.sum(grad_normed * values * factor, axis=0)
    return (grad_values, grad_gain)


def adamw_step(param_vals, grad_vals, first_vals, second_vals, weight_decay):
    first_new = beta_one * first_vals + (1.0 - beta_one) * grad_vals
    second_new = beta_two * second_vals + (1.0 - beta_two) * grad_vals * grad_vals
    update = (
        first_new
        / (1.0 - beta_one**STEP)
        / (jnp.sqrt(second_new / (1.0 - beta_two**STEP)) + adam_eps)
    )
    return (param_vals - learn_rate * (update + weight_decay * param_vals), first_new, second_new)


def adam_direction(grad_vals, first_vals, second_vals):
    first_new = beta_one * first_vals + (1.0 - beta_one) * grad_vals
    second_new = beta_two * second_vals + (1.0 - beta_two) * grad_vals * grad_vals
    update = (
        first_new
        / (1.0 - beta_one**STEP)
        / (jnp.sqrt(second_new / (1.0 - beta_two**STEP)) + adam_eps)
    )
    return (update, first_new, second_new)


def shards(
    planes,
    hidden,
    out_grad,
    decay_log,
    doc_lengths,
    weights,
    first_moment,
    second_moment,
    small_params,
    small_first,
    small_second,
):
    local_rows = hidden.shape[1]
    count = 4 * planes
    ctx_index = lax.axis_index("ctx")
    first_pos = ctx_index * local_rows
    contract_last = (((1,), (1,)), ((), ()))
    lengths = doc_lengths[0]
    token_positions = first_pos + jnp.arange(local_rows, dtype=jnp.int32)
    cosine_table, sine_table = rope_tables(doc_layout(lengths, token_positions)[1])
    cos_wide = jnp.tile(cosine_table, (1, 4))
    sin_wide = jnp.tile(jnp.concatenate([-sine_table, sine_table], axis=1), (1, 2))
    size = small_params.shape[0]
    packed = jnp.pad(small_params, (0, SMALL_ROWS * 128 - size)).reshape(SMALL_ROWS, 128)
    log_decay = decay_log[0]
    root_t = jnp.sqrt(-jnp.expm1(2.0 * log_decay)).T
    block = 512
    own_b = weights.astype(jnp.bfloat16)
    own_first = jnp.concatenate([own_b[:, :GATE_AT], own_b[:, XBC_AT:MIXIN]], axis=1)
    own_rest = jnp.concatenate([own_b[:, GATE_AT:XBC_AT], own_b[:, MIXIN:]], axis=1)
    (
        normed_one, scale_one, first_w, rest_w, query_rows, kv_all, xe, decays, pre, xo, mix_local,
        state_in, attended, log_sums,
    ) = front(
        planes, doc_lengths, hidden[0], own_first, own_rest, cos_wide, sin_wide, log_decay, root_t,
        packed, block, 0,
    )
    rest_flat = rest_w.reshape(D, rest_w.shape[-1])
    mixout_w = rest_flat[:, INNER : INNER + MIXOUT]
    mlp_w = rest_flat[:, INNER + MIXOUT :]
    gate_in = jnp.dot(normed_one, rest_flat[:, :INNER], preferred_element_type=jnp.float32)
    mixed, branch = gate_out(
        planes, doc_lengths, mix_local, xo, state_in, log_decay, gate_in, packed, attended
    )

    tok_f = hidden[0].astype(jnp.float32)
    gain_two = small_params[D : 2 * D]
    resid_one = tok_f + lax.dot_general(
        branch, mixout_w, contract_last, preferred_element_type=jnp.float32
    )
    scale_two = lax.rsqrt(jnp.mean(resid_one * resid_one, axis=1, keepdims=True) + norm_eps)
    normed_two = (resid_one * scale_two * gain_two).astype(jnp.bfloat16)
    gate_up = jnp.dot(normed_two, mlp_w[:, : 2 * FF], preferred_element_type=jnp.float32)
    gate_part = gate_up[:, :FF]
    up_part = gate_up[:, FF:]
    sigma_gate = jax.nn.sigmoid(gate_part)
    silu_gate = gate_part * sigma_gate
    hidden_mid = (silu_gate * up_part).astype(jnp.bfloat16)
    block_out = resid_one + lax.dot_general(
        hidden_mid, mlp_w[:, 2 * FF :], contract_last, preferred_element_type=jnp.float32
    )
    out_hidden = block_out.astype(jnp.bfloat16)[None]
    grad_out = out_grad[0]
    grad_mid = jnp.dot(grad_out, mlp_w[:, 2 * FF :], preferred_element_type=jnp.float32)
    silu_slope = sigma_gate * (1.0 + gate_part * (1.0 - sigma_gate))
    grad_gate_up = jnp.concatenate(
        [grad_mid * up_part * silu_slope, grad_mid * silu_gate], axis=1
    ).astype(jnp.bfloat16)
    grad_normed_two = lax.dot_general(
        grad_gate_up, mlp_w[:, : 2 * FF], contract_last, preferred_element_type=jnp.float32
    )
    grad_norm_two, grad_gain_two = norm_backward(grad_normed_two, resid_one, scale_two, gain_two)
    grad_resid_one = grad_out.astype(jnp.float32) + grad_norm_two
    grad_resid_b = grad_resid_one.astype(jnp.bfloat16)

    grad_branch = jnp.dot(grad_resid_b, mixout_w, preferred_element_type=jnp.float32)
    lefts = [by_core(v, planes) for v in (grad_resid_b, normed_two, grad_out)]
    rights = [branch, grad_gate_up, hidden_mid]
    args = (
        doc_lengths, grad_branch, mixed, gate_in, xo, state_in, query_rows,
        kv_all.reshape(count * local_rows, 2 * KEY_WIDTH), log_sums, cos_wide, sin_wide, decays,
        xe, log_decay, root_t, packed, pre,
    )
    if planes <= 4:
        early, grad_proj, gate_gain_grads, conv_grads, skip_grads = back(
            planes, lefts, rights, args, block, 3
        )
    else:
        early = scatter_rows(planes, lefts, rights, 4)
        grad_proj, gate_gain_grads, conv_grads, skip_grads = back(planes, [], [], (branch,) + args, block, 3)
    small_local = jnp.concatenate(
        [
            jnp.zeros((D,), jnp.float32),
            grad_gain_two,
            gate_gain_grads[0],
            conv_grads.reshape(-1),
            jnp.sum(skip_grads.reshape(MH, MP), axis=1),
        ]
    )
    padded = jnp.pad(small_local, (0, SMALL_ROWS * 128 - size)).reshape(SMALL_ROWS, 128)
    mixin_grads, grad_hidden, totals = last(
        planes, by_core(normed_one, planes), grad_proj, first_w, rest_w, hidden[0], scale_one,
        packed, grad_resid_one, padded, 5,
    )
    grad_hidden = grad_hidden[None]
    small_grads = totals.reshape(-1)[:size]
    grad_weights = jnp.concatenate([mixin_grads, early], axis=1)
    new_weights, new_first, new_second = adamw_step(
        weights, grad_weights, first_moment, second_moment, decay_rate
    )
    small_step, small_first_new, small_second_new = adam_direction(
        small_grads, small_first, small_second
    )
    return (
        out_hidden,
        grad_hidden,
        grad_weights,
        new_weights,
        new_first,
        new_second,
        small_grads,
        small_step,
        small_first_new,
        small_second_new,
    )


def solution(mesh):
    placed = (
        P("fsdp", "ctx", None),
        P("fsdp", "ctx", None),
        P("fsdp", None, "ctx"),
        P("fsdp", None),
        P(("ctx", "fsdp"), None),
        P(("ctx", "fsdp"), None),
        P(("ctx", "fsdp"), None),
        P(),
        P(),
        P(),
    )
    return jax.shard_map(
        functools.partial(shards, mesh.shape["ctx"] // 4),
        mesh=mesh,
        in_specs=placed,
        out_specs=(
            P("fsdp", "ctx", None),
            P("fsdp", "ctx", None),
            P(("ctx", "fsdp"), None),
            P(("ctx", "fsdp"), None),
            P(("ctx", "fsdp"), None),
            P(("ctx", "fsdp"), None),
            P(),
            P(),
            P(),
            P(),
        ),
        check_vma=False,
    )
```

```python
import functools
import math

import jax
import jax.numpy as jnp
from jax import lax
from jax.experimental import pallas as pl
from jax.experimental.pallas import tpu as pltpu
from jax.sharding import PartitionSpec as P

D = 1024
QUERY_HEADS = 8
KEY_VALUE_HEADS = 2
HEAD_WIDTH = 64
MH = 24
MP = 64
NS = 128
FF = 2048
CONV = 4
STEP = 3
QUERY_WIDTH = 512
KEY_WIDTH = 128
INNER = 1536
XBC = 1792
MIXIN = 4096
MIXOUT = 2048
SMALL_ROWS = 104
TOKENS = 256
PIECE = 256

norm_eps = 1e-05
rope_base = 100000000000.0
large_negative = -1e30
learn_rate = 0.02
beta_one = 0.9
beta_two = 0.95
adam_eps = 1e-08
decay_rate = 0.1

MESH = pl.DeviceIdType.MESH
BF = jnp.bfloat16
F32 = jnp.float32
VM = pl.BlockSpec(memory_space=pltpu.VMEM)
SM = pl.BlockSpec(memory_space=pltpu.SMEM)
HB = pl.BlockSpec(memory_space=pl.ANY)
DMA = pltpu.SemaphoreType.DMA


def params(collective=None):
    if collective is None:
        return pltpu.CompilerParams(vmem_limit_bytes=62 * 2**20)
    return pltpu.CompilerParams(
        collective_id=collective, has_side_effects=True, vmem_limit_bytes=62 * 2**20
    )


def nt(a, b):
    return lax.dot_general(a, b, (((1,), (1,)), ((), ())), preferred_element_type=F32)


def tn(a, b):
    return lax.dot_general(a, b, (((0,), (0,)), ((), ())), preferred_element_type=F32)


def nn(a, b):
    return lax.dot_general(a, b, (((1,), (0,)), ((), ())), preferred_element_type=F32)


class Place:
    def __init__(self, planes):
        ctx = lax.axis_index("ctx")
        self.ctx = ctx
        self.Z, self.z, self.x, self.c = planes, ctx // 4, (ctx // 2) % 2, ctx % 2
        self.y = lax.axis_index("fsdp")
        self.up, self.down = self.z + 1 < planes, self.z > 0

    def shard(self, z, x, y, c):
        return ((z * 2 + x) * 2 + c) * 2 + y

    def spot(self, z, x, c):
        return (z * 2 + x) * 2 + c

    def dev(self, z, x, y, c):
        return ((z * 2 + x) * 2 + c, y)

    def near(self, d):
        z, x, y, c = self.z, self.x, self.y, self.c
        return {
            "x": self.dev(z, 1 - x, y, c),
            "y": self.dev(z, x, 1 - y, c),
            "c": self.dev(z, x, y, 1 - c),
            "u": self.dev(z + 1, x, y, c),
            "d": self.dev(z - 1, x, y, c),
        }[d]

    def zord(self, k):
        if k == self.Z - 1:
            return self.z
        low = self.Z - 1 - k
        z = self.z
        return jnp.where(
            2 * z < self.Z, jnp.where(low > z, low, low - 1), jnp.where(k < z, k, k + 1)
        )


def greet(pc, dims="xyc", chain=True):
    bar = pltpu.get_barrier_semaphore()

    def sig(d):
        pl.semaphore_signal(bar, inc=1, device_id=pc.near(d), device_id_type=MESH)

    for d in dims:
        sig(d)
    if chain:
        pl.when(pc.up)(lambda: sig("u"))
        pl.when(pc.down)(lambda: sig("d"))
    peers = len(dims)
    if chain:
        peers = peers + pc.up.astype(jnp.int32) + pc.down.astype(jnp.int32)
    pl.semaphore_wait(bar, peers)


def greet_row(pc, across=False):
    bar = pltpu.get_barrier_semaphore()
    n = 4 * pc.Z

    @pl.loop(1, n)
    def _(d):
        pl.semaphore_signal(
            bar, inc=1, device_id=(lax.rem(pc.ctx + d, n), pc.y), device_id_type=MESH
        )

    if across:
        pl.semaphore_signal(bar, inc=1, device_id=pc.near("y"), device_id_type=MESH)
    pl.semaphore_wait(bar, n - 1 + int(across))


def rcopy(pc, src, dst, ssem, rsem, d):
    return pltpu.make_async_remote_copy(
        src_ref=src,
        dst_ref=dst,
        send_sem=ssem,
        recv_sem=rsem,
        device_id=pc.near(d) if isinstance(d, str) else d,
        device_id_type=MESH,
    )


def add_into(dst, parts, width=512):
    columns = dst.shape[-1]
    step = width if columns % width == 0 else (256 if columns % 256 == 0 else 128)

    @pl.loop(0, columns // step)
    def _(i):
        sl = pl.ds(pl.multiple_of(i * step, step), step)
        total = parts[0][:, sl].astype(F32)
        for r in parts[1:]:
            total = total + r[:, sl].astype(F32)
        dst[:, sl] = total.astype(dst.dtype)


def plane_peers(pc):
    return [pc.dev(lax.rem(pc.z + d, pc.Z), pc.x, pc.y, pc.c) for d in range(1, pc.Z)]


def greet_planes(pc):
    bar = pltpu.get_barrier_semaphore()
    peers = [pc.near(d) for d in "xyc"] + plane_peers(pc)
    for d in peers:
        pl.semaphore_signal(bar, inc=1, device_id=d, device_id_type=MESH)
    pl.semaphore_wait(bar, len(peers))


EVEN = (25, 25, 64)
REST = (35, 19, 64)


def split(columns, shares, unit):
    a, b = (columns * s // shares[2] // unit * unit for s in shares[:2])
    return a, b, columns - a - b


def part_columns(widths, p):
    a, b, w = widths
    return pl.ds((w, w + a, 0)[p], widths[p])


def gather_scratch(planes):
    return [
        DMA((2, planes, 2)),
        DMA((2, planes)),
        DMA((2, planes, 2)),
        DMA((2, planes, 4)),
        DMA((2, planes, 8)),
        DMA((2, planes)),
        DMA((2 + planes,)),
        DMA((4 + 2 * planes,)),
        DMA,
    ]


def gather_steps(pc, w_ref, out_ref, scratch, shares):
    zs, xs, ys, cs, rs, tz, tc, tr, loc = scratch
    Z, z, x, y, c = pc.Z, pc.z, pc.x, pc.y, pc.c
    widths = split(w_ref.shape[-1], shares, 128)

    def cols(p):
        return part_columns(widths, p)

    def spot(q):
        return (x if q < 2 else 1 - x), (y if q % 2 == 0 else 1 - y)

    def cp(p, zz, q, sem, d, own=False, core=None):
        xx, yy = spot(q)
        dst = out_ref.at[zz, xx, c, yy, :, cols(p)]
        return rcopy(pc, w_ref.at[:, cols(p)] if own else dst, dst, sem, rs.at[p, zz, core if core is not None else q], d)

    def along(p, zz, up, own=False):
        return cp(p, zz, 0, zs.at[p, zz, int(up)], "u" if up else "d", own, 0)

    def first(p, zz, own=False):
        return cp(p, zz, 0, xs.at[p, zz], "x" if p == 0 else "y", own, 2 if p == 0 else 1)

    def second(p, zz, q, own=False):
        if p == 0:
            return cp(p, zz, 2 * q, ys.at[p, zz, q], "y", own, 2 * q + 1)
        return cp(p, zz, q, ys.at[p, zz, q], "x", own, 2 + q)

    def core(p, zz, q, own=False):
        return cp(p, zz, q, cs.at[p, zz, q], "c", own, 4 + q)

    def arrived(p, zz, q):
        rcopy(
            pc, w_ref.at[:, cols(p)], out_ref.at[0, 0, 0, 0, :, cols(p)], loc, rs.at[p, zz, q], "c"
        ).wait_recv()

    def t_x():
        return rcopy(
            pc, w_ref.at[:, cols(2)], out_ref.at[z, x, c, y, :, cols(2)], tc.at[0], tr.at[0], "x"
        )

    def t_y():
        v = out_ref.at[z, :, c, y, :, cols(2)]
        return rcopy(pc, v, v, tc.at[1], tr.at[1], "y")

    def t_z(zz, up):
        v = out_ref.at[zz, :, c, :, :, cols(2)]
        return rcopy(pc, v, v, tz.at[int(up), zz], tr.at[4 + zz], "u" if up else "d")

    def t_c(zz):
        v = out_ref.at[zz, :, c, :, :, cols(2)]
        return rcopy(pc, v, v, tc.at[2 + zz], tr.at[4 + Z + zz], "c")

    keep = pltpu.make_async_copy(w_ref, out_ref.at[z, x, c, y], loc)
    keep.start()
    t_x().start()
    for p in (0, 1):
        pl.when(pc.up)(lambda: along(p, z, True, True).start())
        pl.when(pc.down)(lambda: along(p, z, False, True).start())
        first(p, z, True).start()
    for p in (0, 1):
        second(p, z, 0, True).start()
        core(p, z, 0, True).start()
    yield False
    keep.wait()
    t_x().wait_recv()
    t_y().start()
    for d in range(1, Z):
        for p in (0, 1):

            def onward(zz, up, more):
                arrived(p, zz, 0)
                pl.when(more)(lambda: along(p, zz, up).start())
                first(p, zz).start()
                second(p, zz, 0).start()
                core(p, zz, 0).start()

            pl.when(z - d >= 0)(lambda: onward(z - d, True, pc.up))
            pl.when(z + d < Z)(lambda: onward(z + d, False, pc.down))
        if d == 1:
            t_y().wait_recv()
            pl.when(pc.up)(lambda: t_z(z, True).start())
            pl.when(pc.down)(lambda: t_z(z, False).start())
            t_c(z).start()
        yield False

    def hop(d):
        def onward(zz, up, more):
            t_z(zz, up).wait_recv()
            pl.when(more)(lambda: t_z(zz, up).start())
            t_c(zz).start()

        pl.when(z - d >= 0)(lambda: onward(z - d, True, pc.up))
        pl.when(z + d < Z)(lambda: onward(z + d, False, pc.down))

    near = [lax.rem(z + k, Z) for k in range(Z)]
    for k, zz in enumerate(near):
        for p in (0, 1):
            q = 2 if p == 0 else 1
            arrived(p, zz, q)
            second(p, zz, 1).start()
            core(p, zz, q).start()
        if k > 0:
            hop(k)
        yield False
    for i in (0, 1):
        for k, zz in enumerate(near):
            for p in (0, 1):
                q = (1 if i == 0 else 3) if p == 0 else (2 if i == 0 else 3)
                arrived(p, zz, q)
                core(p, zz, q).start()
            yield i == 1 and k == Z - 1
    for zz in near:
        for p in (0, 1):
            for q in range(4):
                arrived(p, zz, 4 + q)
        t_c(zz).wait_recv()
        yield True
    t_x().wait_send()
    t_y().wait_send()
    for zz in range(Z):
        for p in (0, 1):
            pl.when(pc.up & (zz <= z))(lambda: along(p, zz, True).wait_send())
            pl.when(pc.down & (zz >= z))(lambda: along(p, zz, False).wait_send())
            first(p, zz).wait_send()
            for q in (0, 1):
                second(p, zz, q).wait_send()
            for q in range(4):
                core(p, zz, q).wait_send()
        pl.when(pc.up & (zz <= z))(lambda: t_z(zz, True).wait_send())
        pl.when(pc.down & (zz >= z))(lambda: t_z(zz, False).wait_send())
        t_c(zz).wait_send()


def spread_scratch(planes):
    n = 4 * planes
    return [DMA((planes,)), DMA((planes,)), DMA((planes, 2)), DMA((n,)), DMA((n,)), DMA((n,)), DMA((3,))]


def spread_steps(pc, kv_ref, edge_ref, dec_ref, all_ref, got_ref, decs_ref, scratch):
    us, xs, cs, rs, ds, dr, one = scratch
    Z, z, x, c = pc.Z, pc.z, pc.x, pc.c
    n = 4 * Z
    me = pc.ctx

    def cp(zz, xx, sem, d, own=False):
        s = pc.spot(zz, xx, c)
        return rcopy(pc, kv_ref if own else all_ref.at[s], all_ref.at[s], sem, rs.at[s], d)

    def arrived(s):
        rcopy(pc, kv_ref, all_ref.at[s], one.at[0], rs.at[s], "c").wait_recv()

    def decay_copy(d):
        return rcopy(pc, dec_ref, decs_ref.at[me], ds.at[d], dr.at[d], (lax.rem(me + d, n), pc.y))

    edge = rcopy(pc, edge_ref, got_ref, one.at[1], one.at[2], (lax.rem(me + 1, n), pc.y))
    keep = pltpu.make_async_copy(kv_ref, all_ref.at[me], one.at[0])
    pl.when(me < n - 1)(lambda: edge.start())
    keep.start()
    pl.when(pc.up)(lambda: cp(z, x, us.at[z], "u", True).start())
    cp(z, x, xs.at[z], "x", True).start()
    cp(z, x, cs.at[z, 0], "c", True).start()
    decs_ref[me] = dec_ref[...]
    pl.loop(1, n)(lambda d: decay_copy(d).start())
    yield
    pl.when(me > 0)(lambda: edge.wait_recv())

    @pl.when(me == 0)
    def _():
        got_ref[...] = jnp.zeros_like(got_ref)

    yield
    for d in range(1, Z):

        @pl.when(z - d >= 0)
        def _():
            zz = z - d
            arrived(pc.spot(zz, x, c))
            pl.when(pc.up)(lambda: cp(zz, x, us.at[zz], "u").start())
            cp(zz, x, xs.at[zz], "x").start()
            cp(zz, x, cs.at[zz, 0], "c").start()

        yield
    for d in range(Z):

        @pl.when(z - d >= 0)
        def _():
            arrived(pc.spot(z - d, 1 - x, c))
            cp(z - d, 1 - x, cs.at[z - d, 1], "c").start()

    yield
    for d in range(Z):

        @pl.when(z - d >= 0)
        def _():
            for xx in (x, 1 - x):
                arrived(pc.spot(z - d, xx, 1 - c))

    keep.wait()
    pl.loop(1, n)(lambda d: decay_copy(d).wait_recv())
    yield
    for zz in range(Z):

        @pl.when(zz <= z)
        def _():
            pl.when(pc.up)(lambda: cp(zz, x, us.at[zz], "u").wait_send())
            cp(zz, x, xs.at[zz], "x").wait_send()
            cp(zz, x, cs.at[zz, 0], "c").wait_send()
            cp(zz, 1 - x, cs.at[zz, 1], "c").wait_send()

    pl.when(me < n - 1)(lambda: edge.wait_send())
    pl.loop(1, n)(lambda d: decay_copy(d).wait_send())


LAST = (7, 7, 16)
EARLY = (6, 6, 16)
STEP_PIECE = 512


def scatter_scratch(planes, rows, widths, shares):
    columns = sum(widths)
    a, b, w = split(columns, shares, PIECE)
    half = 4 * planes * rows
    return [
        pltpu.VMEM((planes, 2, 2, rows, columns), BF),
        pltpu.VMEM((planes, 2, rows, a + b), BF),
        pltpu.VMEM((planes, rows, a + b), BF),
        pltpu.VMEM((planes, rows, a + b), BF),
        pltpu.VMEM((planes + 1, 2, 2, rows, w), BF),
        pltpu.VMEM((3, rows, w), BF),
        pltpu.VMEM((len(widths), half, TOKENS), BF),
        pltpu.VMEM((TOKENS, columns), BF),
        DMA((len(widths),)),
        DMA((len(widths),)),
        DMA((columns // PIECE,)),
        DMA((columns // PIECE,)),
        DMA((2, planes, 2)),
        DMA((2, planes, 2)),
        DMA((2, planes)),
        DMA((2, planes)),
        DMA((3, planes)),
        DMA((3, planes + 1)),
        DMA((3,)),
        DMA((3,)),
    ]


def scatter_steps(pc, pairs, out_ref, scratch, shares):
    g, r2, r3, rz, rw, rt, la, rb, as_, ar, bs, br, s2, q2, s3, q3, sz, qz, st, qt = scratch
    Z, z, x, y, c = pc.Z, pc.z, pc.x, pc.y, pc.c
    rows = g.shape[3]
    widths = split(g.shape[-1], shares, PIECE)
    w = widths[2]
    depth = 4 * rows

    def cols(p):
        return part_columns(widths, p)

    def got(p):
        return pl.ds(p * widths[0], widths[p])

    pieces = []
    base = 0
    for i, (left, right) in enumerate(pairs):
        for at in range(0, right.shape[1], PIECE):
            pieces.append((i, at, base + at))
        base += right.shape[1]

    def acopy(i):
        return rcopy(pc, pairs[i][0].at[1 - c], la.at[i], as_.at[i], ar.at[i], "c")

    def bcopy(k):
        i, at, to = pieces[k]
        return rcopy(
            pc, pairs[i][1].at[:, pl.ds(at, PIECE)], rb.at[:, pl.ds(to, PIECE)], bs.at[k], br.at[k], "c"
        )

    def make(zz, k, first):
        i, at, to = pieces[k]
        if first:
            if at == 0:
                acopy(i).wait_recv()
            bcopy(k).wait_recv()
        here = pl.ds(pl.multiple_of(zz * depth, depth), depth)
        mine, theirs = pairs[i][0][c, here, :], la[i, here, :]
        tile = nn(mine, pairs[i][1][:, pl.ds(at, PIECE)]) + nn(theirs, rb[:, pl.ds(to, PIECE)])
        g[zz, :, :, :, pl.ds(to, PIECE)] = tile.reshape(2, 2, rows, PIECE).astype(BF)

    def copy2(p, zz, j):
        xx, yy = (x if j == 0 else 1 - x, 1 - y) if p == 0 else (1 - x, y if j == 0 else 1 - y)
        return rcopy(
            pc, g.at[zz, xx, yy, :, cols(p)], r2.at[zz, j, :, got(p)], s2.at[p, zz, j], q2.at[p, zz, j],
            "y" if p == 0 else "x",
        )

    def copy3(p, zz):
        xx, yy = (1 - x, y) if p == 0 else (x, 1 - y)
        return rcopy(
            pc, g.at[zz, xx, yy, :, cols(p)], r3.at[zz, :, got(p)], s3.at[p, zz], q3.at[p, zz],
            "x" if p == 0 else "y",
        )

    def sendz(p, zz):
        return rcopy(
            pc, g.at[zz, x, y, :, cols(p)], rz.at[z, :, got(p)], sz.at[p, zz], qz.at[p, z], pc.dev(zz, x, y, c)
        )

    def gotz(p, zz):
        rcopy(pc, g.at[0, x, y, :, cols(p)], rz.at[zz, :, got(p)], sz.at[p, 0], qz.at[p, zz], "c").wait_recv()

    def send_plane(zz, up):
        slot = jnp.where(zz == z + 1, Z, zz) if up else zz
        return rcopy(
            pc, g.at[zz, :, :, :, cols(2)], rw.at[slot], sz.at[2, zz], qz.at[2, slot], "u" if up else "d"
        )

    def got_plane(slot):
        rcopy(
            pc, g.at[0, :, :, :, cols(2)], rw.at[slot], sz.at[2, 0], qz.at[2, slot], "c"
        ).wait_recv()

    def add_plane(zz, slots):
        for xx in (0, 1):
            for yy in (0, 1):
                a = g.at[zz, xx, yy, :, cols(2)]
                add_into(a, [a] + [rw.at[k, xx, yy] for k in slots])

    def at_time(t, f):
        below, above = t - (Z - 1 - z), Z - 1 - (t - z)
        pl.when((below >= 0) & (below < z))(lambda: f(below, False, pc.up))
        pl.when((above > z) & (above < Z))(lambda: f(above, True, pc.down))

    def chain_first(zz, up, more):
        @pl.when(more)
        def _():
            got_plane(zz)
            add_plane(zz, [zz])

        send_plane(zz, up).start()

    def tail(k):
        if k < 2:
            return rcopy(pc, g.at[z, k, 1 - y, :, cols(2)], rt.at[k], st.at[k], qt.at[k], "y")
        return rcopy(pc, g.at[z, 1 - x, y, :, cols(2)], rt.at[2], st.at[2], qt.at[2], "x")

    for i in range(len(pairs)):
        acopy(i).start()
        for k in range(len(pieces)):
            if pieces[k][0] == i:
                bcopy(k).start()
    yield
    ends = {w + widths[0]: 0, w + widths[0] + widths[1]: 1}

    def own(p, zz):
        copy2(p, zz, 0).wait_recv()
        copy3(p, zz).wait_recv()
        a = g.at[zz, x, y, :, cols(p)]
        return a, [a, r2.at[zz, 0, :, got(p)], r3.at[zz, :, got(p)]]

    def gather_plane(slot):
        got_plane(slot)
        add_plane(z, [slot])

    for k in range(Z + 2):
        if k < Z:
            zz = pc.zord(k)
            for n in range(len(pieces)):
                make(zz, n, k == 0)
                end = pieces[n][2] + PIECE
                if end == w and k == 0 and Z > 1:
                    at_time(0, chain_first)
                if end in ends:
                    copy2(ends[end], zz, 1).start()
                if n == len(pieces) // 2:
                    yield
            yield
        if 0 < k <= Z:
            zz = pc.zord(k - 1)
            for p in (0, 1):
                copy2(p, zz, 1).wait_recv()
                a = g.at[(zz,) + ((1 - x, y) if p == 0 else (x, 1 - y)) + (slice(None), cols(p))]
                add_into(a, [a, r2.at[zz, 1, :, got(p)]])
                copy3(p, zz).start()
            for p in (0, 1):
                copy2(p, zz, 0).start()
            if 0 < k - 1 < Z - 1:
                at_time(k - 1, chain_first)
            yield
        if 1 < k <= Z:
            zz = pc.zord(k - 2)
            for p in (0, 1):
                a, parts = own(p, zz)
                add_into(a, parts)
                sendz(p, zz).start()
            yield
    pl.when(pc.up)(lambda: gather_plane(z))
    pl.when(pc.down)(lambda: gather_plane(Z))
    for k in (0, 1):
        tail(k).start()
    yield
    finals = []
    for p in (0, 1):
        finals.append(own(p, z)[1])
    for k in (0, 1):
        tail(k).wait_recv()
        a = g.at[z, k, y, :, cols(2)]
        add_into(a, [a, rt.at[k]])
    tail(2).start()
    yield
    for p in (0, 1):
        for d in range(1, Z):
            slot = lax.rem(z + d, Z)
            gotz(p, slot)
            finals[p].append(rz.at[slot, :, got(p)])
        add_into(out_ref.at[:, cols(p)], finals[p])
        yield
    tail(2).wait_recv()
    add_into(out_ref.at[:, cols(2)], [g.at[z, x, y, :, cols(2)], rt.at[2]])
    for i in range(len(pairs)):
        acopy(i).wait_send()
    for k in range(len(pieces)):
        bcopy(k).wait_send()
    for k in range(3):
        tail(k).wait_send()
    for zz in range(Z):
        for p in (0, 1):
            for j in (0, 1):
                copy2(p, zz, j).wait_send()
            copy3(p, zz).wait_send()
            pl.when(zz != z)(lambda: sendz(p, zz).wait_send())
        pl.when(zz < z)(lambda: send_plane(zz, False).wait_send())
        pl.when(zz > z)(lambda: send_plane(zz, True).wait_send())


def woven_scratch(planes, rows, widths):
    columns = sum(widths)
    a, b, w = split(columns, EARLY, STEP_PIECE)
    half = 4 * planes * rows
    return [
        pltpu.VMEM((planes, 2, 2, rows, columns), BF),
        pltpu.VMEM((planes, 2, rows, a + b), BF),
        pltpu.VMEM((planes, rows, a + b), BF),
        pltpu.VMEM((planes + 1, rows, a + b), BF),
        pltpu.VMEM((planes + 1, 2, 2, rows, w), BF),
        pltpu.VMEM((3, rows, w), BF),
        pltpu.VMEM((len(widths), half, TOKENS), BF),
        pltpu.VMEM((TOKENS, columns), BF),
        DMA((len(widths),)),
        DMA((len(widths),)),
        DMA((columns // STEP_PIECE,)),
        DMA((columns // STEP_PIECE,)),
        DMA((2, planes, 2)),
        DMA((2, planes, 2)),
        DMA((2, planes)),
        DMA((2, planes)),
        DMA((3, planes)),
        DMA((3, planes + 1)),
        DMA((3,)),
        DMA((3,)),
    ]


def woven_steps(pc, pairs, out_ref, scratch):
    g, r2, r3, rz, rw, rt, la, rb, as_, ar, bs, br, s2, q2, s3, q3, sz, qz, st, qt = scratch
    Z, z, x, y, c = pc.Z, pc.z, pc.x, pc.y, pc.c
    rows = g.shape[3]
    widths = split(g.shape[-1], EARLY, STEP_PIECE)
    w = widths[2]
    depth = 4 * rows

    def cols(p):
        return part_columns(widths, p)

    def got(p):
        return pl.ds(p * widths[0], widths[p])

    pieces = []
    base = 0
    for i, (left, right) in enumerate(pairs):
        for at in range(0, right.shape[1], STEP_PIECE):
            pieces.append((i, at, base + at))
        base += right.shape[1]

    def acopy(i):
        return rcopy(pc, pairs[i][0].at[1 - c], la.at[i], as_.at[i], ar.at[i], "c")

    def bcopy(k):
        i, at, to = pieces[k]
        return rcopy(
            pc, pairs[i][1].at[:, pl.ds(at, STEP_PIECE)], rb.at[:, pl.ds(to, STEP_PIECE)], bs.at[k], br.at[k], "c"
        )

    def make(zz, k, first):
        i, at, to = pieces[k]
        if first:
            if at == 0:
                acopy(i).wait_recv()
            bcopy(k).wait_recv()
        here = pl.ds(pl.multiple_of(zz * depth, depth), depth)
        mine, theirs = pairs[i][0][c, here, :], la[i, here, :]
        for t in range(0, STEP_PIECE, 512):
            tile = nn(mine, pairs[i][1][:, pl.ds(at + t, 512)]) + nn(theirs, rb[:, pl.ds(to + t, 512)])
            g[zz, :, :, :, pl.ds(to + t, 512)] = tile.reshape(2, 2, rows, 512).astype(BF)

    def copy2(p, zz, j):
        xx, yy = (x if j == 0 else 1 - x, 1 - y) if p == 0 else (1 - x, y if j == 0 else 1 - y)
        return rcopy(
            pc, g.at[zz, xx, yy, :, cols(p)], r2.at[zz, j, :, got(p)], s2.at[p, zz, j], q2.at[p, zz, j],
            "y" if p == 0 else "x",
        )

    def copy3(p, zz):
        xx, yy = (1 - x, y) if p == 0 else (x, 1 - y)
        return rcopy(
            pc, g.at[zz, xx, yy, :, cols(p)], r3.at[zz, :, got(p)], s3.at[p, zz], q3.at[p, zz],
            "x" if p == 0 else "y",
        )

    def views(p, zz, slot):
        if p == 2:
            return g.at[zz, :, :, :, cols(p)], rw.at[slot]
        return g.at[zz, x, y, :, cols(p)], rz.at[slot, :, got(p)]

    def sendz(p, zz, up):
        slot = jnp.where(zz == z + 1, Z, zz) if up else zz
        src, dst = views(p, zz, slot)
        return rcopy(pc, src, dst, sz.at[p, zz], qz.at[p, slot], "u" if up else "d")

    def gotz(p, slot):
        src, dst = views(p, 0, slot)
        rcopy(pc, src, dst, sz.at[p, 0], qz.at[p, slot], "c").wait_recv()

    def add_plane(zz, slots):
        for xx in (0, 1):
            for yy in (0, 1):
                a = g.at[zz, xx, yy, :, cols(2)]
                add_into(a, [a] + [rw.at[k, xx, yy] for k in slots])

    def at_time(t, f):
        below, above = t - (Z - 1 - z), Z - 1 - (t - z)
        pl.when((below >= 0) & (below < z))(lambda: f(below, False, pc.up))
        pl.when((above > z) & (above < Z))(lambda: f(above, True, pc.down))

    def chain_first(zz, up, more):
        @pl.when(more)
        def _():
            gotz(2, zz)
            add_plane(zz, [zz])

        sendz(2, zz, up).start()

    def tail(k):
        if k < 2:
            return rcopy(pc, g.at[z, k, 1 - y, :, cols(2)], rt.at[k], st.at[k], qt.at[k], "y")
        return rcopy(pc, g.at[z, 1 - x, y, :, cols(2)], rt.at[2], st.at[2], qt.at[2], "x")

    for i in range(len(pairs)):
        acopy(i).start()
        for k in range(len(pieces)):
            if pieces[k][0] == i:
                bcopy(k).start()
    yield
    ends = {w + widths[0]: 0, w + widths[0] + widths[1]: 1}
    for k in range(Z + 1):
        if k < Z:
            zz = pc.zord(k)
            for n in range(len(pieces)):
                make(zz, n, k == 0)
                end = pieces[n][2] + STEP_PIECE
                if end == w and k == 0 and Z > 1:
                    at_time(0, chain_first)
                if end in ends:
                    copy2(ends[end], zz, 1).start()
            yield
        if k > 0:
            zz = pc.zord(k - 1)
            for p in (0, 1):
                copy2(p, zz, 1).wait_recv()
                a = g.at[(zz,) + ((1 - x, y) if p == 0 else (x, 1 - y)) + (slice(None), cols(p))]
                add_into(a, [a, r2.at[zz, 1, :, got(p)]])
                copy3(p, zz).start()
            for p in (0, 1):
                copy2(p, zz, 0).start()
            if 0 < k - 1 < Z - 1:
                at_time(k - 1, chain_first)
            yield

    def own(p, zz):
        copy2(p, zz, 0).wait_recv()
        copy3(p, zz).wait_recv()
        a = g.at[zz, x, y, :, cols(p)]
        return a, [a, r2.at[zz, 0, :, got(p)], r3.at[zz, :, got(p)]]

    def chain(p, zz, up, more):
        a, parts = own(p, zz)

        @pl.when(more)
        def _():
            gotz(p, zz)
            add_into(a, parts + [rz.at[zz, :, got(p)]])

        @pl.when(jnp.logical_not(more))
        def _():
            add_into(a, parts)

        sendz(p, zz, up).start()

    def gather_plane(slot):
        gotz(2, slot)
        add_plane(z, [slot])

    pl.when(pc.up)(lambda: gather_plane(z))
    pl.when(pc.down)(lambda: gather_plane(Z))
    for k in (0, 1):
        tail(k).start()
    yield
    for t in range(Z - 1):
        for p in (0, 1):
            at_time(t, functools.partial(chain, p))
        if t == 0:
            for k in (0, 1):
                tail(k).wait_recv()
                a = g.at[z, k, y, :, cols(2)]
                add_into(a, [a, rt.at[k]])
            tail(2).start()
        yield
    tail(2).wait_recv()
    add_into(out_ref.at[:, cols(2)], [g.at[z, x, y, :, cols(2)], rt.at[2]])
    for p in (0, 1):
        a, parts = own(p, z)
        o = out_ref.at[:, cols(p)]
        add_into(o, parts)

        def last(slot):
            gotz(p, slot)
            add_into(o, [o, rz.at[slot, :, got(p)]])

        pl.when(pc.up)(lambda: last(z))
        pl.when(pc.down)(lambda: last(Z))
        yield
    for i in range(len(pairs)):
        acopy(i).wait_send()
    for k in range(len(pieces)):
        bcopy(k).wait_send()
    for k in range(3):
        tail(k).wait_send()
    for zz in range(Z):
        for p in (0, 1):
            for j in (0, 1):
                copy2(p, zz, j).wait_send()
            copy3(p, zz).wait_send()
        for p in (0, 1, 2):
            pl.when(zz < z)(lambda: sendz(p, zz, False).wait_send())
            pl.when(zz > z)(lambda: sendz(p, zz, True).wait_send())


def scatter_kernel(planes, count, *refs):
    pc = Place(planes)
    greet_planes(pc)
    pairs = tuple(zip(refs[:count], refs[count : 2 * count]))
    for _ in scatter_steps(pc, pairs, refs[2 * count], refs[2 * count + 1 :], LAST):
        pass


def scatter_rows(planes, lefts, rights, collective):
    rows = lefts[0].shape[1] // (4 * planes)
    widths = [r.shape[1] for r in rights]
    return pl.pallas_call(
        functools.partial(scatter_kernel, planes, len(lefts)),
        out_shape=jax.ShapeDtypeStruct((rows, sum(widths)), F32),
        in_specs=[VM] * (2 * len(lefts)),
        out_specs=VM,
        scratch_shapes=scatter_scratch(planes, rows, widths, LAST),
        compiler_params=params(collective),
    )(*lefts, *rights)


def by_core(rows, planes):
    tokens = rows.shape[0]
    each = D // (8 * planes)
    cut = rows.T.reshape(2 * planes, 2, 2 * each, tokens)
    return cut.transpose(1, 0, 2, 3).reshape(2, D // 2, tokens)


def fold_scratch(planes, rows, columns):
    return [
        pltpu.VMEM((planes, 2, rows, columns), BF),
        pltpu.VMEM((planes, rows, columns), BF),
        pltpu.VMEM((planes, rows, columns), BF),
        pltpu.VMEM((planes, 2, rows, columns), BF),
        DMA((planes, 2)),
        DMA((planes, 2)),
        DMA((planes,)),
        DMA((planes,)),
        DMA((planes,)),
        DMA((planes,)),
    ]


def fold_steps(pc, block, out_ref, scratch):
    rc, rx, rz, acc, cs, cr, xs, xr, zs, zr = scratch
    Z, z, x, c = pc.Z, pc.z, pc.x, pc.c

    def ccopy(zz, q):
        xx = x if q == 0 else 1 - x
        return rcopy(pc, block(pc.spot(zz, xx, 1 - c)), rc.at[zz, q], cs.at[zz, q], cr.at[zz, q], "c")

    def xcopy(zz):
        return rcopy(pc, acc.at[zz, 1], rx.at[zz], xs.at[zz], xr.at[zz], "x")

    def zcopy(zz):
        return rcopy(pc, acc.at[zz, 0], rz.at[zz], zs.at[zz], zr.at[zz], "d")

    def each(f):
        for zz in range(Z):
            pl.when(zz <= z)(functools.partial(f, zz))

    def a(zz):
        ccopy(zz, 1).start()
        ccopy(zz, 0).start()

    def b(zz):
        ccopy(zz, 1).wait_recv()
        add_into(acc.at[zz, 1], [block(pc.spot(zz, 1 - x, c)), rc.at[zz, 1]], 128)
        xcopy(zz).start()

    def m(zz):
        ccopy(zz, 0).wait_recv()
        add_into(acc.at[zz, 0], [block(pc.spot(zz, x, c)), rc.at[zz, 0]], 128)

    def e(zz):
        xcopy(zz).wait_recv()

        def finish(parts):
            @pl.when(zz < z)
            def _():
                add_into(acc.at[zz, 0], parts, 128)
                zcopy(zz).start()

            pl.when(zz == z)(lambda: add_into(out_ref, parts, 128))

        @pl.when(pc.up)
        def _():
            zcopy(zz).wait_recv()
            finish([acc.at[zz, 0], rx.at[zz], rz.at[zz]])

        pl.when(jnp.logical_not(pc.up))(lambda: finish([acc.at[zz, 0], rx.at[zz]]))

    def w(zz):
        ccopy(zz, 1).wait_send()
        ccopy(zz, 0).wait_send()
        xcopy(zz).wait_send()
        pl.when(zz < z)(lambda: zcopy(zz).wait_send())

    for f in (a, b, m, e):
        each(f)
        yield
    each(w)


def relay_scratch(planes):
    n = 4 * planes
    piece = pltpu.VMEM((n, NS // n, INNER), BF)
    return [piece, piece, DMA((n,)), DMA((n,)), DMA((n,)), DMA((n,))]


def relay_steps(pc, reverse, s_ref, dec_ref, out_ref, scratch):
    got, part, ss, sr, bs, br = scratch
    n = 4 * pc.Z
    me = pc.ctx

    def to(d):
        return lax.rem(me + d, n)

    def there(d):
        return rcopy(pc, s_ref.at[to(d)], got.at[me], ss.at[d], sr.at[d], (to(d), pc.y))

    def back(d):
        return rcopy(pc, part.at[to(d)], out_ref.at[me], bs.at[d], br.at[d], (to(d), pc.y))

    pl.loop(1, n)(lambda d: there(d).start())
    got[me] = s_ref[me]
    yield
    pl.loop(1, n)(lambda d: there(d).wait_recv())
    total = jnp.zeros(got.shape[1:], F32)
    for k in range(n):
        j = n - 1 - k if reverse else k
        part[j] = total.astype(BF)
        total = total * dec_ref[pl.ds(j, 1), :] + got[j].astype(F32)
    pl.loop(1, n)(lambda d: back(d).start())
    out_ref[me] = part[me]
    yield
    pl.loop(1, n)(lambda d: back(d).wait_recv())
    yield

    @pl.loop(1, n)
    def _(d):
        there(d).wait_send()
        back(d).wait_send()


def total_scratch(planes):
    shape = (SMALL_ROWS, 128)
    return [
        pltpu.VMEM((6,) + shape, F32),
        pltpu.VMEM((planes,) + shape, F32),
        DMA((3,)),
        DMA((3,)),
        DMA((planes,)),
        DMA((planes,)),
    ]


def total_steps(pc, out_ref, scratch):
    rx, rz, ss, sr, zs, zr = scratch
    Z, z = pc.Z, pc.z
    for i, d in enumerate("cxy"):
        rx[2 * i] = out_ref[...]
        cp = rcopy(pc, rx.at[2 * i], rx.at[2 * i + 1], ss.at[i], sr.at[i], d)
        cp.start()
        yield
        cp.wait()
        out_ref[...] = out_ref[...] + rx[2 * i + 1]
    rz[z] = out_ref[...]
    copies = [rcopy(pc, rz.at[z], rz.at[z], zs.at[d], zr.at[d], to) for d, to in enumerate(plane_peers(pc))]
    for cp in copies:
        cp.start()
    yield
    for cp in copies:
        cp.wait()
    total = rz[0]
    for k in range(1, Z):
        total = total + rz[k]
    out_ref[...] = total


def visible(start, block, pos_ref):
    kpos = start + lax.broadcasted_iota(jnp.int32, (block, pos_ref.shape[1]), 0)
    return (kpos <= pos_ref[0:1, :]) & (kpos >= pos_ref[1:2, :])


def split_heads(src, dst, scale=None):
    rows = src.shape[0]
    for h in range(QUERY_HEADS):
        v = src[:, pl.ds(h * HEAD_WIDTH, HEAD_WIDTH)]
        dst[pl.ds(h * rows, rows), :] = v if scale is None else v * scale


def swap_halves(v):
    width = v.shape[1]
    lane = lax.broadcasted_iota(jnp.int32, v.shape, 1)
    low = lax.rem(lane, HEAD_WIDTH) < HEAD_WIDTH // 2
    ahead = pltpu.roll(v, width - HEAD_WIDTH // 2, 1)
    behind = pltpu.roll(v, HEAD_WIDTH // 2, 1)
    return jnp.where(low, ahead, behind)


def rotate(v, cos_ref, sin_ref, sign=1.0):
    return v * cos_ref[...] + swap_halves(v) * (sign * sin_ref[...])


def attend_block(j, block, q_ref, kv, pos_ref, m_ref, l_ref, acc_ref, heads):
    rows = pos_ref.shape[1]
    start = pl.multiple_of(j * block, block)
    ok = visible(start, block, pos_ref)
    for h in heads:
        g = h // (QUERY_HEADS // KEY_VALUE_HEADS)
        keys = kv[:, g * HEAD_WIDTH : (g + 1) * HEAD_WIDTH]
        vals = kv[:, KEY_WIDTH + g * HEAD_WIDTH : KEY_WIDTH + (g + 1) * HEAD_WIDTH]
        s = jnp.where(ok, nt(keys, q_ref[pl.ds(h * rows, rows), :]), 2.0 * large_negative)
        m0 = m_ref[h : h + 1, :]
        m1 = jnp.maximum(m0, jnp.max(s, axis=0, keepdims=True))
        p = jnp.exp(s - m1)
        a = jnp.exp(m0 - m1)
        l_ref[h : h + 1, :] = l_ref[h : h + 1, :] * a + jnp.sum(p, axis=0, keepdims=True)
        m_ref[h : h + 1, :] = m1
        r = pl.ds(h * HEAD_WIDTH, HEAD_WIDTH)
        acc_ref[r, :] = acc_ref[r, :] * a + tn(vals, p.astype(BF))


def attend_end(o_ref, lse_ref, m_ref, l_ref, acc_ref):
    lse_ref[...] = m_ref[...] + jnp.log(l_ref[...])
    inv = 1.0 / l_ref[...]
    for h in range(QUERY_HEADS):
        r = pl.ds(h * HEAD_WIDTH, HEAD_WIDTH)
        acc_ref[r, :] = acc_ref[r, :] * inv[h : h + 1, :]
    o_ref[...] = acc_ref[...].T.astype(o_ref.dtype)


def attend_back_block(j, g, block, q_ref, do_ref, kv_ref, pos_ref, lse_ref, dl_ref, dkv_ref, acc_ref):
    rows = pos_ref.shape[1]
    start = pl.multiple_of(j * block, block)
    ok = visible(start, block, pos_ref)
    at = pl.ds(start, block)
    keys = kv_ref[at, pl.ds(g * HEAD_WIDTH, HEAD_WIDTH)]
    vals = kv_ref[at, pl.ds(KEY_WIDTH + g * HEAD_WIDTH, HEAD_WIDTH)]
    dk = dv = None
    for h in range(4 * g, 4 * g + 4):
        q = q_ref[pl.ds(h * rows, rows), :]
        do = do_ref[pl.ds(h * rows, rows), :]
        p = jnp.where(ok, jnp.exp(nt(keys, q) - lse_ref[h : h + 1, :]), 0.0)
        ds = (p * (nt(vals, do) - dl_ref[h : h + 1, :])).astype(BF)
        r = pl.ds(h * HEAD_WIDTH, HEAD_WIDTH)
        acc_ref[r, :] += tn(keys, ds)
        a, b = nn(ds, q), nn(p.astype(BF), do)
        dk = a if dk is None else dk + a
        dv = b if dv is None else dv + b
    dkv_ref[at, pl.ds(g * HEAD_WIDTH, HEAD_WIDTH)] = dk.astype(BF)
    dkv_ref[at, pl.ds(KEY_WIDTH + g * HEAD_WIDTH, HEAD_WIDTH)] = dv.astype(BF)


def two(left, right, lanes):
    return jnp.where(lanes < MP, left, right)


def pair_columns(ref, p, lanes):
    return two(ref[:, 2 * p : 2 * p + 1], ref[:, 2 * p + 1 : 2 * p + 2], lanes)


def mixer_steps(
    xe, mk, cw, cb, cum_t, cum, dt_t, we_t, skip, doc_c, doc_r, pre, xo, mix, so, xw, bias
):
    rows = pre.shape[0]
    for i in range(XBC // 256):
        sl = pl.ds(i * 256, 256)
        acc = jnp.broadcast_to(cb[:, sl], (rows, 256))
        for j in range(CONV):
            acc = acc + cw[j : j + 1, sl] * (xe[pl.ds(5 + j, rows), sl] * mk[:, j : j + 1])
        pre[:, sl] = acc.astype(BF)
        act = acc * jax.nn.sigmoid(acc)
        xo[:, sl] = act.astype(BF)
        if i < INNER // 256:
            mix[:, sl] = skip[:, sl] * act
        if i == 3:
            yield
    yield
    b_rows, c_rows = xo[:, pl.ds(INNER, NS)], xo[:, pl.ds(INNER + NS, NS)]
    cross = nt(c_rows, b_rows)
    t_at = lax.broadcasted_iota(jnp.int32, (rows, rows), 0)
    s_at = lax.broadcasted_iota(jnp.int32, (rows, rows), 1)
    bias[...] = jnp.where((doc_c[...] == doc_r[...]) & (s_at <= t_at), 0.0, large_negative)
    lanes = lax.broadcasted_iota(jnp.int32, (rows, 2 * MP), 1)
    for p in range(MH // 2):
        sl = pl.ds(p * 2 * MP, 2 * MP)
        xd = xo[:, sl].astype(F32) * pair_columns(dt_t, p, lanes)
        xw[:, sl] = (xd * pair_columns(we_t, p, lanes)).astype(BF)
        xb = xd.astype(BF)
        outs = []
        for h in (2 * p, 2 * p + 1):
            low = jnp.exp(jnp.minimum(cum_t[:, h : h + 1] - cum[h : h + 1, :], bias[...]))
            outs.append(nn((low * cross).astype(BF), xb))
        mix[:, sl] = mix[:, sl] + two(outs[0], outs[1], lanes)
        if p % 3 == 2:
            yield
    so[...] = tn(b_rows, xw[...]).astype(BF).reshape(so.shape)


def spread_heads():
    head = lax.broadcasted_iota(jnp.int32, (MH, INNER), 0)
    lane = lax.broadcasted_iota(jnp.int32, (MH, INNER), 1)
    return (lane // MP == head).astype(F32)


def exact(a, b, dims):
    return lax.dot_general(
        a, b, (dims, ((), ())), precision=lax.Precision.HIGHEST, preferred_element_type=F32
    )


def wide(columns, spread_mat):
    return exact(columns, spread_mat, ((1,), (0,)))


def gate_kernel(planes, lens, mix, xo, state_in, ldec, gate, small, att, mixed, branch, gain, state, din_t):
    rows = mix.shape[0]
    spread_mat = spread_heads()
    unpack(small, "gate", gain)
    state[...] = state_in[...].reshape(state.shape)
    first = Place(planes).ctx * rows
    a = lax.broadcasted_iota(jnp.int32, (rows, rows), 0)
    b = lax.broadcasted_iota(jnp.int32, (rows, rows), 1)
    docs = doc_of(first + lax.broadcasted_iota(jnp.int32, (rows, 1), 0), lens)
    before = doc_of(jnp.full((1, 1), first - 1, jnp.int32), lens)
    ct = exact((b <= a).astype(F32), ldec[...], ((1,), (1,)))
    din_t[...] = jnp.where(docs == before, jnp.exp(ct), 0.0)

    @pl.loop(0, rows // 64)
    def _(i):
        r = pl.ds(pl.multiple_of(i * 64, 64), 64)
        carried = nn(xo[r, pl.ds(INNER + NS, NS)], state[...])
        m = mix[r, :] + carried * wide(din_t[r, :], spread_mat)
        mixed[r, :] = m.astype(BF)
        gv = gate[r, :]
        gated = m * (gv * jax.nn.sigmoid(gv))
        factor = lax.rsqrt(jnp.mean(gated * gated, axis=1, keepdims=True) + norm_eps)
        branch[r, pl.ds(0, QUERY_WIDTH)] = att[r, :]
        branch[r, pl.ds(QUERY_WIDTH, INNER)] = (gated * factor * gain[...]).astype(BF)


def gate_out(planes, lens, mix, xo, state, ldec, gate, small, att):
    rows = mix.shape[0]
    return pl.pallas_call(
        functools.partial(gate_kernel, planes),
        out_shape=(
            jax.ShapeDtypeStruct((rows, INNER), BF),
            jax.ShapeDtypeStruct((rows, MIXOUT), BF),
        ),
        in_specs=[SM] + [VM] * 7,
        out_specs=(VM,) * 2,
        scratch_shapes=[
            pltpu.VMEM((1, INNER), F32),
            pltpu.VMEM((NS, INNER), BF),
            pltpu.VMEM((rows, MH), F32),
        ],
        compiler_params=params(),
    )(lens, mix, xo, state, ldec, gate, small, att)


def doc_of(pos, lens):
    start = 0
    found = jnp.full_like(pos, -1)
    for d in range(lens.shape[1]):
        found = found + (pos >= start).astype(jnp.int32)
        start = start + lens[0, d]
    return found


def begin_of(pos, lens):
    start = 0
    found = jnp.zeros_like(pos)
    for d in range(lens.shape[1]):
        found = jnp.maximum(found, jnp.where(pos >= start, start, 0))
        start = start + lens[0, d]
    return found


def table_scratch(rows):
    return [
        pltpu.VMEM((2, rows), jnp.int32),
        pltpu.VMEM((rows, 8), F32),
        pltpu.VMEM((rows, 1), jnp.int32),
        pltpu.VMEM((1, rows), jnp.int32),
        pltpu.VMEM((MH, rows), F32),
        pltpu.VMEM((rows, MH), F32),
        pltpu.VMEM((rows, MH), F32),
        pltpu.VMEM((rows, MH), F32),
        pltpu.VMEM((rows, MH), F32),
    ]


def make_tables(pc, lens, ldec, root_t, tables):
    pos, same, doc_c, doc_r, cum, cum_t, dt_t, we_t, din_t = tables
    rows = ldec.shape[1]
    first = pc.ctx * rows
    at_c = first + lax.broadcasted_iota(jnp.int32, (rows, 1), 0)
    at_r = first + lax.broadcasted_iota(jnp.int32, (1, rows), 1)
    pos[0:1, :] = at_r
    pos[1:2, :] = begin_of(at_r, lens)
    dc = doc_of(at_c, lens)
    doc_c[...] = dc
    doc_r[...] = doc_of(at_r, lens)
    for j in range(CONV):
        same[:, j : j + 1] = (doc_of(at_c - (CONV - 1) + j, lens) == dc).astype(F32)
        same[:, CONV + j : CONV + j + 1] = (doc_of(at_c + (CONV - 1) - j, lens) == dc).astype(F32)
    a = lax.broadcasted_iota(jnp.int32, (rows, rows), 0)
    b = lax.broadcasted_iota(jnp.int32, (rows, rows), 1)
    cum[...] = exact(ldec[...], (a <= b).astype(F32), ((1,), (0,)))
    ct = exact((b <= a).astype(F32), ldec[...], ((1,), (1,)))
    cum_t[...] = ct
    fresh = doc_of(at_c - 1, lens) != dc
    dt_t[...] = jnp.where(fresh, 1.0, root_t[...])
    before = doc_of(jnp.full((1, 1), first - 1, jnp.int32), lens)
    end = doc_of(jnp.full((1, 1), first + rows - 1, jnp.int32), lens)
    din_t[...] = jnp.where(dc == before, jnp.exp(ct), 0.0)
    we_t[...] = jnp.where(dc == end, jnp.exp(jnp.minimum(ct[rows - 1 : rows, :] - ct, 0.0)), 0.0)


SMALL_AT = {"one": (0, 8), "two": (8, 8), "gate": (16, 12), "bias": (84, 14), "skip": (98, 1)}


def unpack(small, name, dst, row=0):
    at, tiles = SMALL_AT[name] if isinstance(name, str) else name
    for i in range(tiles):
        dst[row : row + 1, pl.ds(i * 128, 128)] = small[at + i : at + i + 1, :]


def unpack_conv(small, dst):
    for j in range(CONV):
        unpack(small, (28 + 14 * j, 14), dst, j)


def wide_skip(small, spread_mat, dst):
    dst[...] = wide(jnp.broadcast_to(small[98:99, 0:MH], (8, MH)), spread_mat)[0:1, :]


GATE_AT = QUERY_WIDTH + 2 * KEY_WIDTH
XBC_AT = GATE_AT + INNER
FIRST = QUERY_WIDTH + 2 * KEY_WIDTH + XBC


def front_kernel(
    planes, block, lens, hid, w1, w2, cos_w, sin_w, ldec, root_t, small,
    normed, scale, g1, g2, q_out, kv_all, xe, decays, pre, xo, mix, state_in, att, lse,
    kv_own, edge_out, edge_in, dec_own, decs, dec_rows, gains, conv_w, conv_b, skip, so, qh, m_ref, l_ref,
    acc, xw, bias, *refs,
):
    tables, refs = refs[:9], refs[9:]
    pos, same, doc_c, doc_r, cum, cum_t, dt_t, we_t, din_t = tables
    first_refs, refs = refs[:9], refs[9:]
    rest_refs, refs = refs[:9], refs[9:]
    spread_refs, refs = refs[:7], refs[7:]
    relay_refs = refs[:6]
    pc = Place(planes)
    n = 4 * planes
    rows = hid.shape[0]
    greet_row(pc, True)
    gather = gather_steps(pc, w1, g1, first_refs, EVEN)
    rest = gather_steps(pc, w2, g2, rest_refs, REST)
    next(gather)

    def pump(count=1):
        for _ in range(count):
            next(rest, None)

    unpack(small, "one", gains)
    unpack(small, "bias", conv_b)
    unpack_conv(small, conv_w)
    spread_mat = spread_heads()
    wide_skip(small, spread_mat, skip)
    for i in range(rows // 64):
        r = pl.ds(i * 64, 64)
        v = hid[r, :].astype(F32)
        f = lax.rsqrt(jnp.mean(v * v, axis=1, keepdims=True) + norm_eps)
        scale[r, :] = f
        normed[r, :] = (v * f * gains[...]).astype(BF)
        next(gather)
    make_tables(pc, lens, ldec, root_t, tables)
    dec_own[...] = jnp.zeros_like(dec_own)
    dec_own[0:1, 0:MH] = din_t[rows - 1 : rows, :]
    for k, _ in enumerate(gather):
        if k == planes:
            pump()

    def project(at, width):
        return nn(normed[...], g1[:, :, :, :, :, pl.ds(at, width)].reshape(D, width))

    base = GATE_AT
    for i in range(XBC // 256):
        sl = pl.ds(i * 256, 256)
        xb = project(base + i * 256, 256).astype(BF)
        xe[pl.ds(8, rows), sl] = xb.astype(F32)
        edge_out[:, sl] = xb[rows - 16 :, :]
    kv = project(QUERY_WIDTH, 2 * KEY_WIDTH)
    kv_own[:, pl.ds(0, KEY_WIDTH)] = rotate(kv[:, :KEY_WIDTH], cos_w, sin_w).astype(BF)
    kv_own[:, pl.ds(KEY_WIDTH, KEY_WIDTH)] = kv[:, KEY_WIDTH:].astype(BF)
    spreads = spread_steps(pc, kv_own, edge_out, dec_own, kv_all, edge_in, decs, spread_refs)
    next(spreads)
    for i in range(QUERY_WIDTH // 256):
        qv = project(i * 256, 256)
        for t in (0, 1):
            q_out[:, pl.ds(i * 256 + t * 128, 128)] = rotate(
                qv[:, t * 128 : (t + 1) * 128], cos_w, sin_w
            ).astype(BF)
    split_heads(q_out, qh, jnp.asarray(HEAD_WIDTH**-0.5, BF))
    next(spreads)
    xe[pl.ds(0, 8), :] = edge_in[pl.ds(8, 8), :].astype(F32)
    pump()
    next(spreads)
    mixing = mixer_steps(
        xe, same, conv_w, conv_b, cum_t, cum, dt_t, we_t, skip, doc_c, doc_r, pre, xo, mix, so, xw, bias
    )
    for _ in mixing:
        next(spreads, None)
        pump()
    for k in range(n):
        dec_rows[k : k + 1, :] = decs[k, 0:1, :]
    decays[...] = wide(dec_rows[:, 0:MH], spread_mat)
    states = relay_steps(pc, False, so, decays, state_in, relay_refs)
    next(states)
    m_ref[...] = jnp.full_like(m_ref, large_negative)
    l_ref[...] = jnp.zeros_like(l_ref)
    acc[...] = jnp.zeros_like(acc)
    seen = (pc.ctx * rows + rows + block - 1) // block
    per = block // rows
    parts = 8
    each = n // per // parts

    def keys_at(j):
        return kv_all[pl.ds(j * per, per), :, :].reshape(block, 2 * KEY_WIDTH)

    for k in range(parts):
        lo = each * k

        @pl.loop(jnp.minimum(lo, seen), jnp.minimum(lo + each, seen))
        def _(j):
            attend_block(j, block, qh, keys_at(j), pos, m_ref, l_ref, acc, range(QUERY_HEADS))

        pump(2)
        if k in (4, 7):
            next(states)
    attend_end(att, lse, m_ref, l_ref, acc)
    for _ in spreads:
        pass
    for _ in rest:
        pass
    for _ in states:
        pass


def front(planes, lens, hid, w1, w2, cos_w, sin_w, ldec, root_t, small, block, collective):
    n = 4 * planes
    rows = hid.shape[0]
    each = w1.shape[0]
    sds = jax.ShapeDtypeStruct
    return pl.pallas_call(
        functools.partial(front_kernel, planes, block),
        out_shape=(
            sds((rows, D), BF),
            sds((rows, 1), F32),
            sds((planes, 2, 2, 2, each, w1.shape[1]), BF),
            sds((planes, 2, 2, 2, each, w2.shape[1]), BF),
            sds((rows, QUERY_WIDTH), BF),
            sds((n, rows, 2 * KEY_WIDTH), BF),
            sds((rows + 8, XBC), F32),
            sds((n, INNER), F32),
            sds((rows, XBC), BF),
            sds((rows, XBC), BF),
            sds((rows, INNER), F32),
            sds((n, NS // n, INNER), BF),
            sds((rows, QUERY_WIDTH), BF),
            sds((QUERY_HEADS, rows), F32),
        ),
        in_specs=[SM, VM, VM, HB] + [VM] * 5,
        out_specs=(VM, VM, VM, HB) + (VM,) * 10,
        scratch_shapes=[
            pltpu.VMEM((rows, 2 * KEY_WIDTH), BF),
            pltpu.VMEM((16, XBC), BF),
            pltpu.VMEM((16, XBC), BF),
            pltpu.VMEM((8, 128), F32),
            pltpu.VMEM((n, 8, 128), F32),
            pltpu.VMEM((n, 128), F32),
            pltpu.VMEM((1, D), F32),
            pltpu.VMEM((CONV, XBC), F32),
            pltpu.VMEM((1, XBC), F32),
            pltpu.VMEM((1, INNER), F32),
            pltpu.VMEM((n, NS // n, INNER), BF),
            pltpu.VMEM((QUERY_HEADS * rows, HEAD_WIDTH), BF),
            pltpu.VMEM((QUERY_HEADS, rows), F32),
            pltpu.VMEM((QUERY_HEADS, rows), F32),
            pltpu.VMEM((QUERY_WIDTH, rows), F32),
            pltpu.VMEM((rows, INNER), BF),
            pltpu.VMEM((rows, rows), F32),
        ]
        + table_scratch(rows)
        + gather_scratch(planes)
        + gather_scratch(planes)
        + spread_scratch(planes)
        + relay_scratch(planes),
        compiler_params=params(collective),
    )(lens, hid, w1, w2, cos_w, sin_w, ldec, root_t, small)


def gate_back_rows(i, grad, mixed, gate, gain, din_t, spread_mat, dm, dproj, dgain, dinc):
    r = pl.ds(pl.multiple_of(i * 64, 64), 64)
    m, gv, gr = mixed[r, :].astype(F32), gate[r, :], grad[r, pl.ds(QUERY_WIDTH, INNER)]
    sig = jax.nn.sigmoid(gv)
    sil = gv * sig
    gated = m * sil
    factor = lax.rsqrt(jnp.mean(gated * gated, axis=1, keepdims=True) + norm_eps)
    w = gr * gain[...]
    dg = factor * (w - gated * factor * factor * jnp.mean(w * gated, axis=1, keepdims=True))
    dgain[...] += jnp.sum(gr * gated * factor, axis=0, keepdims=True)
    dproj[r, pl.ds(GATE_AT, INNER)] = (dg * m * (sig * (1.0 + gv * (1.0 - sig)))).astype(BF)
    d = dg * sil
    dm[r, :] = d.astype(BF)
    dinc[r, :] = (d * wide(din_t[r, :], spread_mat)).astype(BF)


def mixer_back_steps(
    xe, mk, cw, cum_t, cum, dt_t, we_t, skip, doc_c, doc_r, pre, xo, dm, dc_in, ds, dpre, dcw, dskip, xw, bias
):
    rows = pre.shape[0]
    here = pl.ds(0, rows)
    b_rows, c_rows = xo[:, pl.ds(INNER, NS)], xo[:, pl.ds(INNER + NS, NS)]
    cross = nt(b_rows, c_rows)
    s_at = lax.broadcasted_iota(jnp.int32, (rows, rows), 0)
    t_at = lax.broadcasted_iota(jnp.int32, (rows, rows), 1)
    bias[...] = jnp.where((doc_c[...] == doc_r[...]) & (s_at <= t_at), 0.0, large_negative)
    lanes = lax.broadcasted_iota(jnp.int32, (rows, 2 * MP), 1)

    def slope(sl):
        v = pre[:, sl].astype(F32)
        sig = jax.nn.sigmoid(v)
        return sig * (1.0 + v * (1.0 - sig))

    dcross = jnp.zeros((rows, rows), F32)
    for p in range(MH // 2):
        sl = pl.ds(p * 2 * MP, 2 * MP)
        xv = xo[:, sl].astype(F32)
        dt2, we2 = pair_columns(dt_t, p, lanes), pair_columns(we_t, p, lanes)
        xd = xv * dt2
        xw[:, sl] = (xd * we2).astype(BF)
        g = dm[:, sl]
        outs = []
        for k in (0, 1):
            h = 2 * p + k
            low = jnp.exp(jnp.minimum(cum[h : h + 1, :] - cum_t[:, h : h + 1], bias[...]))
            outs.append(nn((low * cross).astype(BF), g))
            part = jnp.where((lanes < MP) == (k == 0), xd, 0.0).astype(BF)
            dcross = dcross + nt(part, g) * low
        dxd = two(outs[0], outs[1], lanes) + we2 * nn(b_rows, ds[:, sl])
        gf = g.astype(F32)
        dskip[:, sl] = jnp.sum(gf * xv, axis=0, keepdims=True)
        dpre[here, sl] = (dxd * dt2 + skip[:, sl] * gf) * slope(sl)
        if p % 4 == 3:
            yield
    db16 = dcross.astype(BF)
    slb, slc = pl.ds(INNER, NS), pl.ds(INNER + NS, NS)
    dpre[here, slb] = (nn(db16, c_rows) + nt(xw[...], ds[...])) * slope(slb)
    dpre[here, slc] = (tn(db16, b_rows) + dc_in[...]) * slope(slc)
    yield
    for i in range(XBC // 256):
        sl = pl.ds(i * 256, 256)
        d = dpre[here, sl]
        for j in range(CONV):
            dcw[j : j + 1, sl] = jnp.sum(
                d * (xe[pl.ds(5 + j, rows), sl] * mk[:, j : j + 1]), axis=0, keepdims=True
            )
        dcw[CONV : CONV + 1, sl] = jnp.sum(d, axis=0, keepdims=True)


def back_kernel(planes, count, block, *refs):
    lefts, rights, refs = refs[:count], refs[count : 2 * count], refs[2 * count :]
    if count:
        branch = rights[0]
    else:
        branch, refs = refs[0], refs[1:]
    (
        lens, grad, mixed, gate, xo, state_in, q_in, kv, lse, cos_w, sin_w, decays, xe, ldec, root_t, small, pre,
    ) = refs[:17]
    refs = refs[17:]
    if count:
        scattered, refs = refs[0], refs[1:]
    dproj, dgain, dcw, dskip = refs[:4]
    (
        dm, dinc, dc, dstate, dsnew, flat, qh, doh, dl, acc, dkv, dkv_own, dpre, edge, bias, esem
    ) = refs[4:20]
    gain, cw, skip, state = refs[20:24]
    tables, refs = refs[24:33], refs[33:]
    pos, same, doc_c, doc_r, cum, cum_t, dt_t, we_t, din_t = tables
    relay_refs, refs = refs[:6], refs[6:]
    fold_refs, refs = refs[:10], refs[10:]
    pc = Place(planes)
    n = 4 * planes
    rows = mixed.shape[0]
    greet_row(pc, count > 0)
    side = (
        woven_steps(pc, tuple(zip(lefts, rights)), scattered, refs) if count else iter(())
    )

    def pump():
        next(side, None)

    pump()
    spread_mat = spread_heads()
    unpack(small, "gate", gain)
    unpack_conv(small, cw)
    wide_skip(small, spread_mat, skip)
    make_tables(pc, lens, ldec, root_t, tables)
    state[...] = state_in[...].reshape(state.shape)
    dgain[...] = jnp.zeros_like(dgain)
    pl.loop(0, rows // 64)(
        lambda i: gate_back_rows(i, grad, mixed, gate, gain, din_t, spread_mat, dm, dproj, dgain, dinc)
    )
    ds0 = tn(xo[:, pl.ds(INNER + NS, NS)], dinc[...]).astype(BF)
    dc[...] = nt(dinc[...], state[...])
    dstate[...] = ds0.reshape(dstate.shape)
    states = relay_steps(pc, True, dstate, decays, dsnew, relay_refs)
    next(states)
    for _ in range(planes):
        pump()
    split_heads(q_in, qh, jnp.asarray(HEAD_WIDTH**-0.5, BF))
    go = grad[:, pl.ds(0, QUERY_WIDTH)].astype(BF)
    head = lax.broadcasted_iota(jnp.int32, (QUERY_HEADS, QUERY_WIDTH), 0)
    lane = lax.broadcasted_iota(jnp.int32, (QUERY_HEADS, QUERY_WIDTH), 1)
    for h in range(QUERY_HEADS):
        doh[pl.ds(h * rows, rows), :] = go[:, h * HEAD_WIDTH : (h + 1) * HEAD_WIDTH]
    dl[...] = exact(
        (lane // HEAD_WIDTH == head).astype(F32),
        go.astype(F32) * branch[:, pl.ds(0, QUERY_WIDTH)].astype(F32),
        ((1,), (1,)),
    )
    acc[...] = jnp.zeros_like(acc)
    total = kv.shape[0] // block
    seen = (pc.ctx * rows + rows + block - 1) // block
    parts = 4
    each = total // parts

    @pl.loop(seen, (pc.z + 1) * 4 * rows // block)
    def _(j):
        dkv[pl.ds(pl.multiple_of(j * block, block), block), :] = jnp.zeros((block, 2 * KEY_WIDTH), BF)

    for k in range(parts):
        lo = each * k

        @pl.loop(jnp.minimum(lo, seen), jnp.minimum(lo + each, seen))
        def _(j):
            for g in range(KEY_VALUE_HEADS):
                attend_back_block(j, g, block, qh, doh, kv, pos, lse, dl, dkv, acc)

        pump()
        if k == 1:
            next(states)
    folds = fold_steps(
        pc, lambda s: dkv.at[pl.ds(pl.multiple_of(s * rows, rows), rows), :], dkv_own, fold_refs
    )
    next(folds)
    for t in range(QUERY_WIDTH // 128):
        dq = acc[pl.ds(t * 128, 128), :].T * (HEAD_WIDTH**-0.5)
        dproj[:, pl.ds(t * 128, 128)] = rotate(dq, cos_w, sin_w, -1.0).astype(BF)
    next(states)
    flat[...] = dsnew[...].reshape(flat.shape)
    next(folds)
    mixing = mixer_back_steps(
        xe, same, cw, cum_t, cum, dt_t, we_t, skip, doc_c, doc_r, pre, xo, dm, dc, flat, dpre, dcw, dskip, dinc, bias
    )
    next(mixing)
    next(folds)
    pump()
    next(mixing)
    pump()
    next(mixing)
    next(folds)
    pump()
    next(mixing)
    prior = rcopy(pc, dpre.at[pl.ds(0, 8), :], edge, esem.at[0], esem.at[1], (lax.rem(pc.ctx + n - 1, n), pc.y))
    pl.when(pc.ctx > 0)(lambda: prior.start())
    for _ in mixing:
        pass
    pump()
    for _ in folds:
        pass
    dproj[:, pl.ds(QUERY_WIDTH, KEY_WIDTH)] = rotate(dkv_own[:, pl.ds(0, KEY_WIDTH)], cos_w, sin_w, -1.0).astype(BF)
    dproj[:, pl.ds(QUERY_WIDTH + KEY_WIDTH, KEY_WIDTH)] = dkv_own[:, pl.ds(KEY_WIDTH, KEY_WIDTH)].astype(BF)
    pl.when(pc.ctx < n - 1)(lambda: prior.wait_recv())

    @pl.when(pc.ctx == n - 1)
    def _():
        edge[...] = jnp.zeros_like(edge)

    dpre[pl.ds(rows, 8), :] = edge[...]
    for i in range(XBC // 256):
        sl = pl.ds(i * 256, 256)
        total_grad = jnp.zeros((rows, 256), F32)
        for j in range(CONV):
            total_grad = total_grad + cw[j : j + 1, sl] * (
                dpre[pl.ds(CONV - 1 - j, rows), sl] * same[:, CONV + j : CONV + j + 1]
            )
        dproj[:, pl.ds(XBC_AT + i * 256, 256)] = total_grad.astype(BF)
    for _ in states:
        pass
    pl.when(pc.ctx > 0)(lambda: prior.wait_send())
    for _ in side:
        pass


def back(planes, lefts, rights, args, block, collective):
    count = len(lefts)
    n = 4 * planes
    rows = args[-1].shape[0]
    keys = n * rows
    outs = [
        jax.ShapeDtypeStruct((rows, MIXIN), BF),
        jax.ShapeDtypeStruct((1, INNER), F32),
        jax.ShapeDtypeStruct((CONV + 1, XBC), F32),
        jax.ShapeDtypeStruct((1, INNER), F32),
    ]
    scratch = [
        pltpu.VMEM((rows, INNER), BF),
        pltpu.VMEM((rows, INNER), BF),
        pltpu.VMEM((rows, NS), F32),
        pltpu.VMEM((n, NS // n, INNER), BF),
        pltpu.VMEM((n, NS // n, INNER), BF),
        pltpu.VMEM((NS, INNER), BF),
        pltpu.VMEM((QUERY_HEADS * rows, HEAD_WIDTH), BF),
        pltpu.VMEM((QUERY_HEADS * rows, HEAD_WIDTH), BF),
        pltpu.VMEM((QUERY_HEADS, rows), F32),
        pltpu.VMEM((QUERY_WIDTH, rows), F32),
        pltpu.VMEM((keys, 2 * KEY_WIDTH), BF),
        pltpu.VMEM((rows, 2 * KEY_WIDTH), F32),
        pltpu.VMEM((rows + 8, XBC), F32),
        pltpu.VMEM((8, XBC), F32),
        pltpu.VMEM((rows, rows), F32),
        DMA((2,)),
        pltpu.VMEM((1, INNER), F32),
        pltpu.VMEM((CONV, XBC), F32),
        pltpu.VMEM((1, INNER), F32),
        pltpu.VMEM((NS, INNER), BF),
    ]
    scratch += table_scratch(rows)
    scratch += relay_scratch(planes) + fold_scratch(planes, rows, 2 * KEY_WIDTH)
    if count:
        widths = [r.shape[1] for r in rights]
        each = lefts[0].shape[1] // n
        outs = [jax.ShapeDtypeStruct((each, sum(widths)), F32)] + outs
        scratch += woven_scratch(planes, each, widths)
    return pl.pallas_call(
        functools.partial(back_kernel, planes, count, block),
        out_shape=tuple(outs),
        in_specs=[VM] * (2 * count + (not count)) + [SM] + [VM] * (len(args) - 2 + bool(count)),
        out_specs=(VM,) * len(outs),
        scratch_shapes=scratch,
        compiler_params=params(collective),
    )(*lefts, *rights, *args)


def last_kernel(
    planes, left, dproj, w1, w2, tok, scale, packed, dres, small, scattered, dhid, totals, dn, wg, wsem, gain, *scratch
):
    pc = Place(planes)
    greet_planes(pc)
    rows = dproj.shape[0]
    fetch = pltpu.make_async_copy(w2.at[:, :, :, :, :, pl.ds(0, INNER)], wg, wsem)
    fetch.start()
    side = scatter_steps(pc, ((left, dproj),), scattered, scratch[6:], LAST)
    next(side)
    unpack(packed, "one", gain)
    fetch.wait()
    next(side)
    part = planes // 4
    for i in range(4):
        at = pl.ds(i * part, part)
        a, b = w1[at].reshape(D // 4, FIRST), wg[at].reshape(D // 4, INNER)
        dn[:, pl.ds(i * 256, 256)] = (
            nt(dproj[:, pl.ds(0, GATE_AT)], a[:, :GATE_AT])
            + nt(dproj[:, pl.ds(GATE_AT, INNER)], b)
            + nt(dproj[:, pl.ds(XBC_AT, XBC)], a[:, GATE_AT:])
        )
        next(side)
        next(side)
    totals[...] = small[...]
    for i in range(rows // 64):
        r = pl.ds(i * 64, 64)
        v, g, f = tok[r, :].astype(F32), dn[r, :], scale[r, :]
        w = g * gain[...]
        dhid[r, :] = dres[r, :] + f * (w - v * f * f * jnp.mean(w * v, axis=1, keepdims=True))
        part = jnp.sum(g * v * f, axis=0, keepdims=True)
        for t in range(D // 128):
            totals[t : t + 1, :] = totals[t : t + 1, :] + part[:, t * 128 : (t + 1) * 128]
    sums = total_steps(pc, totals, scratch[:6])
    next(sums)
    for _ in side:
        next(sums, None)
    for _ in sums:
        pass


def last(planes, left, dproj, w1, w2, tok, scale, packed, dres, small, collective):
    rows = dproj.shape[0]
    each = left.shape[1] // (4 * planes)
    return pl.pallas_call(
        functools.partial(last_kernel, planes),
        out_shape=(
            jax.ShapeDtypeStruct((each, MIXIN), F32),
            jax.ShapeDtypeStruct((rows, D), F32),
            jax.ShapeDtypeStruct((SMALL_ROWS, 128), F32),
        ),
        in_specs=[VM] * 3 + [HB] + [VM] * 5,
        out_specs=(VM,) * 3,
        scratch_shapes=[
            pltpu.VMEM((rows, D), F32),
            pltpu.VMEM(w2.shape[:-1] + (INNER,), BF),
            DMA,
            pltpu.VMEM((1, D), F32),
        ]
        + total_scratch(planes)
        + scatter_scratch(planes, each, [MIXIN], LAST),
        compiler_params=params(collective),
    )(left, dproj, w1, w2, tok, scale, packed, dres, small)


def doc_layout(lengths, token_positions):
    starts = jnp.cumsum(lengths) - lengths
    inside = token_positions[:, None] >= starts[None, :]
    document_index = jnp.sum(inside.astype(jnp.int32), axis=1) - 1
    begins = jnp.max(jnp.where(inside, starts[None, :], 0), axis=1)
    return (document_index, token_positions - begins)


def rope_tables(rel_pos):
    half_dim = HEAD_WIDTH // 2
    inv_freq = rope_base ** (-2.0 * jnp.arange(half_dim, dtype=jnp.float32) / HEAD_WIDTH)
    angles = rel_pos.astype(jnp.float32)[:, None] * inv_freq[None, :]
    return (jnp.cos(angles), jnp.sin(angles))


def norm_backward(grad_normed, values, factor, gain_vals):
    weighted = grad_normed * gain_vals
    grad_values = factor * (
        weighted - values * factor * factor * jnp.mean(weighted * values, axis=1, keepdims=True)
    )
    grad_gain = jnp.sum(grad_normed * values * factor, axis=0)
    return (grad_values, grad_gain)


def adamw_step(param_vals, grad_vals, first_vals, second_vals, weight_decay):
    first_new = beta_one * first_vals + (1.0 - beta_one) * grad_vals
    second_new = beta_two * second_vals + (1.0 - beta_two) * grad_vals * grad_vals
    update = (
        first_new
        / (1.0 - beta_one**STEP)
        / (jnp.sqrt(second_new / (1.0 - beta_two**STEP)) + adam_eps)
    )
    return (param_vals - learn_rate * (update + weight_decay * param_vals), first_new, second_new)


def adam_direction(grad_vals, first_vals, second_vals):
    first_new = beta_one * first_vals + (1.0 - beta_one) * grad_vals
    second_new = beta_two * second_vals + (1.0 - beta_two) * grad_vals * grad_vals
    update = (
        first_new
        / (1.0 - beta_one**STEP)
        / (jnp.sqrt(second_new / (1.0 - beta_two**STEP)) + adam_eps)
    )
    return (update, first_new, second_new)


def shards(
    planes,
    hidden,
    out_grad,
    decay_log,
    doc_lengths,
    weights,
    first_moment,
    second_moment,
    small_params,
    small_first,
    small_second,
):
    local_rows = hidden.shape[1]
    count = 4 * planes
    ctx_index = lax.axis_index("ctx")
    first_pos = ctx_index * local_rows
    contract_last = (((1,), (1,)), ((), ()))
    lengths = doc_lengths[0]
    token_positions = first_pos + jnp.arange(local_rows, dtype=jnp.int32)
    cosine_table, sine_table = rope_tables(doc_layout(lengths, token_positions)[1])
    cos_wide = jnp.tile(cosine_table, (1, 4))
    sin_wide = jnp.tile(jnp.concatenate([-sine_table, sine_table], axis=1), (1, 2))
    size = small_params.shape[0]
    packed = jnp.pad(small_params, (0, SMALL_ROWS * 128 - size)).reshape(SMALL_ROWS, 128)
    log_decay = decay_log[0]
    root_t = jnp.sqrt(-jnp.expm1(2.0 * log_decay)).T
    block = 512
    own_b = weights.astype(jnp.bfloat16)
    own_first = jnp.concatenate([own_b[:, :GATE_AT], own_b[:, XBC_AT:MIXIN]], axis=1)
    own_rest = jnp.concatenate([own_b[:, GATE_AT:XBC_AT], own_b[:, MIXIN:]], axis=1)
    (
        normed_one, scale_one, first_w, rest_w, query_rows, kv_all, xe, decays, pre, xo, mix_local,
        state_in, attended, log_sums,
    ) = front(
        planes, doc_lengths, hidden[0], own_first, own_rest, cos_wide, sin_wide, log_decay, root_t,
        packed, block, 0,
    )
    rest_flat = rest_w.reshape(D, rest_w.shape[-1])
    mixout_w = rest_flat[:, INNER : INNER + MIXOUT]
    mlp_w = rest_flat[:, INNER + MIXOUT :]
    gate_in = jnp.dot(normed_one, rest_flat[:, :INNER], preferred_element_type=jnp.float32)
    mixed, branch = gate_out(
        planes, doc_lengths, mix_local, xo, state_in, log_decay, gate_in, packed, attended
    )

    tok_f = hidden[0].astype(jnp.float32)
    gain_two = small_params[D : 2 * D]
    resid_one = tok_f + lax.dot_general(
        branch, mixout_w, contract_last, preferred_element_type=jnp.float32
    )
    scale_two = lax.rsqrt(jnp.mean(resid_one * resid_one, axis=1, keepdims=True) + norm_eps)
    normed_two = (resid_one * scale_two * gain_two).astype(jnp.bfloat16)
    gate_up = jnp.dot(normed_two, mlp_w[:, : 2 * FF], preferred_element_type=jnp.float32)
    gate_part = gate_up[:, :FF]
    up_part = gate_up[:, FF:]
    sigma_gate = jax.nn.sigmoid(gate_part)
    silu_gate = gate_part * sigma_gate
    hidden_mid = (silu_gate * up_part).astype(jnp.bfloat16)
    block_out = resid_one + lax.dot_general(
        hidden_mid, mlp_w[:, 2 * FF :], contract_last, preferred_element_type=jnp.float32
    )
    out_hidden = block_out.astype(jnp.bfloat16)[None]
    grad_out = out_grad[0]
    grad_mid = jnp.dot(grad_out, mlp_w[:, 2 * FF :], preferred_element_type=jnp.float32)
    silu_slope = sigma_gate * (1.0 + gate_part * (1.0 - sigma_gate))
    grad_gate_up = jnp.concatenate(
        [grad_mid * up_part * silu_slope, grad_mid * silu_gate], axis=1
    ).astype(jnp.bfloat16)
    grad_normed_two = lax.dot_general(
        grad_gate_up, mlp_w[:, : 2 * FF], contract_last, preferred_element_type=jnp.float32
    )
    grad_norm_two, grad_gain_two = norm_backward(grad_normed_two, resid_one, scale_two, gain_two)
    grad_resid_one = grad_out.astype(jnp.float32) + grad_norm_two
    grad_resid_b = grad_resid_one.astype(jnp.bfloat16)

    grad_branch = jnp.dot(grad_resid_b, mixout_w, preferred_element_type=jnp.float32)
    lefts = [by_core(v, planes) for v in (grad_resid_b, normed_two, grad_out)]
    rights = [branch, grad_gate_up, hidden_mid]
    args = (
        doc_lengths, grad_branch, mixed, gate_in, xo, state_in, query_rows,
        kv_all.reshape(count * local_rows, 2 * KEY_WIDTH), log_sums, cos_wide, sin_wide, decays,
        xe, log_decay, root_t, packed, pre,
    )
    if planes <= 4:
        early, grad_proj, gate_gain_grads, conv_grads, skip_grads = back(
            planes, lefts, rights, args, block, 3
        )
    else:
        early = scatter_rows(planes, lefts, rights, 4)
        grad_proj, gate_gain_grads, conv_grads, skip_grads = back(planes, [], [], (branch,) + args, block, 3)
    small_local = jnp.concatenate(
        [
            jnp.zeros((D,), jnp.float32),
            grad_gain_two,
            gate_gain_grads[0],
            conv_grads.reshape(-1),
            jnp.sum(skip_grads.reshape(MH, MP), axis=1),
        ]
    )
    padded = jnp.pad(small_local, (0, SMALL_ROWS * 128 - size)).reshape(SMALL_ROWS, 128)
    mixin_grads, grad_hidden, totals = last(
        planes, by_core(normed_one, planes), grad_proj, first_w, rest_w, hidden[0], scale_one,
        packed, grad_resid_one, padded, 5,
    )
    grad_hidden = grad_hidden[None]
    small_grads = totals.reshape(-1)[:size]
    grad_weights = jnp.concatenate([mixin_grads, early], axis=1)
    new_weights, new_first, new_second = adamw_step(
        weights, grad_weights, first_moment, second_moment, decay_rate
    )
    small_step, small_first_new, small_second_new = adam_direction(
        small_grads, small_first, small_second
    )
    return (
        out_hidden,
        grad_hidden,
        grad_weights,
        new_weights,
        new_first,
        new_second,
        small_grads,
        small_step,
        small_first_new,
        small_second_new,
    )


def solution(mesh):
    placed = (
        P("fsdp", "ctx", None),
        P("fsdp", "ctx", None),
        P("fsdp", None, "ctx"),
        P("fsdp", None),
        P(("ctx", "fsdp"), None),
        P(("ctx", "fsdp"), None),
        P(("ctx", "fsdp"), None),
        P(),
        P(),
        P(),
    )
    return jax.shard_map(
        functools.partial(shards, mesh.shape["ctx"] // 4),
        mesh=mesh,
        in_specs=placed,
        out_specs=(
            P("fsdp", "ctx", None),
            P("fsdp", "ctx", None),
            P(("ctx", "fsdp"), None),
            P(("ctx", "fsdp"), None),
            P(("ctx", "fsdp"), None),
            P(("ctx", "fsdp"), None),
            P(),
            P(),
            P(),
            P(),
        ),
        check_vma=False,
    )
```
